32 devices in a mesh: dp: 8 (over z, x), mp: 4 (over y, core).
Axes of the slice: x: 2, y: 2, z: 4, core: 2. Of those that a mesh axis runs over, the one named last changes fastest.
Arguments:
- tokens: bfloat16 [15360, 512], P('dp'), may hold values from -6 to 6
- cotangent: bfloat16 [15360, 512], P('dp'), may hold values from -6 to 6
- context_sizes: int32 [8, 5], P('dp'), may hold values from 100 to 800, as said below
- query_hoods: int32 [2560], P('dp'), may hold values from 0 to 4
- owners: int32 [64], replicated, may hold values from 0 to 63, as said below
- master_blocks: float32 [64, 512, 128], P('dp', 'mp')
- first_blocks: float32 [64, 512, 128], P('dp', 'mp')
- second_blocks: float32 [64, 512, 128], P('dp', 'mp'), as said below
- left_blocks: float32 [64, 512, 128], P('dp', 'mp'), as said below
- right_blocks: float32 [64, 512, 128], P('dp', 'mp'), as said below
- left_bases: float32 [64, 512, 128], P('dp', 'mp'), may hold values from -1 to 1, as said below
- right_bases: float32 [64, 512, 128], P('dp', 'mp'), may hold values from -1 to 1, as said below
- vector_master: float32 [4096], P(('dp', 'mp'))
- vector_moment: float32 [4096], P(('dp', 'mp')), may hold values from -80 to 80
- vector_square: float32 [4096], P(('dp', 'mp')), may hold values from 399.36 to 6451.2
Outputs:
- layer_out: float32 [15360, 512], P(('dp', 'mp'))
- tokens_grad: float32 [15360, 512], P(('dp', 'mp'))
- first_moment: float32 [64, 512, 128], P('dp', 'mp')
- second_moment: float32 [64, 512, 128], P('dp', 'mp')
- left_stats: float32 [64, 512, 128], P('dp', 'mp')
- right_stats: float32 [64, 512, 128], P('dp', 'mp')
- left_rotation: float32 [64, 512, 128], P('dp', 'mp')
- right_rotation: float32 [64, 512, 128], P('dp', 'mp')
- master_weight: float32 [64, 512, 128], P('dp', 'mp')
- vector_first: float32 [4096], P(('dp', 'mp'))
- vector_second: float32 [4096], P(('dp', 'mp'))
- vector_weight: float32 [4096], P(('dp', 'mp'))
The draws below stay inside these ranges and needn't reach their ends.
Inputs may be any that keep to these rules, and one draw needn't show every extreme that they name: `context_sizes`: row g holds the 5 context sizes of group g, which sum to 1600; in every row exactly one size is 800 and the smallest is 100 or more. `owners`: a permutation of the 64 slots. `second_blocks`: positive. `left_blocks`: each block is symmetric and positive definite. `right_blocks`: each block is symmetric and positive definite. `left_bases`: each block is orthogonal. `right_bases`: each block is orthogonal.
All inputs are finite; a program needn't handle non-finite values.
Results may differ from the reference program's by a relative error of at most 0.028.
Values may be sent and summed in bfloat16 or wider, within the bound.
A program may use at most 192 MiB of HBM per device.

```python
import math
import jax
import jax.numpy as jnp
from jax import lax

D = 512
HD = 128
FF = 1024
LAYERS = 2
BLK = 128
STEP = 10
SEG_DEV = 5
CTX_FLOOR = 100
CTX_DEV = 1600
QRY_DEV = 320
TOK_DEV = 1920
TOKENS = 15360
CTX_MOST = 800
FFS = 256
NVEC = 8
NBLK = 64
N_DP = 8
N_MP = 4


GRAD_FACTORS = (0.5, 0.07, 0.35, 0.45)


def block_order(key):
    return jax.random.permutation(jax.random.fold_in(key, 11), NBLK).astype(jnp.int32)


def slot_factor(key, factors):
    inverse = jnp.argsort(block_order(key))
    place = inverse % (NBLK // LAYERS)
    first_end = D // BLK * (3 * HD // BLK)
    second_end = first_end + HD // BLK * (D // BLK)
    third_end = second_end + D // BLK * (FFS // BLK)
    picked = jnp.where(place < first_end, factors[0], jnp.where(place < second_end, factors[1], jnp.where(place < third_end, factors[2], factors[3])))
    return picked.astype(jnp.float32).reshape(NBLK, 1, 1, 1)


def grad_size(key):
    return slot_factor(key, GRAD_FACTORS) * math.sqrt(TOKENS)


def draw_context_sizes(key, part):
    rest = CTX_DEV - CTX_MOST - (SEG_DEV - 1) * CTX_FLOOR
    cuts = jnp.sort(jax.random.randint(jax.random.fold_in(key, 101), (N_DP, SEG_DEV - 2), 0, rest + 1), axis=1).astype(jnp.int32)
    bounds = jnp.concatenate([jnp.zeros((N_DP, 1), jnp.int32), cuts, jnp.full((N_DP, 1), rest, jnp.int32)], axis=1)
    others = CTX_FLOOR + (bounds[:, 1:] - bounds[:, :-1])
    place = jax.random.randint(jax.random.fold_in(key, 102), (N_DP, 1), 0, SEG_DEV).astype(jnp.int32)
    index = jnp.arange(SEG_DEV, dtype=jnp.int32)[None, :]
    source = jnp.clip(jnp.where(index < place, index, index - 1), 0, SEG_DEV - 2)
    picked = jnp.take_along_axis(others, source, axis=1)
    return jnp.where(index == place, CTX_MOST, picked).astype(jnp.int32)


def draw_owners(key, part):
    return block_order(key)


def draw_master_blocks(key, part):
    spread = slot_factor(key, (D ** (-0.5), 10.0 * D ** (-0.5), D ** (-0.5), FF ** (-0.5)))
    shape = (NBLK, N_MP, BLK, BLK)
    values = jax.random.truncated_normal(jax.random.fold_in(key, 21), -4.0, 4.0, shape, jnp.float32)
    return (values * spread).reshape(NBLK, N_MP * BLK, BLK)


def draw_first_blocks(key, part):
    shape = (NBLK, N_MP, BLK, BLK)
    values = jax.random.truncated_normal(jax.random.fold_in(key, 31), -4.0, 4.0, shape, jnp.float32)
    return (values * 0.111 * grad_size(key)).reshape(NBLK, N_MP * BLK, BLK)


def draw_second_blocks(key, part):
    shape = (NBLK, N_MP, BLK, BLK)
    factor = jnp.exp(jax.random.uniform(jax.random.fold_in(key, 41), shape, jnp.float32, math.log(0.5), math.log(8.0)))
    sizes = grad_size(key)
    return (0.0526 * sizes * sizes * factor).reshape(NBLK, N_MP * BLK, BLK)


def draw_stats(key, salt):
    shape = (NBLK, N_MP, BLK, BLK)
    sizes = grad_size(key)
    base = 0.0526 * BLK * sizes * sizes
    diagonal = base * jnp.exp(jax.random.uniform(jax.random.fold_in(key, salt), (NBLK, N_MP, BLK, 1), jnp.float32, 0.0, math.log(4.0)))
    noise = jax.random.uniform(jax.random.fold_in(key, salt + 1), shape, jnp.float32, -1.0, 1.0)
    symmetric = 0.5 * (noise + jnp.swapaxes(noise, -1, -2))
    bound = 0.2
    offdiag = symmetric * bound * base / BLK
    indices = jnp.arange(BLK)
    result = jnp.where(indices[:, None] == indices[None, :], diagonal, offdiag)
    return result.reshape(NBLK, N_MP * BLK, BLK)


def draw_left_blocks(key, part):
    return draw_stats(key, 51)


def draw_right_blocks(key, part):
    return draw_stats(key, 61)


def draw_bases(key, salt):
    signs = jnp.where(jax.random.bernoulli(jax.random.fold_in(key, salt), 0.5, (NBLK, N_MP, BLK, 1)), 1.0, -1.0)
    scores = jax.random.randint(jax.random.fold_in(key, salt + 1), (NBLK, N_MP, 1, BLK), 0, 2 ** 20) * BLK + jnp.arange(BLK, dtype=jnp.int32)
    order = jnp.argsort(scores, axis=-1).astype(jnp.float32)
    rows = jnp.arange(BLK, dtype=jnp.float32)[:, None]
    angle = math.pi * (rows + 0.5) * order / BLK
    weight = jnp.where(order == 0.0, math.sqrt(1.0 / BLK), math.sqrt(2.0 / BLK))
    return (signs * weight * jnp.cos(angle)).astype(jnp.float32).reshape(NBLK, N_MP * BLK, BLK)


def draw_left_bases(key, part):
    return draw_bases(key, 71)


def draw_right_bases(key, part):
    return draw_bases(key, 81)


def draw_vector_master(key, part):
    index = jnp.arange(NVEC * D)
    kind = index // D % 2
    gains = 1.0 + 0.15 * jax.random.truncated_normal(jax.random.fold_in(key, 91), -3.0, 3.0, (NVEC * D,), jnp.float32)
    shifts = 0.3 * jax.random.truncated_normal(jax.random.fold_in(key, 92), -3.0, 3.0, (NVEC * D,), jnp.float32)
    return jnp.where(kind == 0, gains, shifts).astype(jnp.float32)


def with_ends(values, rng, smallest, largest):
    index_at = [jax.random.randint(jax.random.fold_in(rng, axis), (), 0, length) for axis, length in enumerate(values.shape)]
    longest = values.shape.index(max(values.shape))
    beside = index_at[:longest] + [(index_at[longest] + 1) % values.shape[longest]] + index_at[longest + 1:]
    return values.at[tuple(index_at)].set(smallest).at[tuple(beside)].set(largest)


def level_of(key, dims, shards, smallest, high):
    def one(position, blocks):
        steps = jax.random.uniform(jax.random.fold_in(jax.random.fold_in(key, 6), position), (blocks,), jnp.float32, smallest / len(shards), high / len(shards))
        return jnp.repeat(jnp.exp(steps), dims[position] // blocks).reshape((-1,) + (1,) * (len(dims) - position - 1))

    level = one(*shards[0])
    for cut in shards[1:]:
        level = level * one(*cut)
    return level


def centred(stream_key, shape, deviation, most, cuts=(), held_as=jnp.bfloat16):
    array = deviation * jax.random.normal(stream_key, shape, jnp.float32)
    if cuts:
        array = array * level_of(stream_key, shape, cuts, -0.22, 0.18)
    return jnp.clip(array, -most, most).astype(held_as)


def setup_inputs(seed: int = 0) -> dict:
    seeds = jax.random.split(jax.random.key(seed), 16)
    return {
        "tokens": centred(seeds[0], (TOKENS, D), 1.0, 6.0, ((0, 8),)),
        "cotangent": centred(seeds[1], (TOKENS, D), 1.0, 6.0, ((0, 8),)),
        "context_sizes": draw_context_sizes(jax.random.fold_in(seeds[15], 71), 0),
        "query_hoods": with_ends(jax.random.randint(seeds[3], (N_DP * QRY_DEV,), 0, SEG_DEV), jax.random.fold_in(seeds[3], 1), 0, SEG_DEV - 1).astype(jnp.int32),
        "owners": draw_owners(jax.random.fold_in(seeds[15], 71), 0),
        "master_blocks": draw_master_blocks(jax.random.fold_in(seeds[15], 71), 0),
        "first_blocks": draw_first_blocks(jax.random.fold_in(seeds[15], 71), 0),
        "second_blocks": draw_second_blocks(jax.random.fold_in(seeds[15], 71), 0),
        "left_blocks": draw_left_blocks(jax.random.fold_in(seeds[15], 71), 0),
        "right_blocks": draw_right_blocks(jax.random.fold_in(seeds[15], 71), 0),
        "left_bases": draw_left_bases(jax.random.fold_in(seeds[15], 71), 0),
        "right_bases": draw_right_bases(jax.random.fold_in(seeds[15], 71), 0),
        "vector_master": draw_vector_master(jax.random.fold_in(seeds[15], 71), 0),
        "vector_moment": centred(seeds[13], (NVEC * D,), (0.11 * TOKENS ** 0.5), 80.0, ((0, 32),), jnp.float32),
        "vector_square": jnp.clip(jnp.exp(math.log(6451.2) - 2.7821582 * jax.random.uniform(seeds[14], (NVEC * D,), jnp.float32) ** level_of(seeds[14], (NVEC * D,), ((0, 32),), -0.2, 0.2)), 399.36, 6451.2),
    }


HIGHEST = lax.Precision.HIGHEST
NORM_EPSILON = 1e-05
ADAM_EPSILON = 1e-08
BETA_ONE = 0.9
BETA_TWO = 0.95
BETA_STATS = 0.95
RATE_MATRIX = 0.12
RATE_VECTOR = 0.6
DECAY_WEIGHT = 0.01
MASK_VALUE = -1e+30

@jax.custom_vjp
def low(v):
    return lax.optimization_barrier(v.astype(jnp.bfloat16)).astype(jnp.float32)

@jax.custom_vjp
def low_back(v):
    return v

def low_keep(v):
    return (low(v), None)

def low_pass(kept, grad):
    return (grad,)

def back_keep(v):
    return (v, None)

def back_low(kept, grad):
    return (low(grad),)
low.defvjp(low_keep, low_pass)
low_back.defvjp(back_keep, back_low)

def layer_norm(resid, gain, shift):
    center = resid - lax.optimization_barrier(jnp.mean(resid, axis=-1, keepdims=True))
    scaled = lax.rsqrt(lax.optimization_barrier(jnp.mean(center * center, axis=-1, keepdims=True)) + NORM_EPSILON)
    normed = center * scaled
    return (normed * gain + shift, normed, scaled)

def tile_shapes(ffs):
    return ((D // BLK, 3 * HD // BLK), (HD // BLK, D // BLK), (D // BLK, ffs // BLK), (ffs // BLK, D // BLK))

def unpack_all(blocks):
    layers = []
    offset = 0
    for layer_index in range(LAYERS):
        matrices = []
        for row_tiles, column_tiles in tile_shapes(FFS):
            count = row_tiles * column_tiles
            tiles = blocks[offset:offset + count]
            matrices.append(tiles.reshape(row_tiles, column_tiles, N_MP, BLK, BLK).transpose(2, 0, 3, 1, 4).reshape(N_MP, row_tiles * BLK, column_tiles * BLK))
            offset += count
        layers.append(matrices)
    return layers

def model_layer(rows, hoods, matrices, gains):
    joint_weight, out_weight, up_weight, down_weight = matrices
    low_rows = low(rows)
    projected = low(low_back(jnp.einsum('td,jde->jte', low_rows, low(joint_weight), precision=HIGHEST)))
    queries = projected[:, :, :HD]
    keys = projected[:, :CTX_DEV, HD:2 * HD]
    values = projected[:, :CTX_DEV, 2 * HD:]
    scores = low_back(jnp.einsum('jtc,jkc->jtk', queries, keys, precision=HIGHEST) * HD ** (-0.5))
    allowed = hoods[:, None] == hoods[None, :CTX_DEV]
    scores = jnp.where(allowed[None], scores, MASK_VALUE)
    probs = jax.nn.softmax(scores, axis=-1)
    heads_out = low(low_back(jnp.einsum('jtk,jkc->jtc', low(probs), values, precision=HIGHEST)))
    attended = low_back(lax.optimization_barrier(jnp.sum(low(jnp.einsum('jtc,jcd->jtd', heads_out, low(out_weight), precision=HIGHEST)), axis=0)))
    first_norm = layer_norm(rows + attended, gains[0], gains[1])[0]
    hidden = low_back(jnp.einsum('td,jdf->jtf', low(first_norm), low(up_weight), precision=HIGHEST))
    activated = low(jax.nn.gelu(hidden, approximate=True))
    mixed = low_back(lax.optimization_barrier(jnp.sum(low(jnp.einsum('jtf,jfd->jtd', activated, low(down_weight), precision=HIGHEST)), axis=0)))
    return layer_norm(first_norm + mixed, gains[2], gains[3])[0]

def group_hoods(context_sizes, query_hoods):
    ends = jnp.cumsum(context_sizes, axis=1)
    positions = jnp.arange(CTX_DEV, dtype=jnp.int32)
    context_hoods = lax.optimization_barrier(jnp.sum((positions[None, :, None] >= ends[:, None, :]).astype(jnp.int32), axis=2))
    return jnp.concatenate([context_hoods, query_hoods.reshape(N_DP, QRY_DEV)], axis=1)

def orthonormal(matrix):
    gram = jnp.einsum('...ai,...aj->...ij', matrix, matrix, precision=HIGHEST)
    factor = jnp.linalg.cholesky(gram)
    return jnp.swapaxes(jax.scipy.linalg.solve_triangular(factor, jnp.swapaxes(matrix, -1, -2), lower=True), -1, -2)

def soap_update(grad, first, second, left, right, left_basis, right_basis, master):

    def turn_in(value):
        return jnp.einsum('...ai,...aj,...jk->...ik', left_basis, value, right_basis, precision=HIGHEST)
    first_new = BETA_ONE * first + (1.0 - BETA_ONE) * grad
    turned = turn_in(grad)
    second_new = BETA_TWO * second + (1.0 - BETA_TWO) * turned * turned
    direction = turn_in(first_new) / (1.0 - BETA_ONE ** STEP) / (jnp.sqrt(second_new / (1.0 - BETA_TWO ** STEP)) + ADAM_EPSILON)
    update = jnp.einsum('...ia,...ab,...jb->...ij', left_basis, direction, right_basis, precision=HIGHEST)
    master_new = master - RATE_MATRIX * (update + DECAY_WEIGHT * master)
    left_new = BETA_STATS * left + (1.0 - BETA_STATS) * jnp.einsum('...ik,...jk->...ij', grad, grad, precision=HIGHEST)
    right_new = BETA_STATS * right + (1.0 - BETA_STATS) * jnp.einsum('...ki,...kj->...ij', grad, grad, precision=HIGHEST)
    left_turn = orthonormal(jnp.einsum('...ij,...jk->...ik', left_new, left_basis, precision=HIGHEST))
    right_turn = orthonormal(jnp.einsum('...ij,...jk->...ik', right_new, right_basis, precision=HIGHEST))
    return (first_new, second_new, left_new, right_new, left_turn, right_turn, master_new)

def adam_vector(grad, first, second, weight):
    first_new = BETA_ONE * first + (1.0 - BETA_ONE) * grad
    second_new = BETA_TWO * second + (1.0 - BETA_TWO) * grad * grad
    weight_new = weight - RATE_VECTOR * (first_new / (1.0 - BETA_ONE ** STEP)) / (jnp.sqrt(second_new / (1.0 - BETA_TWO ** STEP)) + ADAM_EPSILON)
    return (first_new, second_new, weight_new)

def reference(tokens, cotangent, context_sizes, query_hoods, owners, master_blocks, first_blocks, second_blocks, left_blocks, right_blocks, left_bases, right_bases, vector_master, vector_moment, vector_square):
    hoods_all = group_hoods(context_sizes, query_hoods)

    def in_blocks(value):
        return value.reshape(NBLK, N_MP, BLK, BLK)[owners]

    def to_slots(value):
        return jnp.zeros((NBLK, N_MP, BLK, BLK), jnp.float32).at[owners].set(value).reshape(NBLK, N_MP * BLK, BLK)

    def forward_all(inputs, weights, vectors):
        layers = unpack_all(weights)
        gains = vectors.reshape(LAYERS, 4, D)

        def group(pieces):
            rows, hoods = pieces
            for layer_index in range(LAYERS):
                rows = model_layer(rows, hoods, layers[layer_index], gains[layer_index])
            return rows
        outputs = lax.map(jax.checkpoint(group), (inputs.reshape(N_DP, TOK_DEV, D), hoods_all))
        return outputs.reshape(TOKENS, D)
    blocks = in_blocks(master_blocks)
    layer_out, pullback = jax.vjp(forward_all, tokens.astype(jnp.float32), blocks, vector_master)
    tokens_grad, block_grads, vector_grads = pullback(cotangent.astype(jnp.float32))
    first_new, second_new, left_new, right_new, left_turn, right_turn, master_new = soap_update(block_grads, in_blocks(first_blocks), in_blocks(second_blocks), in_blocks(left_blocks), in_blocks(right_blocks), in_blocks(left_bases), in_blocks(right_bases), blocks)
    vector_first, vector_second, vector_weight = adam_vector(vector_grads, vector_moment, vector_square, vector_master)
    return (layer_out, tokens_grad, to_slots(first_new), to_slots(second_new), to_slots(left_new), to_slots(right_new), to_slots(left_turn), to_slots(right_turn), to_slots(master_new), vector_first, vector_second, vector_weight)
```

```python
from functools import partial

import jax
import jax.numpy as jnp
from jax import lax
from jax.experimental import pallas as pl
from jax.experimental.pallas import tpu as pltpu
from jax.sharding import PartitionSpec as P

D = 512
HD = 128
FF = 1024
LAYERS = 2
BLK = 128
STEP = 10


HIGHEST = lax.Precision.HIGHEST
NORM_EPSILON = 1e-05
ADAM_EPSILON = 1e-08
BETA_ONE = 0.9
BETA_TWO = 0.95
BETA_STATS = 0.95
RATE_MATRIX = 0.12
RATE_VECTOR = 0.6
DECAY_WEIGHT = 0.01
MASK_VALUE = -1e30


def in_blocks(array, dim, length):
    before, after = (array.shape[:dim], array.shape[dim + 1 :])
    return jnp.moveaxis(array.reshape(*before, length, -1, *after), dim, 0)


def summed_on_arrival(array, axis, dim):
    length = lax.axis_size(axis)
    blocks = lax.all_to_all(in_blocks(array, dim, length), axis, 0, 0, tiled=True)
    return jnp.sum(blocks.astype(jnp.float32), axis=0)


def layer_norm(resid, gain, shift):
    center = resid - jnp.mean(resid, axis=-1, keepdims=True)
    scaled = lax.rsqrt(jnp.mean(center * center, axis=-1, keepdims=True) + NORM_EPSILON)
    normed = center * scaled
    return (normed * gain + shift, normed, scaled)


def norm_back(upper, normed, scaled, gain):
    inner = upper * gain
    lower = scaled * (
        inner
        - jnp.mean(inner, axis=-1, keepdims=True)
        - normed * jnp.mean(inner * normed, axis=-1, keepdims=True)
    )
    return (lower, jnp.sum(upper * normed, axis=0), jnp.sum(upper, axis=0))


def inner_rows(left, right):
    return lax.dot_general(
        left, right, (((0,), (0,)), ((), ())), preferred_element_type=jnp.float32
    )


def outer_last(left, right):
    return lax.dot_general(
        left, right, (((1,), (1,)), ((), ())), preferred_element_type=jnp.float32
    )


def tile_shapes(ffs):
    return (
        (D // BLK, 3 * HD // BLK),
        (HD // BLK, D // BLK),
        (D // BLK, ffs // BLK),
        (ffs // BLK, D // BLK),
    )


def unpack_layers(blocks, ffs):
    layers = []
    offset = 0
    for layer_index in range(LAYERS):
        matrices = []
        for row_tiles, column_tiles in tile_shapes(ffs):
            count = row_tiles * column_tiles
            tiles = blocks[offset : offset + count]
            matrices.append(
                tiles.reshape(row_tiles, column_tiles, BLK, BLK)
                .transpose(0, 2, 1, 3)
                .reshape(row_tiles * BLK, column_tiles * BLK)
            )
            offset += count
        layers.append(matrices)
    return layers


def pack_layers(layer_grads, ffs):
    pieces = []
    for matrices in layer_grads:
        for matrix, sizes in zip(matrices, tile_shapes(ffs)):
            row_tiles, column_tiles = sizes
            pieces.append(
                matrix.reshape(row_tiles, BLK, column_tiles, BLK)
                .transpose(0, 2, 1, 3)
                .reshape(row_tiles * column_tiles, BLK, BLK)
            )
    return jnp.concatenate(pieces, axis=0)


def pick_block(rows_here):
    for candidate in range(512, rows_here + 1):
        if rows_here % candidate == 0:
            return candidate
    return rows_here


def branch_total(partial_sum):
    return lax.psum(partial_sum.astype(jnp.bfloat16), "mp").astype(jnp.float32)


def grad_total(partial_sum):
    return lax.psum(partial_sum.astype(jnp.bfloat16), "mp").astype(jnp.float32)


def final_rows(value):
    share = value.shape[0] // lax.axis_size("mp")
    return lax.dynamic_slice_in_dim(value, lax.axis_index("mp") * share, share, 0)


def vector_part(grads):
    arranged = grads.reshape(lax.axis_size("dp"), lax.axis_size("mp"), -1)
    return lax.dynamic_index_in_dim(arranged, lax.axis_index("mp"), 1, keepdims=False).reshape(-1)


def attend(projected, row_hoods, context_rows, block_rows):
    scale = HD ** (-0.5)
    keys = projected[:context_rows, HD : 2 * HD]
    values = projected[:context_rows, 2 * HD :]
    key_hoods = row_hoods[:context_rows]
    count = projected.shape[0] // block_rows

    def one_block(pieces):
        query_block, hood_block = pieces
        scores = jnp.where(
            hood_block[:, None] == key_hoods[None, :],
            outer_last(query_block, keys) * scale,
            MASK_VALUE,
        )
        peak = jnp.max(scores, axis=1, keepdims=True)
        weights = jnp.exp(scores - peak)
        total = jnp.sum(weights, axis=1, keepdims=True)
        output = jnp.dot(
            (weights / total).astype(jnp.bfloat16), values, preferred_element_type=jnp.float32
        )
        return (output.astype(jnp.bfloat16), (peak + jnp.log(total))[:, 0])

    outputs, totals = lax.map(
        one_block,
        (projected[:, :HD].reshape(count, block_rows, HD), row_hoods.reshape(count, block_rows)),
    )
    return (outputs.reshape(-1, HD), totals.reshape(-1))


def attend_back(projected, row_hoods, context_rows, log_totals, heads_grad, block_rows):
    scale = HD ** (-0.5)
    keys = projected[:context_rows, HD : 2 * HD]
    values = projected[:context_rows, 2 * HD :]
    key_hoods = row_hoods[:context_rows]
    count = projected.shape[0] // block_rows

    def one_block(carry, pieces):
        key_grad, value_grad = carry
        query_block, hood_block, total_block, grad_block = pieces
        scores = outer_last(query_block, keys) * scale
        allowed = hood_block[:, None] == key_hoods[None, :]
        probs = jnp.where(allowed, jnp.exp(scores - total_block[:, None]), 0.0)
        value_grad = value_grad + inner_rows(probs.astype(jnp.bfloat16), grad_block)
        prob_grad = outer_last(grad_block, values)
        score_grad = (
            probs * (prob_grad - jnp.sum(probs * prob_grad, axis=1, keepdims=True))
        ).astype(jnp.bfloat16)
        query_grad = jnp.dot(score_grad, keys, preferred_element_type=jnp.float32) * scale
        key_grad = key_grad + inner_rows(score_grad, query_block) * scale
        return ((key_grad, value_grad), query_grad)

    zeros_start = jnp.zeros((context_rows, HD), jnp.float32)
    pieces = (
        projected[:, :HD].reshape(count, block_rows, HD),
        row_hoods.reshape(count, block_rows),
        log_totals.reshape(count, block_rows),
        heads_grad.reshape(count, block_rows, HD),
    )
    carried, query_grad = lax.scan(one_block, (zeros_start, zeros_start), pieces)
    return (query_grad.reshape(-1, HD), jnp.concatenate([carried[0], carried[1]], axis=1))


def forward_layer(stream, low_rows, matrices, gains, row_hoods, context_rows, block_rows):
    joint_weight, out_weight, up_weight, down_weight = matrices
    projected = jnp.dot(low_rows, joint_weight, preferred_element_type=jnp.float32).astype(
        jnp.bfloat16
    )
    heads_out, log_totals = attend(projected, row_hoods, context_rows, block_rows)
    attended = branch_total(jnp.dot(heads_out, out_weight, preferred_element_type=jnp.float32))
    first_norm, first_hat, first_scale = layer_norm(stream + attended, gains[0], gains[1])
    normed_low = first_norm.astype(jnp.bfloat16)
    hidden = jnp.dot(normed_low, up_weight, preferred_element_type=jnp.float32)
    activated = jax.nn.gelu(hidden, approximate=True).astype(jnp.bfloat16)
    mixed = branch_total(jnp.dot(activated, down_weight, preferred_element_type=jnp.float32))
    second_norm, second_hat, second_scale = layer_norm(first_norm + mixed, gains[2], gains[3])
    return (
        second_norm,
        (
            low_rows,
            projected,
            heads_out,
            log_totals,
            first_hat,
            first_scale,
            normed_low,
            hidden,
            activated,
            second_hat,
            second_scale,
        ),
    )


def backward_layer(upper, matrices, gains, kept, row_hoods, context_rows, block_rows):
    joint_weight, out_weight, up_weight, down_weight = matrices
    (
        low_rows,
        projected,
        heads_out,
        log_totals,
        first_hat,
        first_scale,
        normed_low,
        hidden,
        activated,
        second_hat,
        second_scale,
    ) = kept
    second_grad, gain_two, shift_two = norm_back(upper, second_hat, second_scale, gains[2])
    mixed_low = second_grad.astype(jnp.bfloat16)
    down_grad = inner_rows(activated, mixed_low)
    unused_value, gelu_back = jax.vjp(partial(jax.nn.gelu, approximate=True), hidden)
    hidden_grad = gelu_back(outer_last(mixed_low, down_weight))[0].astype(jnp.bfloat16)
    up_grad = inner_rows(normed_low, hidden_grad)
    first_upper = second_grad + grad_total(outer_last(hidden_grad, up_weight))
    first_grad, gain_one, shift_one = norm_back(first_upper, first_hat, first_scale, gains[0])
    attended_low = first_grad.astype(jnp.bfloat16)
    out_grad = inner_rows(heads_out, attended_low)
    heads_grad = outer_last(attended_low, out_weight).astype(jnp.bfloat16)
    query_grad, key_value_grad = attend_back(
        projected, row_hoods, context_rows, log_totals, heads_grad, block_rows
    )
    padding = jnp.zeros((projected.shape[0] - context_rows, 2 * HD), jnp.float32)
    joint_low = jnp.concatenate(
        [query_grad, jnp.concatenate([key_value_grad, padding], axis=0)], axis=1
    ).astype(jnp.bfloat16)
    joint_grad = inner_rows(low_rows, joint_low)
    lower = first_grad + grad_total(outer_last(joint_low, joint_weight))
    return (
        lower,
        (joint_grad, out_grad, up_grad, down_grad),
        jnp.stack([gain_one, shift_one, gain_two, shift_two]),
    )


def split(x):
    hi=x.astype(jnp.bfloat16)
    return hi,(x-hi.astype(jnp.float32)).astype(jnp.bfloat16)
def dot3(a,b,ca,cb):
    dims=(((ca,),(cb,)),((),()))
    ah,al=a; bh,bl=b
    d=lambda x,y: lax.dot_general(x,y,dims,preferred_element_type=jnp.float32)
    return d(ah,bh)+(d(ah,bl)+d(al,bh))
def dotf(a,b,ca,cb):
    return lax.dot_general(a,b,(((ca,),(cb,)),((),())),preferred_element_type=jnp.float32,precision=lax.Precision.HIGHEST)

def soap_kernel(slots, g_ref,m_ref,v_ref,l_ref,r_ref,ql_ref,qr_ref,w_ref, mo,vo,lo,ro,qlo,qro,wo, x_ref, a_ref):
    def first(i,_):
        g=g_ref[i]; ql=split(ql_ref[i]); qr=split(qr_ref[i])
        gs=split(g)
        m=BETA_ONE*m_ref[i]+(1-BETA_ONE)*g
        mo[i]=m
        def turn(v):
            return dot3(split(dot3(ql,v,0,0)),qr,1,0)
        tg=turn(gs)
        v=BETA_TWO*v_ref[i]+(1-BETA_TWO)*tg*tg
        vo[i]=v
        d=turn(split(m))/(1-BETA_ONE**STEP)/(jnp.sqrt(v/(1-BETA_TWO**STEP))+ADAM_EPSILON)
        u=dot3(split(dot3(ql,split(d),1,0)),qr,1,1)
        w=w_ref[i]
        wo[i]=w-RATE_MATRIX*(u+DECAY_WEIGHT*w)
        ln=BETA_STATS*l_ref[i]+(1-BETA_STATS)*dot3(gs,gs,1,1)
        rn=BETA_STATS*r_ref[i]+(1-BETA_STATS)*dot3(gs,gs,0,0)
        lo[i]=ln; ro[i]=rn
        al=dotf(ln,ql_ref[i],1,0); ar=dotf(rn,qr_ref[i],1,0)
        a_ref[2*i]=al; a_ref[2*i+1]=ar
        x_ref[2*i]=dotf(al,al,0,0); x_ref[2*i+1]=dotf(ar,ar,0,0)
        return 0
    lax.fori_loop(0,slots,first,0)
    n=2*slots
    lane=lax.broadcasted_iota(jnp.int32,(8,BLK),1)
    sub=lax.broadcasted_iota(jnp.int32,(8,BLK),0)
    for p in range(BLK//8):
        def step(kk,_):
            k=p*8+kk
            idx=jnp.full((8,BLK),k,jnp.int32)
            atk=lane==k
            below=sub>kk
            rows=[jnp.broadcast_to(x_ref[m,pl.ds(k,1),:],(8,BLK)) for m in range(n)]
            rinv=[1.0/jnp.take_along_axis(row,idx,axis=1) for row in rows]
            scaled=[jnp.where(atk,1.0,row)*ri for row,ri in zip(rows,rinv)]
            for m in range(n):
                for t in range(p,BLK//8):
                    v=x_ref[m,t*8:(t+1)*8,:]
                    f=jnp.take_along_axis(v,idx,axis=1)
                    new=jnp.where(atk,0.0,v)-f*scaled[m]
                    if t==p: new=jnp.where(below,new,v)
                    x_ref[m,t*8:(t+1)*8,:]=new
            return 0
        lax.fori_loop(0,8,step,0)
    r=lax.broadcasted_iota(jnp.int32,(BLK,BLK),0); c=lax.broadcasted_iota(jnp.int32,(BLK,BLK),1)
    def last(i,_):
        for s,out in ((0,qlo),(1,qro)):
            x=x_ref[2*i+s]
            piv=jnp.sum(jnp.where(r==c,x,0.0),axis=1,keepdims=True)
            inv=jnp.where(r==c,1.0,jnp.where(r>c,x,0.0))*lax.rsqrt(piv)
            out[i]=dotf(a_ref[2*i+s],inv,1,1)
        return 0
    lax.fori_loop(0,slots,last,0)

def soap(g,m,v,l,r,ql,qr,w):
    slots=g.shape[0]
    sh=jax.ShapeDtypeStruct((slots,BLK,BLK),jnp.float32)
    vm=pl.BlockSpec(memory_space=pltpu.VMEM)
    return pl.pallas_call(partial(soap_kernel,slots),out_shape=[sh]*7,in_specs=[vm]*8,out_specs=[vm]*7,
        scratch_shapes=[pltpu.VMEM((2*slots,BLK,BLK),jnp.float32)]*2,
        compiler_params=pltpu.CompilerParams(vmem_limit_bytes=48<<20),name="soap")(g,m,v,l,r,ql,qr,w)


def adam_vector(grad, first, second, weight):
    first_new = BETA_ONE * first + (1.0 - BETA_ONE) * grad
    second_new = BETA_TWO * second + (1.0 - BETA_TWO) * grad * grad
    weight_new = weight - RATE_VECTOR * (first_new / (1.0 - BETA_ONE**STEP)) / (
        jnp.sqrt(second_new / (1.0 - BETA_TWO**STEP)) + ADAM_EPSILON
    )
    return (first_new, second_new, weight_new)


def local(
    tokens,
    cotangent,
    context_sizes,
    query_hoods,
    owners,
    master_blocks,
    first_blocks,
    second_blocks,
    left_blocks,
    right_blocks,
    left_bases,
    right_bases,
    vector_master,
    vector_moment,
    vector_square,
):
    ffs = FF // lax.axis_size("mp")
    rows_here = tokens.shape[0]
    context_rows = rows_here - query_hoods.shape[0]
    gathered = lax.all_gather(master_blocks.astype(jnp.bfloat16), "dp", axis=0, tiled=True)
    slots = jnp.arange(owners.shape[0], dtype=jnp.int32)
    place = (owners[:, None] == slots[None, :]).astype(jnp.bfloat16)
    ordered = jnp.einsum("bs,sij->bij", place, gathered)
    layers = unpack_layers(ordered, ffs)
    gains = lax.all_gather(vector_master, ("dp", "mp"), axis=0, tiled=True).reshape(LAYERS, 4, D)
    sizes = context_sizes[0]
    order = jnp.arange(sizes.shape[0], dtype=jnp.int32)
    ends = jnp.sum(jnp.where(order[None, :] <= order[:, None], sizes[None, :], 0), axis=1)
    positions = jnp.arange(context_rows, dtype=jnp.int32)
    context_hoods = jnp.sum((positions[:, None] >= ends[None, :]).astype(jnp.int32), axis=1)
    row_hoods = jnp.concatenate([context_hoods, query_hoods])
    block_rows = pick_block(rows_here)
    stream = tokens.astype(jnp.float32)
    low_rows = tokens
    saved = []
    for layer_index in range(LAYERS):
        stream, kept = forward_layer(
            stream,
            low_rows,
            layers[layer_index],
            gains[layer_index],
            row_hoods,
            context_rows,
            block_rows,
        )
        saved.append(kept)
        if layer_index + 1 < LAYERS:
            low_rows = stream.astype(jnp.bfloat16)
    layer_out = final_rows(stream)
    upper = cotangent.astype(jnp.float32)
    weight_grads = [None] * LAYERS
    norm_grads = [None] * LAYERS
    for layer_index in reversed(range(LAYERS)):
        upper, weight_grads[layer_index], norm_grads[layer_index] = backward_layer(
            upper,
            layers[layer_index],
            gains[layer_index],
            saved[layer_index],
            row_hoods,
            context_rows,
            block_rows,
        )
    tokens_grad = final_rows(upper)
    block_grads = pack_layers(weight_grads, ffs)
    slot_grads = jnp.einsum("bs,bij->sij", place, block_grads.astype(jnp.bfloat16))
    vector_terms = vector_part(jnp.stack(norm_grads).reshape(-1))
    reduced, vector_reduced = (
        summed_on_arrival(slot_grads.astype(jnp.bfloat16), "dp", 0),
        summed_on_arrival(vector_terms.astype(jnp.bfloat16), "dp", 0),
    )
    results = soap(
        reduced,
        first_blocks,
        second_blocks,
        left_blocks,
        right_blocks,
        left_bases,
        right_bases,
        master_blocks,
    )
    vector_results = adam_vector(vector_reduced, vector_moment, vector_square, vector_master)
    return (layer_out, tokens_grad) + results + vector_results


def solution(mesh):
    return jax.shard_map(
        local,
        mesh=mesh,
        in_specs=(
            P("dp", None),
            P("dp", None),
            P("dp", None),
            P("dp"),
            P(),
            P("dp", "mp", None),
            P("dp", "mp", None),
            P("dp", "mp", None),
            P("dp", "mp", None),
            P("dp", "mp", None),
            P("dp", "mp", None),
            P("dp", "mp", None),
            P(("dp", "mp")),
            P(("dp", "mp")),
            P(("dp", "mp")),
        ),
        out_specs=(
            P(("dp", "mp"), None),
            P(("dp", "mp"), None),
            P("dp", "mp", None),
            P("dp", "mp", None),
            P("dp", "mp", None),
            P("dp", "mp", None),
            P("dp", "mp", None),
            P("dp", "mp", None),
            P("dp", "mp", None),
            P(("dp", "mp")),
            P(("dp", "mp")),
            P(("dp", "mp")),
        ),
        check_vma=False,
    )
```

```python
import math
from functools import partial

import jax
import jax.numpy as jnp
from jax import lax
from jax.experimental import pallas as pl
from jax.experimental.pallas import tpu as pltpu
from jax.sharding import PartitionSpec as P

RATE_VECTOR = 0.6
MESH=pl.DeviceIdType.MESH
VMEM_SPEC=pl.BlockSpec(memory_space=pltpu.VMEM)
ANY_SPEC=pl.BlockSpec(memory_space=pl.ANY)

def remote(src,dst,send,recv,device):
    return pltpu.make_async_remote_copy(src_ref=src,dst_ref=dst,send_sem=send,recv_sem=recv,device_id=device,device_id_type=MESH)

class Spot:
    def __init__(self,planes):
        dp,mp=lax.axis_index("dp"),lax.axis_index("mp")
        self.dp,self.mp,self.planes=dp,mp,planes
        self.z,self.x=dp//2,dp%2
        self.y,self.c=mp//2,mp%2
        self.across_x=(dp+1-2*self.x,mp)
        self.across_y=(dp,(mp+2)%4)
        self.sibling=(dp,mp+1-2*self.c)
        self.up=(jnp.minimum(dp+2,2*planes-1),mp)
        self.down=(jnp.maximum(dp-2,0),mp)
    def greet(self):
        bar=pltpu.get_barrier_semaphore()
        for who in (self.across_x,self.across_y,self.sibling):
            pl.semaphore_signal(bar,inc=1,device_id=who,device_id_type=MESH)
        @pl.when(self.z<self.planes-1)
        def _(): pl.semaphore_signal(bar,inc=1,device_id=self.up,device_id_type=MESH)
        @pl.when(self.z>0)
        def _(): pl.semaphore_signal(bar,inc=1,device_id=self.down,device_id_type=MESH)
        pl.semaphore_wait(bar,3+jnp.minimum(self.z,1)+jnp.minimum(self.planes-1-self.z,1))
    def ring(self,r,action):
        if r==0:
            action(self.z,None); return
        @pl.when(self.z>=r)
        def _(): action(self.z-r,True)
        @pl.when(self.z+r<self.planes)
        def _(): action(self.z+r,False)

def gather_kernel(planes,half,slab,out,send,recv,zsend,zrecv,lsem):
    s=Spot(planes); rows=slab.shape[0]; z,x,y,c,mp=s.z,s.x,s.y,s.c,s.mp
    A,B=pl.ds(0,half),pl.ds(half,rows-half)
    mx,my=s.across_x,s.across_y
    own=pltpu.make_async_copy(slab,out.at[s.dp,mp],lsem); own.start()
    s.greet()
    def at(p,xx,yy,cc): return out.at[p*2+xx,yy*2+cc]
    xo,yo=1-x,1-y
    def copies(p,src):
        here=at(p,x,y,c) if src is None else src
        f=lambda k,a,b,w: remote(a,b,send.at[k,p],recv.at[k,p],w)
        return dict(
            xown=lambda: f(0,here,at(p,x,y,c),mx), yown=lambda: f(1,here,at(p,x,y,c),my), cown=lambda: f(2,here,at(p,x,y,c),s.sibling),
            yfwd=lambda: f(3,at(p,xo,y,c).at[A],at(p,xo,y,c).at[A],my),
            xfwd=lambda: f(4,at(p,x,yo,c).at[B],at(p,x,yo,c).at[B],mx),
            cx=lambda: f(5,at(p,xo,y,c),at(p,xo,y,c),s.sibling), cy=lambda: f(6,at(p,x,yo,c),at(p,x,yo,c),s.sibling),
            ca=lambda: f(7,at(p,xo,yo,c).at[A],at(p,xo,yo,c).at[A],s.sibling),
            cb=lambda: f(8,at(p,xo,yo,c).at[B],at(p,xo,yo,c).at[B],s.sibling))
    def zcopy(p,up,src=None):
        here=at(p,x,y,c) if src is None else src
        return remote(here,at(p,x,y,c),zsend.at[0 if up else 1,p],zrecv.at[p],s.up if up else s.down)
    def arrive(r):
        def act(p,below):
            src=None
            if below is None: src=slab
            else: zcopy(p,below).wait_recv()
            if below is None or below:
                @pl.when(z<planes-1)
                def _(): zcopy(p,True,src).start()
            if below is None or not below:
                @pl.when(z>0)
                def _(): zcopy(p,False,src).start()
            k=copies(p,src)
            k["xown"]().start(); k["yown"]().start(); k["cown"]().start()
        s.ring(r,act)
    def second(r):
        def act(p,below):
            k=copies(p,None)
            k["xown"]().wait_recv(); k["yfwd"]().start(); k["cx"]().start()
            k["yown"]().wait_recv(); k["xfwd"]().start(); k["cy"]().start()
        s.ring(r,act)
    def third(r):
        def act(p,below):
            k=copies(p,None)
            k["yfwd"]().wait_recv(); k["ca"]().start()
            k["xfwd"]().wait_recv(); k["cb"]().start()
        s.ring(r,act)
    def finish(r):
        def act(p,below):
            src=slab if below is None else None
            k=copies(p,src)
            for n in ("cown","cx","cy","ca","cb"): k[n]().wait_recv()
            for n in k: k[n]().wait_send()
            if below is None or below:
                @pl.when(z<planes-1)
                def _(): zcopy(p,True,src).wait_send()
            if below is None or not below:
                @pl.when(z>0)
                def _(): zcopy(p,False,src).wait_send()
        s.ring(r,act)
    for r in range(planes+2):
        if r<planes: arrive(r)
        if 1<=r<=planes: second(r-1)
        if r>=2: third(r-2)
    for r in range(planes): finish(r)
    own.wait()

def gather_all(slab,dp,collective):
    rows=slab.shape[0]; planes=dp//2; half=rows//2//16*16
    dma=pltpu.SemaphoreType.DMA
    return pl.pallas_call(partial(gather_kernel,planes,half),
        out_shape=jax.ShapeDtypeStruct((dp,4,rows,slab.shape[1]),slab.dtype),
        in_specs=[ANY_SPEC],out_specs=ANY_SPEC,
        scratch_shapes=[dma((9,planes)),dma((9,planes)),dma((2,planes)),dma((planes,)),dma],
        compiler_params=pltpu.CompilerParams(collective_id=collective,has_side_effects=True),name="gather_all")(slab)

def reduce_kernel(planes,half,g,out,rc,acc,ya,xb,xa,yb,own,zin,send,recv,zsend,zrecv):
    s=Spot(planes); rows=g.shape[2]; z,x,y,c,mp=s.z,s.x,s.y,s.c,s.mp
    A,B=pl.ds(0,half),pl.ds(half,rows-half)
    mx,my=s.across_x,s.across_y
    xo,yo,co=1-x,1-y,1-c
    s.greet()
    f32=lambda v: v.astype(jnp.float32)
    def core(p,xx,yy):
        k=xx*2+yy
        return remote(g.at[p*2+xx,yy*2+co],rc.at[p*4+k],send.at[k,p],recv.at[k,p],s.sibling)
    def toya(p,xx): return remote(acc.at[p*4+xx*2+yo,A],ya.at[p*2+xx],send.at[4+xx,p],recv.at[4+xx,p],my)
    def toxb(p,yy): return remote(acc.at[p*4+xo*2+yy,B],xb.at[p*2+yy],send.at[6+yy,p],recv.at[6+yy,p],mx)
    def toxa(p): return remote(ya.at[p*2+xo],xa.at[p],send.at[8,p],recv.at[8,p],mx)
    def toyb(p): return remote(xb.at[p*2+yo],yb.at[p],send.at[9,p],recv.at[9,p],my)
    def toz(p,up): return remote(own.at[p],zin.at[0 if up else 1,p],zsend.at[p],zrecv.at[0 if up else 1,p],s.up if up else s.down)
    def start(p,_):
        for xx in (0,1):
            for yy in (0,1): core(p,xx,yy).start()
    def first(p,_):
        for xx in (0,1):
            for yy in (0,1):
                core(p,xx,yy).wait_recv()
                acc[p*4+xx*2+yy]=(f32(g[p*2+xx,yy*2+c])+f32(rc[p*4+xx*2+yy])).astype(acc.dtype)
        for e in (0,1): toya(p,e).start(); toxb(p,e).start()
    def second(p,_):
        for e in (0,1):
            toya(p,e).wait_recv()
            ya[p*2+e]=(f32(acc[p*4+e*2+y,A])+f32(ya[p*2+e])).astype(ya.dtype)
        toxa(p).start()
        for e in (0,1):
            toxb(p,e).wait_recv()
            xb[p*2+e]=(f32(acc[p*4+x*2+e,B])+f32(xb[p*2+e])).astype(xb.dtype)
        toyb(p).start()
    def third(p,below):
        toxa(p).wait_recv()
        av=f32(ya[p*2+x])+f32(xa[p])
        toyb(p).wait_recv()
        bv=f32(xb[p*2+y])+f32(yb[p])
        if below is None:
            out[A]=av; out[B]=bv
            @pl.when(z>0)
            def _():
                toz(p,True).wait_recv()
                out[...]=out[...]+f32(zin[0,p])
            @pl.when(z<planes-1)
            def _():
                toz(p,False).wait_recv()
                out[...]=out[...]+f32(zin[1,p])
            return
        own[p,A]=av.astype(own.dtype); own[p,B]=bv.astype(own.dtype)
        up=not below
        has=(z>0) if up else (z<planes-1)
        @pl.when(has)
        def _():
            toz(p,up).wait_recv()
            own[p,A]=(av+f32(zin[0 if up else 1,p,A])).astype(own.dtype)
            own[p,B]=(bv+f32(zin[0 if up else 1,p,B])).astype(own.dtype)
        toz(p,up).start()
    def finish(p,below):
        for xx in (0,1):
            for yy in (0,1): core(p,xx,yy).wait_send()
        for e in (0,1): toya(p,e).wait_send(); toxb(p,e).wait_send()
        toxa(p).wait_send(); toyb(p).wait_send()
        if below is not None: toz(p,not below).wait_send()
    order=list(range(planes-1,-1,-1))
    for r in order: s.ring(r,start)
    n=len(order)
    for i in range(n+2):
        if i<n: s.ring(order[i],first)
        if 0<=i-1<n: s.ring(order[i-1],second)
        if 0<=i-2<n: s.ring(order[i-2],third)
    for r in order: s.ring(r,finish)

def reduce_all(g,collective):
    dp,_,rows,cols=g.shape; planes=dp//2; half=rows//2//16*16
    dma=pltpu.SemaphoreType.DMA; bf=lambda *sh: pltpu.VMEM(sh+(cols,),g.dtype)
    return pl.pallas_call(partial(reduce_kernel,planes,half),
        out_shape=jax.ShapeDtypeStruct((rows,cols),jnp.float32),in_specs=[VMEM_SPEC],out_specs=VMEM_SPEC,
        scratch_shapes=[bf(planes*4,rows),bf(planes*4,rows),bf(planes*2,half),bf(planes*2,rows-half),bf(planes,half),bf(planes,rows-half),
            bf(planes,rows),bf(2,planes,rows),dma((10,planes)),dma((10,planes)),dma((planes,)),dma((2,planes))],
        compiler_params=pltpu.CompilerParams(collective_id=collective,has_side_effects=True,vmem_limit_bytes=56<<20),name="reduce_all")(g)

def share_kernel(mine,full,send,recv,lsem):
    s=Spot(1); rows=mine.shape[0]; n=send.shape[1]; step=rows//n
    bar=pltpu.get_barrier_semaphore()
    for who in (s.across_y,s.sibling): pl.semaphore_signal(bar,inc=1,device_id=who,device_id_type=MESH)
    local=pltpu.make_async_copy(mine,full.at[s.mp],lsem); local.start()
    pl.semaphore_wait(bar,2)
    far=s.across_y[1]
    part=lambda i: pl.ds(i*step,step)
    over=lambda i: remote(mine.at[part(i)],full.at[s.mp,part(i)],send.at[0,i],recv.at[0,i],s.across_y)
    near=lambda i: remote(mine.at[part(i)],full.at[s.mp,part(i)],send.at[1,i],recv.at[1,i],s.sibling)
    on=lambda i: remote(full.at[far,part(i)],full.at[far,part(i)],send.at[2,i],recv.at[2,i],s.sibling)
    for i in range(n): over(i).start()
    for i in range(n): near(i).start()
    for i in range(n):
        over(i).wait_recv(); on(i).start()
    for i in range(n):
        near(i).wait_recv(); on(i).wait_recv()
        for k in (over,near,on): k(i).wait_send()
    local.wait()

def share_rows(mine,collective,n=3):
    rows,cols=mine.shape; dma=pltpu.SemaphoreType.DMA
    out=pl.pallas_call(share_kernel,out_shape=jax.ShapeDtypeStruct((4,rows,cols),mine.dtype),in_specs=[VMEM_SPEC],out_specs=VMEM_SPEC,
        scratch_shapes=[dma((3,n)),dma((3,n)),dma],
        compiler_params=pltpu.CompilerParams(collective_id=collective,has_side_effects=True,vmem_limit_bytes=24<<20),name="share_rows")(mine)
    return out.reshape(4*rows,cols)

def total_kernel(terms,own,out,rc,acc,ry,send,recv):
    s=Spot(1); rows=own.shape[0]; n=send.shape[1]; step=rows//n
    bar=pltpu.get_barrier_semaphore()
    for who in (s.across_y,s.sibling): pl.semaphore_signal(bar,inc=1,device_id=who,device_id_type=MESH)
    pl.semaphore_wait(bar,2)
    far=s.across_y[1]; co=1-s.c
    part=lambda i: pl.ds(i*step,step)
    f32=lambda v: v.astype(jnp.float32)
    a=lambda i: remote(terms.at[(1-s.y)*2+co,part(i)],rc.at[0,part(i)],send.at[0,i],recv.at[0,i],s.sibling)
    b=lambda i: remote(terms.at[s.y*2+co,part(i)],rc.at[1,part(i)],send.at[1,i],recv.at[1,i],s.sibling)
    o=lambda i: remote(acc.at[part(i)],ry.at[part(i)],send.at[2,i],recv.at[2,i],s.across_y)
    for i in range(n): a(i).start()
    for i in range(n): b(i).start()
    for i in range(n):
        a(i).wait_recv()
        acc[part(i)]=(f32(terms[far,part(i)])+f32(rc[0,part(i)])).astype(acc.dtype)
        o(i).start()
    for i in range(n):
        b(i).wait_recv()
        out[part(i)]=own[part(i)]+(f32(terms[s.mp,part(i)])+f32(rc[1,part(i)]))
    for i in range(n):
        o(i).wait_recv()
        out[part(i)]=out[part(i)]+f32(ry[part(i)])
    for i in range(n):
        for k in (a,b,o): k(i).wait_send()

def total_rows(terms,own,collective,n=3):
    rows,cols=own.shape; dma=pltpu.SemaphoreType.DMA
    return pl.pallas_call(total_kernel,out_shape=jax.ShapeDtypeStruct((rows,cols),jnp.float32),in_specs=[VMEM_SPEC]*2,out_specs=VMEM_SPEC,
        scratch_shapes=[pltpu.VMEM((2,rows,cols),terms.dtype),pltpu.VMEM((rows,cols),terms.dtype),pltpu.VMEM((rows,cols),terms.dtype),dma((3,n)),dma((3,n))],
        compiler_params=pltpu.CompilerParams(collective_id=collective,has_side_effects=True,vmem_limit_bytes=24<<20),name="total_rows")(terms.reshape(4,rows,cols),own)
D=512; HD=128; FF=1024; LAYERS=2; BLK=128
NORM_EPSILON=1e-5; MASK_VALUE=-1e30
HEADS=4
f32=jnp.float32; bf16=jnp.bfloat16
VMEM_SPEC=pl.BlockSpec(memory_space=pltpu.VMEM)
ANY_SPEC=pl.BlockSpec(memory_space=pl.ANY)
SMEM_SPEC=pl.BlockSpec(memory_space=pltpu.SMEM)
SCALE=HD**-0.5; LOG2E=math.log2(math.e)
ROOT=math.sqrt(2/math.pi)

def nn(a,b): return lax.dot_general(a,b,(((1,),(0,)),((),())),preferred_element_type=f32)
def nt(a,b): return lax.dot_general(a,b,(((1,),(1,)),((),())),preferred_element_type=f32)
def tn(a,b): return lax.dot_general(a,b,(((0,),(0,)),((),())),preferred_element_type=f32)

def normed(r):
    center=r-jnp.mean(r,axis=-1,keepdims=True)
    rho=lax.rsqrt(jnp.mean(center*center,axis=-1,keepdims=True)+NORM_EPSILON)
    return center*rho,rho
def norm_back(dy,xhat,rho,gain):
    inner=dy*gain
    return rho*(inner-jnp.mean(inner,axis=-1,keepdims=True)-xhat*jnp.mean(inner*xhat,axis=-1,keepdims=True))
def gelu(v): return 0.5*v*(1+jnp.tanh(ROOT*(v+0.044715*v*v*v)))
def gelu_both(v):
    sq=v*v
    t=jnp.tanh(ROOT*v*(1+0.044715*sq))
    half=0.5*(1+t)
    return v*half,half+0.5*v*(1-t*t)*(ROOT*(1+3*0.044715*sq))

ROWS_TILE=(4,1,4,2); COLS_TILE=(3,4,2,4)
FIRST_BLOCK=(0,12,16,24)
LAYER_BLOCKS=32

def weight_shapes():
    return [pltpu.VMEM((D,D),bf16),pltpu.VMEM((HEADS,D,2*HD),bf16),pltpu.VMEM((D,D),bf16),pltpu.VMEM((D,FF),bf16),pltpu.VMEM((FF,D),bf16)]

class Weights:
    def __init__(self,layer,owners,wall,slots,refs,sems):
        self.q,self.kv,self.out,self.up,self.down=refs
        self.sems=sems
        fs=FF//HEADS
        def tile(kind,r,c,j,dst,sem):
            slot=owners[layer*LAYER_BLOCKS+FIRST_BLOCK[kind]+r*COLS_TILE[kind]+c]
            src=wall.at[slot//slots,j,pl.ds(pl.multiple_of(slot%slots*BLK,BLK),BLK),:]
            pltpu.make_async_copy(src,dst,sems.at[sem]).start()
        for r in range(4):
            for c in (1,2):
                for j in range(HEADS): tile(0,r,c,j,self.kv.at[j,r*BLK:(r+1)*BLK,(c-1)*BLK:c*BLK],1)
        for r in range(4):
            for j in range(HEADS): tile(0,r,0,j,self.q.at[r*BLK:(r+1)*BLK,j*BLK:(j+1)*BLK],0)
        for c in range(4):
            for j in range(HEADS): tile(1,0,c,j,self.out.at[j*BLK:(j+1)*BLK,c*BLK:(c+1)*BLK],2)
        for r in range(4):
            for c in range(2):
                for j in range(HEADS): tile(2,r,c,j,self.up.at[r*BLK:(r+1)*BLK,j*fs+c*BLK:j*fs+(c+1)*BLK],3)
        for r in range(2):
            for c in range(4):
                for j in range(HEADS): tile(3,r,c,j,self.down.at[j*fs+r*BLK:j*fs+(r+1)*BLK,c*BLK:(c+1)*BLK],4)
    def wait(self,*which):
        refs=(self.q,self.kv,self.out,self.up,self.down)
        for k in which: pltpu.make_async_copy(refs[k],refs[k],self.sems.at[k]).wait()

def rows_at(i,n): return pl.ds(pl.multiple_of(i*n,n),n)

CH=160
KB=320

def forward(w,gains,mp,h_full,own_rows,key_hoods,row_hoods,K,V,q,heads,lse,bias,hidden,r1,r2,emit):
    share=q.shape[0]; keys=K.shape[1]; chunks=share//CH
    start=mp*share
    def mask(i,_):
        rows=rows_at(i,CH)
        bias[rows,:]=jnp.where(row_hoods[rows,:]==key_hoods[...],0.0,MASK_VALUE)
        return 0
    lax.fori_loop(0,chunks,mask,0)
    w.wait(1)
    def project(i,_):
        j,kb=i//(keys//KB),i%(keys//KB)
        rows=rows_at(kb,KB)
        kv=nn(h_full[rows,:],w.kv[j]).astype(bf16)
        K[j,rows,:]=kv[:,:HD]; V[j,rows,:]=kv[:,HD:]
        return 0
    lax.fori_loop(0,HEADS*(keys//KB),project,0)
    w.wait(0)
    def queries(i,_):
        rows=rows_at(i,CH)
        x=h_full[pl.ds(pl.multiple_of(start+i*CH,CH),CH),:]
        q[rows,:]=nn(x,w.q[...]).astype(bf16)
        return 0
    lax.fori_loop(0,chunks,queries,0)
    lane=lax.broadcasted_iota(jnp.int32,(CH,BLK),1)
    def attend(i,_):
        rows=rows_at(i,CH)
        stats=jnp.zeros((CH,BLK),f32)
        for j in range(HEADS):
            s=nt(q[rows,j*HD:(j+1)*HD],K[j])+bias[rows,:]
            peak=jnp.max(s,axis=1,keepdims=True)
            p=jnp.exp2((s-peak)*(SCALE*LOG2E))
            total=jnp.sum(p,axis=1,keepdims=True)
            o=nn(p.astype(bf16),V[j])/total
            heads[rows,j*HD:(j+1)*HD]=o.astype(bf16)
            stats=jnp.where(lane==j,peak*(SCALE*LOG2E)+jnp.log2(total),stats)
        lse[rows,:]=stats
        return 0
    lax.fori_loop(0,chunks,attend,0)
    w.wait(2,3,4)
    def rest(i,_):
        rows=rows_at(i,CH)
        a=own_rows(i)+nn(heads[rows,:],w.out[...])
        r1[rows,:]=a
        first=normed(a)[0]*gains[0:1,:]+gains[1:2,:]
        hid=nn(first.astype(bf16),w.up[...])
        hidden[rows,:]=hid
        b=first+nn(gelu(hid).astype(bf16),w.down[...])
        r2[rows,:]=b
        emit(i,normed(b)[0]*gains[2:3,:]+gains[3:4,:])
        return 0
    lax.fori_loop(0,chunks,rest,0)

def backward(w,gains,mp,h_full,upper,key_hoods_col,row_hoods_row,K,V,q,heads,lse,biasT,hidden,r1,r2,
        dm,act,dhid,first,datt,dheads,delta,fg,dq,dkv,dhp,own_part,vec,put):
    share=q.shape[0]; keys=K.shape[1]; chunks=share//CH
    start=mp*share
    lane=lax.broadcasted_iota(jnp.int32,(CH,BLK),1)
    def colsum(v): return jnp.sum(v,axis=0,keepdims=True)
    def mask(i,_):
        rows=rows_at(i,KB)
        biasT[rows,:]=jnp.where(key_hoods_col[rows,:]==row_hoods_row[...],0.0,MASK_VALUE)
        return 0
    lax.fori_loop(0,keys//KB,mask,0)
    w.wait(0,1,2,3,4)
    def part(i,carry):
        rows=rows_at(i,CH)
        dy=upper(i)
        xhat,rho=normed(r2[rows,:])
        g2,s2=colsum(dy*xhat),colsum(dy)
        sg=norm_back(dy,xhat,rho,gains[2:3,:])
        dmb=sg.astype(bf16); dm[rows,:]=dmb
        a,slope=gelu_both(hidden[rows,:])
        act[rows,:]=a.astype(bf16)
        dh=(nt(dmb,w.down[...])*slope).astype(bf16)
        dhid[rows,:]=dh
        fu=sg+nt(dh,w.up[...])
        xhat,rho=normed(r1[rows,:])
        first[rows,:]=(xhat*gains[0:1,:]+gains[1:2,:]).astype(bf16)
        g1,s1=colsum(fu*xhat),colsum(fu)
        f=norm_back(fu,xhat,rho,gains[0:1,:])
        fg[rows,:]=f
        fb=f.astype(bf16); datt[rows,:]=fb
        dhe=nt(fb,w.out[...]).astype(bf16)
        dheads[rows,:]=dhe
        prod=dhe.astype(f32)*heads[rows,:].astype(f32)
        stats=jnp.zeros((CH,BLK),f32)
        for j in range(HEADS):
            stats=jnp.where(lane==j,jnp.sum(prod[:,j*HD:(j+1)*HD],axis=1,keepdims=True),stats)
        delta[rows,:]=stats
        return tuple(c+v for c,v in zip(carry,(g1,s1,g2,s2)))
    zero=jnp.zeros((1,D),f32)
    g1,s1,g2,s2=lax.fori_loop(0,chunks,part,(zero,)*4)
    vec[0:1,:]=g1; vec[1:2,:]=s1; vec[2:3,:]=g2; vec[3:4,:]=s2
    fs=FF//HEADS
    def tiles(kind,j,value,rr=None,c0=0):
        for r in range(value.shape[0]//BLK):
            for c in range(value.shape[1]//BLK):
                put(FIRST_BLOCK[kind]+r*COLS_TILE[kind]+c+c0,j,value[r*BLK:(r+1)*BLK,c*BLK:(c+1)*BLK].astype(bf16))
    for j in range(HEADS):
        tiles(3,j,tn(act[:,j*fs:(j+1)*fs],dm[...]))
        tiles(2,j,tn(first[...],dhid[:,j*fs:(j+1)*fs]))
        tiles(1,j,tn(heads[:,j*HD:(j+1)*HD],datt[...]))
    lseT=jnp.transpose(lse[...]); deltaT=jnp.transpose(delta[...])
    for j in range(HEADS):
        L=lseT[j:j+1,:]; dl=deltaT[j:j+1,:]
        qj=q[:,j*HD:(j+1)*HD]; doj=dheads[:,j*HD:(j+1)*HD]
        def keyblock(kb,acc):
            rows=rows_at(kb,KB)
            k=K[j,rows,:]; v=V[j,rows,:]
            p=jnp.exp2((nt(k,qj)+biasT[rows,:])*(SCALE*LOG2E)-L)
            dv=nn(p.astype(bf16),doj)
            ds=(p*(nt(v,doj)-dl)).astype(bf16)
            dk=nn(ds,qj)*SCALE
            dkv[j,rows,:]=jnp.concatenate([dk,dv],axis=1).astype(bf16)
            return acc+tn(ds,k)
        acc=lax.fori_loop(0,keys//KB,keyblock,jnp.zeros((share,HD),f32))
        dq[:,j*HD:(j+1)*HD]=(acc*SCALE).astype(bf16)
    def own(i,_):
        rows=rows_at(i,CH)
        own_part[rows,:]=fg[rows,:]+nt(dq[rows,:],w.q[...])
        return 0
    lax.fori_loop(0,chunks,own,0)
    def context(kb,_):
        rows=rows_at(kb,KB)
        t=nt(dkv[0,rows,:],w.kv[0])
        for j in range(1,HEADS): t=t+nt(dkv[j,rows,:],w.kv[j])
        dhp[rows,:]=t.astype(bf16)
        return 0
    lax.fori_loop(0,keys//KB,context,0)
    dhp[keys:,:]=jnp.zeros((dhp.shape[0]-keys,D),bf16)
    hown=h_full[pl.ds(pl.multiple_of(start,CH),share),:]
    hctx=h_full[:keys,:]
    for j in range(HEADS):
        tiles(0,j,tn(hown,dq[:,j*HD:(j+1)*HD]))
        tiles(0,j,tn(hctx,dkv[j]),c0=1)
BLK=128; STEP=10
BETA_ONE=0.9; BETA_TWO=0.95; BETA_STATS=0.95; RATE_MATRIX=0.12; DECAY_WEIGHT=0.01; ADAM_EPSILON=1e-8

def split(x):
    hi=x.astype(jnp.bfloat16)
    return hi,(x-hi.astype(jnp.float32)).astype(jnp.bfloat16)
def dot3(a,b,ca,cb):
    dims=(((ca,),(cb,)),((),()))
    ah,al=a; bh,bl=b
    d=lambda x,y: lax.dot_general(x,y,dims,preferred_element_type=jnp.float32)
    return d(ah,bh)+(d(ah,bl)+d(al,bh))
def dotf(a,b,ca,cb):
    return lax.dot_general(a,b,(((ca,),(cb,)),((),())),preferred_element_type=jnp.float32,precision=lax.Precision.HIGHEST)

def soap_kernel(slots, g_ref,m_ref,v_ref,l_ref,r_ref,ql_ref,qr_ref,w_ref, mo,vo,lo,ro,qlo,qro,wo, x_ref, a_ref):
    def first(i,_):
        g=g_ref[i]; ql=split(ql_ref[i]); qr=split(qr_ref[i])
        gs=split(g)
        m=BETA_ONE*m_ref[i]+(1-BETA_ONE)*g
        mo[i]=m
        def turn(v):
            return dot3(split(dot3(ql,v,0,0)),qr,1,0)
        tg=turn(gs)
        v=BETA_TWO*v_ref[i]+(1-BETA_TWO)*tg*tg
        vo[i]=v
        d=turn(split(m))/(1-BETA_ONE**STEP)/(jnp.sqrt(v/(1-BETA_TWO**STEP))+ADAM_EPSILON)
        u=dot3(split(dot3(ql,split(d),1,0)),qr,1,1)
        w=w_ref[i]
        wo[i]=w-RATE_MATRIX*(u+DECAY_WEIGHT*w)
        ln=BETA_STATS*l_ref[i]+(1-BETA_STATS)*dot3(gs,gs,1,1)
        rn=BETA_STATS*r_ref[i]+(1-BETA_STATS)*dot3(gs,gs,0,0)
        lo[i]=ln; ro[i]=rn
        al=dotf(ln,ql_ref[i],1,0); ar=dotf(rn,qr_ref[i],1,0)
        a_ref[2*i]=al; a_ref[2*i+1]=ar
        x_ref[2*i]=dotf(al,al,0,0); x_ref[2*i+1]=dotf(ar,ar,0,0)
        return 0
    lax.fori_loop(0,slots,first,0)
    n=2*slots
    lane=lax.broadcasted_iota(jnp.int32,(8,BLK),1)
    sub=lax.broadcasted_iota(jnp.int32,(8,BLK),0)
    for p in range(BLK//8):
        def step(kk,_):
            k=p*8+kk
            idx=jnp.full((8,BLK),k,jnp.int32)
            atk=lane==k
            below=sub>kk
            rows=[jnp.broadcast_to(x_ref[m,pl.ds(k,1),:],(8,BLK)) for m in range(n)]
            rinv=[1.0/jnp.take_along_axis(row,idx,axis=1) for row in rows]
            scaled=[jnp.where(atk,1.0,row)*ri for row,ri in zip(rows,rinv)]
            for m in range(n):
                for t in range(p,BLK//8):
                    v=x_ref[m,t*8:(t+1)*8,:]
                    f=jnp.take_along_axis(v,idx,axis=1)
                    new=jnp.where(atk,0.0,v)-f*scaled[m]
                    if t==p: new=jnp.where(below,new,v)
                    x_ref[m,t*8:(t+1)*8,:]=new
            return 0
        lax.fori_loop(0,8,step,0)
    r=lax.broadcasted_iota(jnp.int32,(BLK,BLK),0); c=lax.broadcasted_iota(jnp.int32,(BLK,BLK),1)
    def last(i,_):
        for s,out in ((0,qlo),(1,qro)):
            x=x_ref[2*i+s]
            piv=jnp.sum(jnp.where(r==c,x,0.0),axis=1,keepdims=True)
            inv=jnp.where(r==c,1.0,jnp.where(r>c,x,0.0))*lax.rsqrt(piv)
            out[i]=dotf(a_ref[2*i+s],inv,1,1)
        return 0
    lax.fori_loop(0,slots,last,0)

def soap(g,m,v,l,r,ql,qr,w):
    slots=g.shape[0]
    sh=jax.ShapeDtypeStruct((slots,BLK,BLK),jnp.float32)
    vm=pl.BlockSpec(memory_space=pltpu.VMEM)
    return pl.pallas_call(partial(soap_kernel,slots),out_shape=[sh]*7,in_specs=[vm]*8,out_specs=[vm]*7,
        scratch_shapes=[pltpu.VMEM((2*slots,BLK,BLK),jnp.float32)]*2,
        compiler_params=pltpu.CompilerParams(vmem_limit_bytes=48<<20),name="soap")(g,m,v,l,r,ql,qr,w)
def adam_vector(grad, first, second, weight):
    first_new = BETA_ONE * first + (1.0 - BETA_ONE) * grad
    second_new = BETA_TWO * second + (1.0 - BETA_TWO) * grad * grad
    weight_new = weight - RATE_VECTOR * (first_new / (1.0 - BETA_ONE**STEP)) / (
        jnp.sqrt(second_new / (1.0 - BETA_TWO**STEP)) + ADAM_EPSILON
    )
    return (first_new, second_new, weight_new)


def pl_shape(shape,dtype): return jax.ShapeDtypeStruct(shape,dtype)

def first_kernel(slots,owners,h_full,wall,gains,key_hoods,row_hoods,out,out_low,K,V,q,heads,lse,hidden,r1,r2,bias,sems,*wrefs):
    w=Weights(0,owners,wall,slots,wrefs,sems)
    mp=lax.axis_index("mp"); share=q.shape[0]
    def own(i): return h_full[pl.ds(pl.multiple_of(mp*share+i*CH,CH),CH),:].astype(f32)
    def emit(i,v):
        out[rows_at(i,CH),:]=v; out_low[rows_at(i,CH),:]=v.astype(bf16)
    forward(w,gains,mp,h_full,own,key_hoods,row_hoods,K,V,q,heads,lse,bias,hidden,r1,r2,emit)

def second_kernel(slots,owners,h_full,h_own,wall,gains,key_hoods,row_hoods,key_col,row_line,cot,
        layer_out,g2,dhp,own_part,vec,K,V,q,heads,lse,hidden,r1,r2,bias,biasT,dm,act,dhid,first,datt,dheads,delta,fg,dq,dkv,sems,*wrefs):
    w=Weights(1,owners,wall,slots,wrefs,sems)
    mp=lax.axis_index("mp"); share=q.shape[0]
    def emit(i,v): layer_out[rows_at(i,CH),:]=v
    forward(w,gains,mp,h_full,lambda i: h_own[rows_at(i,CH),:],key_hoods,row_hoods,K,V,q,heads,lse,bias,hidden,r1,r2,emit)
    w.wait=lambda *k: None
    def upper(i): return cot[pl.ds(pl.multiple_of(mp*share+i*CH,CH),CH),:].astype(f32)
    def put(b,j,v): g2[b,j]=v
    backward(w,gains,mp,h_full,upper,key_col,row_line,K,V,q,heads,lse,biasT,hidden,r1,r2,dm,act,dhid,first,datt,dheads,delta,fg,dq,dkv,dhp,own_part,vec,put)

def third_kernel(slots,owners,h_full,wall,gains,key_col,row_line,K,V,q,heads,lse,hidden,r1,r2,up,g2,
        gout,dhp,own_part,vec,biasT,dm,act,dhid,first,datt,dheads,delta,fg,dq,dkv,sems,*wrefs):
    w=Weights(0,owners,wall,slots,wrefs,sems)
    mp=lax.axis_index("mp"); share=q.shape[0]
    def place(b):
        slot=owners[b]
        return slot//slots,pl.ds(pl.multiple_of(slot%slots*BLK,BLK),BLK)
    def move(b,_):
        d,rows=place(b+LAYER_BLOCKS)
        for j in range(HEADS): gout[d,j,rows,:]=g2[b,j]
        return 0
    lax.fori_loop(0,LAYER_BLOCKS,move,0)
    def put(b,j,v):
        d,rows=place(b)
        gout[d,j,rows,:]=v
    backward(w,gains,mp,h_full,lambda i: up[rows_at(i,CH),:],key_col,row_line,K,V,q,heads,lse,biasT,hidden,r1,r2,dm,act,dhid,first,datt,dheads,delta,fg,dq,dkv,dhp,own_part,vec,put)

def kept_shapes(share,keys):
    return [((HEADS,keys,HD),bf16),((HEADS,keys,HD),bf16),((share,D),bf16),((share,D),bf16),((share,BLK),f32),((share,FF),f32),((share,D),f32),((share,D),f32)]
def back_scratch(share,keys):
    v=pltpu.VMEM
    return [v((keys,share),f32),v((share,D),bf16),v((share,FF),bf16),v((share,FF),bf16),v((share,D),bf16),v((share,D),bf16),v((share,D),bf16),
        v((share,BLK),f32),v((share,D),f32),v((share,D),bf16),v((HEADS,keys,2*HD),bf16)]

def params(mib): return pltpu.CompilerParams(vmem_limit_bytes=mib<<20)

def local(tokens,cotangent,context_sizes,query_hoods,owners,master_blocks,first_blocks,second_blocks,left_blocks,right_blocks,
        left_bases,right_bases,vector_master,vector_moment,vector_square):
    dp=lax.axis_size("dp"); mp=lax.axis_index("mp")
    rows=tokens.shape[0]; keys=rows-query_hoods.shape[0]; share=rows//HEADS; slots=master_blocks.shape[0]
    n=vector_master.shape[0]
    high=vector_master.astype(bf16)
    rest=(vector_master-high.astype(f32)).astype(bf16)
    extra=jnp.pad(jnp.stack([high,rest]),((0,14),(0,BLK-n)))
    slab=jnp.concatenate([master_blocks.astype(bf16).reshape(slots*BLK,BLK),extra],axis=0)
    wall=gather_all(slab,dp,0)
    pair=wall[:,:,slots*BLK:slots*BLK+2,:n].astype(f32)
    gains=(pair[:,:,0]+pair[:,:,1]).reshape(LAYERS,4,D)
    sizes=context_sizes[0]
    order=jnp.arange(sizes.shape[0],dtype=jnp.int32)
    ends=jnp.sum(jnp.where(order[None,:]<=order[:,None],sizes[None,:],0),axis=1)
    positions=jnp.arange(keys,dtype=jnp.int32)
    key_hoods=jnp.sum((positions[:,None]>=ends[None,:]).astype(jnp.int32),axis=1)
    own_hoods=lax.dynamic_slice_in_dim(jnp.concatenate([key_hoods,query_hoods]),mp*share,share)
    key_line,key_col=key_hoods[None,:],key_hoods[:,None]
    row_line,row_col=own_hoods[None,:],own_hoods[:,None]
    kept=kept_shapes(share,keys)
    wsc=[pltpu.SemaphoreType.DMA((5,))]+weight_shapes()
    V_=VMEM_SPEC
    out=pl.pallas_call(partial(first_kernel,slots),
        out_shape=[pl_shape((share,D),f32),pl_shape((share,D),bf16)]+[pl_shape(*k) for k in kept],
        in_specs=[SMEM_SPEC,V_,ANY_SPEC,V_,V_,V_],out_specs=[V_]*10,
        scratch_shapes=[pltpu.VMEM((share,keys),f32)]+wsc,compiler_params=params(56),name="first_layer")(
        owners,tokens,wall,gains[0],key_line,row_col)
    h_own,h_low,saved=out[0],out[1],out[2:]
    h_full=share_rows(h_low,2)
    layer_out,g2,dhp,own_part,vec2=pl.pallas_call(partial(second_kernel,slots),
        out_shape=[pl_shape((share,D),f32),pl_shape((LAYER_BLOCKS,HEADS,BLK,BLK),bf16),pl_shape((rows,D),bf16),pl_shape((share,D),f32),pl_shape((4,D),f32)],
        in_specs=[SMEM_SPEC,V_,V_,ANY_SPEC]+[V_]*6,out_specs=[V_]*5,
        scratch_shapes=[pltpu.VMEM(*k) for k in kept]+[pltpu.VMEM((share,keys),f32)]+back_scratch(share,keys)+wsc,
        compiler_params=params(60),name="second_layer")(
        owners,h_full,h_own,wall,gains[1],key_line,row_col,key_col,row_line,cotangent)
    upper=total_rows(dhp,own_part,3)
    gout,dhp,own_part,vec1=pl.pallas_call(partial(third_kernel,slots),
        out_shape=[pl_shape(wall.shape,bf16),pl_shape((rows,D),bf16),pl_shape((share,D),f32),pl_shape((4,D),f32)],
        in_specs=[SMEM_SPEC,V_,ANY_SPEC]+[V_]*13,out_specs=[V_]*4,
        scratch_shapes=back_scratch(share,keys)+wsc,
        compiler_params=params(60),name="first_layer_back")(
        owners,tokens,wall,gains[0],key_col,row_line,*saved,upper,g2)
    tokens_grad=total_rows(dhp,own_part,4)
    vec=jnp.stack([vec1,vec2]).astype(bf16).reshape(dp,HEADS,1,n)
    vec=jnp.pad(vec,((0,0),(0,0),(0,15),(0,BLK-n)))
    gout=lax.dynamic_update_slice(gout,vec,(0,0,slots*BLK,0))
    total=reduce_all(gout,1)
    results=soap(total[:slots*BLK].reshape(slots,BLK,BLK),first_blocks,second_blocks,left_blocks,right_blocks,left_bases,right_bases,master_blocks)
    vector_results=adam_vector(total[slots*BLK,:n],vector_moment,vector_square,vector_master)
    return (layer_out,tokens_grad)+tuple(results)+vector_results


def solution(mesh):
    return jax.shard_map(
        local,
        mesh=mesh,
        in_specs=(
            P("dp", None),
            P("dp", None),
            P("dp", None),
            P("dp"),
            P(),
            P("dp", "mp", None),
            P("dp", "mp", None),
            P("dp", "mp", None),
            P("dp", "mp", None),
            P("dp", "mp", None),
            P("dp", "mp", None),
            P("dp", "mp", None),
            P(("dp", "mp")),
            P(("dp", "mp")),
            P(("dp", "mp")),
        ),
        out_specs=(
            P(("dp", "mp"), None),
            P(("dp", "mp"), None),
            P("dp", "mp", None),
            P("dp", "mp", None),
            P("dp", "mp", None),
            P("dp", "mp", None),
            P("dp", "mp", None),
            P("dp", "mp", None),
            P("dp", "mp", None),
            P(("dp", "mp")),
            P(("dp", "mp")),
            P(("dp", "mp")),
        ),
        check_vma=False,
    )
```

```python
import math
from functools import partial

import jax
import jax.numpy as jnp
from jax import lax
from jax.experimental import pallas as pl
from jax.experimental.pallas import tpu as pltpu
from jax.sharding import PartitionSpec as P

RATE_VECTOR = 0.6
MESH=pl.DeviceIdType.MESH
BLK=128
VMEM_SPEC=pl.BlockSpec(memory_space=pltpu.VMEM)
ANY_SPEC=pl.BlockSpec(memory_space=pl.ANY)

def remote(src,dst,send,recv,device):
    return pltpu.make_async_remote_copy(src_ref=src,dst_ref=dst,send_sem=send,recv_sem=recv,device_id=device,device_id_type=MESH)

class Spot:
    def __init__(self,planes):
        dp,mp=lax.axis_index("dp"),lax.axis_index("mp")
        self.dp,self.mp,self.planes=dp,mp,planes
        self.z,self.x=dp//2,dp%2
        self.y,self.c=mp//2,mp%2
        self.across_x=(dp+1-2*self.x,mp)
        self.across_y=(dp,(mp+2)%4)
        self.sibling=(dp,mp+1-2*self.c)
        self.up=(jnp.minimum(dp+2,2*planes-1),mp)
        self.down=(jnp.maximum(dp-2,0),mp)
    def greet(self):
        bar=pltpu.get_barrier_semaphore()
        for who in (self.across_x,self.across_y,self.sibling):
            pl.semaphore_signal(bar,inc=1,device_id=who,device_id_type=MESH)
        @pl.when(self.z<self.planes-1)
        def _(): pl.semaphore_signal(bar,inc=1,device_id=self.up,device_id_type=MESH)
        @pl.when(self.z>0)
        def _(): pl.semaphore_signal(bar,inc=1,device_id=self.down,device_id_type=MESH)
        pl.semaphore_wait(bar,3+jnp.minimum(self.z,1)+jnp.minimum(self.planes-1-self.z,1))
    def ring(self,r,action):
        if r==0:
            action(self.z,None); return
        @pl.when(self.z>=r)
        def _(): action(self.z-r,True)
        @pl.when(self.z+r<self.planes)
        def _(): action(self.z+r,False)

def gather_kernel(planes,half,slab,out,send,recv,zsend,zrecv,lsem):
    s=Spot(planes); rows=slab.shape[0]; z,x,y,c,mp=s.z,s.x,s.y,s.c,s.mp
    A,B=pl.ds(0,half),pl.ds(half,rows-half)
    mx,my=s.across_x,s.across_y
    own=pltpu.make_async_copy(slab,out.at[s.dp,mp],lsem); own.start()
    s.greet()
    def at(p,xx,yy,cc): return out.at[p*2+xx,yy*2+cc]
    xo,yo=1-x,1-y
    def copies(p,src):
        here=at(p,x,y,c) if src is None else src
        f=lambda k,a,b,w: remote(a,b,send.at[k,p],recv.at[k,p],w)
        return dict(
            xown=lambda: f(0,here,at(p,x,y,c),mx), yown=lambda: f(1,here,at(p,x,y,c),my), cown=lambda: f(2,here,at(p,x,y,c),s.sibling),
            yfwd=lambda: f(3,at(p,xo,y,c).at[A],at(p,xo,y,c).at[A],my),
            xfwd=lambda: f(4,at(p,x,yo,c).at[B],at(p,x,yo,c).at[B],mx),
            cx=lambda: f(5,at(p,xo,y,c),at(p,xo,y,c),s.sibling), cy=lambda: f(6,at(p,x,yo,c),at(p,x,yo,c),s.sibling),
            ca=lambda: f(7,at(p,xo,yo,c).at[A],at(p,xo,yo,c).at[A],s.sibling),
            cb=lambda: f(8,at(p,xo,yo,c).at[B],at(p,xo,yo,c).at[B],s.sibling))
    def zcopy(p,up,src=None):
        here=at(p,x,y,c) if src is None else src
        return remote(here,at(p,x,y,c),zsend.at[0 if up else 1,p],zrecv.at[p],s.up if up else s.down)
    def arrive(r):
        def act(p,below):
            src=None
            if below is None: src=slab
            else: zcopy(p,below).wait_recv()
            if below is None or below:
                @pl.when(z<planes-1)
                def _(): zcopy(p,True,src).start()
            if below is None or not below:
                @pl.when(z>0)
                def _(): zcopy(p,False,src).start()
            k=copies(p,src)
            k["xown"]().start(); k["yown"]().start(); k["cown"]().start()
        s.ring(r,act)
    def second(r):
        def act(p,below):
            k=copies(p,None)
            k["xown"]().wait_recv(); k["yfwd"]().start(); k["cx"]().start()
            k["yown"]().wait_recv(); k["xfwd"]().start(); k["cy"]().start()
        s.ring(r,act)
    def third(r):
        def act(p,below):
            k=copies(p,None)
            k["yfwd"]().wait_recv(); k["ca"]().start()
            k["xfwd"]().wait_recv(); k["cb"]().start()
        s.ring(r,act)
    def finish(r):
        def act(p,below):
            src=slab if below is None else None
            k=copies(p,src)
            for n in ("cown","cx","cy","ca","cb"): k[n]().wait_recv()
            for n in k: k[n]().wait_send()
            if below is None or below:
                @pl.when(z<planes-1)
                def _(): zcopy(p,True,src).wait_send()
            if below is None or not below:
                @pl.when(z>0)
                def _(): zcopy(p,False,src).wait_send()
        s.ring(r,act)
    for r in range(planes+2):
        if r<planes: arrive(r)
        if 1<=r<=planes: second(r-1)
        if r>=2: third(r-2)
    for r in range(planes): finish(r)
    own.wait()

def gather_all(slab,dp,collective):
    rows=slab.shape[0]; planes=dp//2; half=rows//2//16*16
    dma=pltpu.SemaphoreType.DMA
    return pl.pallas_call(partial(gather_kernel,planes,half),
        out_shape=jax.ShapeDtypeStruct((dp,4,rows,slab.shape[1]),slab.dtype),
        in_specs=[ANY_SPEC],out_specs=ANY_SPEC,
        scratch_shapes=[dma((9,planes)),dma((9,planes)),dma((2,planes)),dma((planes,)),dma],
        compiler_params=pltpu.CompilerParams(collective_id=collective,has_side_effects=True),name="gather_all")(slab)

def reduce_kernel(planes,half,slots,blocks,inner,extra,out,g,rc,acc,ya,xb,xa,yb,own,zin,send,recv,zsend,zrecv):
    s=Spot(planes); rows=g.shape[2]; z,x,y,c,mp=s.z,s.x,s.y,s.c,s.mp
    A,B=pl.ds(0,half),pl.ds(half,rows-half)
    mx,my=s.across_x,s.across_y
    xo,yo,co=1-x,1-y,1-c
    s.greet()
    f32=lambda v: v.astype(jnp.float32)
    def core(p,xx,yy):
        k=xx*2+yy
        return remote(g.at[p*2+xx,yy*2+co],rc.at[p*4+k],send.at[k,p],recv.at[k,p],s.sibling)
    def toya(p,xx): return remote(acc.at[p*4+xx*2+yo,A],ya.at[p*2+xx],send.at[4+xx,p],recv.at[4+xx,p],my)
    def toxb(p,yy): return remote(acc.at[p*4+xo*2+yy,B],xb.at[p*2+yy],send.at[6+yy,p],recv.at[6+yy,p],mx)
    def toxa(p): return remote(ya.at[p*2+xo],xa.at[p],send.at[8,p],recv.at[8,p],mx)
    def toyb(p): return remote(xb.at[p*2+yo],yb.at[p],send.at[9,p],recv.at[9,p],my)
    def toz(p,up): return remote(own.at[p],zin.at[0 if up else 1,p],zsend.at[p],zrecv.at[0 if up else 1,p],s.up if up else s.down)
    def pack(p,parity):
        for xx in (0,1):
            d=p*2+xx
            def one(k,_):
                block=inner[d*slots+k]
                for yy in (0,1):
                    g[d,yy*2+parity,pl.ds(pl.multiple_of(k*BLK,BLK),BLK),:]=blocks[block,yy*2+parity]
                return 0
            lax.fori_loop(0,slots,one,0)
            for yy in (0,1): g[d,yy*2+parity,slots*BLK:,:]=extra[d,yy*2+parity]
    def start(p,_):
        pack(p,co)
        for xx in (0,1):
            for yy in (0,1): core(p,xx,yy).start()
    def first(p,_):
        pack(p,c)
        for xx in (0,1):
            for yy in (0,1):
                core(p,xx,yy).wait_recv()
                acc[p*4+xx*2+yy]=(f32(g[p*2+xx,yy*2+c])+f32(rc[p*4+xx*2+yy])).astype(acc.dtype)
        for e in (0,1): toya(p,e).start(); toxb(p,e).start()
    def second(p,_):
        for e in (0,1):
            toya(p,e).wait_recv()
            ya[p*2+e]=(f32(acc[p*4+e*2+y,A])+f32(ya[p*2+e])).astype(ya.dtype)
        toxa(p).start()
        for e in (0,1):
            toxb(p,e).wait_recv()
            xb[p*2+e]=(f32(acc[p*4+x*2+e,B])+f32(xb[p*2+e])).astype(xb.dtype)
        toyb(p).start()
    def third(p,below):
        toxa(p).wait_recv()
        av=f32(ya[p*2+x])+f32(xa[p])
        toyb(p).wait_recv()
        bv=f32(xb[p*2+y])+f32(yb[p])
        if below is None:
            out[A]=av; out[B]=bv
            @pl.when(z>0)
            def _():
                toz(p,True).wait_recv()
                out[...]=out[...]+f32(zin[0,p])
            @pl.when(z<planes-1)
            def _():
                toz(p,False).wait_recv()
                out[...]=out[...]+f32(zin[1,p])
            return
        own[p,A]=av.astype(own.dtype); own[p,B]=bv.astype(own.dtype)
        up=not below
        has=(z>0) if up else (z<planes-1)
        @pl.when(has)
        def _():
            toz(p,up).wait_recv()
            own[p,A]=(av+f32(zin[0 if up else 1,p,A])).astype(own.dtype)
            own[p,B]=(bv+f32(zin[0 if up else 1,p,B])).astype(own.dtype)
        toz(p,up).start()
    def finish(p,below):
        for xx in (0,1):
            for yy in (0,1): core(p,xx,yy).wait_send()
        for e in (0,1): toya(p,e).wait_send(); toxb(p,e).wait_send()
        toxa(p).wait_send(); toyb(p).wait_send()
        if below is not None: toz(p,not below).wait_send()
    order=list(range(planes-1,-1,-1))
    for r in order: s.ring(r,start)
    n=len(order)
    for i in range(n+2):
        if i<n: s.ring(order[i],first)
        if 0<=i-1<n: s.ring(order[i-1],second)
        if 0<=i-2<n: s.ring(order[i-2],third)
    for r in order: s.ring(r,finish)

def reduce_all(g,extra,inner,slots,collective):
    dp=extra.shape[0]; rows,cols=slots*BLK+extra.shape[2],g.shape[3]; planes=dp//2; half=rows//2//16*16
    dma=pltpu.SemaphoreType.DMA; bf=lambda *sh: pltpu.VMEM(sh+(cols,),g.dtype)
    return pl.pallas_call(partial(reduce_kernel,planes,half,slots),
        out_shape=jax.ShapeDtypeStruct((rows,cols),jnp.float32),in_specs=[VMEM_SPEC,pl.BlockSpec(memory_space=pltpu.SMEM),VMEM_SPEC],out_specs=VMEM_SPEC,
        scratch_shapes=[bf(dp,4,rows),bf(planes*4,rows),bf(planes*4,rows),bf(planes*2,half),bf(planes*2,rows-half),bf(planes,half),bf(planes,rows-half),
            bf(planes,rows),bf(2,planes,rows),dma((10,planes)),dma((10,planes)),dma((planes,)),dma((2,planes))],
        compiler_params=pltpu.CompilerParams(collective_id=collective,has_side_effects=True,vmem_limit_bytes=56<<20),name="reduce_all")(g,inner,extra)
D=512; HD=128; FF=1024; LAYERS=2; BLK=128; HEADS=4
NORM_EPSILON=1e-5; MASK_VALUE=-1e30
f32=jnp.float32; bf16=jnp.bfloat16
SMEM_SPEC=pl.BlockSpec(memory_space=pltpu.SMEM)
SCALE=HD**-0.5; LOG2E=math.log2(math.e)
ROOT=math.sqrt(2/math.pi)

def nn(a,b): return lax.dot_general(a,b,(((1,),(0,)),((),())),preferred_element_type=f32)
def nt(a,b): return lax.dot_general(a,b,(((1,),(1,)),((),())),preferred_element_type=f32)
def tn(a,b): return lax.dot_general(a,b,(((0,),(0,)),((),())),preferred_element_type=f32)

def normed(r):
    center=r-jnp.mean(r,axis=-1,keepdims=True)
    rho=lax.rsqrt(jnp.mean(center*center,axis=-1,keepdims=True)+NORM_EPSILON)
    return center*rho,rho
def norm_back(dy,xhat,rho,gain):
    inner=dy*gain
    return rho*(inner-jnp.mean(inner,axis=-1,keepdims=True)-xhat*jnp.mean(inner*xhat,axis=-1,keepdims=True))
def gelu(v): return 0.5*v*(1+jnp.tanh(ROOT*(v+0.044715*v*v*v)))
def gelu_both(v):
    sq=v*v
    t=jnp.tanh(ROOT*v*(1+0.044715*sq))
    half=0.5*(1+t)
    return v*half,half+0.5*v*(1-t*t)*(ROOT*(1+3*0.044715*sq))
def colsum(v): return jnp.sum(v,axis=0,keepdims=True)

COLS_TILE=(3,4,2,4)
FIRST_BLOCK=(0,12,16,24)
LAYER_BLOCKS=32
CH=160
KB=320
FS=FF//HEADS

def rows_at(i,n): return pl.ds(pl.multiple_of(i*n,n),n)

class Weights:
    def __init__(self,refs): self.q,self.kv,self.out,self.up,self.down=refs
    def fill(self,layer,owners,wallv):
        base=layer*LAYER_BLOCKS
        def tiles(b):
            slot=owners[b]
            return [wallv[slot,j] for j in range(HEADS)]
        def by_row(r,_):
            rows=rows_at(r,BLK)
            for c in range(3):
                for j,v in enumerate(tiles(base+r*3+c)):
                    if c==0: self.q[rows,j*BLK:(j+1)*BLK]=v
                    else: self.kv[j,rows,(c-1)*BLK:c*BLK]=v
            for c in range(2):
                for j,v in enumerate(tiles(base+FIRST_BLOCK[2]+r*2+c)): self.up[rows,j*FS+c*BLK:j*FS+(c+1)*BLK]=v
            return 0
        lax.fori_loop(0,D//BLK,by_row,0)
        for c in range(4):
            for j,v in enumerate(tiles(base+FIRST_BLOCK[1]+c)): self.out[j*BLK:(j+1)*BLK,c*BLK:(c+1)*BLK]=v
            for r in range(2):
                for j,v in enumerate(tiles(base+FIRST_BLOCK[3]+r*4+c)): self.down[j*FS+r*BLK:j*FS+(r+1)*BLK,c*BLK:(c+1)*BLK]=v

def forward(w,gains,start,h_full,own_rows,KV,q,heads,lse,bias,hidden,r1,r2,emit):
    keys=KV.shape[1]; chunks=q.shape[0]//CH; blocks=keys//KB
    def project(i,_):
        j,rows=i//blocks,rows_at(i%blocks,KB)
        KV[j,rows,:]=nn(h_full[rows,:],w.kv[j]).astype(bf16)
        return 0
    lax.fori_loop(0,HEADS*blocks,project,0)
    def queries(i,_):
        q[rows_at(i,CH),:]=nn(h_full[pl.ds(pl.multiple_of(start+i*CH,CH),CH),:],w.q[...]).astype(bf16)
        return 0
    lax.fori_loop(0,chunks,queries,0)
    lane=lax.broadcasted_iota(jnp.int32,(CH,BLK),1)
    def attend(i,_):
        rows=rows_at(i,CH)
        stats=jnp.zeros((CH,BLK),f32)
        for j in range(HEADS):
            s=nt(q[rows,j*HD:(j+1)*HD],KV[j,:,:HD])+bias[rows,:].astype(f32)
            peak=jnp.max(s,axis=1,keepdims=True)
            p=jnp.exp2((s-peak)*(SCALE*LOG2E))
            total=jnp.sum(p,axis=1,keepdims=True)
            o=nn(p.astype(bf16),KV[j,:,HD:])/total
            heads[rows,j*HD:(j+1)*HD]=o.astype(bf16)
            stats=jnp.where(lane==j,peak*(SCALE*LOG2E)+jnp.log2(total),stats)
        lse[rows,:]=stats
        return 0
    lax.fori_loop(0,chunks,attend,0)
    for i in range(chunks):
        rows=pl.ds(i*CH,CH)
        a=own_rows(i)+nn(heads[rows,:],w.out[...])
        r1[rows,:]=a
        first=normed(a)[0]*gains[0:1,:]+gains[1:2,:]
        hid=nn(first.astype(bf16),w.up[...])
        hidden[rows,:]=hid
        b=first+nn(gelu(hid).astype(bf16),w.down[...])
        r2[rows,:]=b
        emit(i,normed(b)[0]*gains[2:3,:]+gains[3:4,:])

def backward(w,gains,start,h_full,upper,KV,q,heads,lse,biasT,hidden,r1,r2,
        dm,act,dhid,first,datt,dheads,delta,grad,dq,dhp,vec,put,exchange):
    share=q.shape[0]; keys=KV.shape[1]; chunks=share//CH
    lane=lax.broadcasted_iota(jnp.int32,(CH,BLK),1)
    def part(i,carry):
        rows=rows_at(i,CH)
        dy=upper(i)
        xhat,rho=normed(r2[rows,:])
        g2,s2=colsum(dy*xhat),colsum(dy)
        sg=norm_back(dy,xhat,rho,gains[2:3,:])
        dmb=sg.astype(bf16); dm[rows,:]=dmb
        a,slope=gelu_both(hidden[rows,:])
        act[rows,:]=a.astype(bf16)
        dh=(nt(dmb,w.down[...])*slope).astype(bf16)
        dhid[rows,:]=dh
        fu=sg+nt(dh,w.up[...])
        xhat,rho=normed(r1[rows,:])
        first[rows,:]=(xhat*gains[0:1,:]+gains[1:2,:]).astype(bf16)
        g1,s1=colsum(fu*xhat),colsum(fu)
        f=norm_back(fu,xhat,rho,gains[0:1,:])
        grad[rows,:]=f
        fb=f.astype(bf16); datt[rows,:]=fb
        dhe=nt(fb,w.out[...]).astype(bf16)
        dheads[rows,:]=dhe
        prod=dhe.astype(f32)*heads[rows,:].astype(f32)
        stats=jnp.zeros((CH,BLK),f32)
        for j in range(HEADS):
            stats=jnp.where(lane==j,jnp.sum(prod[:,j*HD:(j+1)*HD],axis=1,keepdims=True),stats)
        delta[rows,:]=stats
        return tuple(c+v for c,v in zip(carry,(g1,s1,g2,s2)))
    zero=jnp.zeros((1,D),f32)
    for k,v in enumerate(lax.fori_loop(0,chunks,part,(zero,)*4)): vec(k,v)
    lseT=jnp.transpose(lse[...]); deltaT=jnp.transpose(delta[...])
    for j in range(HEADS):
        L=lseT[j:j+1,:]; dl=deltaT[j:j+1,:]
        qj=q[:,j*HD:(j+1)*HD]; doj=dheads[:,j*HD:(j+1)*HD]
        def keyblock(kb,acc):
            rows=rows_at(kb,KB)
            k=KV[j,rows,:HD]; v=KV[j,rows,HD:]
            p=jnp.exp2((nt(k,qj)+biasT[rows,:].astype(f32))*(SCALE*LOG2E)-L)
            dv=nn(p.astype(bf16),doj)
            ds=(p*(nt(v,doj)-dl)).astype(bf16)
            dk=nn(ds,qj)*SCALE
            acc=acc+tn(ds,k)
            KV[j,rows,:]=jnp.concatenate([dk,dv],axis=1).astype(bf16)
            return acc
        acc=lax.fori_loop(0,keys//KB,keyblock,jnp.zeros((share,HD),f32))
        dq[:,j*HD:(j+1)*HD]=(acc*SCALE).astype(bf16)
    def context(kb,_):
        rows=rows_at(kb,KB)
        t=nt(KV[0,rows,:],w.kv[0])
        for j in range(1,HEADS): t=t+nt(KV[j,rows,:],w.kv[j])
        dhp[rows,:]=t.astype(bf16)
        return 0
    lax.fori_loop(0,keys//KB,context,0)
    dhp[keys:,:]=jnp.zeros((dhp.shape[0]-keys,D),bf16)
    exchange.start()
    def own(i,_):
        rows=rows_at(i,CH)
        grad[rows,:]=grad[rows,:]+nt(dq[rows,:],w.q[...])
        return 0
    lax.fori_loop(0,chunks,own,0)
    def tiles(kind,j,value,c0=0):
        for r in range(value.shape[0]//BLK):
            for c in range(value.shape[1]//BLK):
                put(FIRST_BLOCK[kind]+r*COLS_TILE[kind]+c+c0,j,value[r*BLK:(r+1)*BLK,c*BLK:(c+1)*BLK].astype(bf16))
    for j in range(HEADS): tiles(3,j,tn(act[:,j*FS:(j+1)*FS],dm[...]))
    exchange.middle()
    for j in range(HEADS):
        tiles(2,j,tn(first[...],dhid[:,j*FS:(j+1)*FS]))
        tiles(1,j,tn(heads[:,j*HD:(j+1)*HD],datt[...]))
    hown=h_full[pl.ds(pl.multiple_of(start,CH),share),:]
    hctx=h_full[:keys,:]
    for j in range(HEADS):
        tiles(0,j,tn(hown,dq[:,j*HD:(j+1)*HD]))
        tiles(0,j,tn(hctx,KV[j]),c0=1)
    exchange.finish()

class Exchange:
    def __init__(self,s,terms,grad,rc,acc,ry,send,recv):
        self.s,self.terms,self.grad,self.rc,self.acc,self.ry=s,terms,grad,rc,acc,ry
        self.n=send.shape[1]; rows=grad.shape[0]; step=rows//self.n
        self.far=s.across_y[1]; co=1-s.c
        self.part=lambda i: pl.ds(i*step,step)
        self.at=lambda k,i: pl.ds(pl.multiple_of(k*rows+i*step,16),step)
        self.a=lambda i: remote(terms.at[self.at((1-s.y)*2+co,i)],rc.at[0,self.part(i)],send.at[0,i],recv.at[0,i],s.sibling)
        self.b=lambda i: remote(terms.at[self.at(s.y*2+co,i)],rc.at[1,self.part(i)],send.at[1,i],recv.at[1,i],s.sibling)
        self.o=lambda i: remote(acc.at[self.part(i)],ry.at[self.part(i)],send.at[2,i],recv.at[2,i],s.across_y)
    def start(self):
        for i in range(self.n): self.a(i).start()
        for i in range(self.n): self.b(i).start()
    def middle(self):
        for i in range(self.n):
            self.a(i).wait_recv()
            self.acc[self.part(i)]=(self.terms[self.at(self.far,i)].astype(f32)+self.rc[0,self.part(i)].astype(f32)).astype(bf16)
            self.o(i).start()
    def finish(self):
        for i in range(self.n):
            rows=self.part(i)
            self.b(i).wait_recv()
            t=self.grad[rows]+(self.terms[self.at(self.s.mp,i)].astype(f32)+self.rc[1,rows].astype(f32))
            self.o(i).wait_recv()
            self.grad[rows]=t+self.ry[rows].astype(f32)
        for i in range(self.n):
            for k in (self.a,self.b,self.o): k(i).wait_send()

def layers_kernel(slots,owners,sizes,tokens,cot,wall,gains,qline,qcol, layer_out,tokens_grad,g,vec,
        wallv,tok,h2,cotv,KV1,KV2,q1,q2,heads1,heads2,lse1,lse2,hid1,hid2,ra1,ra2,rb1,rb2,bias,biasT,
        dm,act,dhid,first,datt,dheads,delta,dq,dhp,rc,acc,ry,wa,wb,wc,wd,we,xa,xb,xc,xd,xe,lsem,ssend,srecv,tsend,trecv):
    s=Spot(1); mp=s.mp; share=q1.shape[0]; keys=KV1.shape[1]; chunks=share//CH
    start=mp*share
    def bring(k,_):
        pltpu.make_async_copy(wall.at[k//slots,:,rows_at(k%slots,BLK),:],wallv.at[k],lsem.at[1]).start()
        return 0
    lax.fori_loop(0,wallv.shape[0],bring,0)
    loads=[pltpu.make_async_copy(tokens,tok,lsem.at[0]),pltpu.make_async_copy(wallv,wallv,lsem.at[1]),
           pltpu.make_async_copy(cot.at[pl.ds(pl.multiple_of(start,CH),share)],cotv,lsem.at[2])]
    for c in (0,2): loads[c].start()
    bar=pltpu.get_barrier_semaphore()
    for who in (s.across_y,s.sibling): pl.semaphore_signal(bar,inc=1,device_id=who,device_id_type=MESH)
    ends=[]; total=jnp.int32(0)
    for k in range(sizes.shape[1]):
        total=total+sizes[0,k]; ends.append(total)
    def hood(index):
        h=jnp.zeros(index.shape,jnp.int32)
        for e in ends: h=h+(index>=e).astype(jnp.int32)
        return h
    def own_hood(index,queries):
        row=start+index
        return jnp.where(row<keys,hood(row),queries)
    key_line=hood(lax.broadcasted_iota(jnp.int32,(1,keys),1))
    row_line=own_hood(lax.broadcasted_iota(jnp.int32,(1,share),1),qline[...])
    def mask(i,_):
        rows=rows_at(i,CH)
        col=own_hood(lax.broadcasted_iota(jnp.int32,(CH,1),0)+i*CH,qcol[rows,:])
        bias[rows,:]=jnp.where(col==key_line,0.0,MASK_VALUE).astype(bf16)
        return 0
    lax.fori_loop(0,chunks,mask,0)
    def maskT(i,_):
        rows=rows_at(i,KB)
        col=hood(lax.broadcasted_iota(jnp.int32,(KB,1),0)+i*KB)
        biasT[rows,:]=jnp.where(col==row_line,0.0,MASK_VALUE).astype(bf16)
        return 0
    lax.fori_loop(0,keys//KB,maskT,0)
    w1,w2=Weights((wa,wb,wc,wd,we)),Weights((xa,xb,xc,xd,xe))
    loads[1].wait()
    w1.fill(0,owners,wallv)
    loads[0].wait()
    pl.semaphore_wait(bar,2)
    at=lambda k,i: pl.ds(pl.multiple_of(k*share+i*CH,CH),CH)
    far=s.across_y[1]
    over=lambda i: remote(h2.at[at(mp,i)],h2.at[at(mp,i)],ssend.at[0,i],srecv.at[0,i],s.across_y)
    near=lambda i: remote(h2.at[at(mp,i)],h2.at[at(mp,i)],ssend.at[1,i],srecv.at[1,i],s.sibling)
    on=lambda i: remote(h2.at[at(far,i)],h2.at[at(far,i)],ssend.at[2,i],srecv.at[2,i],s.sibling)
    g1,g2=gains[0:4],gains[4:8]
    def emit1(i,v):
        layer_out[pl.ds(i*CH,CH),:]=v
        h2[at(mp,i),:]=v.astype(bf16)
        over(i).start(); near(i).start()
    forward(w1,g1,start,tok,lambda i: tok[at(mp,i),:].astype(f32),KV1,q1,heads1,lse1,bias,hid1,ra1,rb1,emit1)
    w2.fill(1,owners,wallv)
    for i in range(chunks):
        over(i).wait_recv(); on(i).start()
    for i in range(chunks):
        near(i).wait_recv(); on(i).wait_recv()
    def emit2(i,v): layer_out[pl.ds(i*CH,CH),:]=v
    forward(w2,g2,start,h2,lambda i: layer_out[pl.ds(i*CH,CH),:],KV2,q2,heads2,lse2,bias,hid2,ra2,rb2,emit2)
    for i in range(chunks):
        for k in (over,near,on): k(i).wait_send()
    def put(layer):
        def store(b,j,v):
            b=b+layer*LAYER_BLOCKS
            wallv[b,j]=v
        return store
    def keep(layer):
        def store(k,v): vec[layer*4+k:layer*4+k+1,:]=v
        return store
    loads[2].wait()
    half=wallv.shape[0]//2
    flush=[pltpu.make_async_copy(wallv.at[pl.ds(k*half,half)],g.at[pl.ds(k*half,half)],lsem.at[3+k]) for k in range(2)]
    backward(w2,g2,start,h2,lambda i: cotv[rows_at(i,CH),:].astype(f32),KV2,q2,heads2,lse2,biasT,hid2,ra2,rb2,
        dm,act,dhid,first,datt,dheads,delta,tokens_grad,dq,dhp,keep(1),put(1),Exchange(s,dhp,tokens_grad,rc.at[0],acc,ry.at[0],tsend.at[0],trecv.at[0]))
    flush[1].start()
    backward(w1,g1,start,tok,lambda i: tokens_grad[rows_at(i,CH),:],KV1,q1,heads1,lse1,biasT,hid1,ra1,rb1,
        dm,act,dhid,first,datt,dheads,delta,tokens_grad,dq,dhp,keep(0),put(0),Exchange(s,dhp,tokens_grad,rc.at[1],acc,ry.at[1],tsend.at[1],trecv.at[1]))
    flush[0].start()
    flush[1].wait(); flush[0].wait()

def run_layers(owners,sizes,tokens,cot,wall,gains,qline,qcol,keys,slots,collective):
    rows=tokens.shape[0]; share=rows//HEADS; chunks=share//CH
    v=pltpu.VMEM; dma=pltpu.SemaphoreType.DMA; V_=VMEM_SPEC
    two=lambda shape,t: [v(shape,t)]*2
    weights=[v((D,D),bf16),v((HEADS,D,2*HD),bf16),v((D,D),bf16),v((D,FF),bf16),v((FF,D),bf16)]
    blocks=(LAYERS*LAYER_BLOCKS,HEADS,BLK,BLK)
    scratch=[v(blocks,bf16),v((rows,D),bf16),v((rows,D),bf16),v((share,D),bf16)]
    scratch+=two((HEADS,keys,2*HD),bf16)+two((share,D),bf16)+two((share,D),bf16)+two((share,BLK),f32)+two((share,FF),f32)+two((share,D),f32)+two((share,D),f32)
    scratch+=[v((share,keys),bf16),v((keys,share),bf16)]
    scratch+=[v((share,D),bf16),v((share,FF),bf16),v((share,FF),bf16),v((share,D),bf16),v((share,D),bf16),v((share,D),bf16),v((share,BLK),f32),v((share,D),bf16)]
    scratch+=[v((rows,D),bf16),v((2,2,share,D),bf16),v((share,D),bf16),v((2,share,D),bf16)]+weights+weights
    scratch+=[dma((5,)),dma((3,chunks)),dma((3,chunks)),dma((2,3,chunks)),dma((2,3,chunks))]
    shape=jax.ShapeDtypeStruct
    return pl.pallas_call(partial(layers_kernel,slots),
        out_shape=[shape((share,D),f32),shape((share,D),f32),shape(blocks,bf16),shape((2*LAYERS*2,D),f32)],
        in_specs=[SMEM_SPEC,SMEM_SPEC,ANY_SPEC,ANY_SPEC,ANY_SPEC,V_,V_,V_],out_specs=[V_,V_,ANY_SPEC,V_],scratch_shapes=scratch,
        compiler_params=pltpu.CompilerParams(collective_id=collective,has_side_effects=True,vmem_limit_bytes=62<<20),name="layers")(
        owners,sizes,tokens,cot,wall,gains,qline,qcol)
BLK=128; STEP=10
BETA_ONE=0.9; BETA_TWO=0.95; BETA_STATS=0.95; RATE_MATRIX=0.12; DECAY_WEIGHT=0.01; ADAM_EPSILON=1e-8

def split(x):
    hi=x.astype(jnp.bfloat16)
    return hi,(x-hi.astype(jnp.float32)).astype(jnp.bfloat16)
def dot3(a,b,ca,cb):
    dims=(((ca,),(cb,)),((),()))
    ah,al=a; bh,bl=b
    d=lambda x,y: lax.dot_general(x,y,dims,preferred_element_type=jnp.float32)
    return d(ah,bh)+(d(ah,bl)+d(al,bh))
def dotf(a,b,ca,cb):
    return lax.dot_general(a,b,(((ca,),(cb,)),((),())),preferred_element_type=jnp.float32,precision=lax.Precision.HIGHEST)

def soap_kernel(slots, g_ref,m_ref,v_ref,l_ref,r_ref,ql_ref,qr_ref,w_ref, mo,vo,lo,ro,qlo,qro,wo, x_ref, a_ref):
    def first(i,_):
        g=g_ref[i]; ql=split(ql_ref[i]); qr=split(qr_ref[i])
        gs=split(g)
        m=BETA_ONE*m_ref[i]+(1-BETA_ONE)*g
        mo[i]=m
        def turn(v):
            return dot3(split(dot3(ql,v,0,0)),qr,1,0)
        tg=turn(gs)
        v=BETA_TWO*v_ref[i]+(1-BETA_TWO)*tg*tg
        vo[i]=v
        d=turn(split(m))/(1-BETA_ONE**STEP)/(jnp.sqrt(v/(1-BETA_TWO**STEP))+ADAM_EPSILON)
        u=dot3(split(dot3(ql,split(d),1,0)),qr,1,1)
        w=w_ref[i]
        wo[i]=w-RATE_MATRIX*(u+DECAY_WEIGHT*w)
        ln=BETA_STATS*l_ref[i]+(1-BETA_STATS)*dot3(gs,gs,1,1)
        rn=BETA_STATS*r_ref[i]+(1-BETA_STATS)*dot3(gs,gs,0,0)
        lo[i]=ln; ro[i]=rn
        al=dotf(ln,ql_ref[i],1,0); ar=dotf(rn,qr_ref[i],1,0)
        a_ref[2*i]=al; a_ref[2*i+1]=ar
        x_ref[2*i]=dotf(al,al,0,0); x_ref[2*i+1]=dotf(ar,ar,0,0)
        return 0
    lax.fori_loop(0,slots,first,0)
    n=2*slots
    lane=lax.broadcasted_iota(jnp.int32,(8,BLK),1)
    sub=lax.broadcasted_iota(jnp.int32,(8,BLK),0)
    for p in range(BLK//8):
        def step(kk,_):
            k=p*8+kk
            idx=jnp.full((8,BLK),k,jnp.int32)
            atk=lane==k
            below=sub>kk
            rows=[jnp.broadcast_to(x_ref[m,pl.ds(k,1),:],(8,BLK)) for m in range(n)]
            rinv=[1.0/jnp.take_along_axis(row,idx,axis=1) for row in rows]
            scaled=[jnp.where(atk,1.0,row)*ri for row,ri in zip(rows,rinv)]
            for m in range(n):
                for t in range(p,BLK//8):
                    v=x_ref[m,t*8:(t+1)*8,:]
                    f=jnp.take_along_axis(v,idx,axis=1)
                    new=jnp.where(atk,0.0,v)-f*scaled[m]
                    if t==p: new=jnp.where(below,new,v)
                    x_ref[m,t*8:(t+1)*8,:]=new
            return 0
        lax.fori_loop(0,8,step,0)
    r=lax.broadcasted_iota(jnp.int32,(BLK,BLK),0); c=lax.broadcasted_iota(jnp.int32,(BLK,BLK),1)
    def last(i,_):
        for s,out in ((0,qlo),(1,qro)):
            x=x_ref[2*i+s]
            piv=jnp.sum(jnp.where(r==c,x,0.0),axis=1,keepdims=True)
            inv=jnp.where(r==c,1.0,jnp.where(r>c,x,0.0))*lax.rsqrt(piv)
            out[i]=dotf(a_ref[2*i+s],inv,1,1)
        return 0
    lax.fori_loop(0,slots,last,0)

def soap(g,m,v,l,r,ql,qr,w):
    slots=g.shape[0]
    sh=jax.ShapeDtypeStruct((slots,BLK,BLK),jnp.float32)
    vm=pl.BlockSpec(memory_space=pltpu.VMEM)
    return pl.pallas_call(partial(soap_kernel,slots),out_shape=[sh]*7,in_specs=[vm]*8,out_specs=[vm]*7,
        scratch_shapes=[pltpu.VMEM((2*slots,BLK,BLK),jnp.float32)]*2,
        compiler_params=pltpu.CompilerParams(vmem_limit_bytes=48<<20),name="soap")(g,m,v,l,r,ql,qr,w)
def adam_vector(grad, first, second, weight):
    first_new = BETA_ONE * first + (1.0 - BETA_ONE) * grad
    second_new = BETA_TWO * second + (1.0 - BETA_TWO) * grad * grad
    weight_new = weight - RATE_VECTOR * (first_new / (1.0 - BETA_ONE**STEP)) / (
        jnp.sqrt(second_new / (1.0 - BETA_TWO**STEP)) + ADAM_EPSILON
    )
    return (first_new, second_new, weight_new)


def inverse(owners):
    index=jnp.arange(owners.shape[0],dtype=jnp.int32)
    return jnp.sum(jnp.where(owners[:,None]==index[None,:],index[:,None],0),axis=0)

def local(tokens,cotangent,context_sizes,query_hoods,owners,master_blocks,first_blocks,second_blocks,left_blocks,right_blocks,
        left_bases,right_bases,vector_master,vector_moment,vector_square):
    dp=lax.axis_size("dp")
    rows=tokens.shape[0]; keys=rows-query_hoods.shape[0]; share=rows//HEADS; slots=master_blocks.shape[0]
    n=vector_master.shape[0]
    high=vector_master.astype(bf16)
    rest=(vector_master-high.astype(f32)).astype(bf16)
    extra=jnp.pad(jnp.stack([high,rest]),((0,14),(0,BLK-n)))
    slab=jnp.concatenate([master_blocks.astype(bf16).reshape(slots*BLK,BLK),extra],axis=0)
    wall=gather_all(slab,dp,0)
    pair=wall[:,:,slots*BLK:slots*BLK+2,:n].astype(f32)
    gains=(pair[:,:,0]+pair[:,:,1]).reshape(LAYERS*4,D)
    hoods=jnp.pad(query_hoods,(share-query_hoods.shape[0],0))
    layer_out,tokens_grad,g,vec=run_layers(owners,context_sizes,tokens,cotangent,wall,gains,hoods[None,:],hoods[:,None],keys,slots,1)
    vec=jnp.pad(vec.astype(bf16).reshape(dp,HEADS,1,n),((0,0),(0,0),(0,15),(0,BLK-n)))
    total=reduce_all(g,vec,inverse(owners),slots,2)
    results=soap(total[:slots*BLK].reshape(slots,BLK,BLK),first_blocks,second_blocks,left_blocks,right_blocks,left_bases,right_bases,master_blocks)
    vector_results=adam_vector(total[slots*BLK,:n],vector_moment,vector_square,vector_master)
    return (layer_out,tokens_grad)+tuple(results)+vector_results


def solution(mesh):
    return jax.shard_map(
        local,
        mesh=mesh,
        in_specs=(
            P("dp", None),
            P("dp", None),
            P("dp", None),
            P("dp"),
            P(),
            P("dp", "mp", None),
            P("dp", "mp", None),
            P("dp", "mp", None),
            P("dp", "mp", None),
            P("dp", "mp", None),
            P("dp", "mp", None),
            P("dp", "mp", None),
            P(("dp", "mp")),
            P(("dp", "mp")),
            P(("dp", "mp")),
        ),
        out_specs=(
            P(("dp", "mp"), None),
            P(("dp", "mp"), None),
            P("dp", "mp", None),
            P("dp", "mp", None),
            P("dp", "mp", None),
            P("dp", "mp", None),
            P("dp", "mp", None),
            P("dp", "mp", None),
            P("dp", "mp", None),
            P(("dp", "mp")),
            P(("dp", "mp")),
            P(("dp", "mp")),
        ),
        check_vma=False,
    )
```

```python
import math
from functools import partial

import jax
import jax.numpy as jnp
from jax import lax
from jax.experimental import pallas as pl
from jax.experimental.pallas import tpu as pltpu
from jax.sharding import PartitionSpec as P

RATE_VECTOR = 0.6
MESH=pl.DeviceIdType.MESH
BLK=128
VMEM_SPEC=pl.BlockSpec(memory_space=pltpu.VMEM)
ANY_SPEC=pl.BlockSpec(memory_space=pl.ANY)

def remote(src,dst,send,recv,device):
    return pltpu.make_async_remote_copy(src_ref=src,dst_ref=dst,send_sem=send,recv_sem=recv,device_id=device,device_id_type=MESH)

class Spot:
    def __init__(self,planes):
        dp,mp=lax.axis_index("dp"),lax.axis_index("mp")
        self.dp,self.mp,self.planes=dp,mp,planes
        self.z,self.x=dp//2,dp%2
        self.y,self.c=mp//2,mp%2
        self.across_x=(dp+1-2*self.x,mp)
        self.across_y=(dp,(mp+2)%4)
        self.sibling=(dp,mp+1-2*self.c)
        self.up=(jnp.minimum(dp+2,2*planes-1),mp)
        self.down=(jnp.maximum(dp-2,0),mp)
    def greet(self):
        bar=pltpu.get_barrier_semaphore()
        for who in (self.across_x,self.across_y,self.sibling):
            pl.semaphore_signal(bar,inc=1,device_id=who,device_id_type=MESH)
        @pl.when(self.z<self.planes-1)
        def _(): pl.semaphore_signal(bar,inc=1,device_id=self.up,device_id_type=MESH)
        @pl.when(self.z>0)
        def _(): pl.semaphore_signal(bar,inc=1,device_id=self.down,device_id_type=MESH)
        pl.semaphore_wait(bar,3+jnp.minimum(self.z,1)+jnp.minimum(self.planes-1-self.z,1))
    def ring(self,r,action):
        if r==0:
            action(self.z,None); return
        @pl.when(self.z>=r)
        def _(): action(self.z-r,True)
        @pl.when(self.z+r<self.planes)
        def _(): action(self.z+r,False)

def gather_kernel(planes,half,slab,out,send,recv,zsend,zrecv,lsem):
    s=Spot(planes); rows=slab.shape[0]; z,x,y,c,mp=s.z,s.x,s.y,s.c,s.mp
    A,B=pl.ds(0,half),pl.ds(half,rows-half)
    mx,my=s.across_x,s.across_y
    own=pltpu.make_async_copy(slab,out.at[s.dp,mp],lsem); own.start()
    s.greet()
    def at(p,xx,yy,cc): return out.at[p*2+xx,yy*2+cc]
    xo,yo=1-x,1-y
    def copies(p,src):
        here=at(p,x,y,c) if src is None else src
        f=lambda k,a,b,w: remote(a,b,send.at[k,p],recv.at[k,p],w)
        return dict(
            xown=lambda: f(0,here,at(p,x,y,c),mx), yown=lambda: f(1,here,at(p,x,y,c),my), cown=lambda: f(2,here,at(p,x,y,c),s.sibling),
            yfwd=lambda: f(3,at(p,xo,y,c).at[A],at(p,xo,y,c).at[A],my),
            xfwd=lambda: f(4,at(p,x,yo,c).at[B],at(p,x,yo,c).at[B],mx),
            cx=lambda: f(5,at(p,xo,y,c),at(p,xo,y,c),s.sibling), cy=lambda: f(6,at(p,x,yo,c),at(p,x,yo,c),s.sibling),
            ca=lambda: f(7,at(p,xo,yo,c).at[A],at(p,xo,yo,c).at[A],s.sibling),
            cb=lambda: f(8,at(p,xo,yo,c).at[B],at(p,xo,yo,c).at[B],s.sibling))
    def zcopy(p,up,src=None):
        here=at(p,x,y,c) if src is None else src
        return remote(here,at(p,x,y,c),zsend.at[0 if up else 1,p],zrecv.at[p],s.up if up else s.down)
    def arrive(r):
        def act(p,below):
            src=None
            if below is None: src=slab
            else: zcopy(p,below).wait_recv()
            if below is None or below:
                @pl.when(z<planes-1)
                def _(): zcopy(p,True,src).start()
            if below is None or not below:
                @pl.when(z>0)
                def _(): zcopy(p,False,src).start()
            k=copies(p,src)
            k["xown"]().start(); k["yown"]().start(); k["cown"]().start()
        s.ring(r,act)
    def second(r):
        def act(p,below):
            k=copies(p,None)
            k["xown"]().wait_recv(); k["yfwd"]().start(); k["cx"]().start()
            k["yown"]().wait_recv(); k["xfwd"]().start(); k["cy"]().start()
        s.ring(r,act)
    def third(r):
        def act(p,below):
            k=copies(p,None)
            k["yfwd"]().wait_recv(); k["ca"]().start()
            k["xfwd"]().wait_recv(); k["cb"]().start()
        s.ring(r,act)
    def finish(r):
        def act(p,below):
            src=slab if below is None else None
            k=copies(p,src)
            for n in ("cown","cx","cy","ca","cb"): k[n]().wait_recv()
            for n in k: k[n]().wait_send()
            if below is None or below:
                @pl.when(z<planes-1)
                def _(): zcopy(p,True,src).wait_send()
            if below is None or not below:
                @pl.when(z>0)
                def _(): zcopy(p,False,src).wait_send()
        s.ring(r,act)
    for r in range(planes+2):
        if r<planes: arrive(r)
        if 1<=r<=planes: second(r-1)
        if r>=2: third(r-2)
    for r in range(planes): finish(r)
    own.wait()

def gather_all(slab,dp,collective):
    rows=slab.shape[0]; planes=dp//2; half=rows//2//16*16
    dma=pltpu.SemaphoreType.DMA
    return pl.pallas_call(partial(gather_kernel,planes,half),
        out_shape=jax.ShapeDtypeStruct((dp,4,rows,slab.shape[1]),slab.dtype),
        in_specs=[ANY_SPEC],out_specs=ANY_SPEC,
        scratch_shapes=[dma((9,planes)),dma((9,planes)),dma((2,planes)),dma((planes,)),dma],
        compiler_params=pltpu.CompilerParams(collective_id=collective,has_side_effects=True),name="gather_all")(slab)

def reduce_kernel(planes,half,slots,blocks,inner,extra,out,g,rc,acc,ya,xb,xa,yb,own,zin,send,recv,zsend,zrecv):
    s=Spot(planes); rows=g.shape[2]; z,x,y,c,mp=s.z,s.x,s.y,s.c,s.mp
    A,B=pl.ds(0,half),pl.ds(half,rows-half)
    mx,my=s.across_x,s.across_y
    xo,yo,co=1-x,1-y,1-c
    s.greet()
    f32=lambda v: v.astype(jnp.float32)
    def core(p,xx,yy):
        k=xx*2+yy
        return remote(g.at[p*2+xx,yy*2+co],rc.at[p*4+k],send.at[k,p],recv.at[k,p],s.sibling)
    def toya(p,xx): return remote(acc.at[p*4+xx*2+yo,A],ya.at[p*2+xx],send.at[4+xx,p],recv.at[4+xx,p],my)
    def toxb(p,yy): return remote(acc.at[p*4+xo*2+yy,B],xb.at[p*2+yy],send.at[6+yy,p],recv.at[6+yy,p],mx)
    def toxa(p): return remote(ya.at[p*2+xo],xa.at[p],send.at[8,p],recv.at[8,p],mx)
    def toyb(p): return remote(xb.at[p*2+yo],yb.at[p],send.at[9,p],recv.at[9,p],my)
    def toz(p,up): return remote(own.at[p],zin.at[0 if up else 1,p],zsend.at[p],zrecv.at[0 if up else 1,p],s.up if up else s.down)
    def pack(p,parity):
        for xx in (0,1):
            d=p*2+xx
            def one(k,_):
                block=inner[d*slots+k]
                for yy in (0,1):
                    g[d,yy*2+parity,pl.ds(pl.multiple_of(k*BLK,BLK),BLK),:]=blocks[block,yy*2+parity]
                return 0
            lax.fori_loop(0,slots,one,0)
            for yy in (0,1): g[d,yy*2+parity,slots*BLK:,:]=extra[d,yy*2+parity]
    def start(p,_):
        pack(p,co)
        for xx in (0,1):
            for yy in (0,1): core(p,xx,yy).start()
    def first(p,_):
        pack(p,c)
        for xx in (0,1):
            for yy in (0,1):
                core(p,xx,yy).wait_recv()
                acc[p*4+xx*2+yy]=(f32(g[p*2+xx,yy*2+c])+f32(rc[p*4+xx*2+yy])).astype(acc.dtype)
        for e in (0,1): toya(p,e).start(); toxb(p,e).start()
    def second(p,_):
        for e in (0,1):
            toya(p,e).wait_recv()
            ya[p*2+e]=(f32(acc[p*4+e*2+y,A])+f32(ya[p*2+e])).astype(ya.dtype)
        toxa(p).start()
        for e in (0,1):
            toxb(p,e).wait_recv()
            xb[p*2+e]=(f32(acc[p*4+x*2+e,B])+f32(xb[p*2+e])).astype(xb.dtype)
        toyb(p).start()
    def third(p,below):
        toxa(p).wait_recv()
        av=f32(ya[p*2+x])+f32(xa[p])
        toyb(p).wait_recv()
        bv=f32(xb[p*2+y])+f32(yb[p])
        if below is None:
            out[A]=av; out[B]=bv
            @pl.when(z>0)
            def _():
                toz(p,True).wait_recv()
                out[...]=out[...]+f32(zin[0,p])
            @pl.when(z<planes-1)
            def _():
                toz(p,False).wait_recv()
                out[...]=out[...]+f32(zin[1,p])
            return
        own[p,A]=av.astype(own.dtype); own[p,B]=bv.astype(own.dtype)
        up=not below
        has=(z>0) if up else (z<planes-1)
        @pl.when(has)
        def _():
            toz(p,up).wait_recv()
            own[p,A]=(av+f32(zin[0 if up else 1,p,A])).astype(own.dtype)
            own[p,B]=(bv+f32(zin[0 if up else 1,p,B])).astype(own.dtype)
        toz(p,up).start()
    def finish(p,below):
        for xx in (0,1):
            for yy in (0,1): core(p,xx,yy).wait_send()
        for e in (0,1): toya(p,e).wait_send(); toxb(p,e).wait_send()
        toxa(p).wait_send(); toyb(p).wait_send()
        if below is not None: toz(p,not below).wait_send()
    order=list(range(planes-1,-1,-1))
    for r in order: s.ring(r,start)
    n=len(order)
    for i in range(n+2):
        if i<n: s.ring(order[i],first)
        if 0<=i-1<n: s.ring(order[i-1],second)
        if 0<=i-2<n: s.ring(order[i-2],third)
    for r in order: s.ring(r,finish)

def reduce_all(g,extra,inner,slots,collective):
    dp=extra.shape[0]; rows,cols=slots*BLK+extra.shape[2],g.shape[3]; planes=dp//2; half=rows//2//16*16
    dma=pltpu.SemaphoreType.DMA; bf=lambda *sh: pltpu.VMEM(sh+(cols,),g.dtype)
    return pl.pallas_call(partial(reduce_kernel,planes,half,slots),
        out_shape=jax.ShapeDtypeStruct((rows,cols),jnp.float32),in_specs=[VMEM_SPEC,pl.BlockSpec(memory_space=pltpu.SMEM),VMEM_SPEC],out_specs=VMEM_SPEC,
        scratch_shapes=[bf(dp,4,rows),bf(planes*4,rows),bf(planes*4,rows),bf(planes*2,half),bf(planes*2,rows-half),bf(planes,half),bf(planes,rows-half),
            bf(planes,rows),bf(2,planes,rows),dma((10,planes)),dma((10,planes)),dma((planes,)),dma((2,planes))],
        compiler_params=pltpu.CompilerParams(collective_id=collective,has_side_effects=True,vmem_limit_bytes=56<<20),name="reduce_all")(g,inner,extra)
D=512; HD=128; FF=1024; LAYERS=2; BLK=128; HEADS=4
NORM_EPSILON=1e-5; MASK_VALUE=-1e30
f32=jnp.float32; bf16=jnp.bfloat16
SMEM_SPEC=pl.BlockSpec(memory_space=pltpu.SMEM)
SCALE=HD**-0.5; LOG2E=math.log2(math.e)
ROOT=math.sqrt(2/math.pi)

def nn(a,b): return lax.dot_general(a,b,(((1,),(0,)),((),())),preferred_element_type=f32)
def nt(a,b): return lax.dot_general(a,b,(((1,),(1,)),((),())),preferred_element_type=f32)
def tn(a,b): return lax.dot_general(a,b,(((0,),(0,)),((),())),preferred_element_type=f32)

def normed(r):
    center=r-jnp.mean(r,axis=-1,keepdims=True)
    rho=lax.rsqrt(jnp.mean(center*center,axis=-1,keepdims=True)+NORM_EPSILON)
    return center*rho,rho
def norm_back(dy,xhat,rho,gain):
    inner=dy*gain
    return rho*(inner-jnp.mean(inner,axis=-1,keepdims=True)-xhat*jnp.mean(inner*xhat,axis=-1,keepdims=True))
def gelu(v): return 0.5*v*(1+jnp.tanh(ROOT*(v+0.044715*v*v*v)))
def gelu_both(v):
    sq=v*v
    t=jnp.tanh(ROOT*v*(1+0.044715*sq))
    half=0.5*(1+t)
    return v*half,half+0.5*v*(1-t*t)*(ROOT*(1+3*0.044715*sq))
def colsum(v): return jnp.sum(v,axis=0,keepdims=True)

COLS_TILE=(3,4,2,4)
FIRST_BLOCK=(0,12,16,24)
LAYER_BLOCKS=32
CH=160
KB=320
FS=FF//HEADS

def rows_at(i,n): return pl.ds(pl.multiple_of(i*n,n),n)

class Weights:
    def __init__(self,refs): self.q,self.kv,self.out,self.up,self.down=refs
    def fill(self,layer,owners,wallv):
        base=layer*LAYER_BLOCKS
        def tiles(b):
            slot=owners[b]
            return [wallv[slot,j] for j in range(HEADS)]
        def by_row(r,_):
            rows=rows_at(r,BLK)
            for c in range(3):
                for j,v in enumerate(tiles(base+r*3+c)):
                    if c==0: self.q[rows,j*BLK:(j+1)*BLK]=v
                    else: self.kv[j,rows,(c-1)*BLK:c*BLK]=v
            for c in range(2):
                for j,v in enumerate(tiles(base+FIRST_BLOCK[2]+r*2+c)): self.up[rows,j*FS+c*BLK:j*FS+(c+1)*BLK]=v
            return 0
        lax.fori_loop(0,D//BLK,by_row,0)
        for c in range(4):
            for j,v in enumerate(tiles(base+FIRST_BLOCK[1]+c)): self.out[j*BLK:(j+1)*BLK,c*BLK:(c+1)*BLK]=v
            for r in range(2):
                for j,v in enumerate(tiles(base+FIRST_BLOCK[3]+r*4+c)): self.down[j*FS+r*BLK:j*FS+(r+1)*BLK,c*BLK:(c+1)*BLK]=v

def forward(w,gains,start,h_full,own_rows,KV,q,heads,lse,bias,hidden,r1,r2,emit):
    keys=KV.shape[1]; chunks=q.shape[0]//CH; blocks=keys//KB
    def project(i,_):
        j,rows=i//blocks,rows_at(i%blocks,KB)
        KV[j,rows,:]=nn(h_full[rows,:],w.kv[j]).astype(bf16)
        return 0
    lax.fori_loop(0,HEADS*blocks,project,0)
    def queries(i,_):
        q[rows_at(i,CH),:]=nn(h_full[pl.ds(pl.multiple_of(start+i*CH,CH),CH),:],w.q[...]).astype(bf16)
        return 0
    lax.fori_loop(0,chunks,queries,0)
    lane=lax.broadcasted_iota(jnp.int32,(CH,BLK),1)
    def attend(i,_):
        rows=rows_at(i,CH)
        stats=jnp.zeros((CH,BLK),f32)
        for j in range(HEADS):
            s=nt(q[rows,j*HD:(j+1)*HD],KV[j,:,:HD])+bias[rows,:].astype(f32)
            peak=jnp.max(s,axis=1,keepdims=True)
            p=jnp.exp2((s-peak)*(SCALE*LOG2E))
            total=jnp.sum(p,axis=1,keepdims=True)
            o=nn(p.astype(bf16),KV[j,:,HD:])/total
            heads[rows,j*HD:(j+1)*HD]=o.astype(bf16)
            stats=jnp.where(lane==j,peak*(SCALE*LOG2E)+jnp.log2(total),stats)
        lse[rows,:]=stats
        return 0
    lax.fori_loop(0,chunks,attend,0)
    for i in range(chunks):
        rows=pl.ds(i*CH,CH)
        a=own_rows(i)+nn(heads[rows,:],w.out[...])
        r1[rows,:]=a
        first=normed(a)[0]*gains[0:1,:]+gains[1:2,:]
        hid=nn(first.astype(bf16),w.up[...])
        hidden[rows,:]=hid
        b=first+nn(gelu(hid).astype(bf16),w.down[...])
        r2[rows,:]=b
        emit(i,normed(b)[0]*gains[2:3,:]+gains[3:4,:])

def backward(w,gains,start,h_full,upper,KV,q,heads,lse,biasT,hidden,r1,r2,
        dm,act,dhid,first,datt,dheads,delta,grad,dq,dhp,vec,put,exchange):
    share=q.shape[0]; keys=KV.shape[1]; chunks=share//CH
    lane=lax.broadcasted_iota(jnp.int32,(CH,BLK),1)
    def part(i,carry):
        rows=rows_at(i,CH)
        dy=upper(i)
        xhat,rho=normed(r2[rows,:])
        g2,s2=colsum(dy*xhat),colsum(dy)
        sg=norm_back(dy,xhat,rho,gains[2:3,:])
        dmb=sg.astype(bf16); dm[rows,:]=dmb
        a,slope=gelu_both(hidden[rows,:])
        act[rows,:]=a.astype(bf16)
        dh=(nt(dmb,w.down[...])*slope).astype(bf16)
        dhid[rows,:]=dh
        fu=sg+nt(dh,w.up[...])
        xhat,rho=normed(r1[rows,:])
        first[rows,:]=(xhat*gains[0:1,:]+gains[1:2,:]).astype(bf16)
        g1,s1=colsum(fu*xhat),colsum(fu)
        f=norm_back(fu,xhat,rho,gains[0:1,:])
        grad[rows,:]=f
        fb=f.astype(bf16); datt[rows,:]=fb
        dhe=nt(fb,w.out[...]).astype(bf16)
        dheads[rows,:]=dhe
        prod=dhe.astype(f32)*heads[rows,:].astype(f32)
        stats=jnp.zeros((CH,BLK),f32)
        for j in range(HEADS):
            stats=jnp.where(lane==j,jnp.sum(prod[:,j*HD:(j+1)*HD],axis=1,keepdims=True),stats)
        delta[rows,:]=stats
        return tuple(c+v for c,v in zip(carry,(g1,s1,g2,s2)))
    zero=jnp.zeros((1,D),f32)
    for k,v in enumerate(lax.fori_loop(0,chunks,part,(zero,)*4)): vec(k,v)
    lseT=jnp.transpose(lse[...]); deltaT=jnp.transpose(delta[...])
    for j in range(HEADS):
        L=lseT[j:j+1,:]; dl=deltaT[j:j+1,:]
        qj=q[:,j*HD:(j+1)*HD]; doj=dheads[:,j*HD:(j+1)*HD]
        def keyblock(kb,acc):
            rows=rows_at(kb,KB)
            k=KV[j,rows,:HD]; v=KV[j,rows,HD:]
            p=jnp.exp2((nt(k,qj)+biasT[rows,:].astype(f32))*(SCALE*LOG2E)-L)
            dv=nn(p.astype(bf16),doj)
            ds=(p*(nt(v,doj)-dl)).astype(bf16)
            dk=nn(ds,qj)*SCALE
            acc=acc+tn(ds,k)
            KV[j,rows,:]=jnp.concatenate([dk,dv],axis=1).astype(bf16)
            return acc
        acc=lax.fori_loop(0,keys//KB,keyblock,jnp.zeros((share,HD),f32))
        dq[:,j*HD:(j+1)*HD]=(acc*SCALE).astype(bf16)
    def context(kb,_):
        rows=rows_at(kb,KB)
        t=nt(KV[0,rows,:],w.kv[0])
        for j in range(1,HEADS): t=t+nt(KV[j,rows,:],w.kv[j])
        dhp[rows,:]=t.astype(bf16)
        return 0
    lax.fori_loop(0,keys//KB,context,0)
    dhp[keys:,:]=jnp.zeros((dhp.shape[0]-keys,D),bf16)
    exchange.start()
    def own(i,_):
        rows=rows_at(i,CH)
        grad[rows,:]=grad[rows,:]+nt(dq[rows,:],w.q[...])
        return 0
    lax.fori_loop(0,chunks,own,0)
    def tiles(kind,j,value,c0=0):
        for r in range(value.shape[0]//BLK):
            for c in range(value.shape[1]//BLK):
                put(FIRST_BLOCK[kind]+r*COLS_TILE[kind]+c+c0,j,value[r*BLK:(r+1)*BLK,c*BLK:(c+1)*BLK].astype(bf16))
    for j in range(HEADS): tiles(3,j,tn(act[:,j*FS:(j+1)*FS],dm[...]))
    exchange.middle()
    for j in range(HEADS):
        tiles(2,j,tn(first[...],dhid[:,j*FS:(j+1)*FS]))
        tiles(1,j,tn(heads[:,j*HD:(j+1)*HD],datt[...]))
    hown=h_full[pl.ds(pl.multiple_of(start,CH),share),:]
    hctx=h_full[:keys,:]
    for j in range(HEADS):
        tiles(0,j,tn(hown,dq[:,j*HD:(j+1)*HD]))
        tiles(0,j,tn(hctx,KV[j]),c0=1)
    exchange.finish()

class Exchange:
    def __init__(self,s,terms,grad,rc,acc,ry,send,recv):
        self.s,self.terms,self.grad,self.rc,self.acc,self.ry=s,terms,grad,rc,acc,ry
        self.n=send.shape[1]; rows=grad.shape[0]; step=rows//self.n
        self.far=s.across_y[1]; co=1-s.c
        self.part=lambda i: pl.ds(i*step,step)
        self.at=lambda k,i: pl.ds(pl.multiple_of(k*rows+i*step,16),step)
        self.a=lambda i: remote(terms.at[self.at((1-s.y)*2+co,i)],rc.at[0,self.part(i)],send.at[0,i],recv.at[0,i],s.sibling)
        self.b=lambda i: remote(terms.at[self.at(s.y*2+co,i)],rc.at[1,self.part(i)],send.at[1,i],recv.at[1,i],s.sibling)
        self.o=lambda i: remote(acc.at[self.part(i)],ry.at[self.part(i)],send.at[2,i],recv.at[2,i],s.across_y)
    def start(self):
        for i in range(self.n): self.a(i).start()
        for i in range(self.n): self.b(i).start()
    def middle(self):
        for i in range(self.n):
            self.a(i).wait_recv()
            self.acc[self.part(i)]=(self.terms[self.at(self.far,i)].astype(f32)+self.rc[0,self.part(i)].astype(f32)).astype(bf16)
            self.o(i).start()
    def finish(self):
        for i in range(self.n):
            rows=self.part(i)
            self.b(i).wait_recv()
            t=self.grad[rows]+(self.terms[self.at(self.s.mp,i)].astype(f32)+self.rc[1,rows].astype(f32))
            self.o(i).wait_recv()
            self.grad[rows]=t+self.ry[rows].astype(f32)
        for i in range(self.n):
            for k in (self.a,self.b,self.o): k(i).wait_send()

def layers_kernel(slots,owners,sizes,tokens,cot,wall,gains,qline,qcol, layer_out,tokens_grad,g,vec,
        wallv,tok,h2,cotv,KV1,KV2,q1,q2,heads1,heads2,lse1,lse2,hid1,hid2,ra1,ra2,rb1,rb2,bias,biasT,
        dm,act,dhid,first,datt,dheads,delta,dq,dhp,rc,acc,ry,wa,wb,wc,wd,we,xa,xb,xc,xd,xe,lsem,ssend,srecv,tsend,trecv):
    s=Spot(1); mp=s.mp; share=q1.shape[0]; keys=KV1.shape[1]; chunks=share//CH
    start=mp*share
    def bring(k,_):
        pltpu.make_async_copy(wall.at[k//slots,:,rows_at(k%slots,BLK),:],wallv.at[k],lsem.at[1]).start()
        return 0
    lax.fori_loop(0,wallv.shape[0],bring,0)
    loads=[pltpu.make_async_copy(tokens,tok,lsem.at[0]),pltpu.make_async_copy(wallv,wallv,lsem.at[1]),
           pltpu.make_async_copy(cot.at[pl.ds(pl.multiple_of(start,CH),share)],cotv,lsem.at[2])]
    for c in (0,2): loads[c].start()
    bar=pltpu.get_barrier_semaphore()
    for who in (s.across_y,s.sibling): pl.semaphore_signal(bar,inc=1,device_id=who,device_id_type=MESH)
    ends=[]; total=jnp.int32(0)
    for k in range(sizes.shape[1]):
        total=total+sizes[0,k]; ends.append(total)
    def hood(index):
        h=jnp.zeros(index.shape,jnp.int32)
        for e in ends: h=h+(index>=e).astype(jnp.int32)
        return h
    def own_hood(index,queries):
        row=start+index
        return jnp.where(row<keys,hood(row),queries)
    key_line=hood(lax.broadcasted_iota(jnp.int32,(1,keys),1))
    row_line=own_hood(lax.broadcasted_iota(jnp.int32,(1,share),1),qline[...])
    def mask(i,_):
        rows=rows_at(i,CH)
        col=own_hood(lax.broadcasted_iota(jnp.int32,(CH,1),0)+i*CH,qcol[rows,:])
        bias[rows,:]=jnp.where(col==key_line,0.0,MASK_VALUE).astype(bf16)
        return 0
    lax.fori_loop(0,chunks,mask,0)
    def maskT(i,_):
        rows=rows_at(i,KB)
        col=hood(lax.broadcasted_iota(jnp.int32,(KB,1),0)+i*KB)
        biasT[rows,:]=jnp.where(col==row_line,0.0,MASK_VALUE).astype(bf16)
        return 0
    lax.fori_loop(0,keys//KB,maskT,0)
    w1,w2=Weights((wa,wb,wc,wd,we)),Weights((xa,xb,xc,xd,xe))
    loads[1].wait()
    w1.fill(0,owners,wallv)
    loads[0].wait()
    pl.semaphore_wait(bar,2)
    at=lambda k,i: pl.ds(pl.multiple_of(k*share+i*CH,CH),CH)
    far=s.across_y[1]
    over=lambda i: remote(h2.at[at(mp,i)],h2.at[at(mp,i)],ssend.at[0,i],srecv.at[0,i],s.across_y)
    near=lambda i: remote(h2.at[at(mp,i)],h2.at[at(mp,i)],ssend.at[1,i],srecv.at[1,i],s.sibling)
    on=lambda i: remote(h2.at[at(far,i)],h2.at[at(far,i)],ssend.at[2,i],srecv.at[2,i],s.sibling)
    g1,g2=gains[0:4],gains[4:8]
    def emit1(i,v):
        layer_out[pl.ds(i*CH,CH),:]=v
        h2[at(mp,i),:]=v.astype(bf16)
        over(i).start(); near(i).start()
    forward(w1,g1,start,tok,lambda i: tok[at(mp,i),:].astype(f32),KV1,q1,heads1,lse1,bias,hid1,ra1,rb1,emit1)
    w2.fill(1,owners,wallv)
    for i in range(chunks):
        over(i).wait_recv(); on(i).start()
    for i in range(chunks):
        near(i).wait_recv(); on(i).wait_recv()
    def emit2(i,v): layer_out[pl.ds(i*CH,CH),:]=v
    forward(w2,g2,start,h2,lambda i: layer_out[pl.ds(i*CH,CH),:],KV2,q2,heads2,lse2,bias,hid2,ra2,rb2,emit2)
    for i in range(chunks):
        for k in (over,near,on): k(i).wait_send()
    def put(layer):
        def store(b,j,v):
            b=b+layer*LAYER_BLOCKS
            wallv[b,j]=v
        return store
    def keep(layer):
        def store(k,v): vec[layer*4+k:layer*4+k+1,:]=v
        return store
    loads[2].wait()
    half=wallv.shape[0]//2
    flush=[pltpu.make_async_copy(wallv.at[pl.ds(k*half,half)],g.at[pl.ds(k*half,half)],lsem.at[3+k]) for k in range(2)]
    backward(w2,g2,start,h2,lambda i: cotv[rows_at(i,CH),:].astype(f32),KV2,q2,heads2,lse2,biasT,hid2,ra2,rb2,
        dm,act,dhid,first,datt,dheads,delta,tokens_grad,dq,dhp,keep(1),put(1),Exchange(s,dhp,tokens_grad,rc.at[0],acc,ry.at[0],tsend.at[0],trecv.at[0]))
    flush[1].start()
    backward(w1,g1,start,tok,lambda i: tokens_grad[rows_at(i,CH),:],KV1,q1,heads1,lse1,biasT,hid1,ra1,rb1,
        dm,act,dhid,first,datt,dheads,delta,tokens_grad,dq,dhp,keep(0),put(0),Exchange(s,dhp,tokens_grad,rc.at[1],acc,ry.at[1],tsend.at[1],trecv.at[1]))
    flush[0].start()
    flush[1].wait(); flush[0].wait()

def run_layers(owners,sizes,tokens,cot,wall,gains,qline,qcol,keys,slots,collective):
    rows=tokens.shape[0]; share=rows//HEADS; chunks=share//CH
    v=pltpu.VMEM; dma=pltpu.SemaphoreType.DMA; V_=VMEM_SPEC
    two=lambda shape,t: [v(shape,t)]*2
    weights=[v((D,D),bf16),v((HEADS,D,2*HD),bf16),v((D,D),bf16),v((D,FF),bf16),v((FF,D),bf16)]
    blocks=(LAYERS*LAYER_BLOCKS,HEADS,BLK,BLK)
    scratch=[v(blocks,bf16),v((rows,D),bf16),v((rows,D),bf16),v((share,D),bf16)]
    scratch+=two((HEADS,keys,2*HD),bf16)+two((share,D),bf16)+two((share,D),bf16)+two((share,BLK),f32)+two((share,FF),f32)+two((share,D),f32)+two((share,D),f32)
    scratch+=[v((share,keys),bf16),v((keys,share),bf16)]
    scratch+=[v((share,D),bf16),v((share,FF),bf16),v((share,FF),bf16),v((share,D),bf16),v((share,D),bf16),v((share,D),bf16),v((share,BLK),f32),v((share,D),bf16)]
    scratch+=[v((rows,D),bf16),v((2,2,share,D),bf16),v((share,D),bf16),v((2,share,D),bf16)]+weights+weights
    scratch+=[dma((5,)),dma((3,chunks)),dma((3,chunks)),dma((2,3,chunks)),dma((2,3,chunks))]
    shape=jax.ShapeDtypeStruct
    return pl.pallas_call(partial(layers_kernel,slots),
        out_shape=[shape((share,D),f32),shape((share,D),f32),shape(blocks,bf16),shape((2*LAYERS*2,D),f32)],
        in_specs=[SMEM_SPEC,SMEM_SPEC,ANY_SPEC,ANY_SPEC,ANY_SPEC,V_,V_,V_],out_specs=[V_,V_,ANY_SPEC,V_],scratch_shapes=scratch,
        compiler_params=pltpu.CompilerParams(collective_id=collective,has_side_effects=True,vmem_limit_bytes=58<<20),name="layers")(
        owners,sizes,tokens,cot,wall,gains,qline,qcol)
BLK=128; STEP=10
BETA_ONE=0.9; BETA_TWO=0.95; BETA_STATS=0.95; RATE_MATRIX=0.12; DECAY_WEIGHT=0.01; ADAM_EPSILON=1e-8

def split(x):
    hi=x.astype(jnp.bfloat16)
    return hi,(x-hi.astype(jnp.float32)).astype(jnp.bfloat16)
def dot3(a,b,ca,cb):
    dims=(((ca,),(cb,)),((),()))
    ah,al=a; bh,bl=b
    d=lambda x,y: lax.dot_general(x,y,dims,preferred_element_type=jnp.float32)
    return d(ah,bh)+(d(ah,bl)+d(al,bh))
def dotf(a,b,ca,cb):
    return lax.dot_general(a,b,(((ca,),(cb,)),((),())),preferred_element_type=jnp.float32,precision=lax.Precision.HIGHEST)

def in_groups(count,step,body):
    step=math.gcd(count,step)
    def run(i,_):
        for k in range(step): body(i*step+k)
        return 0
    lax.fori_loop(0,count//step,run,0)

PANEL=32
def soap_kernel(slots, g_ref,m_ref,v_ref,l_ref,r_ref,ql_ref,qr_ref,w_ref, mo,vo,lo,ro,qlo,qro,wo, x_ref, a_ref, b_ref):
    def first(i):
        g=g_ref[i]; ql=split(ql_ref[i]); qr=split(qr_ref[i])
        gs=split(g)
        m=BETA_ONE*m_ref[i]+(1-BETA_ONE)*g
        mo[i]=m
        def turn(v):
            return dot3(split(dot3(ql,v,0,0)),qr,1,0)
        tg=turn(gs)
        v=BETA_TWO*v_ref[i]+(1-BETA_TWO)*tg*tg
        vo[i]=v
        d=turn(split(m))/(1-BETA_ONE**STEP)/(jnp.sqrt(v/(1-BETA_TWO**STEP))+ADAM_EPSILON)
        u=dot3(split(dot3(ql,split(d),1,0)),qr,1,1)
        w=w_ref[i]
        wo[i]=w-RATE_MATRIX*(u+DECAY_WEIGHT*w)
        ln=BETA_STATS*l_ref[i]+(1-BETA_STATS)*dot3(gs,gs,1,1)
        rn=BETA_STATS*r_ref[i]+(1-BETA_STATS)*dot3(gs,gs,0,0)
        lo[i]=ln; ro[i]=rn
        al=dotf(ln,ql_ref[i],1,0); ar=dotf(rn,qr_ref[i],1,0)
        a_ref[2*i]=al; a_ref[2*i+1]=ar
        x_ref[2*i]=dotf(al,al,0,0); x_ref[2*i+1]=dotf(ar,ar,0,0)
    in_groups(slots,4,first)
    n=2*slots
    lane=lax.broadcasted_iota(jnp.int32,(8,BLK),1)
    sub=lax.broadcasted_iota(jnp.int32,(8,BLK),0)
    for p in range(BLK//8):
        end=(p*8//PANEL+1)*PANEL//8
        def step(kk,_):
            k=p*8+kk
            idx=jnp.full((8,BLK),k,jnp.int32)
            atk=lane==k
            below=sub>kk
            done=(lane<=k)|(lane>=end*8)
            rows=[jnp.broadcast_to(x_ref[m,pl.ds(k,1),:],(8,BLK)) for m in range(n)]
            rinv=[1.0/jnp.take_along_axis(row,idx,axis=1) for row in rows]
            scaled=[jnp.where(atk,1.0,row)*ri for row,ri in zip(rows,rinv)]
            for m in range(n):
                b_ref[m,pl.ds(k%PANEL,1),:]=jnp.where(done,scaled[m],0.0)[0:1,:]
                for t in range(p,end):
                    v=x_ref[m,t*8:(t+1)*8,:]
                    f=jnp.take_along_axis(v,idx,axis=1)
                    new=jnp.where(atk,0.0,v)-f*scaled[m]
                    if t==p: new=jnp.where(below,new,v)
                    x_ref[m,t*8:(t+1)*8,:]=new
            return 0
        lax.fori_loop(0,8,step,0)
        if (p+1)*8%PANEL==0 and p<BLK//8-1:
            lo_,hi_=(p+1)*8-PANEL,(p+1)*8
            keep=lax.broadcasted_iota(jnp.int32,(BLK-hi_,BLK),1)
            keep=(keep<lo_)|(keep>=hi_)
            def trail(m):
                u=dotf(x_ref[m,lo_:hi_,:],b_ref[m],0,0)
                x_ref[m,hi_:,:]=jnp.where(keep,x_ref[m,hi_:,:],0.0)-u[hi_:,:]
            in_groups(n,8,trail)
    r=lax.broadcasted_iota(jnp.int32,(BLK,BLK),0); c=lax.broadcasted_iota(jnp.int32,(BLK,BLK),1)
    def last(i):
        for s,out in ((0,qlo),(1,qro)):
            x=x_ref[2*i+s]
            piv=jnp.sum(jnp.where(r==c,x,0.0),axis=1,keepdims=True)
            inv=jnp.where(r==c,1.0,jnp.where(r>c,x,0.0))*lax.rsqrt(piv)
            out[i]=dotf(a_ref[2*i+s],inv,1,1)
    in_groups(slots,4,last)

def soap(g,m,v,l,r,ql,qr,w):
    slots=g.shape[0]
    sh=jax.ShapeDtypeStruct((slots,BLK,BLK),jnp.float32)
    vm=pl.BlockSpec(memory_space=pltpu.VMEM)
    return pl.pallas_call(partial(soap_kernel,slots),out_shape=[sh]*7,in_specs=[vm]*8,out_specs=[vm]*7,
        scratch_shapes=[pltpu.VMEM((2*slots,BLK,BLK),jnp.float32)]*2+[pltpu.VMEM((2*slots,PANEL,BLK),jnp.float32)],
        compiler_params=pltpu.CompilerParams(vmem_limit_bytes=48<<20),name="soap")(g,m,v,l,r,ql,qr,w)
def adam_vector(grad, first, second, weight):
    first_new = BETA_ONE * first + (1.0 - BETA_ONE) * grad
    second_new = BETA_TWO * second + (1.0 - BETA_TWO) * grad * grad
    weight_new = weight - RATE_VECTOR * (first_new / (1.0 - BETA_ONE**STEP)) / (
        jnp.sqrt(second_new / (1.0 - BETA_TWO**STEP)) + ADAM_EPSILON
    )
    return (first_new, second_new, weight_new)


def inverse(owners):
    index=jnp.arange(owners.shape[0],dtype=jnp.int32)
    return jnp.sum(jnp.where(owners[:,None]==index[None,:],index[:,None],0),axis=0)

def local(tokens,cotangent,context_sizes,query_hoods,owners,master_blocks,first_blocks,second_blocks,left_blocks,right_blocks,
        left_bases,right_bases,vector_master,vector_moment,vector_square):
    dp=lax.axis_size("dp")
    rows=tokens.shape[0]; keys=rows-query_hoods.shape[0]; share=rows//HEADS; slots=master_blocks.shape[0]
    n=vector_master.shape[0]
    high=vector_master.astype(bf16)
    rest=(vector_master-high.astype(f32)).astype(bf16)
    extra=jnp.pad(jnp.stack([high,rest]),((0,14),(0,BLK-n)))
    slab=jnp.concatenate([master_blocks.astype(bf16).reshape(slots*BLK,BLK),extra],axis=0)
    wall=gather_all(slab,dp,0)
    pair=wall[:,:,slots*BLK:slots*BLK+2,:n].astype(f32)
    gains=(pair[:,:,0]+pair[:,:,1]).reshape(LAYERS*4,D)
    hoods=jnp.pad(query_hoods,(share-query_hoods.shape[0],0))
    layer_out,tokens_grad,g,vec=run_layers(owners,context_sizes,tokens,cotangent,wall,gains,hoods[None,:],hoods[:,None],keys,slots,1)
    vec=jnp.pad(vec.astype(bf16).reshape(dp,HEADS,1,n),((0,0),(0,0),(0,15),(0,BLK-n)))
    total=reduce_all(g,vec,inverse(owners),slots,2)
    results=soap(total[:slots*BLK].reshape(slots,BLK,BLK),first_blocks,second_blocks,left_blocks,right_blocks,left_bases,right_bases,master_blocks)
    vector_results=adam_vector(total[slots*BLK,:n],vector_moment,vector_square,vector_master)
    return (layer_out,tokens_grad)+tuple(results)+vector_results


def solution(mesh):
    return jax.shard_map(
        local,
        mesh=mesh,
        in_specs=(
            P("dp", None),
            P("dp", None),
            P("dp", None),
            P("dp"),
            P(),
            P("dp", "mp", None),
            P("dp", "mp", None),
            P("dp", "mp", None),
            P("dp", "mp", None),
            P("dp", "mp", None),
            P("dp", "mp", None),
            P("dp", "mp", None),
            P(("dp", "mp")),
            P(("dp", "mp")),
            P(("dp", "mp")),
        ),
        out_specs=(
            P(("dp", "mp"), None),
            P(("dp", "mp"), None),
            P("dp", "mp", None),
            P("dp", "mp", None),
            P("dp", "mp", None),
            P("dp", "mp", None),
            P("dp", "mp", None),
            P("dp", "mp", None),
            P("dp", "mp", None),
            P(("dp", "mp")),
            P(("dp", "mp")),
            P(("dp", "mp")),
        ),
        check_vma=False,
    )
```

```python
import math
from functools import partial

import jax
import jax.numpy as jnp
from jax import lax
from jax.experimental import pallas as pl
from jax.experimental.pallas import tpu as pltpu
from jax.sharding import PartitionSpec as P

RATE_VECTOR = 0.6
MESH=pl.DeviceIdType.MESH
BLK=128
VMEM_SPEC=pl.BlockSpec(memory_space=pltpu.VMEM)
ANY_SPEC=pl.BlockSpec(memory_space=pl.ANY)

def remote(src,dst,send,recv,device):
    return pltpu.make_async_remote_copy(src_ref=src,dst_ref=dst,send_sem=send,recv_sem=recv,device_id=device,device_id_type=MESH)

class Spot:
    def __init__(self,planes):
        dp,mp=lax.axis_index("dp"),lax.axis_index("mp")
        self.dp,self.mp,self.planes=dp,mp,planes
        self.z,self.x=dp//2,dp%2
        self.y,self.c=mp//2,mp%2
        self.across_x=(dp+1-2*self.x,mp)
        self.across_y=(dp,(mp+2)%4)
        self.sibling=(dp,mp+1-2*self.c)
        self.y_sibling=3-mp
        self.up=(jnp.minimum(dp+2,2*planes-1),mp)
        self.down=(jnp.maximum(dp-2,0),mp)
    def greet(self):
        bar=pltpu.get_barrier_semaphore()
        for who in (self.across_x,self.across_y,self.sibling):
            pl.semaphore_signal(bar,inc=1,device_id=who,device_id_type=MESH)
        @pl.when(self.z<self.planes-1)
        def _(): pl.semaphore_signal(bar,inc=1,device_id=self.up,device_id_type=MESH)
        @pl.when(self.z>0)
        def _(): pl.semaphore_signal(bar,inc=1,device_id=self.down,device_id_type=MESH)
        pl.semaphore_wait(bar,3+jnp.minimum(self.z,1)+jnp.minimum(self.planes-1-self.z,1))
    def ring(self,r,action):
        if r==0:
            action(self.z,None); return
        @pl.when(self.z>=r)
        def _(): action(self.z-r,True)
        @pl.when(self.z+r<self.planes)
        def _(): action(self.z+r,False)

def gather_kernel(planes,half,slab,out,send,recv,zsend,zrecv,lsem):
    s=Spot(planes); rows=slab.shape[0]; z,x,y,c,mp=s.z,s.x,s.y,s.c,s.mp
    A,B=pl.ds(0,half),pl.ds(half,rows-half)
    mx,my=s.across_x,s.across_y
    own=pltpu.make_async_copy(slab,out.at[s.dp,mp],lsem); own.start()
    s.greet()
    def at(p,xx,yy,cc): return out.at[p*2+xx,yy*2+cc]
    xo,yo=1-x,1-y
    def copies(p,src):
        here=at(p,x,y,c) if src is None else src
        f=lambda k,a,b,w: remote(a,b,send.at[k,p],recv.at[k,p],w)
        return dict(
            xown=lambda: f(0,here,at(p,x,y,c),mx), yown=lambda: f(1,here,at(p,x,y,c),my), cown=lambda: f(2,here,at(p,x,y,c),s.sibling),
            yfwd=lambda: f(3,at(p,xo,y,c).at[A],at(p,xo,y,c).at[A],my),
            xfwd=lambda: f(4,at(p,x,yo,c).at[B],at(p,x,yo,c).at[B],mx),
            cx=lambda: f(5,at(p,xo,y,c),at(p,xo,y,c),s.sibling), cy=lambda: f(6,at(p,x,yo,c),at(p,x,yo,c),s.sibling),
            ca=lambda: f(7,at(p,xo,yo,c).at[A],at(p,xo,yo,c).at[A],s.sibling),
            cb=lambda: f(8,at(p,xo,yo,c).at[B],at(p,xo,yo,c).at[B],s.sibling))
    def zcopy(p,up,src=None):
        here=at(p,x,y,c) if src is None else src
        return remote(here,at(p,x,y,c),zsend.at[0 if up else 1,p],zrecv.at[p],s.up if up else s.down)
    def arrive(r):
        def act(p,below):
            src=None
            if below is None: src=slab
            else: zcopy(p,below).wait_recv()
            if below is None or below:
                @pl.when(z<planes-1)
                def _(): zcopy(p,True,src).start()
            if below is None or not below:
                @pl.when(z>0)
                def _(): zcopy(p,False,src).start()
            k=copies(p,src)
            k["xown"]().start(); k["yown"]().start(); k["cown"]().start()
        s.ring(r,act)
    def second(r):
        def act(p,below):
            k=copies(p,None)
            k["xown"]().wait_recv(); k["yfwd"]().start(); k["cx"]().start()
            k["yown"]().wait_recv(); k["xfwd"]().start(); k["cy"]().start()
        s.ring(r,act)
    def third(r):
        def act(p,below):
            k=copies(p,None)
            k["yfwd"]().wait_recv(); k["ca"]().start()
            k["xfwd"]().wait_recv(); k["cb"]().start()
        s.ring(r,act)
    def finish(r):
        def act(p,below):
            src=slab if below is None else None
            k=copies(p,src)
            for n in ("cown","cx","cy","ca","cb"): k[n]().wait_recv()
            for n in k: k[n]().wait_send()
            if below is None or below:
                @pl.when(z<planes-1)
                def _(): zcopy(p,True,src).wait_send()
            if below is None or not below:
                @pl.when(z>0)
                def _(): zcopy(p,False,src).wait_send()
        s.ring(r,act)
    for r in range(planes+2):
        if r<planes: arrive(r)
        if 1<=r<=planes: second(r-1)
        if r>=2: third(r-2)
    for r in range(planes): finish(r)
    own.wait()

def gather_all(slab,dp,collective):
    rows=slab.shape[0]; planes=dp//2; half=rows//2//16*16
    dma=pltpu.SemaphoreType.DMA
    return pl.pallas_call(partial(gather_kernel,planes,half),
        out_shape=jax.ShapeDtypeStruct((dp,4,rows,slab.shape[1]),slab.dtype),
        in_specs=[ANY_SPEC],out_specs=ANY_SPEC,
        scratch_shapes=[dma((9,planes)),dma((9,planes)),dma((2,planes)),dma((planes,)),dma],
        compiler_params=pltpu.CompilerParams(collective_id=collective,has_side_effects=True),name="gather_all")(slab)

def reduce_kernel(planes,half,slots,blocks,inner,extra,out,g,rc,acc,ya,xb,xa,yb,own,zin,send,recv,zsend,zrecv):
    s=Spot(planes); rows=g.shape[2]; z,x,y,c,mp=s.z,s.x,s.y,s.c,s.mp
    A,B=pl.ds(0,half),pl.ds(half,rows-half)
    mx,my=s.across_x,s.across_y
    xo,yo,co=1-x,1-y,1-c
    s.greet()
    f32=lambda v: v.astype(jnp.float32)
    def core(p,xx,yy):
        k=xx*2+yy
        return remote(g.at[p*2+xx,yy*2+co],rc.at[p*4+k],send.at[k,p],recv.at[k,p],s.sibling)
    def toya(p,xx): return remote(acc.at[p*4+xx*2+yo,A],ya.at[p*2+xx],send.at[4+xx,p],recv.at[4+xx,p],my)
    def toxb(p,yy): return remote(acc.at[p*4+xo*2+yy,B],xb.at[p*2+yy],send.at[6+yy,p],recv.at[6+yy,p],mx)
    def toxa(p): return remote(ya.at[p*2+xo],xa.at[p],send.at[8,p],recv.at[8,p],mx)
    def toyb(p): return remote(xb.at[p*2+yo],yb.at[p],send.at[9,p],recv.at[9,p],my)
    def toz(p,up): return remote(own.at[p],zin.at[0 if up else 1,p],zsend.at[p],zrecv.at[0 if up else 1,p],s.up if up else s.down)
    def pack(p,parity):
        for xx in (0,1):
            d=p*2+xx
            def one(k,_):
                block=inner[d*slots+k]
                for yy in (0,1):
                    g[d,yy*2+parity,pl.ds(pl.multiple_of(k*BLK,BLK),BLK),:]=blocks[block,yy*2+parity]
                return 0
            lax.fori_loop(0,slots,one,0)
            for yy in (0,1): g[d,yy*2+parity,slots*BLK:,:]=extra[d,yy*2+parity]
    def start(p,_):
        pack(p,co)
        for xx in (0,1):
            for yy in (0,1): core(p,xx,yy).start()
    def first(p,_):
        pack(p,c)
        for xx in (0,1):
            for yy in (0,1):
                core(p,xx,yy).wait_recv()
                acc[p*4+xx*2+yy]=(f32(g[p*2+xx,yy*2+c])+f32(rc[p*4+xx*2+yy])).astype(acc.dtype)
        for e in (0,1): toya(p,e).start(); toxb(p,e).start()
    def second(p,_):
        for e in (0,1):
            toya(p,e).wait_recv()
            ya[p*2+e]=(f32(acc[p*4+e*2+y,A])+f32(ya[p*2+e])).astype(ya.dtype)
        toxa(p).start()
        for e in (0,1):
            toxb(p,e).wait_recv()
            xb[p*2+e]=(f32(acc[p*4+x*2+e,B])+f32(xb[p*2+e])).astype(xb.dtype)
        toyb(p).start()
    def third(p,below):
        toxa(p).wait_recv()
        av=f32(ya[p*2+x])+f32(xa[p])
        toyb(p).wait_recv()
        bv=f32(xb[p*2+y])+f32(yb[p])
        if below is None:
            out[A]=av; out[B]=bv
            @pl.when(z>0)
            def _():
                toz(p,True).wait_recv()
                out[...]=out[...]+f32(zin[0,p])
            @pl.when(z<planes-1)
            def _():
                toz(p,False).wait_recv()
                out[...]=out[...]+f32(zin[1,p])
            return
        own[p,A]=av.astype(own.dtype); own[p,B]=bv.astype(own.dtype)
        up=not below
        has=(z>0) if up else (z<planes-1)
        @pl.when(has)
        def _():
            toz(p,up).wait_recv()
            own[p,A]=(av+f32(zin[0 if up else 1,p,A])).astype(own.dtype)
            own[p,B]=(bv+f32(zin[0 if up else 1,p,B])).astype(own.dtype)
        toz(p,up).start()
    def finish(p,below):
        for xx in (0,1):
            for yy in (0,1): core(p,xx,yy).wait_send()
        for e in (0,1): toya(p,e).wait_send(); toxb(p,e).wait_send()
        toxa(p).wait_send(); toyb(p).wait_send()
        if below is not None: toz(p,not below).wait_send()
    order=list(range(planes-1,-1,-1))
    for r in order: s.ring(r,start)
    n=len(order)
    for i in range(n+2):
        if i<n: s.ring(order[i],first)
        if 0<=i-1<n: s.ring(order[i-1],second)
        if 0<=i-2<n: s.ring(order[i-2],third)
    for r in order: s.ring(r,finish)

def reduce_all(g,extra,inner,slots,collective):
    dp=extra.shape[0]; rows,cols=slots*BLK+extra.shape[2],g.shape[3]; planes=dp//2; half=rows//2//16*16
    dma=pltpu.SemaphoreType.DMA; bf=lambda *sh: pltpu.VMEM(sh+(cols,),g.dtype)
    return pl.pallas_call(partial(reduce_kernel,planes,half,slots),
        out_shape=jax.ShapeDtypeStruct((rows,cols),jnp.float32),in_specs=[VMEM_SPEC,pl.BlockSpec(memory_space=pltpu.SMEM),VMEM_SPEC],out_specs=VMEM_SPEC,
        scratch_shapes=[bf(dp,4,rows),bf(planes*4,rows),bf(planes*4,rows),bf(planes*2,half),bf(planes*2,rows-half),bf(planes,half),bf(planes,rows-half),
            bf(planes,rows),bf(2,planes,rows),dma((10,planes)),dma((10,planes)),dma((planes,)),dma((2,planes))],
        compiler_params=pltpu.CompilerParams(collective_id=collective,has_side_effects=True,vmem_limit_bytes=56<<20),name="reduce_all")(g,inner,extra)
D=512; HD=128; FF=1024; LAYERS=2; BLK=128; HEADS=4
NORM_EPSILON=1e-5; MASK_VALUE=-1e30
f32=jnp.float32; bf16=jnp.bfloat16
SMEM_SPEC=pl.BlockSpec(memory_space=pltpu.SMEM)
SCALE=HD**-0.5; LOG2E=math.log2(math.e)
ROOT=math.sqrt(2/math.pi)

def nn(a,b): return lax.dot_general(a,b,(((1,),(0,)),((),())),preferred_element_type=f32)
def nt(a,b): return lax.dot_general(a,b,(((1,),(1,)),((),())),preferred_element_type=f32)
def tn(a,b): return lax.dot_general(a,b,(((0,),(0,)),((),())),preferred_element_type=f32)

def normed(r):
    center=r-jnp.mean(r,axis=-1,keepdims=True)
    rho=lax.rsqrt(jnp.mean(center*center,axis=-1,keepdims=True)+NORM_EPSILON)
    return center*rho,rho
def norm_back(dy,xhat,rho,gain):
    inner=dy*gain
    return rho*(inner-jnp.mean(inner,axis=-1,keepdims=True)-xhat*jnp.mean(inner*xhat,axis=-1,keepdims=True))
def gelu(v): return 0.5*v*(1+jnp.tanh(ROOT*(v+0.044715*v*v*v)))
def gelu_both(v):
    sq=v*v
    t=jnp.tanh(ROOT*v*(1+0.044715*sq))
    half=0.5*(1+t)
    return v*half,half+0.5*v*(1-t*t)*(ROOT*(1+3*0.044715*sq))
def colsum(v): return jnp.sum(v,axis=0,keepdims=True)

COLS_TILE=(3,4,2,4)
FIRST_BLOCK=(0,12,16,24)
LAYER_BLOCKS=32
CH=160
KB=320
FS=FF//HEADS

def rows_at(i,n): return pl.ds(pl.multiple_of(i*n,n),n)

class Weights:
    def __init__(self,refs): self.q,self.kv,self.out,self.up,self.down=refs
    def fill(self,layer,owners,wallv):
        base=layer*LAYER_BLOCKS
        def tiles(b):
            slot=owners[b]
            return [wallv[slot,j] for j in range(HEADS)]
        def by_row(r,_):
            rows=rows_at(r,BLK)
            for c in range(3):
                for j,v in enumerate(tiles(base+r*3+c)):
                    if c==0: self.q[rows,j*BLK:(j+1)*BLK]=v
                    else: self.kv[rows,j*2*BLK+(c-1)*BLK:j*2*BLK+c*BLK]=v
            for c in range(2):
                for j,v in enumerate(tiles(base+FIRST_BLOCK[2]+r*2+c)): self.up[rows,j*FS+c*BLK:j*FS+(c+1)*BLK]=v
            return 0
        lax.fori_loop(0,D//BLK,by_row,0)
        for c in range(4):
            for j,v in enumerate(tiles(base+FIRST_BLOCK[1]+c)): self.out[j*BLK:(j+1)*BLK,c*BLK:(c+1)*BLK]=v
            for r in range(2):
                for j,v in enumerate(tiles(base+FIRST_BLOCK[3]+r*4+c)): self.down[j*FS+r*BLK:j*FS+(r+1)*BLK,c*BLK:(c+1)*BLK]=v

def key_of(j): return slice(j*2*HD,j*2*HD+HD)
def value_of(j): return slice(j*2*HD+HD,(j+1)*2*HD)

def project(w,h_full,KV,rows): KV[rows,:]=nn(h_full[rows,:],w.kv[...]).astype(bf16)

def queries(w,h_full,start,q):
    def one(i,_):
        q[rows_at(i,CH),:]=nn(h_full[pl.ds(pl.multiple_of(start+i*CH,CH),CH),:],w.q[...]).astype(bf16)
        return 0
    lax.fori_loop(0,q.shape[0]//CH,one,0)

def forward(w,gains,own_rows,KV,q,heads,lse,bias,hidden,r1,r2,emit):
    keys=KV.shape[0]; chunks=q.shape[0]//CH
    lane=lax.broadcasted_iota(jnp.int32,(CH,BLK),1)
    def attend(i,_):
        rows=rows_at(i,CH)
        stats=jnp.zeros((CH,BLK),f32)
        scores=lambda j: nt(q[rows,j*HD:(j+1)*HD],KV[:,key_of(j)])
        s=scores(0)
        for j in range(HEADS):
            later=scores(j+1) if j+1<HEADS else None
            s=s+bias[rows,:].astype(f32)
            peak=jnp.max(s,axis=1,keepdims=True)
            p=jnp.exp2((s-peak)*(SCALE*LOG2E))
            total=jnp.sum(p,axis=1,keepdims=True)
            o=nn(p.astype(bf16),KV[:,value_of(j)])/total
            heads[rows,j*HD:(j+1)*HD]=o.astype(bf16)
            stats=jnp.where(lane==j,peak*(SCALE*LOG2E)+jnp.log2(total),stats)
            s=later
        lse[rows,:]=stats
        return 0
    lax.fori_loop(0,chunks,attend,0)
    for i in range(chunks):
        rows=pl.ds(i*CH,CH)
        a=own_rows(i)+nn(heads[rows,:],w.out[...])
        r1[rows,:]=a
        first=normed(a)[0]*gains[0:1,:]+gains[1:2,:]
        hid=nn(first.astype(bf16),w.up[...])
        hidden[rows,:]=hid
        b=first+nn(gelu(hid).astype(bf16),w.down[...])
        r2[rows,:]=b
        emit(i,normed(b)[0]*gains[2:3,:]+gains[3:4,:])

def backward(w,gains,start,h_full,upper,KV,q,heads,lse,biasT,hidden,r1,r2,
        dm,act,dhid,first,datt,dheads,delta,grad,dq,dqa,dhp,vec,put,exchange):
    share=q.shape[0]; keys=KV.shape[0]; chunks=share//CH
    lane=lax.broadcasted_iota(jnp.int32,(CH,BLK),1)
    def part(i,carry):
        rows=rows_at(i,CH)
        dy=upper(i)
        xhat,rho=normed(r2[rows,:])
        g2,s2=colsum(dy*xhat),colsum(dy)
        sg=norm_back(dy,xhat,rho,gains[2:3,:])
        dmb=sg.astype(bf16); dm[rows,:]=dmb
        a,slope=gelu_both(hidden[rows,:])
        act[rows,:]=a.astype(bf16)
        dh=(nt(dmb,w.down[...])*slope).astype(bf16)
        dhid[rows,:]=dh
        fu=sg+nt(dh,w.up[...])
        xhat,rho=normed(r1[rows,:])
        first[rows,:]=(xhat*gains[0:1,:]+gains[1:2,:]).astype(bf16)
        g1,s1=colsum(fu*xhat),colsum(fu)
        f=norm_back(fu,xhat,rho,gains[0:1,:])
        grad[rows,:]=f
        fb=f.astype(bf16); datt[rows,:]=fb
        dhe=nt(fb,w.out[...]).astype(bf16)
        dheads[rows,:]=dhe
        prod=dhe.astype(f32)*heads[rows,:].astype(f32)
        stats=jnp.zeros((CH,BLK),f32)
        for j in range(HEADS):
            stats=jnp.where(lane==j,jnp.sum(prod[:,j*HD:(j+1)*HD],axis=1,keepdims=True),stats)
        delta[rows,:]=stats
        return tuple(c+v for c,v in zip(carry,(g1,s1,g2,s2)))
    zero=jnp.zeros((1,D),f32)
    for k,v in enumerate(lax.fori_loop(0,chunks,part,(zero,)*4)): vec(k,v)
    lseT=jnp.transpose(lse[...]); deltaT=jnp.transpose(delta[...])
    dqa[...]=jnp.zeros(dqa.shape,f32)
    def keyblock(kb,_):
        rows=rows_at(kb,KB)
        head=lambda j: slice(j*HD,(j+1)*HD)
        both=lambda j: (nt(KV[rows,key_of(j)],q[:,head(j)]),nt(KV[rows,value_of(j)],dheads[:,head(j)]))
        now=both(0)
        for j in range(HEADS):
            later=both(j+1) if j+1<HEADS else None
            s,dp=now
            p=jnp.exp2((s+biasT[rows,:].astype(f32))*(SCALE*LOG2E)-lseT[j:j+1,:])
            ds=(p*(dp-deltaT[j:j+1,:])).astype(bf16)
            dqa[:,head(j)]+=tn(ds,KV[rows,key_of(j)])
            dv=nn(p.astype(bf16),dheads[:,head(j)])
            dk=nn(ds,q[:,head(j)])*SCALE
            KV[rows,key_of(j)]=dk.astype(bf16)
            KV[rows,value_of(j)]=dv.astype(bf16)
            now=later
        dhp[rows,:]=nt(KV[rows,:],w.kv[...]).astype(bf16)
        for sub in range(KB//CH): exchange.send(kb*(KB//CH)+sub)
        @pl.when(kb>0)
        def _():
            for sub in range(KB//CH): exchange.turn((kb-1)*(KB//CH)+sub)
        return 0
    lax.fori_loop(0,keys//KB,keyblock,0)
    dq[...]=(dqa[...]*SCALE).astype(bf16)
    def own(i,_):
        rows=rows_at(i,CH)
        grad[rows,:]=grad[rows,:]+nt(dq[rows,:],w.q[...])
        return 0
    lax.fori_loop(0,chunks,own,0)
    def tiles(kind,j,value,c0=0):
        for r in range(value.shape[0]//BLK):
            for c in range(value.shape[1]//BLK):
                put(FIRST_BLOCK[kind]+r*COLS_TILE[kind]+c+c0,j,value[r*BLK:(r+1)*BLK,c*BLK:(c+1)*BLK].astype(bf16))
    for j in range(HEADS): tiles(3,j,tn(act[:,j*FS:(j+1)*FS],dm[...]))
    for sub in range(KB//CH): exchange.turn(keys//CH-KB//CH+sub)
    for j in range(HEADS):
        tiles(2,j,tn(first[...],dhid[:,j*FS:(j+1)*FS]))
        tiles(1,j,tn(heads[:,j*HD:(j+1)*HD],datt[...]))
    hown=h_full[pl.ds(pl.multiple_of(start,CH),share),:]
    hctx=h_full[:keys,:]
    for j in range(HEADS):
        tiles(0,j,tn(hown,dq[:,j*HD:(j+1)*HD]))
        tiles(0,j,tn(hctx,KV[:,j*2*HD:(j+1)*2*HD]),c0=1)
    exchange.finish()

class Exchange:
    def __init__(self,s,terms,grad,rc,acc,ry,send,recv,count):
        self.s,self.terms,self.grad,self.rc,self.acc,self.ry,self.count=s,terms,grad,rc,acc,ry,count
        self.n=send.shape[1]
        at=lambda k,i: rows_at(k*self.n+i,CH)
        self.at=at
        co=1-s.c
        self.a=lambda i: remote(terms.at[at((1-s.y)*2+co,i)],rc.at[0,rows_at(i,CH)],send.at[0,i],recv.at[0,i],s.sibling)
        self.b=lambda i: remote(terms.at[at(s.y*2+co,i)],rc.at[1,rows_at(i,CH)],send.at[1,i],recv.at[1,i],s.sibling)
        self.o=lambda i: remote(acc.at[rows_at(i,CH)],ry.at[rows_at(i,CH)],send.at[2,i],recv.at[2,i],s.across_y)
    def owner(self,b):
        o=b//self.n
        return o//2==self.s.y,o%2==self.s.c,b%self.n
    def send(self,b):
        y,c,i=self.owner(b)
        @pl.when(jnp.logical_not(c)&jnp.logical_not(y))
        def _(): self.a(i).start()
        @pl.when(jnp.logical_not(c)&y)
        def _(): self.b(i).start()
    def turn(self,b):
        y,c,i=self.owner(b)
        @pl.when(c&jnp.logical_not(y))
        def _():
            self.a(i).wait_recv()
            rows=rows_at(i,CH)
            self.acc[rows,:]=(self.terms[rows_at(b,CH),:].astype(f32)+self.rc[0,rows,:].astype(f32)).astype(bf16)
            self.o(i).start()
    def finish(self):
        s=self.s
        for i in range(self.n):
            rows=pl.ds(i*CH,CH)
            @pl.when(s.mp*self.n+i<self.count)
            def _():
                self.b(i).wait_recv()
                t=self.grad[rows]+(self.terms[self.at(s.mp,i)].astype(f32)+self.rc[1,rows].astype(f32))
                self.o(i).wait_recv()
                self.grad[rows]=t+self.ry[rows].astype(f32)
        for i in range(self.n):
            @pl.when(((1-s.y)*2+1-s.c)*self.n+i<self.count)
            def _(): self.a(i).wait_send()
            @pl.when((s.y*2+1-s.c)*self.n+i<self.count)
            def _(): self.b(i).wait_send()
            @pl.when(((1-s.y)*2+s.c)*self.n+i<self.count)
            def _(): self.o(i).wait_send()

def layers_kernel(slots,owners,sizes,tokens,cot,wall,gains,qline,qcol, layer_out,tokens_grad,g,vec,
        wallv,tok,h2,cotv,KV1,KV2,q1,q2,heads1,heads2,lse1,lse2,hid1,hid2,ra1,ra2,rb1,rb2,bias,biasT,
        dm,act,dhid,first,datt,dheads,delta,dq,dqa,dhp,rc,acc,ry,wa,wb,wc,wd,we,xa,xb,xc,xd,xe,lsem,ssend,srecv,tsend,trecv):
    s=Spot(1); mp=s.mp; share=q1.shape[0]; keys=KV1.shape[0]; chunks=share//CH
    start=mp*share
    def bring(k,_):
        pltpu.make_async_copy(wall.at[k//slots,:,rows_at(k%slots,BLK),:],wallv.at[k],lsem.at[1]).start()
        return 0
    lax.fori_loop(0,wallv.shape[0],bring,0)
    loads=[pltpu.make_async_copy(tokens,tok,lsem.at[0]),pltpu.make_async_copy(wallv,wallv,lsem.at[1]),
           pltpu.make_async_copy(cot.at[pl.ds(pl.multiple_of(start,CH),share)],cotv,lsem.at[2])]
    for c in (0,2): loads[c].start()
    bar=pltpu.get_barrier_semaphore()
    for who in (s.across_y,s.sibling): pl.semaphore_signal(bar,inc=1,device_id=who,device_id_type=MESH)
    ends=[]; total=jnp.int32(0)
    for k in range(sizes.shape[1]):
        total=total+sizes[0,k]; ends.append(total)
    def hood(index):
        h=jnp.zeros(index.shape,jnp.int32)
        for e in ends: h=h+(index>=e).astype(jnp.int32)
        return h
    def own_hood(index,queries):
        row=start+index
        return jnp.where(row<keys,hood(row),queries)
    key_line=hood(lax.broadcasted_iota(jnp.int32,(1,keys),1))
    row_line=own_hood(lax.broadcasted_iota(jnp.int32,(1,share),1),qline[...])
    def mask(i,_):
        rows=rows_at(i,CH)
        col=own_hood(lax.broadcasted_iota(jnp.int32,(CH,1),0)+i*CH,qcol[rows,:])
        bias[rows,:]=jnp.where(col==key_line,0.0,MASK_VALUE).astype(bf16)
        return 0
    lax.fori_loop(0,chunks,mask,0)
    def maskT(i,_):
        rows=rows_at(i,KB)
        col=hood(lax.broadcasted_iota(jnp.int32,(KB,1),0)+i*KB)
        biasT[rows,:]=jnp.where(col==row_line,0.0,MASK_VALUE).astype(bf16)
        return 0
    lax.fori_loop(0,keys//KB,maskT,0)
    w1,w2=Weights((wa,wb,wc,wd,we)),Weights((xa,xb,xc,xd,xe))
    loads[1].wait()
    w1.fill(0,owners,wallv)
    loads[0].wait()
    pl.semaphore_wait(bar,2)
    at=lambda k,i: pl.ds(pl.multiple_of(k*share+i*CH,CH),CH)
    far=s.across_y[1]
    over=lambda i: remote(h2.at[at(mp,i)],h2.at[at(mp,i)],ssend.at[0,i],srecv.at[0,i],s.across_y)
    near=lambda i: remote(h2.at[at(mp,i)],h2.at[at(mp,i)],ssend.at[1,i],srecv.at[1,i],s.sibling)
    on=lambda i: remote(h2.at[at(far,i)],h2.at[at(far,i)],ssend.at[2,i],srecv.at[2,i],s.sibling)
    g1,g2=gains[0:4],gains[4:8]
    def emit1(i,v):
        layer_out[pl.ds(i*CH,CH),:]=v
        h2[at(mp,i),:]=v.astype(bf16)
        over(i).start(); near(i).start()
    def every(kb,_):
        project(w1,tok,KV1,rows_at(kb,KB))
        return 0
    lax.fori_loop(0,keys//KB,every,0)
    queries(w1,tok,start,q1)
    forward(w1,g1,lambda i: tok[at(mp,i),:].astype(f32),KV1,q1,heads1,lse1,bias,hid1,ra1,rb1,emit1)
    w2.fill(1,owners,wallv)
    def arrived(k,i):
        @pl.when(k*chunks+i<keys//CH)
        def _(): project(w2,h2,KV2,at(k,i))
    for i in range(chunks): arrived(mp,i)
    queries(w2,h2,start,q2)
    for i in range(chunks):
        near(i).wait_recv(); arrived(s.sibling[1],i)
    for i in range(chunks):
        over(i).wait_recv(); on(i).start(); arrived(far,i)
    for i in range(chunks):
        on(i).wait_recv(); arrived(s.y_sibling,i)
    def emit2(i,v): layer_out[pl.ds(i*CH,CH),:]=v
    forward(w2,g2,lambda i: layer_out[pl.ds(i*CH,CH),:],KV2,q2,heads2,lse2,bias,hid2,ra2,rb2,emit2)
    for i in range(chunks):
        for k in (over,near,on): k(i).wait_send()
    def put(layer):
        def store(b,j,v):
            b=b+layer*LAYER_BLOCKS
            wallv[b,j]=v
        return store
    def keep(layer):
        def store(k,v): vec[layer*4+k:layer*4+k+1,:]=v
        return store
    loads[2].wait()
    half=wallv.shape[0]//2
    flush=[pltpu.make_async_copy(wallv.at[pl.ds(k*half,half)],g.at[pl.ds(k*half,half)],lsem.at[3+k]) for k in range(2)]
    backward(w2,g2,start,h2,lambda i: cotv[rows_at(i,CH),:].astype(f32),KV2,q2,heads2,lse2,biasT,hid2,ra2,rb2,
        dm,act,dhid,first,datt,dheads,delta,tokens_grad,dq,dqa,dhp,keep(1),put(1),Exchange(s,dhp,tokens_grad,rc.at[0],acc,ry.at[0],tsend.at[0],trecv.at[0],keys//CH))
    flush[1].start()
    backward(w1,g1,start,tok,lambda i: tokens_grad[rows_at(i,CH),:],KV1,q1,heads1,lse1,biasT,hid1,ra1,rb1,
        dm,act,dhid,first,datt,dheads,delta,tokens_grad,dq,dqa,dhp,keep(0),put(0),Exchange(s,dhp,tokens_grad,rc.at[1],acc,ry.at[1],tsend.at[1],trecv.at[1],keys//CH))
    flush[0].start()
    flush[1].wait(); flush[0].wait()

def run_layers(owners,sizes,tokens,cot,wall,gains,qline,qcol,keys,slots,collective):
    rows=tokens.shape[0]; share=rows//HEADS; chunks=share//CH
    v=pltpu.VMEM; dma=pltpu.SemaphoreType.DMA; V_=VMEM_SPEC
    two=lambda shape,t: [v(shape,t)]*2
    weights=[v((D,D),bf16),v((D,HEADS*2*HD),bf16),v((D,D),bf16),v((D,FF),bf16),v((FF,D),bf16)]
    blocks=(LAYERS*LAYER_BLOCKS,HEADS,BLK,BLK)
    scratch=[v(blocks,bf16),v((rows,D),bf16),v((rows,D),bf16),v((share,D),bf16)]
    scratch+=two((keys,HEADS*2*HD),bf16)+two((share,D),bf16)+two((share,D),bf16)+two((share,BLK),f32)+two((share,FF),f32)+two((share,D),f32)+two((share,D),f32)
    scratch+=[v((share,keys),bf16),v((keys,share),bf16)]
    scratch+=[v((share,D),bf16),v((share,FF),bf16),v((share,FF),bf16),v((share,D),bf16),v((share,D),bf16),v((share,D),bf16),v((share,BLK),f32),v((share,D),bf16),v((share,D),f32)]
    scratch+=[v((rows,D),bf16),v((2,2,share,D),bf16),v((share,D),bf16),v((2,share,D),bf16)]+weights+weights
    scratch+=[dma((5,)),dma((3,chunks)),dma((3,chunks)),dma((2,3,chunks)),dma((2,3,chunks))]
    shape=jax.ShapeDtypeStruct
    return pl.pallas_call(partial(layers_kernel,slots),
        out_shape=[shape((share,D),f32),shape((share,D),f32),shape(blocks,bf16),shape((2*LAYERS*2,D),f32)],
        in_specs=[SMEM_SPEC,SMEM_SPEC,ANY_SPEC,ANY_SPEC,ANY_SPEC,V_,V_,V_],out_specs=[V_,V_,ANY_SPEC,V_],scratch_shapes=scratch,
        compiler_params=pltpu.CompilerParams(collective_id=collective,has_side_effects=True,vmem_limit_bytes=58<<20),name="layers")(
        owners,sizes,tokens,cot,wall,gains,qline,qcol)
BLK=128; STEP=10
BETA_ONE=0.9; BETA_TWO=0.95; BETA_STATS=0.95; RATE_MATRIX=0.12; DECAY_WEIGHT=0.01; ADAM_EPSILON=1e-8

def split(x):
    hi=x.astype(jnp.bfloat16)
    return hi,(x-hi.astype(jnp.float32)).astype(jnp.bfloat16)
def dot3(a,b,ca,cb):
    dims=(((ca,),(cb,)),((),()))
    ah,al=a; bh,bl=b
    d=lambda x,y: lax.dot_general(x,y,dims,preferred_element_type=jnp.float32)
    return d(ah,bh)+(d(ah,bl)+d(al,bh))
def dotf(a,b,ca,cb):
    return lax.dot_general(a,b,(((ca,),(cb,)),((),())),preferred_element_type=jnp.float32,precision=lax.Precision.HIGHEST)

def in_groups(count,step,body):
    step=math.gcd(count,step)
    def run(i,_):
        for k in range(step): body(i*step+k)
        return 0
    lax.fori_loop(0,count//step,run,0)

PANEL=32
def soap_kernel(slots, g_ref,m_ref,v_ref,l_ref,r_ref,ql_ref,qr_ref,w_ref, mo,vo,lo,ro,qlo,qro,wo, x_ref, a_ref, b_ref):
    def first(i):
        g=g_ref[i]; ql=split(ql_ref[i]); qr=split(qr_ref[i])
        gs=split(g)
        m=BETA_ONE*m_ref[i]+(1-BETA_ONE)*g
        mo[i]=m
        def turn(v):
            return dot3(split(dot3(ql,v,0,0)),qr,1,0)
        tg=turn(gs)
        v=BETA_TWO*v_ref[i]+(1-BETA_TWO)*tg*tg
        vo[i]=v
        d=turn(split(m))/(1-BETA_ONE**STEP)/(jnp.sqrt(v/(1-BETA_TWO**STEP))+ADAM_EPSILON)
        u=dot3(split(dot3(ql,split(d),1,0)),qr,1,1)
        w=w_ref[i]
        wo[i]=w-RATE_MATRIX*(u+DECAY_WEIGHT*w)
        ln=BETA_STATS*l_ref[i]+(1-BETA_STATS)*dot3(gs,gs,1,1)
        rn=BETA_STATS*r_ref[i]+(1-BETA_STATS)*dot3(gs,gs,0,0)
        lo[i]=ln; ro[i]=rn
        al=dotf(ln,ql_ref[i],1,0); ar=dotf(rn,qr_ref[i],1,0)
        a_ref[2*i]=al; a_ref[2*i+1]=ar
        x_ref[2*i]=dotf(al,al,0,0); x_ref[2*i+1]=dotf(ar,ar,0,0)
    in_groups(slots,4,first)
    n=2*slots
    lane=lax.broadcasted_iota(jnp.int32,(8,BLK),1)
    sub=lax.broadcasted_iota(jnp.int32,(8,BLK),0)
    for p in range(BLK//8):
        end=(p*8//PANEL+1)*PANEL//8
        def step(kk,_):
            k=p*8+kk
            idx=jnp.full((8,BLK),k,jnp.int32)
            atk=lane==k
            below=sub>kk
            done=(lane<=k)|(lane>=end*8)
            rows=[jnp.broadcast_to(x_ref[m,pl.ds(k,1),:],(8,BLK)) for m in range(n)]
            rinv=[1.0/jnp.take_along_axis(row,idx,axis=1) for row in rows]
            scaled=[jnp.where(atk,1.0,row)*ri for row,ri in zip(rows,rinv)]
            for m in range(n):
                b_ref[m,pl.ds(k%PANEL,1),:]=jnp.where(done,scaled[m],0.0)[0:1,:]
                for t in range(p,end):
                    v=x_ref[m,t*8:(t+1)*8,:]
                    f=jnp.take_along_axis(v,idx,axis=1)
                    new=jnp.where(atk,0.0,v)-f*scaled[m]
                    if t==p: new=jnp.where(below,new,v)
                    x_ref[m,t*8:(t+1)*8,:]=new
            return 0
        lax.fori_loop(0,8,step,0)
        if (p+1)*8%PANEL==0 and p<BLK//8-1:
            lo_,hi_=(p+1)*8-PANEL,(p+1)*8
            keep=lax.broadcasted_iota(jnp.int32,(BLK-hi_,BLK),1)
            keep=(keep<lo_)|(keep>=hi_)
            def trail(m):
                u=dotf(x_ref[m,lo_:hi_,:],b_ref[m],0,0)
                x_ref[m,hi_:,:]=jnp.where(keep,x_ref[m,hi_:,:],0.0)-u[hi_:,:]
            in_groups(n,8,trail)
    r=lax.broadcasted_iota(jnp.int32,(BLK,BLK),0); c=lax.broadcasted_iota(jnp.int32,(BLK,BLK),1)
    def last(i):
        for s,out in ((0,qlo),(1,qro)):
            x=x_ref[2*i+s]
            piv=jnp.sum(jnp.where(r==c,x,0.0),axis=1,keepdims=True)
            inv=jnp.where(r==c,1.0,jnp.where(r>c,x,0.0))*lax.rsqrt(piv)
            out[i]=dotf(a_ref[2*i+s],inv,1,1)
    in_groups(slots,4,last)

def soap(g,m,v,l,r,ql,qr,w):
    slots=g.shape[0]
    sh=jax.ShapeDtypeStruct((slots,BLK,BLK),jnp.float32)
    vm=pl.BlockSpec(memory_space=pltpu.VMEM)
    return pl.pallas_call(partial(soap_kernel,slots),out_shape=[sh]*7,in_specs=[vm]*8,out_specs=[vm]*7,
        scratch_shapes=[pltpu.VMEM((2*slots,BLK,BLK),jnp.float32)]*2+[pltpu.VMEM((2*slots,PANEL,BLK),jnp.float32)],
        compiler_params=pltpu.CompilerParams(vmem_limit_bytes=48<<20),name="soap")(g,m,v,l,r,ql,qr,w)
def adam_vector(grad, first, second, weight):
    first_new = BETA_ONE * first + (1.0 - BETA_ONE) * grad
    second_new = BETA_TWO * second + (1.0 - BETA_TWO) * grad * grad
    weight_new = weight - RATE_VECTOR * (first_new / (1.0 - BETA_ONE**STEP)) / (
        jnp.sqrt(second_new / (1.0 - BETA_TWO**STEP)) + ADAM_EPSILON
    )
    return (first_new, second_new, weight_new)


def inverse(owners):
    index=jnp.arange(owners.shape[0],dtype=jnp.int32)
    return jnp.sum(jnp.where(owners[:,None]==index[None,:],index[:,None],0),axis=0)

def local(tokens,cotangent,context_sizes,query_hoods,owners,master_blocks,first_blocks,second_blocks,left_blocks,right_blocks,
        left_bases,right_bases,vector_master,vector_moment,vector_square):
    dp=lax.axis_size("dp")
    rows=tokens.shape[0]; keys=rows-query_hoods.shape[0]; share=rows//HEADS; slots=master_blocks.shape[0]
    n=vector_master.shape[0]
    high=vector_master.astype(bf16)
    rest=(vector_master-high.astype(f32)).astype(bf16)
    extra=jnp.pad(jnp.stack([high,rest]),((0,14),(0,BLK-n)))
    slab=jnp.concatenate([master_blocks.astype(bf16).reshape(slots*BLK,BLK),extra],axis=0)
    wall=gather_all(slab,dp,0)
    pair=wall[:,:,slots*BLK:slots*BLK+2,:n].astype(f32)
    gains=(pair[:,:,0]+pair[:,:,1]).reshape(LAYERS*4,D)
    hoods=jnp.pad(query_hoods,(share-query_hoods.shape[0],0))
    layer_out,tokens_grad,g,vec=run_layers(owners,context_sizes,tokens,cotangent,wall,gains,hoods[None,:],hoods[:,None],keys,slots,1)
    vec=jnp.pad(vec.astype(bf16).reshape(dp,HEADS,1,n),((0,0),(0,0),(0,15),(0,BLK-n)))
    total=reduce_all(g,vec,inverse(owners),slots,2)
    results=soap(total[:slots*BLK].reshape(slots,BLK,BLK),first_blocks,second_blocks,left_blocks,right_blocks,left_bases,right_bases,master_blocks)
    vector_results=adam_vector(total[slots*BLK,:n],vector_moment,vector_square,vector_master)
    return (layer_out,tokens_grad)+tuple(results)+vector_results


def solution(mesh):
    return jax.shard_map(
        local,
        mesh=mesh,
        in_specs=(
            P("dp", None),
            P("dp", None),
            P("dp", None),
            P("dp"),
            P(),
            P("dp", "mp", None),
            P("dp", "mp", None),
            P("dp", "mp", None),
            P("dp", "mp", None),
            P("dp", "mp", None),
            P("dp", "mp", None),
            P("dp", "mp", None),
            P(("dp", "mp")),
            P(("dp", "mp")),
            P(("dp", "mp")),
        ),
        out_specs=(
            P(("dp", "mp"), None),
            P(("dp", "mp"), None),
            P("dp", "mp", None),
            P("dp", "mp", None),
            P("dp", "mp", None),
            P("dp", "mp", None),
            P("dp", "mp", None),
            P("dp", "mp", None),
            P("dp", "mp", None),
            P(("dp", "mp")),
            P(("dp", "mp")),
            P(("dp", "mp")),
        ),
        check_vma=False,
    )
```

```python
import math
from functools import partial

import jax
import jax.numpy as jnp
from jax import lax
from jax.experimental import pallas as pl
from jax.experimental.pallas import tpu as pltpu
from jax.sharding import PartitionSpec as P

RATE_VECTOR = 0.6
def adam_vector(grad, first, second, weight):
    first_new = BETA_ONE * first + (1.0 - BETA_ONE) * grad
    second_new = BETA_TWO * second + (1.0 - BETA_TWO) * grad * grad
    weight_new = weight - RATE_VECTOR * (first_new / (1.0 - BETA_ONE**STEP)) / (
        jnp.sqrt(second_new / (1.0 - BETA_TWO**STEP)) + ADAM_EPSILON
    )
    return (first_new, second_new, weight_new)


MESH=pl.DeviceIdType.MESH
BLK=128
VMEM_SPEC=pl.BlockSpec(memory_space=pltpu.VMEM)
ANY_SPEC=pl.BlockSpec(memory_space=pl.ANY)

def remote(src,dst,send,recv,device):
    return pltpu.make_async_remote_copy(src_ref=src,dst_ref=dst,send_sem=send,recv_sem=recv,device_id=device,device_id_type=MESH)

class Spot:
    def __init__(self,planes):
        dp,mp=lax.axis_index("dp"),lax.axis_index("mp")
        self.dp,self.mp,self.planes=dp,mp,planes
        self.z,self.x=dp//2,dp%2
        self.y,self.c=mp//2,mp%2
        self.across_x=(dp+1-2*self.x,mp)
        self.across_y=(dp,(mp+2)%4)
        self.sibling=(dp,mp+1-2*self.c)
        self.y_sibling=3-mp
        self.up=(jnp.minimum(dp+2,2*planes-1),mp)
        self.down=(jnp.maximum(dp-2,0),mp)
    def greet(self):
        bar=pltpu.get_barrier_semaphore()
        for who in (self.across_x,self.across_y,self.sibling):
            pl.semaphore_signal(bar,inc=1,device_id=who,device_id_type=MESH)
        @pl.when(self.z<self.planes-1)
        def _(): pl.semaphore_signal(bar,inc=1,device_id=self.up,device_id_type=MESH)
        @pl.when(self.z>0)
        def _(): pl.semaphore_signal(bar,inc=1,device_id=self.down,device_id_type=MESH)
        pl.semaphore_wait(bar,3+jnp.minimum(self.z,1)+jnp.minimum(self.planes-1-self.z,1))
    def ring(self,r,action):
        if r==0:
            action(self.z,None); return
        @pl.when(self.z>=r)
        def _(): action(self.z-r,True)
        @pl.when(self.z+r<self.planes)
        def _(): action(self.z+r,False)

def gather_kernel(planes,half,master,vector,out,slab,send,recv,zsend,zrecv,lsem):
    for k in range(master.shape[0]): slab[k*BLK:(k+1)*BLK,:]=master[k].astype(slab.dtype)
    n=vector.shape[1]
    high=vector[...].astype(slab.dtype).astype(jnp.float32)
    pair=jnp.where(lax.broadcasted_iota(jnp.int32,(16,n),0)==0,high,vector[...]-high)
    if n<BLK: pair=jnp.concatenate([pair,jnp.zeros((16,BLK-n),jnp.float32)],axis=1)
    slab[master.shape[0]*BLK:,:]=pair.astype(slab.dtype)
    s=Spot(planes); rows=slab.shape[0]; z,x,y,c,mp=s.z,s.x,s.y,s.c,s.mp
    A,B=pl.ds(0,half),pl.ds(half,rows-half)
    mx,my=s.across_x,s.across_y
    own=pltpu.make_async_copy(slab,out.at[s.dp,mp],lsem); own.start()
    s.greet()
    def at(p,xx,yy,cc): return out.at[p*2+xx,yy*2+cc]
    xo,yo=1-x,1-y
    def copies(p,src):
        here=at(p,x,y,c) if src is None else src
        f=lambda k,a,b,w: remote(a,b,send.at[k,p],recv.at[k,p],w)
        return dict(
            xown=lambda: f(0,here,at(p,x,y,c),mx), yown=lambda: f(1,here,at(p,x,y,c),my), cown=lambda: f(2,here,at(p,x,y,c),s.sibling),
            yfwd=lambda: f(3,at(p,xo,y,c).at[A],at(p,xo,y,c).at[A],my),
            xfwd=lambda: f(4,at(p,x,yo,c).at[B],at(p,x,yo,c).at[B],mx),
            cx=lambda: f(5,at(p,xo,y,c),at(p,xo,y,c),s.sibling), cy=lambda: f(6,at(p,x,yo,c),at(p,x,yo,c),s.sibling),
            ca=lambda: f(7,at(p,xo,yo,c).at[A],at(p,xo,yo,c).at[A],s.sibling),
            cb=lambda: f(8,at(p,xo,yo,c).at[B],at(p,xo,yo,c).at[B],s.sibling))
    def zcopy(p,up,src=None):
        here=at(p,x,y,c) if src is None else src
        return remote(here,at(p,x,y,c),zsend.at[0 if up else 1,p],zrecv.at[p],s.up if up else s.down)
    def arrive(r):
        def act(p,below):
            src=None
            if below is None: src=slab
            else: zcopy(p,below).wait_recv()
            if below is None or below:
                @pl.when(z<planes-1)
                def _(): zcopy(p,True,src).start()
            if below is None or not below:
                @pl.when(z>0)
                def _(): zcopy(p,False,src).start()
            k=copies(p,src)
            k["xown"]().start(); k["yown"]().start(); k["cown"]().start()
        s.ring(r,act)
    def second(r):
        def act(p,below):
            k=copies(p,None)
            k["xown"]().wait_recv(); k["yfwd"]().start(); k["cx"]().start()
            k["yown"]().wait_recv(); k["xfwd"]().start(); k["cy"]().start()
        s.ring(r,act)
    def third(r):
        def act(p,below):
            k=copies(p,None)
            k["yfwd"]().wait_recv(); k["ca"]().start()
            k["xfwd"]().wait_recv(); k["cb"]().start()
        s.ring(r,act)
    def finish(r):
        def act(p,below):
            src=slab if below is None else None
            k=copies(p,src)
            for n in ("cown","cx","cy","ca","cb"): k[n]().wait_recv()
            for n in k: k[n]().wait_send()
            if below is None or below:
                @pl.when(z<planes-1)
                def _(): zcopy(p,True,src).wait_send()
            if below is None or not below:
                @pl.when(z>0)
                def _(): zcopy(p,False,src).wait_send()
        s.ring(r,act)
    for r in range(planes+2):
        if r<planes: arrive(r)
        if 1<=r<=planes: second(r-1)
        if r>=2: third(r-2)
    for r in range(planes): finish(r)
    own.wait()

def gather_all(master,vector,dp,collective):
    rows=master.shape[0]*BLK+16; planes=dp//2; half=rows//2//16*16
    dma=pltpu.SemaphoreType.DMA
    return pl.pallas_call(partial(gather_kernel,planes,half),
        out_shape=jax.ShapeDtypeStruct((dp,4,rows,BLK),jnp.bfloat16),
        in_specs=[VMEM_SPEC,VMEM_SPEC],out_specs=ANY_SPEC,
        scratch_shapes=[pltpu.VMEM((rows,BLK),jnp.bfloat16),dma((9,planes)),dma((9,planes)),dma((2,planes)),dma((planes,)),dma],
        compiler_params=pltpu.CompilerParams(collective_id=collective,has_side_effects=True),name="gather_all")(master,vector[None,:])

def reduce_kernel(planes,half,slots,blocks,inner,extra,out,g,rc,acc,ya,xb,xa,yb,own,zin,send,recv,zsend,zrecv):
    s=Spot(planes); rows=g.shape[2]; z,x,y,c,mp=s.z,s.x,s.y,s.c,s.mp
    A,B=pl.ds(0,half),pl.ds(half,rows-half)
    mx,my=s.across_x,s.across_y
    xo,yo,co=1-x,1-y,1-c
    s.greet()
    f32=lambda v: v.astype(jnp.float32)
    def core(p,xx,yy):
        k=xx*2+yy
        return remote(g.at[p*2+xx,yy*2+co],rc.at[p*4+k],send.at[k,p],recv.at[k,p],s.sibling)
    def toya(p,xx): return remote(acc.at[p*4+xx*2+yo,A],ya.at[p*2+xx],send.at[4+xx,p],recv.at[4+xx,p],my)
    def toxb(p,yy): return remote(acc.at[p*4+xo*2+yy,B],xb.at[p*2+yy],send.at[6+yy,p],recv.at[6+yy,p],mx)
    def toxa(p): return remote(ya.at[p*2+xo],xa.at[p],send.at[8,p],recv.at[8,p],mx)
    def toyb(p): return remote(xb.at[p*2+yo],yb.at[p],send.at[9,p],recv.at[9,p],my)
    def toz(p,up): return remote(own.at[p],zin.at[0 if up else 1,p],zsend.at[p],zrecv.at[0 if up else 1,p],s.up if up else s.down)
    def pack(p,parity):
        for xx in (0,1):
            d=p*2+xx
            def one(k,_):
                block=inner[d*slots+k]
                for yy in (0,1):
                    g[d,yy*2+parity,pl.ds(pl.multiple_of(k*BLK,BLK),BLK),:]=blocks[block,yy*2+parity]
                return 0
            lax.fori_loop(0,slots,one,0)
            for yy in (0,1): g[d,yy*2+parity,slots*BLK:,:]=extra[d,yy*2+parity]
    def start(p,_):
        pack(p,co)
        for xx in (0,1):
            for yy in (0,1): core(p,xx,yy).start()
    def first(p,_):
        pack(p,c)
        for xx in (0,1):
            for yy in (0,1):
                core(p,xx,yy).wait_recv()
                acc[p*4+xx*2+yy]=(f32(g[p*2+xx,yy*2+c])+f32(rc[p*4+xx*2+yy])).astype(acc.dtype)
        for e in (0,1): toya(p,e).start(); toxb(p,e).start()
    def second(p,_):
        for e in (0,1):
            toya(p,e).wait_recv()
            ya[p*2+e]=(f32(acc[p*4+e*2+y,A])+f32(ya[p*2+e])).astype(ya.dtype)
        toxa(p).start()
        for e in (0,1):
            toxb(p,e).wait_recv()
            xb[p*2+e]=(f32(acc[p*4+x*2+e,B])+f32(xb[p*2+e])).astype(xb.dtype)
        toyb(p).start()
    def third(p,below):
        toxa(p).wait_recv()
        av=f32(ya[p*2+x])+f32(xa[p])
        toyb(p).wait_recv()
        bv=f32(xb[p*2+y])+f32(yb[p])
        if below is None:
            out[A]=av; out[B]=bv
            @pl.when(z>0)
            def _():
                toz(p,True).wait_recv()
                out[...]=out[...]+f32(zin[0,p])
            @pl.when(z<planes-1)
            def _():
                toz(p,False).wait_recv()
                out[...]=out[...]+f32(zin[1,p])
            return
        own[p,A]=av.astype(own.dtype); own[p,B]=bv.astype(own.dtype)
        up=not below
        has=(z>0) if up else (z<planes-1)
        @pl.when(has)
        def _():
            toz(p,up).wait_recv()
            own[p,A]=(av+f32(zin[0 if up else 1,p,A])).astype(own.dtype)
            own[p,B]=(bv+f32(zin[0 if up else 1,p,B])).astype(own.dtype)
        toz(p,up).start()
    def finish(p,below):
        for xx in (0,1):
            for yy in (0,1): core(p,xx,yy).wait_send()
        for e in (0,1): toya(p,e).wait_send(); toxb(p,e).wait_send()
        toxa(p).wait_send(); toyb(p).wait_send()
        if below is not None: toz(p,not below).wait_send()
    order=list(range(planes-1,-1,-1))
    for r in order: s.ring(r,start)
    n=len(order)
    for i in range(n+2):
        if i<n: s.ring(order[i],first)
        if 0<=i-1<n: s.ring(order[i-1],second)
        if 0<=i-2<n: s.ring(order[i-2],third)
    for r in order: s.ring(r,finish)

def reduce_all(g,extra,inner,slots,collective):
    dp=extra.shape[0]; rows,cols=slots*BLK+extra.shape[2],g.shape[3]; planes=dp//2; half=rows//2//16*16
    dma=pltpu.SemaphoreType.DMA; bf=lambda *sh: pltpu.VMEM(sh+(cols,),g.dtype)
    return pl.pallas_call(partial(reduce_kernel,planes,half,slots),
        out_shape=jax.ShapeDtypeStruct((rows,cols),jnp.float32),in_specs=[VMEM_SPEC,pl.BlockSpec(memory_space=pltpu.SMEM),VMEM_SPEC],out_specs=VMEM_SPEC,
        scratch_shapes=[bf(dp,4,rows),bf(planes*4,rows),bf(planes*4,rows),bf(planes*2,half),bf(planes*2,rows-half),bf(planes,half),bf(planes,rows-half),
            bf(planes,rows),bf(2,planes,rows),dma((10,planes)),dma((10,planes)),dma((planes,)),dma((2,planes))],
        compiler_params=pltpu.CompilerParams(collective_id=collective,has_side_effects=True,vmem_limit_bytes=56<<20),name="reduce_all")(g,inner,extra)
D=512; HD=128; FF=1024; LAYERS=2; BLK=128; HEADS=4
NORM_EPSILON=1e-5; MASK_VALUE=-1e30
f32=jnp.float32; bf16=jnp.bfloat16
SMEM_SPEC=pl.BlockSpec(memory_space=pltpu.SMEM)
SCALE=HD**-0.5; LOG2E=math.log2(math.e)
ROOT=math.sqrt(2/math.pi)

def nn(a,b): return lax.dot_general(a,b,(((1,),(0,)),((),())),preferred_element_type=f32)
def nt(a,b): return lax.dot_general(a,b,(((1,),(1,)),((),())),preferred_element_type=f32)
def tn(a,b): return lax.dot_general(a,b,(((0,),(0,)),((),())),preferred_element_type=f32)

def normed(r):
    center=r-jnp.mean(r,axis=-1,keepdims=True)
    rho=lax.rsqrt(jnp.mean(center*center,axis=-1,keepdims=True)+NORM_EPSILON)
    return center*rho,rho
def norm_back(dy,xhat,rho,gain):
    inner=dy*gain
    return rho*(inner-jnp.mean(inner,axis=-1,keepdims=True)-xhat*jnp.mean(inner*xhat,axis=-1,keepdims=True))
def gelu(v): return 0.5*v*(1+jnp.tanh(ROOT*(v+0.044715*v*v*v)))
def gelu_both(v):
    sq=v*v
    t=jnp.tanh(ROOT*v*(1+0.044715*sq))
    half=0.5*(1+t)
    return v*half,half+0.5*v*(1-t*t)*(ROOT*(1+3*0.044715*sq))
def colsum(v): return jnp.sum(v,axis=0,keepdims=True)

COLS_TILE=(3,4,2,4)
FIRST_BLOCK=(0,12,16,24)
LAYER_BLOCKS=32
CH=160
KB=320
FS=FF//HEADS

def rows_at(i,n): return pl.ds(pl.multiple_of(i*n,n),n)

class Weights:
    def __init__(self,refs): self.q,self.kv,self.out,self.up,self.down=refs
    def fill(self,layer,owners,wallv):
        base=layer*LAYER_BLOCKS
        def tiles(b):
            slot=owners[b]
            return [wallv[slot,j] for j in range(HEADS)]
        def by_row(r,_):
            rows=rows_at(r,BLK)
            for c in range(3):
                for j,v in enumerate(tiles(base+r*3+c)):
                    if c==0: self.q[rows,j*BLK:(j+1)*BLK]=v
                    else: self.kv[rows,j*2*BLK+(c-1)*BLK:j*2*BLK+c*BLK]=v
            for c in range(2):
                for j,v in enumerate(tiles(base+FIRST_BLOCK[2]+r*2+c)): self.up[rows,j*FS+c*BLK:j*FS+(c+1)*BLK]=v
            return 0
        lax.fori_loop(0,D//BLK,by_row,0)
        for c in range(4):
            for j,v in enumerate(tiles(base+FIRST_BLOCK[1]+c)): self.out[j*BLK:(j+1)*BLK,c*BLK:(c+1)*BLK]=v
            for r in range(2):
                for j,v in enumerate(tiles(base+FIRST_BLOCK[3]+r*4+c)): self.down[j*FS+r*BLK:j*FS+(r+1)*BLK,c*BLK:(c+1)*BLK]=v

def key_of(j): return slice(j*2*HD,j*2*HD+HD)
def value_of(j): return slice(j*2*HD+HD,(j+1)*2*HD)

def project(w,h_full,KV,rows): KV[rows,:]=nn(h_full[rows,:],w.kv[...]).astype(bf16)

def queries(w,h_full,start,q):
    def one(i,_):
        q[rows_at(i,CH),:]=nn(h_full[pl.ds(pl.multiple_of(start+i*CH,CH),CH),:],w.q[...]).astype(bf16)
        return 0
    lax.fori_loop(0,q.shape[0]//CH,one,0)

def forward(w,gains,own_rows,KV,q,heads,lse,bias,hidden,r1,r2,emit):
    keys=KV.shape[0]; chunks=q.shape[0]//CH
    lane=lax.broadcasted_iota(jnp.int32,(CH,BLK),1)
    def attend(i,_):
        rows=rows_at(i,CH)
        stats=jnp.zeros((CH,BLK),f32)
        scores=lambda j: nt(q[rows,j*HD:(j+1)*HD],KV[:,key_of(j)])
        s=scores(0)
        for j in range(HEADS):
            later=scores(j+1) if j+1<HEADS else None
            s=s+bias[rows,:].astype(f32)
            peak=jnp.max(s,axis=1,keepdims=True)
            p=jnp.exp2((s-peak)*(SCALE*LOG2E))
            total=jnp.sum(p,axis=1,keepdims=True)
            o=nn(p.astype(bf16),KV[:,value_of(j)])/total
            heads[rows,j*HD:(j+1)*HD]=o.astype(bf16)
            stats=jnp.where(lane==j,peak*(SCALE*LOG2E)+jnp.log2(total),stats)
            s=later
        lse[rows,:]=stats
        return 0
    lax.fori_loop(0,chunks,attend,0)
    for i in range(chunks):
        rows=pl.ds(i*CH,CH)
        a=own_rows(i)+nn(heads[rows,:],w.out[...])
        r1[rows,:]=a
        first=normed(a)[0]*gains[0:1,:]+gains[1:2,:]
        hid=nn(first.astype(bf16),w.up[...])
        hidden[rows,:]=hid
        b=first+nn(gelu(hid).astype(bf16),w.down[...])
        r2[rows,:]=b
        emit(i,normed(b)[0]*gains[2:3,:]+gains[3:4,:])

def backward(w,gains,start,h_full,upper,KV,q,heads,lse,biasT,hidden,r1,r2,
        dm,act,dhid,first,datt,dheads,delta,grad,dq,dqa,dhp,vec,put,exchange):
    share=q.shape[0]; keys=KV.shape[0]; chunks=share//CH
    lane=lax.broadcasted_iota(jnp.int32,(CH,BLK),1)
    def part(i,carry):
        rows=rows_at(i,CH)
        dy=upper(i)
        xhat,rho=normed(r2[rows,:])
        g2,s2=colsum(dy*xhat),colsum(dy)
        sg=norm_back(dy,xhat,rho,gains[2:3,:])
        dmb=sg.astype(bf16); dm[rows,:]=dmb
        a,slope=gelu_both(hidden[rows,:])
        act[rows,:]=a.astype(bf16)
        dh=(nt(dmb,w.down[...])*slope).astype(bf16)
        dhid[rows,:]=dh
        fu=sg+nt(dh,w.up[...])
        xhat,rho=normed(r1[rows,:])
        first[rows,:]=(xhat*gains[0:1,:]+gains[1:2,:]).astype(bf16)
        g1,s1=colsum(fu*xhat),colsum(fu)
        f=norm_back(fu,xhat,rho,gains[0:1,:])
        grad[rows,:]=f
        fb=f.astype(bf16); datt[rows,:]=fb
        dhe=nt(fb,w.out[...]).astype(bf16)
        dheads[rows,:]=dhe
        prod=dhe.astype(f32)*heads[rows,:].astype(f32)
        stats=jnp.zeros((CH,BLK),f32)
        for j in range(HEADS):
            stats=jnp.where(lane==j,jnp.sum(prod[:,j*HD:(j+1)*HD],axis=1,keepdims=True),stats)
        delta[rows,:]=stats
        return tuple(c+v for c,v in zip(carry,(g1,s1,g2,s2)))
    zero=jnp.zeros((1,D),f32)
    for k,v in enumerate(lax.fori_loop(0,chunks,part,(zero,)*4)): vec(k,v)
    lseT=jnp.transpose(lse[...]); deltaT=jnp.transpose(delta[...])
    dqa[...]=jnp.zeros(dqa.shape,f32)
    def keyblock(kb,_):
        rows=rows_at(kb,KB)
        head=lambda j: slice(j*HD,(j+1)*HD)
        both=lambda j: (nt(KV[rows,key_of(j)],q[:,head(j)]),nt(KV[rows,value_of(j)],dheads[:,head(j)]))
        now=both(0)
        for j in range(HEADS):
            later=both(j+1) if j+1<HEADS else None
            s,dp=now
            p=jnp.exp2((s+biasT[rows,:].astype(f32))*(SCALE*LOG2E)-lseT[j:j+1,:])
            ds=(p*(dp-deltaT[j:j+1,:])).astype(bf16)
            dqa[head(j),:]+=tn(KV[rows,key_of(j)],ds)
            dv=nn(p.astype(bf16),dheads[:,head(j)])
            dk=nn(ds,q[:,head(j)])*SCALE
            KV[rows,key_of(j)]=dk.astype(bf16)
            KV[rows,value_of(j)]=dv.astype(bf16)
            now=later
        dhp[rows,:]=nt(KV[rows,:],w.kv[...]).astype(bf16)
        for sub in range(KB//CH): exchange.send(kb*(KB//CH)+sub)
        @pl.when(kb>0)
        def _():
            for sub in range(KB//CH): exchange.turn((kb-1)*(KB//CH)+sub)
        return 0
    lax.fori_loop(0,keys//KB,keyblock,0)
    dq[...]=(jnp.transpose(dqa[...])*SCALE).astype(bf16)
    def own(i,_):
        rows=rows_at(i,CH)
        grad[rows,:]=grad[rows,:]+nt(dq[rows,:],w.q[...])
        return 0
    lax.fori_loop(0,chunks,own,0)
    def tiles(value,place):
        value=value.astype(bf16)
        for r in range(value.shape[0]//BLK):
            for c in range(value.shape[1]//BLK):
                put(*place(r,c),value[r*BLK:(r+1)*BLK,c*BLK:(c+1)*BLK])
    tiles(tn(act[...],dm[...]),lambda r,c: (FIRST_BLOCK[3]+r%2*4+c,r//2))
    for sub in range(KB//CH): exchange.turn(keys//CH-KB//CH+sub)
    tiles(tn(first[...],dhid[...]),lambda r,c: (FIRST_BLOCK[2]+r*2+c%2,c//2))
    tiles(tn(heads[...],datt[...]),lambda r,c: (FIRST_BLOCK[1]+c,r))
    tiles(tn(h_full[pl.ds(pl.multiple_of(start,CH),share),:],dq[...]),lambda r,c: (r*3,c))
    tiles(tn(h_full[:keys,:],KV[...]),lambda r,c: (r*3+1+c%2,c//2))
    exchange.finish()

class Exchange:
    def __init__(self,s,terms,grad,rc,acc,ry,send,recv,count):
        self.s,self.terms,self.grad,self.rc,self.acc,self.ry,self.count=s,terms,grad,rc,acc,ry,count
        self.n=send.shape[1]
        at=lambda k,i: rows_at(k*self.n+i,CH)
        self.at=at
        co=1-s.c
        self.a=lambda i: remote(terms.at[at((1-s.y)*2+co,i)],rc.at[0,rows_at(i,CH)],send.at[0,i],recv.at[0,i],s.sibling)
        self.b=lambda i: remote(terms.at[at(s.y*2+co,i)],rc.at[1,rows_at(i,CH)],send.at[1,i],recv.at[1,i],s.sibling)
        self.o=lambda i: remote(acc.at[rows_at(i,CH)],ry.at[rows_at(i,CH)],send.at[2,i],recv.at[2,i],s.across_y)
    def owner(self,b):
        o=b//self.n
        return o//2==self.s.y,o%2==self.s.c,b%self.n
    def send(self,b):
        y,c,i=self.owner(b)
        @pl.when(jnp.logical_not(c)&jnp.logical_not(y))
        def _(): self.a(i).start()
        @pl.when(jnp.logical_not(c)&y)
        def _(): self.b(i).start()
    def turn(self,b):
        y,c,i=self.owner(b)
        @pl.when(c&jnp.logical_not(y))
        def _():
            self.a(i).wait_recv()
            rows=rows_at(i,CH)
            self.acc[rows,:]=(self.terms[rows_at(b,CH),:].astype(f32)+self.rc[0,rows,:].astype(f32)).astype(bf16)
            self.o(i).start()
    def finish(self):
        s=self.s
        for i in range(self.n):
            rows=pl.ds(i*CH,CH)
            @pl.when(s.mp*self.n+i<self.count)
            def _():
                self.b(i).wait_recv()
                t=self.grad[rows]+(self.terms[self.at(s.mp,i)].astype(f32)+self.rc[1,rows].astype(f32))
                self.o(i).wait_recv()
                self.grad[rows]=t+self.ry[rows].astype(f32)
        for i in range(self.n):
            @pl.when(((1-s.y)*2+1-s.c)*self.n+i<self.count)
            def _(): self.a(i).wait_send()
            @pl.when((s.y*2+1-s.c)*self.n+i<self.count)
            def _(): self.b(i).wait_send()
            @pl.when(((1-s.y)*2+s.c)*self.n+i<self.count)
            def _(): self.o(i).wait_send()

def layers_kernel(slots,owners,sizes,tokens,cot,wall,qline, layer_out,tokens_grad,g,extra,
        more,gains,vec,wallv,tok,h2,cotv,KV1,KV2,q1,q2,heads1,heads2,lse1,lse2,hid1,hid2,ra1,ra2,rb1,rb2,bias,biasT,
        dm,act,dhid,first,datt,dheads,delta,dq,dqa,dhp,rc,acc,ry,wa,wb,wc,wd,we,xa,xb,xc,xd,xe,lsem,ssend,srecv,tsend,trecv):
    s=Spot(1); mp=s.mp; share=q1.shape[0]; keys=KV1.shape[0]; chunks=share//CH
    start=mp*share
    def bring(k,_):
        pltpu.make_async_copy(wall.at[k//slots,:,rows_at(k%slots,BLK),:],wallv.at[k],lsem.at[1]).start()
        return 0
    lax.fori_loop(0,wallv.shape[0],bring,0)
    loads=[pltpu.make_async_copy(tokens,tok,lsem.at[0]),pltpu.make_async_copy(wallv,wallv,lsem.at[1]),
           pltpu.make_async_copy(cot.at[pl.ds(pl.multiple_of(start,CH),share)],cotv,lsem.at[2])]
    loads.append(pltpu.make_async_copy(wall.at[:,:,pl.ds(slots*BLK,wall.shape[2]-slots*BLK),:],more,lsem.at[5]))
    for c in (0,2,3): loads[c].start()
    bar=pltpu.get_barrier_semaphore()
    for who in (s.across_y,s.sibling): pl.semaphore_signal(bar,inc=1,device_id=who,device_id_type=MESH)
    ends=[]; total=jnp.int32(0)
    for k in range(sizes.shape[1]):
        total=total+sizes[0,k]; ends.append(total)
    def hood(index):
        h=jnp.zeros(index.shape,jnp.int32)
        for e in ends: h=h+(index>=e).astype(jnp.int32)
        return h
    def own_hood(index,queries):
        row=start+index
        return jnp.where(row<keys,hood(row),queries)
    key_line=hood(lax.broadcasted_iota(jnp.int32,(1,keys),1))
    row_line=own_hood(lax.broadcasted_iota(jnp.int32,(1,share),1),qline[...])
    column=jnp.transpose(jnp.broadcast_to(row_line.astype(f32),(8,share)))[:,0:1].astype(jnp.int32)
    def mask(i):
        rows=pl.ds(i*CH,CH)
        col=column[i*CH:(i+1)*CH,:]
        bias[rows,:]=jnp.where(col==key_line,0.0,MASK_VALUE).astype(bf16)
    for i in range(chunks): mask(i)
    def maskT(i,_):
        rows=rows_at(i,KB)
        col=hood(lax.broadcasted_iota(jnp.int32,(KB,1),0)+i*KB)
        biasT[rows,:]=jnp.where(col==row_line,0.0,MASK_VALUE).astype(bf16)
        return 0
    lax.fori_loop(0,keys//KB,maskT,0)
    w1,w2=Weights((wa,wb,wc,wd,we)),Weights((xa,xb,xc,xd,xe))
    loads[1].wait()
    w1.fill(0,owners,wallv)
    loads[0].wait()
    pl.semaphore_wait(bar,2)
    at=lambda k,i: pl.ds(pl.multiple_of(k*share+i*CH,CH),CH)
    far=s.across_y[1]
    over=lambda i: remote(h2.at[at(mp,i)],h2.at[at(mp,i)],ssend.at[0,i],srecv.at[0,i],s.across_y)
    near=lambda i: remote(h2.at[at(mp,i)],h2.at[at(mp,i)],ssend.at[1,i],srecv.at[1,i],s.sibling)
    on=lambda i: remote(h2.at[at(far,i)],h2.at[at(far,i)],ssend.at[2,i],srecv.at[2,i],s.sibling)
    loads[3].wait()
    n=LAYERS*4*D//(more.shape[0]*HEADS)
    for e in range(more.shape[0]*HEADS):
        pair=more[e//HEADS,e%HEADS].astype(f32)
        where=e*n
        gains[where//D:where//D+1,where%D:where%D+n]=(pair[0:1]+pair[1:2])[:,:n]
    g1,g2=gains[0:4],gains[4:8]
    def emit1(i,v):
        layer_out[pl.ds(i*CH,CH),:]=v
        h2[at(mp,i),:]=v.astype(bf16)
        over(i).start(); near(i).start()
    def every(kb,_):
        project(w1,tok,KV1,rows_at(kb,KB))
        return 0
    lax.fori_loop(0,keys//KB,every,0)
    queries(w1,tok,start,q1)
    forward(w1,g1,lambda i: tok[at(mp,i),:].astype(f32),KV1,q1,heads1,lse1,bias,hid1,ra1,rb1,emit1)
    w2.fill(1,owners,wallv)
    def arrived(k,i):
        @pl.when(k*chunks+i<keys//CH)
        def _(): project(w2,h2,KV2,at(k,i))
    for i in range(chunks): arrived(mp,i)
    queries(w2,h2,start,q2)
    for i in range(chunks):
        near(i).wait_recv(); arrived(s.sibling[1],i)
    for i in range(chunks):
        over(i).wait_recv(); on(i).start(); arrived(far,i)
    for i in range(chunks):
        on(i).wait_recv(); arrived(s.y_sibling,i)
    def emit2(i,v): layer_out[pl.ds(i*CH,CH),:]=v
    forward(w2,g2,lambda i: layer_out[pl.ds(i*CH,CH),:],KV2,q2,heads2,lse2,bias,hid2,ra2,rb2,emit2)
    for i in range(chunks):
        for k in (over,near,on): k(i).wait_send()
    def put(layer):
        def store(b,j,v):
            b=b+layer*LAYER_BLOCKS
            wallv[b,j]=v
        return store
    def keep(layer):
        def store(k,v): vec[layer*4+k:layer*4+k+1,:]=v
        return store
    loads[2].wait()
    half=wallv.shape[0]//2
    flush=[pltpu.make_async_copy(wallv.at[pl.ds(k*half,half)],g.at[pl.ds(k*half,half)],lsem.at[3+k]) for k in range(2)]
    backward(w2,g2,start,h2,lambda i: cotv[rows_at(i,CH),:].astype(f32),KV2,q2,heads2,lse2,biasT,hid2,ra2,rb2,
        dm,act,dhid,first,datt,dheads,delta,tokens_grad,dq,dqa,dhp,keep(1),put(1),Exchange(s,dhp,tokens_grad,rc.at[0],acc,ry.at[0],tsend.at[0],trecv.at[0],keys//CH))
    flush[1].start()
    backward(w1,g1,start,tok,lambda i: tokens_grad[rows_at(i,CH),:],KV1,q1,heads1,lse1,biasT,hid1,ra1,rb1,
        dm,act,dhid,first,datt,dheads,delta,tokens_grad,dq,dqa,dhp,keep(0),put(0),Exchange(s,dhp,tokens_grad,rc.at[1],acc,ry.at[1],tsend.at[1],trecv.at[1],keys//CH))
    flush[0].start()
    top=lax.broadcasted_iota(jnp.int32,(16,BLK),0)==0
    for e in range(more.shape[0]*HEADS):
        where=e*n
        row=vec[where//D:where//D+1,where%D:where%D+n]
        if n<BLK: row=jnp.concatenate([row,jnp.zeros((1,BLK-n),f32)],axis=1)
        extra[e//HEADS,e%HEADS]=jnp.where(top,row,0.0).astype(bf16)
    flush[1].wait(); flush[0].wait()

def run_layers(owners,sizes,tokens,cot,wall,qline,keys,slots,collective):
    rows=tokens.shape[0]; share=rows//HEADS; chunks=share//CH
    v=pltpu.VMEM; dma=pltpu.SemaphoreType.DMA; V_=VMEM_SPEC
    two=lambda shape,t: [v(shape,t)]*2
    weights=[v((D,D),bf16),v((D,HEADS*2*HD),bf16),v((D,D),bf16),v((D,FF),bf16),v((FF,D),bf16)]
    blocks=(LAYERS*LAYER_BLOCKS,HEADS,BLK,BLK)
    tail=(wall.shape[0],HEADS,wall.shape[2]-slots*BLK,BLK)
    scratch=[v(tail,bf16),v((LAYERS*4,D),f32),v((LAYERS*4,D),f32),v(blocks,bf16),v((rows,D),bf16),v((rows,D),bf16),v((share,D),bf16)]
    scratch+=two((keys,HEADS*2*HD),bf16)+two((share,D),bf16)+two((share,D),bf16)+two((share,BLK),f32)+two((share,FF),f32)+two((share,D),f32)+two((share,D),f32)
    scratch+=[v((share,keys),bf16),v((keys,share),bf16)]
    scratch+=[v((share,D),bf16),v((share,FF),bf16),v((share,FF),bf16),v((share,D),bf16),v((share,D),bf16),v((share,D),bf16),v((share,BLK),f32),v((share,D),bf16),v((D,share),f32)]
    scratch+=[v((rows,D),bf16),v((2,2,share,D),bf16),v((share,D),bf16),v((2,share,D),bf16)]+weights+weights
    scratch+=[dma((6,)),dma((3,chunks)),dma((3,chunks)),dma((2,3,chunks)),dma((2,3,chunks))]
    shape=jax.ShapeDtypeStruct
    return pl.pallas_call(partial(layers_kernel,slots),
        out_shape=[shape((share,D),f32),shape((share,D),f32),shape(blocks,bf16),shape(tail,bf16)],
        in_specs=[SMEM_SPEC,SMEM_SPEC,ANY_SPEC,ANY_SPEC,ANY_SPEC,V_],out_specs=[V_,V_,ANY_SPEC,V_],scratch_shapes=scratch,
        compiler_params=pltpu.CompilerParams(collective_id=collective,has_side_effects=True,vmem_limit_bytes=60<<20),name="layers")(
        owners,sizes,tokens,cot,wall,qline)
BLK=128; STEP=10
BETA_ONE=0.9; BETA_TWO=0.95; BETA_STATS=0.95; RATE_MATRIX=0.12; DECAY_WEIGHT=0.01; ADAM_EPSILON=1e-8

def split(x):
    hi=x.astype(jnp.bfloat16)
    return hi,(x-hi.astype(jnp.float32)).astype(jnp.bfloat16)
def dot3(a,b,ca,cb):
    dims=(((ca,),(cb,)),((),()))
    ah,al=a; bh,bl=b
    d=lambda x,y: lax.dot_general(x,y,dims,preferred_element_type=jnp.float32)
    return d(ah,bh)+(d(ah,bl)+d(al,bh))
def dotf(a,b,ca,cb):
    return lax.dot_general(a,b,(((ca,),(cb,)),((),())),preferred_element_type=jnp.float32,precision=lax.Precision.HIGHEST)

def in_groups(count,step,body):
    step=math.gcd(count,step)
    def run(i,_):
        for k in range(step): body(i*step+k)
        return 0
    lax.fori_loop(0,count//step,run,0)

PANEL=32
def soap_kernel(slots,g_ref,m_ref,v_ref,l_ref,r_ref,ql_ref,qr_ref,w_ref,vm_ref,vs_ref,vw_ref, mo,vo,lo,ro,qlo,qro,wo,vmo,vso,vwo, x_ref, a_ref, b_ref):
    width=vm_ref.shape[1]
    vmo[...],vso[...],vwo[...]=adam_vector(g_ref[slots*BLK:slots*BLK+1,:width],vm_ref[...],vs_ref[...],vw_ref[...])
    def first(i):
        g=g_ref[pl.ds(pl.multiple_of(i*BLK,BLK),BLK),:]; ql=split(ql_ref[i]); qr=split(qr_ref[i])
        gs=split(g)
        m=BETA_ONE*m_ref[i]+(1-BETA_ONE)*g
        mo[i]=m
        def turn(v):
            return dot3(split(dot3(ql,v,0,0)),qr,1,0)
        tg=turn(gs)
        v=BETA_TWO*v_ref[i]+(1-BETA_TWO)*tg*tg
        vo[i]=v
        d=turn(split(m))/(1-BETA_ONE**STEP)/(jnp.sqrt(v/(1-BETA_TWO**STEP))+ADAM_EPSILON)
        u=dot3(split(dot3(ql,split(d),1,0)),qr,1,1)
        w=w_ref[i]
        wo[i]=w-RATE_MATRIX*(u+DECAY_WEIGHT*w)
        ln=BETA_STATS*l_ref[i]+(1-BETA_STATS)*dot3(gs,gs,1,1)
        rn=BETA_STATS*r_ref[i]+(1-BETA_STATS)*dot3(gs,gs,0,0)
        lo[i]=ln; ro[i]=rn
        al=dotf(ln,ql_ref[i],1,0); ar=dotf(rn,qr_ref[i],1,0)
        a_ref[2*i]=al; a_ref[2*i+1]=ar
        x_ref[2*i]=dotf(al,al,0,0); x_ref[2*i+1]=dotf(ar,ar,0,0)
    in_groups(slots,4,first)
    n=2*slots
    lane=lax.broadcasted_iota(jnp.int32,(8,BLK),1)
    sub=lax.broadcasted_iota(jnp.int32,(8,BLK),0)
    for p in range(BLK//8):
        end=(p*8//PANEL+1)*PANEL//8
        def step(kk,_):
            k=p*8+kk
            idx=jnp.full((8,BLK),k,jnp.int32)
            atk=lane==k
            below=sub>kk
            done=(lane<=k)|(lane>=end*8)
            rows=[jnp.broadcast_to(x_ref[m,pl.ds(k,1),:],(8,BLK)) for m in range(n)]
            rinv=[1.0/jnp.take_along_axis(row,idx,axis=1) for row in rows]
            scaled=[jnp.where(atk,1.0,row)*ri for row,ri in zip(rows,rinv)]
            for m in range(n):
                b_ref[m,pl.ds(k%PANEL,1),:]=jnp.where(done,scaled[m],0.0)[0:1,:]
                for t in range(p,end):
                    v=x_ref[m,t*8:(t+1)*8,:]
                    f=jnp.take_along_axis(v,idx,axis=1)
                    new=jnp.where(atk,0.0,v)-f*scaled[m]
                    if t==p: new=jnp.where(below,new,v)
                    x_ref[m,t*8:(t+1)*8,:]=new
            return 0
        lax.fori_loop(0,8,step,0)
        if (p+1)*8%PANEL==0 and p<BLK//8-1:
            lo_,hi_=(p+1)*8-PANEL,(p+1)*8
            keep=lax.broadcasted_iota(jnp.int32,(BLK-hi_,BLK),1)
            keep=(keep<lo_)|(keep>=hi_)
            def trail(m):
                u=dotf(x_ref[m,lo_:hi_,:],b_ref[m],0,0)
                x_ref[m,hi_:,:]=jnp.where(keep,x_ref[m,hi_:,:],0.0)-u[hi_:,:]
            in_groups(n,8,trail)
    r=lax.broadcasted_iota(jnp.int32,(BLK,BLK),0); c=lax.broadcasted_iota(jnp.int32,(BLK,BLK),1)
    def last(i):
        for s,out in ((0,qlo),(1,qro)):
            x=x_ref[2*i+s]
            piv=jnp.sum(jnp.where(r==c,x,0.0),axis=1,keepdims=True)
            inv=jnp.where(r==c,1.0,jnp.where(r>c,x,0.0))*lax.rsqrt(piv)
            out[i]=dotf(a_ref[2*i+s],inv,1,1)
    in_groups(slots,4,last)

def soap(g,m,v,l,r,ql,qr,w,vm,vs,vw):
    slots=m.shape[0]
    sh=jax.ShapeDtypeStruct((slots,BLK,BLK),jnp.float32); line=jax.ShapeDtypeStruct((1,vm.shape[0]),jnp.float32)
    space=pl.BlockSpec(memory_space=pltpu.VMEM)
    out=pl.pallas_call(partial(soap_kernel,slots),out_shape=[sh]*7+[line]*3,in_specs=[space]*11,out_specs=[space]*10,
        scratch_shapes=[pltpu.VMEM((2*slots,BLK,BLK),jnp.float32)]*2+[pltpu.VMEM((2*slots,PANEL,BLK),jnp.float32)],
        compiler_params=pltpu.CompilerParams(vmem_limit_bytes=48<<20),name="soap")(g,m,v,l,r,ql,qr,w,vm[None],vs[None],vw[None])
    return tuple(out[:7])+tuple(o[0] for o in out[7:])

def inverse(owners):
    index=jnp.arange(owners.shape[0],dtype=jnp.int32)
    return jnp.sum(jnp.where(owners[:,None]==index[None,:],index[:,None],0),axis=0)

def local(tokens,cotangent,context_sizes,query_hoods,owners,master_blocks,first_blocks,second_blocks,left_blocks,right_blocks,
        left_bases,right_bases,vector_master,vector_moment,vector_square):
    dp=lax.axis_size("dp")
    rows=tokens.shape[0]; keys=rows-query_hoods.shape[0]; share=rows//HEADS; slots=master_blocks.shape[0]
    wall=gather_all(master_blocks,vector_master,dp,0)
    hoods=jnp.pad(query_hoods,(share-query_hoods.shape[0],0))
    layer_out,tokens_grad,g,extra=run_layers(owners,context_sizes,tokens,cotangent,wall,hoods[None,:],keys,slots,1)
    total=reduce_all(g,extra,inverse(owners),slots,2)
    return (layer_out,tokens_grad)+soap(total,first_blocks,second_blocks,left_blocks,right_blocks,left_bases,right_bases,master_blocks,
        vector_moment,vector_square,vector_master)


def solution(mesh):
    return jax.shard_map(
        local,
        mesh=mesh,
        in_specs=(
            P("dp", None),
            P("dp", None),
            P("dp", None),
            P("dp"),
            P(),
            P("dp", "mp", None),
            P("dp", "mp", None),
            P("dp", "mp", None),
            P("dp", "mp", None),
            P("dp", "mp", None),
            P("dp", "mp", None),
            P("dp", "mp", None),
            P(("dp", "mp")),
            P(("dp", "mp")),
            P(("dp", "mp")),
        ),
        out_specs=(
            P(("dp", "mp"), None),
            P(("dp", "mp"), None),
            P("dp", "mp", None),
            P("dp", "mp", None),
            P("dp", "mp", None),
            P("dp", "mp", None),
            P("dp", "mp", None),
            P("dp", "mp", None),
            P("dp", "mp", None),
            P(("dp", "mp")),
            P(("dp", "mp")),
            P(("dp", "mp")),
        ),
        check_vma=False,
    )
```

```python
import math
from functools import partial

import jax
import jax.numpy as jnp
from jax import lax
from jax.experimental import pallas as pl
from jax.experimental.pallas import tpu as pltpu
from jax.sharding import PartitionSpec as P

RATE_VECTOR = 0.6
def adam_vector(grad, first, second, weight):
    first_new = BETA_ONE * first + (1.0 - BETA_ONE) * grad
    second_new = BETA_TWO * second + (1.0 - BETA_TWO) * grad * grad
    weight_new = weight - RATE_VECTOR * (first_new / (1.0 - BETA_ONE**STEP)) / (
        jnp.sqrt(second_new / (1.0 - BETA_TWO**STEP)) + ADAM_EPSILON
    )
    return (first_new, second_new, weight_new)


MESH=pl.DeviceIdType.MESH
BLK=128
VMEM_SPEC=pl.BlockSpec(memory_space=pltpu.VMEM)
ANY_SPEC=pl.BlockSpec(memory_space=pl.ANY)

def remote(src,dst,send,recv,device):
    return pltpu.make_async_remote_copy(src_ref=src,dst_ref=dst,send_sem=send,recv_sem=recv,device_id=device,device_id_type=MESH)

class Spot:
    def __init__(self,planes):
        dp,mp=lax.axis_index("dp"),lax.axis_index("mp")
        self.dp,self.mp,self.planes=dp,mp,planes
        self.z,self.x=dp//2,dp%2
        self.y,self.c=mp//2,mp%2
        self.across_x=(dp+1-2*self.x,mp)
        self.across_y=(dp,(mp+2)%4)
        self.sibling=(dp,mp+1-2*self.c)
        self.y_sibling=3-mp
        self.up=(jnp.minimum(dp+2,2*planes-1),mp)
        self.down=(jnp.maximum(dp-2,0),mp)
    def greet(self):
        bar=pltpu.get_barrier_semaphore()
        for who in (self.across_x,self.across_y,self.sibling):
            pl.semaphore_signal(bar,inc=1,device_id=who,device_id_type=MESH)
        @pl.when(self.z<self.planes-1)
        def _(): pl.semaphore_signal(bar,inc=1,device_id=self.up,device_id_type=MESH)
        @pl.when(self.z>0)
        def _(): pl.semaphore_signal(bar,inc=1,device_id=self.down,device_id_type=MESH)
        pl.semaphore_wait(bar,3+jnp.minimum(self.z,1)+jnp.minimum(self.planes-1-self.z,1))
    def ring(self,r,action):
        if r==0:
            action(self.z,None); return
        @pl.when(self.z>=r)
        def _(): action(self.z-r,True)
        @pl.when(self.z+r<self.planes)
        def _(): action(self.z+r,False)

def gather_kernel(planes,half,master,vector,out,slab,send,recv,zsend,zrecv,lsem):
    for k in range(master.shape[0]): slab[k*BLK:(k+1)*BLK,:]=master[k].astype(slab.dtype)
    n=vector.shape[1]
    high=vector[...].astype(slab.dtype).astype(jnp.float32)
    pair=jnp.where(lax.broadcasted_iota(jnp.int32,(16,n),0)==0,high,vector[...]-high)
    if n<BLK: pair=jnp.concatenate([pair,jnp.zeros((16,BLK-n),jnp.float32)],axis=1)
    slab[master.shape[0]*BLK:,:]=pair.astype(slab.dtype)
    s=Spot(planes); rows=slab.shape[0]; z,x,y,c,mp=s.z,s.x,s.y,s.c,s.mp
    A,B=pl.ds(0,half),pl.ds(half,rows-half)
    mx,my=s.across_x,s.across_y
    own=pltpu.make_async_copy(slab,out.at[s.dp,mp],lsem); own.start()
    s.greet()
    def at(p,xx,yy,cc): return out.at[p*2+xx,yy*2+cc]
    xo,yo=1-x,1-y
    def copies(p,src):
        here=at(p,x,y,c) if src is None else src
        f=lambda k,a,b,w: remote(a,b,send.at[k,p],recv.at[k,p],w)
        return dict(
            xown=lambda: f(0,here,at(p,x,y,c),mx), yown=lambda: f(1,here,at(p,x,y,c),my), cown=lambda: f(2,here,at(p,x,y,c),s.sibling),
            yfwd=lambda: f(3,at(p,xo,y,c).at[A],at(p,xo,y,c).at[A],my),
            xfwd=lambda: f(4,at(p,x,yo,c).at[B],at(p,x,yo,c).at[B],mx),
            cx=lambda: f(5,at(p,xo,y,c),at(p,xo,y,c),s.sibling), cy=lambda: f(6,at(p,x,yo,c),at(p,x,yo,c),s.sibling),
            ca=lambda: f(7,at(p,xo,yo,c).at[A],at(p,xo,yo,c).at[A],s.sibling),
            cb=lambda: f(8,at(p,xo,yo,c).at[B],at(p,xo,yo,c).at[B],s.sibling))
    def zcopy(p,up,src=None):
        here=at(p,x,y,c) if src is None else src
        return remote(here,at(p,x,y,c),zsend.at[0 if up else 1,p],zrecv.at[p],s.up if up else s.down)
    def arrive(r):
        def act(p,below):
            src=None
            if below is None: src=slab
            else: zcopy(p,below).wait_recv()
            if below is None or below:
                @pl.when(z<planes-1)
                def _(): zcopy(p,True,src).start()
            if below is None or not below:
                @pl.when(z>0)
                def _(): zcopy(p,False,src).start()
            k=copies(p,src)
            k["xown"]().start(); k["yown"]().start(); k["cown"]().start()
        s.ring(r,act)
    def second(r):
        def act(p,below):
            k=copies(p,None)
            k["xown"]().wait_recv(); k["yfwd"]().start(); k["cx"]().start()
            k["yown"]().wait_recv(); k["xfwd"]().start(); k["cy"]().start()
        s.ring(r,act)
    def third(r):
        def act(p,below):
            k=copies(p,None)
            k["yfwd"]().wait_recv(); k["ca"]().start()
            k["xfwd"]().wait_recv(); k["cb"]().start()
        s.ring(r,act)
    def finish(r):
        def act(p,below):
            src=slab if below is None else None
            k=copies(p,src)
            for n in ("cown","cx","cy","ca","cb"): k[n]().wait_recv()
            for n in k: k[n]().wait_send()
            if below is None or below:
                @pl.when(z<planes-1)
                def _(): zcopy(p,True,src).wait_send()
            if below is None or not below:
                @pl.when(z>0)
                def _(): zcopy(p,False,src).wait_send()
        s.ring(r,act)
    for r in range(planes+2):
        if r<planes: arrive(r)
        if 1<=r<=planes: second(r-1)
        if r>=2: third(r-2)
    for r in range(planes): finish(r)
    own.wait()

def gather_all(master,vector,dp,collective):
    rows=master.shape[0]*BLK+16; planes=dp//2; half=rows//2//16*16
    dma=pltpu.SemaphoreType.DMA
    return pl.pallas_call(partial(gather_kernel,planes,half),
        out_shape=jax.ShapeDtypeStruct((dp,4,rows,BLK),jnp.bfloat16),
        in_specs=[VMEM_SPEC,VMEM_SPEC],out_specs=ANY_SPEC,
        scratch_shapes=[pltpu.VMEM((rows,BLK),jnp.bfloat16),dma((9,planes)),dma((9,planes)),dma((2,planes)),dma((planes,)),dma],
        compiler_params=pltpu.CompilerParams(collective_id=collective,has_side_effects=True),name="gather_all")(master,vector[None,:])

def reduce_kernel(planes,half,slots,source,inner,extra,out,theirs,mine,lsem,g,rc,acc,ya,xb,xa,yb,own,zin,send,recv,zsend,zrecv):
    s=Spot(planes); rows=g.shape[2]; z,x,y,c,mp=s.z,s.x,s.y,s.c,s.mp
    A,B=pl.ds(0,half),pl.ds(half,rows-half)
    mx,my=s.across_x,s.across_y
    xo,yo,co=1-x,1-y,1-c
    bring=lambda held,k,parity: pltpu.make_async_copy(source.at[:,k*2+parity],held.at[:,k],lsem.at[k*2+parity])
    for held,parity in ((theirs,co),(mine,c)):
        for k in (0,1): bring(held,k,parity).start()
    s.greet()
    f32=lambda v: v.astype(jnp.float32)
    def core(p,xx,yy):
        k=xx*2+yy
        return remote(g.at[p*2+xx,yy*2+co],rc.at[p*4+k],send.at[k,p],recv.at[k,p],s.sibling)
    def toya(p,xx): return remote(acc.at[p*4+xx*2+yo,A],ya.at[p*2+xx],send.at[4+xx,p],recv.at[4+xx,p],my)
    def toxb(p,yy): return remote(acc.at[p*4+xo*2+yy,B],xb.at[p*2+yy],send.at[6+yy,p],recv.at[6+yy,p],mx)
    def toxa(p): return remote(ya.at[p*2+xo],xa.at[p],send.at[8,p],recv.at[8,p],mx)
    def toyb(p): return remote(xb.at[p*2+yo],yb.at[p],send.at[9,p],recv.at[9,p],my)
    def toz(p,up): return remote(own.at[p],zin.at[0 if up else 1,p],zsend.at[p],zrecv.at[0 if up else 1,p],s.up if up else s.down)
    def pack(p,parity,held):
        for xx in (0,1):
            d=p*2+xx
            def one(k,_):
                block=inner[d*slots+k]
                for yy in (0,1):
                    g[d,yy*2+parity,pl.ds(pl.multiple_of(k*BLK,BLK),BLK),:]=held[block,yy]
                return 0
            lax.fori_loop(0,slots,one,0)
            for yy in (0,1): g[d,yy*2+parity,slots*BLK:,:]=extra[d,yy*2+parity]
    def start(p,_):
        pack(p,co,theirs)
        for xx in (0,1):
            for yy in (0,1): core(p,xx,yy).start()
    def first(p,_):
        pack(p,c,mine)
        for xx in (0,1):
            for yy in (0,1):
                core(p,xx,yy).wait_recv()
                acc[p*4+xx*2+yy]=(f32(g[p*2+xx,yy*2+c])+f32(rc[p*4+xx*2+yy])).astype(acc.dtype)
        for e in (0,1): toya(p,e).start(); toxb(p,e).start()
    def second(p,_):
        for e in (0,1):
            toya(p,e).wait_recv()
            ya[p*2+e]=(f32(acc[p*4+e*2+y,A])+f32(ya[p*2+e])).astype(ya.dtype)
        toxa(p).start()
        for e in (0,1):
            toxb(p,e).wait_recv()
            xb[p*2+e]=(f32(acc[p*4+x*2+e,B])+f32(xb[p*2+e])).astype(xb.dtype)
        toyb(p).start()
    def third(p,below):
        toxa(p).wait_recv()
        av=f32(ya[p*2+x])+f32(xa[p])
        toyb(p).wait_recv()
        bv=f32(xb[p*2+y])+f32(yb[p])
        if below is None:
            out[A]=av; out[B]=bv
            @pl.when(z>0)
            def _():
                toz(p,True).wait_recv()
                out[...]=out[...]+f32(zin[0,p])
            @pl.when(z<planes-1)
            def _():
                toz(p,False).wait_recv()
                out[...]=out[...]+f32(zin[1,p])
            return
        own[p,A]=av.astype(own.dtype); own[p,B]=bv.astype(own.dtype)
        up=not below
        has=(z>0) if up else (z<planes-1)
        @pl.when(has)
        def _():
            toz(p,up).wait_recv()
            own[p,A]=(av+f32(zin[0 if up else 1,p,A])).astype(own.dtype)
            own[p,B]=(bv+f32(zin[0 if up else 1,p,B])).astype(own.dtype)
        toz(p,up).start()
    def finish(p,below):
        for xx in (0,1):
            for yy in (0,1): core(p,xx,yy).wait_send()
        for e in (0,1): toya(p,e).wait_send(); toxb(p,e).wait_send()
        toxa(p).wait_send(); toyb(p).wait_send()
        if below is not None: toz(p,not below).wait_send()
    order=list(range(planes-1,-1,-1))
    for k in (0,1): bring(theirs,k,co).wait()
    for r in order: s.ring(r,start)
    for k in (0,1): bring(mine,k,c).wait()
    n=len(order)
    for i in range(n+2):
        if i<n: s.ring(order[i],first)
        if 0<=i-1<n: s.ring(order[i-1],second)
        if 0<=i-2<n: s.ring(order[i-2],third)
    for r in order: s.ring(r,finish)

def reduce_all(g,extra,inner,slots,collective):
    dp=extra.shape[0]; rows,cols=slots*BLK+extra.shape[2],g.shape[3]; planes=dp//2; half=rows//2//16*16
    dma=pltpu.SemaphoreType.DMA; bf=lambda *sh: pltpu.VMEM(sh+(cols,),g.dtype)
    return pl.pallas_call(partial(reduce_kernel,planes,half,slots),
        out_shape=jax.ShapeDtypeStruct((rows,cols),jnp.float32),in_specs=[ANY_SPEC,pl.BlockSpec(memory_space=pltpu.SMEM),VMEM_SPEC],out_specs=VMEM_SPEC,
        scratch_shapes=[pltpu.VMEM((g.shape[0],2)+g.shape[2:],g.dtype)]*2+[dma((4,)),bf(dp,4,rows),bf(planes*4,rows),bf(planes*4,rows),bf(planes*2,half),bf(planes*2,rows-half),bf(planes,half),bf(planes,rows-half),
            bf(planes,rows),bf(2,planes,rows),dma((10,planes)),dma((10,planes)),dma((planes,)),dma((2,planes))],
        compiler_params=pltpu.CompilerParams(collective_id=collective,has_side_effects=True,vmem_limit_bytes=56<<20),name="reduce_all")(g,inner,extra)
D=512; HD=128; FF=1024; LAYERS=2; BLK=128; HEADS=4
NORM_EPSILON=1e-5; MASK_VALUE=-1e30
f32=jnp.float32; bf16=jnp.bfloat16
SMEM_SPEC=pl.BlockSpec(memory_space=pltpu.SMEM)
SCALE=HD**-0.5; LOG2E=math.log2(math.e)
ROOT=math.sqrt(2/math.pi)

def nn(a,b): return lax.dot_general(a,b,(((1,),(0,)),((),())),preferred_element_type=f32)
def nt(a,b): return lax.dot_general(a,b,(((1,),(1,)),((),())),preferred_element_type=f32)
def tn(a,b): return lax.dot_general(a,b,(((0,),(0,)),((),())),preferred_element_type=f32)

def normed(r):
    center=r-jnp.mean(r,axis=-1,keepdims=True)
    rho=lax.rsqrt(jnp.mean(center*center,axis=-1,keepdims=True)+NORM_EPSILON)
    return center*rho,rho
def norm_back(dy,xhat,rho,gain):
    inner=dy*gain
    return rho*(inner-jnp.mean(inner,axis=-1,keepdims=True)-xhat*jnp.mean(inner*xhat,axis=-1,keepdims=True))
def gelu(v): return 0.5*v*(1+jnp.tanh(ROOT*(v+0.044715*v*v*v)))
def gelu_both(v):
    sq=v*v
    t=jnp.tanh(ROOT*v*(1+0.044715*sq))
    half=0.5*(1+t)
    return v*half,half+0.5*v*(1-t*t)*(ROOT*(1+3*0.044715*sq))
def colsum(v): return jnp.sum(v,axis=0,keepdims=True)

COLS_TILE=(3,4,2,4)
FIRST_BLOCK=(0,12,16,24)
LAYER_BLOCKS=32
CH=160
KB=320
FS=FF//HEADS

def rows_at(i,n): return pl.ds(pl.multiple_of(i*n,n),n)

class Weights:
    def __init__(self,refs): self.q,self.kv,self.out,self.up,self.down=refs
    def fill(self,layer,owners,wallv):
        base=layer*LAYER_BLOCKS
        def tiles(b):
            slot=owners[b]
            return [wallv[slot,j] for j in range(HEADS)]
        def by_row(r,_):
            rows=rows_at(r,BLK)
            for c in range(3):
                for j,v in enumerate(tiles(base+r*3+c)):
                    if c==0: self.q[rows,j*BLK:(j+1)*BLK]=v
                    else: self.kv[rows,j*2*BLK+(c-1)*BLK:j*2*BLK+c*BLK]=v
            for c in range(2):
                for j,v in enumerate(tiles(base+FIRST_BLOCK[2]+r*2+c)): self.up[rows,j*FS+c*BLK:j*FS+(c+1)*BLK]=v
            return 0
        lax.fori_loop(0,D//BLK,by_row,0)
        for c in range(4):
            for j,v in enumerate(tiles(base+FIRST_BLOCK[1]+c)): self.out[j*BLK:(j+1)*BLK,c*BLK:(c+1)*BLK]=v
            for r in range(2):
                for j,v in enumerate(tiles(base+FIRST_BLOCK[3]+r*4+c)): self.down[j*FS+r*BLK:j*FS+(r+1)*BLK,c*BLK:(c+1)*BLK]=v

def key_of(j): return slice(j*2*HD,j*2*HD+HD)
def value_of(j): return slice(j*2*HD+HD,(j+1)*2*HD)

def project(w,h_full,KV,rows): KV[rows,:]=nn(h_full[rows,:],w.kv[...]).astype(bf16)

def queries(w,h_full,start,q):
    def one(i,_):
        q[rows_at(i,CH),:]=nn(h_full[pl.ds(pl.multiple_of(start+i*CH,CH),CH),:],w.q[...]).astype(bf16)
        return 0
    lax.fori_loop(0,q.shape[0]//CH,one,0)

def forward(w,gains,own_rows,KV,q,heads,lse,bias,hidden,r1,r2,emit):
    keys=KV.shape[0]; chunks=q.shape[0]//CH
    lane=lax.broadcasted_iota(jnp.int32,(CH,BLK),1)
    def attend(i,_):
        rows=rows_at(i,CH)
        stats=jnp.zeros((CH,BLK),f32)
        scores=lambda j: nt(q[rows,j*HD:(j+1)*HD],KV[:,key_of(j)])
        s=scores(0)
        for j in range(HEADS):
            later=scores(j+1) if j+1<HEADS else None
            s=s+bias[rows,:].astype(f32)
            peak=jnp.max(s,axis=1,keepdims=True)
            p=jnp.exp2((s-peak)*(SCALE*LOG2E))
            total=jnp.sum(p,axis=1,keepdims=True)
            o=nn(p.astype(bf16),KV[:,value_of(j)])/total
            heads[rows,j*HD:(j+1)*HD]=o.astype(bf16)
            stats=jnp.where(lane==j,peak*(SCALE*LOG2E)+jnp.log2(total),stats)
            s=later
        lse[rows,:]=stats
        a=own_rows(i)+nn(heads[rows,:],w.out[...])
        r1[rows,:]=a
        first=normed(a)[0]*gains[0:1,:]+gains[1:2,:]
        hid=nn(first.astype(bf16),w.up[...])
        hidden[rows,:]=hid
        b=first+nn(gelu(hid).astype(bf16),w.down[...])
        r2[rows,:]=b
        emit(i,normed(b)[0]*gains[2:3,:]+gains[3:4,:])
        return 0
    lax.fori_loop(0,chunks,attend,0)

def backward(w,gains,start,h_full,upper,KV,q,heads,lse,biasT,hidden,r1,r2,
        dm,act,dhid,first,datt,dheads,delta,grad,dq,dqa,dhp,vec,put,exchange):
    share=q.shape[0]; keys=KV.shape[0]; chunks=share//CH
    lane=lax.broadcasted_iota(jnp.int32,(CH,BLK),1)
    def part(i,carry):
        rows=rows_at(i,CH)
        dy=upper(i)
        xhat,rho=normed(r2[rows,:])
        g2,s2=colsum(dy*xhat),colsum(dy)
        sg=norm_back(dy,xhat,rho,gains[2:3,:])
        dmb=sg.astype(bf16); dm[rows,:]=dmb
        a,slope=gelu_both(hidden[rows,:])
        act[rows,:]=a.astype(bf16)
        dh=(nt(dmb,w.down[...])*slope).astype(bf16)
        dhid[rows,:]=dh
        fu=sg+nt(dh,w.up[...])
        xhat,rho=normed(r1[rows,:])
        first[rows,:]=(xhat*gains[0:1,:]+gains[1:2,:]).astype(bf16)
        g1,s1=colsum(fu*xhat),colsum(fu)
        f=norm_back(fu,xhat,rho,gains[0:1,:])
        grad[rows,:]=f
        fb=f.astype(bf16); datt[rows,:]=fb
        dhe=nt(fb,w.out[...]).astype(bf16)
        dheads[rows,:]=dhe
        prod=dhe.astype(f32)*heads[rows,:].astype(f32)
        stats=jnp.zeros((CH,BLK),f32)
        for j in range(HEADS):
            stats=jnp.where(lane==j,jnp.sum(prod[:,j*HD:(j+1)*HD],axis=1,keepdims=True),stats)
        delta[rows,:]=stats
        return tuple(c+v for c,v in zip(carry,(g1,s1,g2,s2)))
    zero=jnp.zeros((1,D),f32)
    for k,v in enumerate(lax.fori_loop(0,chunks,part,(zero,)*4)): vec(k,v)
    lseT=jnp.transpose(lse[...]); deltaT=jnp.transpose(delta[...])
    dqa[...]=jnp.zeros(dqa.shape,f32)
    blocks=keys//KB
    def nth(t): return lax.rem(exchange.lead+t,blocks)
    def keyblock(t,_):
        kb=nth(t)
        rows=rows_at(kb,KB)
        head=lambda j: slice(j*HD,(j+1)*HD)
        both=lambda j: (nt(KV[rows,key_of(j)],q[:,head(j)]),nt(KV[rows,value_of(j)],dheads[:,head(j)]))
        now=both(0)
        for j in range(HEADS):
            later=both(j+1) if j+1<HEADS else None
            s,dp=now
            p=jnp.exp2((s+biasT[rows,:].astype(f32))*(SCALE*LOG2E)-lseT[j:j+1,:])
            ds=(p*(dp-deltaT[j:j+1,:])).astype(bf16)
            dqa[head(j),:]+=tn(KV[rows,key_of(j)],ds)
            dv=nn(p.astype(bf16),dheads[:,head(j)])
            dk=nn(ds,q[:,head(j)])*SCALE
            KV[rows,key_of(j)]=dk.astype(bf16)
            KV[rows,value_of(j)]=dv.astype(bf16)
            now=later
        dhp[rows,:]=nt(KV[rows,:],w.kv[...]).astype(bf16)
        for sub in range(KB//CH): exchange.send(kb*(KB//CH)+sub)
        @pl.when(t>0)
        def _():
            for sub in range(KB//CH): exchange.turn(nth(t-1)*(KB//CH)+sub)
        return 0
    lax.fori_loop(0,blocks,keyblock,0)
    dq[...]=(jnp.transpose(dqa[...])*SCALE).astype(bf16)
    def own(i,_):
        rows=rows_at(i,CH)
        grad[rows,:]=grad[rows,:]+nt(dq[rows,:],w.q[...])
        return 0
    lax.fori_loop(0,chunks,own,0)
    def tiles(value,place):
        value=value.astype(bf16)
        for r in range(value.shape[0]//BLK):
            for c in range(value.shape[1]//BLK):
                put(*place(r,c),value[r*BLK:(r+1)*BLK,c*BLK:(c+1)*BLK])
    tiles(tn(act[...],dm[...]),lambda r,c: (FIRST_BLOCK[3]+r%2*4+c,r//2))
    for sub in range(KB//CH): exchange.turn(nth(blocks-1)*(KB//CH)+sub)
    tiles(tn(first[...],dhid[...]),lambda r,c: (FIRST_BLOCK[2]+r*2+c%2,c//2))
    tiles(tn(heads[...],datt[...]),lambda r,c: (FIRST_BLOCK[1]+c,r))
    tiles(tn(h_full[pl.ds(pl.multiple_of(start,CH),share),:],dq[...]),lambda r,c: (r*3,c))
    tiles(tn(h_full[:keys,:],KV[...]),lambda r,c: (r*3+1+c%2,c//2))
    exchange.finish()

class Exchange:
    def __init__(self,s,terms,grad,rc,acc,ry,send,recv,count):
        self.s,self.terms,self.grad,self.rc,self.acc,self.ry,self.count=s,terms,grad,rc,acc,ry,count
        self.n=send.shape[1]
        self.lead=jnp.where(s.y==0,2*self.n//(KB//CH),0)
        at=lambda k,i: rows_at(k*self.n+i,CH)
        self.at=at
        co=1-s.c
        self.a=lambda i: remote(terms.at[at((1-s.y)*2+co,i)],rc.at[0,rows_at(i,CH)],send.at[0,i],recv.at[0,i],s.sibling)
        self.b=lambda i: remote(terms.at[at(s.y*2+co,i)],rc.at[1,rows_at(i,CH)],send.at[1,i],recv.at[1,i],s.sibling)
        self.o=lambda i: remote(acc.at[rows_at(i,CH)],ry.at[rows_at(i,CH)],send.at[2,i],recv.at[2,i],s.across_y)
    def owner(self,b):
        o=b//self.n
        return o//2==self.s.y,o%2==self.s.c,b%self.n
    def send(self,b):
        y,c,i=self.owner(b)
        @pl.when(jnp.logical_not(c)&jnp.logical_not(y))
        def _(): self.a(i).start()
        @pl.when(jnp.logical_not(c)&y)
        def _(): self.b(i).start()
    def turn(self,b):
        y,c,i=self.owner(b)
        @pl.when(c&jnp.logical_not(y))
        def _():
            self.a(i).wait_recv()
            rows=rows_at(i,CH)
            self.acc[rows,:]=(self.terms[rows_at(b,CH),:].astype(f32)+self.rc[0,rows,:].astype(f32)).astype(bf16)
            self.o(i).start()
    def finish(self):
        s=self.s
        for i in range(self.n):
            rows=pl.ds(i*CH,CH)
            @pl.when(s.mp*self.n+i<self.count)
            def _():
                self.b(i).wait_recv()
                t=self.grad[rows]+(self.terms[self.at(s.mp,i)].astype(f32)+self.rc[1,rows].astype(f32))
                self.o(i).wait_recv()
                self.grad[rows]=t+self.ry[rows].astype(f32)
        for i in range(self.n):
            @pl.when(((1-s.y)*2+1-s.c)*self.n+i<self.count)
            def _(): self.a(i).wait_send()
            @pl.when((s.y*2+1-s.c)*self.n+i<self.count)
            def _(): self.b(i).wait_send()
            @pl.when(((1-s.y)*2+s.c)*self.n+i<self.count)
            def _(): self.o(i).wait_send()

def layers_kernel(slots,owners,sizes,tokens,cot,wall,qline, layer_out,tokens_grad,g,extra,
        more,gains,vec,wallv,tok,h2,cotv,KV1,KV2,q1,q2,heads1,heads2,lse1,lse2,hid1,hid2,ra1,ra2,rb1,rb2,bias,biasT,
        dm,act,dhid,first,datt,dheads,delta,dq,dqa,dhp,rc,acc,ry,wa,wb,wc,wd,we,xa,xb,xc,xd,xe,lsem,ssend,srecv,tsend,trecv):
    s=Spot(1); mp=s.mp; share=q1.shape[0]; keys=KV1.shape[0]; chunks=share//CH
    start=mp*share
    def bring(k,_):
        pltpu.make_async_copy(wall.at[k//slots,:,rows_at(k%slots,BLK),:],wallv.at[k],lsem.at[1]).start()
        return 0
    lax.fori_loop(0,wallv.shape[0],bring,0)
    loads=[pltpu.make_async_copy(tokens,tok,lsem.at[0]),pltpu.make_async_copy(wallv,wallv,lsem.at[1]),
           pltpu.make_async_copy(cot.at[pl.ds(pl.multiple_of(start,CH),share)],cotv,lsem.at[2])]
    loads.append(pltpu.make_async_copy(wall.at[:,:,pl.ds(slots*BLK,wall.shape[2]-slots*BLK),:],more,lsem.at[5]))
    for c in (0,2,3): loads[c].start()
    bar=pltpu.get_barrier_semaphore()
    for who in (s.across_y,s.sibling): pl.semaphore_signal(bar,inc=1,device_id=who,device_id_type=MESH)
    ends=[]; total=jnp.int32(0)
    for k in range(sizes.shape[1]):
        total=total+sizes[0,k]; ends.append(total)
    def hood(index):
        h=jnp.zeros(index.shape,jnp.int32)
        for e in ends: h=h+(index>=e).astype(jnp.int32)
        return h
    def own_hood(index,queries):
        row=start+index
        return jnp.where(row<keys,hood(row),queries)
    key_line=hood(lax.broadcasted_iota(jnp.int32,(1,keys),1))
    row_line=own_hood(lax.broadcasted_iota(jnp.int32,(1,share),1),qline[...])
    column=jnp.transpose(jnp.broadcast_to(row_line.astype(f32),(8,share)))[:,0:1].astype(jnp.int32)
    def mask(i):
        rows=pl.ds(i*CH,CH)
        col=column[i*CH:(i+1)*CH,:]
        bias[rows,:]=jnp.where(col==key_line,0.0,MASK_VALUE).astype(bf16)
    for i in range(chunks): mask(i)
    def maskT(i,_):
        rows=rows_at(i,KB)
        col=hood(lax.broadcasted_iota(jnp.int32,(KB,1),0)+i*KB)
        biasT[rows,:]=jnp.where(col==row_line,0.0,MASK_VALUE).astype(bf16)
        return 0
    lax.fori_loop(0,keys//KB,maskT,0)
    w1,w2=Weights((wa,wb,wc,wd,we)),Weights((xa,xb,xc,xd,xe))
    loads[1].wait()
    w1.fill(0,owners,wallv)
    loads[0].wait()
    pl.semaphore_wait(bar,2)
    at=lambda k,i: pl.ds(pl.multiple_of(k*share+i*CH,CH),CH)
    far=s.across_y[1]
    over=lambda i: remote(h2.at[at(mp,i)],h2.at[at(mp,i)],ssend.at[0,i],srecv.at[0,i],s.across_y)
    near=lambda i: remote(h2.at[at(mp,i)],h2.at[at(mp,i)],ssend.at[1,i],srecv.at[1,i],s.sibling)
    on=lambda i: remote(h2.at[at(far,i)],h2.at[at(far,i)],ssend.at[2,i],srecv.at[2,i],s.sibling)
    loads[3].wait()
    n=LAYERS*4*D//(more.shape[0]*HEADS)
    for e in range(more.shape[0]*HEADS):
        pair=more[e//HEADS,e%HEADS].astype(f32)
        where=e*n
        gains[where//D:where//D+1,where%D:where%D+n]=(pair[0:1]+pair[1:2])[:,:n]
    g1,g2=gains[0:4],gains[4:8]
    def emit1(i,v):
        layer_out[rows_at(i,CH),:]=v
        h2[at(mp,i),:]=v.astype(bf16)
        over(i).start(); near(i).start()
    def every(kb,_):
        project(w1,tok,KV1,rows_at(kb,KB))
        return 0
    lax.fori_loop(0,keys//KB,every,0)
    queries(w1,tok,start,q1)
    forward(w1,g1,lambda i: tok[at(mp,i),:].astype(f32),KV1,q1,heads1,lse1,bias,hid1,ra1,rb1,emit1)
    w2.fill(1,owners,wallv)
    def arrived(k,i):
        @pl.when(k*chunks+i<keys//CH)
        def _(): project(w2,h2,KV2,at(k,i))
    for i in range(chunks): arrived(mp,i)
    queries(w2,h2,start,q2)
    for i in range(chunks):
        near(i).wait_recv(); arrived(s.sibling[1],i)
    for i in range(chunks):
        over(i).wait_recv(); on(i).start(); arrived(far,i)
    for i in range(chunks):
        on(i).wait_recv(); arrived(s.y_sibling,i)
    def emit2(i,v): layer_out[rows_at(i,CH),:]=v
    forward(w2,g2,lambda i: layer_out[rows_at(i,CH),:],KV2,q2,heads2,lse2,bias,hid2,ra2,rb2,emit2)
    for i in range(chunks):
        for k in (over,near,on): k(i).wait_send()
    def put(layer):
        def store(b,j,v):
            b=b+layer*LAYER_BLOCKS
            wallv[b,j]=v
        return store
    def keep(layer):
        def store(k,v): vec[layer*4+k:layer*4+k+1,:]=v
        return store
    loads[2].wait()
    half=wallv.shape[0]//2
    flush=[pltpu.make_async_copy(wallv.at[pl.ds(k*half,half)],g.at[pl.ds(k*half,half)],lsem.at[3+k]) for k in range(2)]
    backward(w2,g2,start,h2,lambda i: cotv[rows_at(i,CH),:].astype(f32),KV2,q2,heads2,lse2,biasT,hid2,ra2,rb2,
        dm,act,dhid,first,datt,dheads,delta,tokens_grad,dq,dqa,dhp,keep(1),put(1),Exchange(s,dhp,tokens_grad,rc.at[0],acc,ry.at[0],tsend.at[0],trecv.at[0],keys//CH))
    flush[1].start()
    backward(w1,g1,start,tok,lambda i: tokens_grad[rows_at(i,CH),:],KV1,q1,heads1,lse1,biasT,hid1,ra1,rb1,
        dm,act,dhid,first,datt,dheads,delta,tokens_grad,dq,dqa,dhp,keep(0),put(0),Exchange(s,dhp,tokens_grad,rc.at[1],acc,ry.at[1],tsend.at[1],trecv.at[1],keys//CH))
    flush[0].start()
    top=lax.broadcasted_iota(jnp.int32,(16,BLK),0)==0
    for e in range(more.shape[0]*HEADS):
        where=e*n
        row=vec[where//D:where//D+1,where%D:where%D+n]
        if n<BLK: row=jnp.concatenate([row,jnp.zeros((1,BLK-n),f32)],axis=1)
        extra[e//HEADS,e%HEADS]=jnp.where(top,row,0.0).astype(bf16)
    flush[1].wait(); flush[0].wait()

def run_layers(owners,sizes,tokens,cot,wall,qline,keys,slots,collective):
    rows=tokens.shape[0]; share=rows//HEADS; chunks=share//CH
    v=pltpu.VMEM; dma=pltpu.SemaphoreType.DMA; V_=VMEM_SPEC
    two=lambda shape,t: [v(shape,t)]*2
    weights=[v((D,D),bf16),v((D,HEADS*2*HD),bf16),v((D,D),bf16),v((D,FF),bf16),v((FF,D),bf16)]
    blocks=(LAYERS*LAYER_BLOCKS,HEADS,BLK,BLK)
    tail=(wall.shape[0],HEADS,wall.shape[2]-slots*BLK,BLK)
    scratch=[v(tail,bf16),v((LAYERS*4,D),f32),v((LAYERS*4,D),f32),v(blocks,bf16),v((rows,D),bf16),v((rows,D),bf16),v((share,D),bf16)]
    scratch+=two((keys,HEADS*2*HD),bf16)+two((share,D),bf16)+two((share,D),bf16)+two((share,BLK),f32)+two((share,FF),f32)+two((share,D),f32)+two((share,D),f32)
    scratch+=[v((share,keys),bf16),v((keys,share),bf16)]
    scratch+=[v((share,D),bf16),v((share,FF),bf16),v((share,FF),bf16),v((share,D),bf16),v((share,D),bf16),v((share,D),bf16),v((share,BLK),f32),v((share,D),bf16),v((D,share),f32)]
    scratch+=[v((rows,D),bf16),v((2,2,share,D),bf16),v((share,D),bf16),v((2,share,D),bf16)]+weights+weights
    scratch+=[dma((6,)),dma((3,chunks)),dma((3,chunks)),dma((2,3,chunks)),dma((2,3,chunks))]
    shape=jax.ShapeDtypeStruct
    return pl.pallas_call(partial(layers_kernel,slots),
        out_shape=[shape((share,D),f32),shape((share,D),f32),shape(blocks,bf16),shape(tail,bf16)],
        in_specs=[SMEM_SPEC,SMEM_SPEC,ANY_SPEC,ANY_SPEC,ANY_SPEC,V_],out_specs=[V_,V_,ANY_SPEC,V_],scratch_shapes=scratch,
        compiler_params=pltpu.CompilerParams(collective_id=collective,has_side_effects=True,vmem_limit_bytes=60<<20),name="layers")(
        owners,sizes,tokens,cot,wall,qline)
BLK=128; STEP=10
BETA_ONE=0.9; BETA_TWO=0.95; BETA_STATS=0.95; RATE_MATRIX=0.12; DECAY_WEIGHT=0.01; ADAM_EPSILON=1e-8

def split(x):
    hi=x.astype(jnp.bfloat16)
    return hi,(x-hi.astype(jnp.float32)).astype(jnp.bfloat16)
def dot3(a,b,ca,cb):
    dims=(((ca,),(cb,)),((),()))
    ah,al=a; bh,bl=b
    d=lambda x,y: lax.dot_general(x,y,dims,preferred_element_type=jnp.float32)
    return d(ah,bh)+(d(ah,bl)+d(al,bh))
def dotf(a,b,ca,cb):
    return lax.dot_general(a,b,(((ca,),(cb,)),((),())),preferred_element_type=jnp.float32,precision=lax.Precision.HIGHEST)

def in_groups(count,step,body):
    step=math.gcd(count,step)
    def run(i,_):
        for k in range(step): body(i*step+k)
        return 0
    lax.fori_loop(0,count//step,run,0)

PANEL=32
def soap_kernel(slots,g_ref,m_ref,v_ref,l_ref,r_ref,ql_ref,qr_ref,w_ref,vm_ref,vs_ref,vw_ref, mo,vo,lo,ro,qlo,qro,wo,vmo,vso,vwo, x_ref, a_ref, b_ref):
    width=vm_ref.shape[1]
    vmo[...],vso[...],vwo[...]=adam_vector(g_ref[slots*BLK:slots*BLK+1,:width],vm_ref[...],vs_ref[...],vw_ref[...])
    def first(i):
        g=g_ref[pl.ds(pl.multiple_of(i*BLK,BLK),BLK),:]; ql=split(ql_ref[i]); qr=split(qr_ref[i])
        gs=split(g)
        m=BETA_ONE*m_ref[i]+(1-BETA_ONE)*g
        mo[i]=m
        def turn(v):
            return dot3(split(dot3(ql,v,0,0)),qr,1,0)
        tg=turn(gs)
        v=BETA_TWO*v_ref[i]+(1-BETA_TWO)*tg*tg
        vo[i]=v
        d=turn(split(m))/(1-BETA_ONE**STEP)/(jnp.sqrt(v/(1-BETA_TWO**STEP))+ADAM_EPSILON)
        u=dot3(split(dot3(ql,split(d),1,0)),qr,1,1)
        w=w_ref[i]
        wo[i]=w-RATE_MATRIX*(u+DECAY_WEIGHT*w)
        ln=BETA_STATS*l_ref[i]+(1-BETA_STATS)*dot3(gs,gs,1,1)
        rn=BETA_STATS*r_ref[i]+(1-BETA_STATS)*dot3(gs,gs,0,0)
        lo[i]=ln; ro[i]=rn
        al=dotf(ln,ql_ref[i],1,0); ar=dotf(rn,qr_ref[i],1,0)
        a_ref[2*i]=al; a_ref[2*i+1]=ar
        x_ref[2*i]=dotf(al,al,0,0); x_ref[2*i+1]=dotf(ar,ar,0,0)
    in_groups(slots,4,first)
    n=2*slots
    lane=lax.broadcasted_iota(jnp.int32,(8,BLK),1)
    sub=lax.broadcasted_iota(jnp.int32,(8,BLK),0)
    for p in range(BLK//8):
        end=(p*8//PANEL+1)*PANEL//8
        def step(kk,_):
            k=p*8+kk
            idx=jnp.full((8,BLK),k,jnp.int32)
            atk=lane==k
            below=sub>kk
            done=(lane<=k)|(lane>=end*8)
            rows=[jnp.broadcast_to(x_ref[m,pl.ds(k,1),:],(8,BLK)) for m in range(n)]
            rinv=[1.0/jnp.take_along_axis(row,idx,axis=1) for row in rows]
            scaled=[jnp.where(atk,1.0,row)*ri for row,ri in zip(rows,rinv)]
            for m in range(n):
                b_ref[m,pl.ds(k%PANEL,1),:]=jnp.where(done,scaled[m],0.0)[0:1,:]
                for t in range(p,end):
                    v=x_ref[m,t*8:(t+1)*8,:]
                    f=jnp.take_along_axis(v,idx,axis=1)
                    new=jnp.where(atk,0.0,v)-f*scaled[m]
                    if t==p: new=jnp.where(below,new,v)
                    x_ref[m,t*8:(t+1)*8,:]=new
            return 0
        lax.fori_loop(0,8,step,0)
        if (p+1)*8%PANEL==0 and p<BLK//8-1:
            lo_,hi_=(p+1)*8-PANEL,(p+1)*8
            keep=lax.broadcasted_iota(jnp.int32,(BLK-hi_,BLK),1)
            keep=(keep<lo_)|(keep>=hi_)
            def trail(m):
                u=dotf(x_ref[m,lo_:hi_,:],b_ref[m],0,0)
                x_ref[m,hi_:,:]=jnp.where(keep,x_ref[m,hi_:,:],0.0)-u[hi_:,:]
            in_groups(n,8,trail)
    r=lax.broadcasted_iota(jnp.int32,(BLK,BLK),0); c=lax.broadcasted_iota(jnp.int32,(BLK,BLK),1)
    def last(i):
        for s,out in ((0,qlo),(1,qro)):
            x=x_ref[2*i+s]
            piv=jnp.sum(jnp.where(r==c,x,0.0),axis=1,keepdims=True)
            inv=jnp.where(r==c,1.0,jnp.where(r>c,x,0.0))*lax.rsqrt(piv)
            out[i]=dotf(a_ref[2*i+s],inv,1,1)
    in_groups(slots,4,last)

def soap(g,m,v,l,r,ql,qr,w,vm,vs,vw):
    slots=m.shape[0]
    sh=jax.ShapeDtypeStruct((slots,BLK,BLK),jnp.float32); line=jax.ShapeDtypeStruct((1,vm.shape[0]),jnp.float32)
    space=pl.BlockSpec(memory_space=pltpu.VMEM)
    out=pl.pallas_call(partial(soap_kernel,slots),out_shape=[sh]*7+[line]*3,in_specs=[space]*11,out_specs=[space]*10,
        scratch_shapes=[pltpu.VMEM((2*slots,BLK,BLK),jnp.float32)]*2+[pltpu.VMEM((2*slots,PANEL,BLK),jnp.float32)],
        compiler_params=pltpu.CompilerParams(vmem_limit_bytes=48<<20),name="soap")(g,m,v,l,r,ql,qr,w,vm[None],vs[None],vw[None])
    return tuple(out[:7])+tuple(o[0] for o in out[7:])

def inverse(owners):
    index=jnp.arange(owners.shape[0],dtype=jnp.int32)
    return jnp.sum(jnp.where(owners[:,None]==index[None,:],index[:,None],0),axis=0)

def local(tokens,cotangent,context_sizes,query_hoods,owners,master_blocks,first_blocks,second_blocks,left_blocks,right_blocks,
        left_bases,right_bases,vector_master,vector_moment,vector_square):
    dp=lax.axis_size("dp")
    rows=tokens.shape[0]; keys=rows-query_hoods.shape[0]; share=rows//HEADS; slots=master_blocks.shape[0]
    wall=gather_all(master_blocks,vector_master,dp,0)
    hoods=jnp.pad(query_hoods,(share-query_hoods.shape[0],0))
    layer_out,tokens_grad,g,extra=run_layers(owners,context_sizes,tokens,cotangent,wall,hoods[None,:],keys,slots,1)
    total=reduce_all(g,extra,inverse(owners),slots,2)
    return (layer_out,tokens_grad)+soap(total,first_blocks,second_blocks,left_blocks,right_blocks,left_bases,right_bases,master_blocks,
        vector_moment,vector_square,vector_master)


def solution(mesh):
    return jax.shard_map(
        local,
        mesh=mesh,
        in_specs=(
            P("dp", None),
            P("dp", None),
            P("dp", None),
            P("dp"),
            P(),
            P("dp", "mp", None),
            P("dp", "mp", None),
            P("dp", "mp", None),
            P("dp", "mp", None),
            P("dp", "mp", None),
            P("dp", "mp", None),
            P("dp", "mp", None),
            P(("dp", "mp")),
            P(("dp", "mp")),
            P(("dp", "mp")),
        ),
        out_specs=(
            P(("dp", "mp"), None),
            P(("dp", "mp"), None),
            P("dp", "mp", None),
            P("dp", "mp", None),
            P("dp", "mp", None),
            P("dp", "mp", None),
            P("dp", "mp", None),
            P("dp", "mp", None),
            P("dp", "mp", None),
            P(("dp", "mp")),
            P(("dp", "mp")),
            P(("dp", "mp")),
        ),
        check_vma=False,
    )
```

```python
import math
from functools import partial

import jax
import jax.numpy as jnp
from jax import lax
from jax.experimental import pallas as pl
from jax.experimental.pallas import tpu as pltpu
from jax.sharding import PartitionSpec as P

RATE_VECTOR = 0.6
def adam_vector(grad, first, second, weight):
    first_new = BETA_ONE * first + (1.0 - BETA_ONE) * grad
    second_new = BETA_TWO * second + (1.0 - BETA_TWO) * grad * grad
    weight_new = weight - RATE_VECTOR * (first_new / (1.0 - BETA_ONE**STEP)) / (
        jnp.sqrt(second_new / (1.0 - BETA_TWO**STEP)) + ADAM_EPSILON
    )
    return (first_new, second_new, weight_new)


MESH=pl.DeviceIdType.MESH
BLK=128
VMEM_SPEC=pl.BlockSpec(memory_space=pltpu.VMEM)
ANY_SPEC=pl.BlockSpec(memory_space=pl.ANY)

def remote(src,dst,send,recv,device):
    return pltpu.make_async_remote_copy(src_ref=src,dst_ref=dst,send_sem=send,recv_sem=recv,device_id=device,device_id_type=MESH)

class Spot:
    def __init__(self,planes):
        dp,mp=lax.axis_index("dp"),lax.axis_index("mp")
        self.dp,self.mp,self.planes=dp,mp,planes
        self.z,self.x=dp//2,dp%2
        self.y,self.c=mp//2,mp%2
        self.across_x=(dp+1-2*self.x,mp)
        self.across_y=(dp,(mp+2)%4)
        self.sibling=(dp,mp+1-2*self.c)
        self.y_sibling=3-mp
        self.up=(jnp.minimum(dp+2,2*planes-1),mp)
        self.down=(jnp.maximum(dp-2,0),mp)
    def greet(self):
        bar=pltpu.get_barrier_semaphore()
        for who in (self.across_x,self.across_y,self.sibling):
            pl.semaphore_signal(bar,inc=1,device_id=who,device_id_type=MESH)
        @pl.when(self.z<self.planes-1)
        def _(): pl.semaphore_signal(bar,inc=1,device_id=self.up,device_id_type=MESH)
        @pl.when(self.z>0)
        def _(): pl.semaphore_signal(bar,inc=1,device_id=self.down,device_id_type=MESH)
        pl.semaphore_wait(bar,3+jnp.minimum(self.z,1)+jnp.minimum(self.planes-1-self.z,1))
    def ring(self,r,action):
        if r==0:
            action(self.z,None); return
        @pl.when(self.z>=r)
        def _(): action(self.z-r,True)
        @pl.when(self.z+r<self.planes)
        def _(): action(self.z+r,False)

def gather_kernel(planes,cuts,master,vector,out,slab,send,recv,zsend,zrecv,lsem,csend,crecv,zcsend,zcrecv,ccsend,ccrecv):
    for k in range(master.shape[0]): slab[k*BLK:(k+1)*BLK,:]=master[k].astype(slab.dtype)
    n=vector.shape[1]
    high=vector[...].astype(slab.dtype).astype(jnp.float32)
    pair=jnp.where(lax.broadcasted_iota(jnp.int32,(16,n),0)==0,high,vector[...]-high)
    if n<BLK: pair=jnp.concatenate([pair,jnp.zeros((16,BLK-n),jnp.float32)],axis=1)
    slab[master.shape[0]*BLK:,:]=pair.astype(slab.dtype)
    s=Spot(planes); rows=slab.shape[0]; z,x,y,c,mp=s.z,s.x,s.y,s.c,s.mp
    A,B,AB,C=pl.ds(0,cuts[0]),pl.ds(cuts[0],cuts[1]-cuts[0]),pl.ds(0,cuts[1]),pl.ds(cuts[1],rows-cuts[1])
    mx,my=s.across_x,s.across_y
    own=pltpu.make_async_copy(slab,out.at[s.dp,mp],lsem); own.start()
    s.greet()
    def at(p,xx,yy,cc): return out.at[p*2+xx,yy*2+cc]
    xo,yo=1-x,1-y
    def copies(p,src):
        here=at(p,x,y,c) if src is None else src
        f=lambda k,a,b,w: remote(a,b,send.at[k,p],recv.at[k,p],w)
        return dict(
            xown=lambda: f(0,here.at[AB],at(p,x,y,c).at[AB],mx), yown=lambda: f(1,here.at[AB],at(p,x,y,c).at[AB],my),
            cown=lambda: f(2,here.at[AB],at(p,x,y,c).at[AB],s.sibling),
            yfwd=lambda: f(3,at(p,xo,y,c).at[A],at(p,xo,y,c).at[A],my),
            xfwd=lambda: f(4,at(p,x,yo,c).at[B],at(p,x,yo,c).at[B],mx),
            cx=lambda: f(5,at(p,xo,y,c).at[AB],at(p,xo,y,c).at[AB],s.sibling), cy=lambda: f(6,at(p,x,yo,c).at[AB],at(p,x,yo,c).at[AB],s.sibling),
            ca=lambda: f(7,at(p,xo,yo,c).at[A],at(p,xo,yo,c).at[A],s.sibling),
            cb=lambda: f(8,at(p,xo,yo,c).at[B],at(p,xo,yo,c).at[B],s.sibling))
    def zcopy(p,up,src=None):
        here=at(p,x,y,c) if src is None else src
        return remote(here.at[AB],at(p,x,y,c).at[AB],zsend.at[0 if up else 1,p],zrecv.at[p],s.up if up else s.down)
    def onward(below,action):
        if below is None or below:
            @pl.when(z<planes-1)
            def _(): action(True)
        if below is None or not below:
            @pl.when(z>0)
            def _(): action(False)
    c_x=lambda: remote(slab.at[C],at(z,x,y,c).at[C],csend.at[0],crecv.at[0],mx)
    c_y=lambda: remote(slab.at[C],at(z,x,y,c).at[C],csend.at[1],crecv.at[1],my)
    c_xy=lambda: remote(at(z,xo,y,c).at[C],at(z,xo,y,c).at[C],csend.at[2],crecv.at[2],my)
    both=lambda p,yy: out.at[pl.ds(p*2,2),yy*2+c,C]
    c_z=lambda p,yy,up: remote(both(p,yy),both(p,yy),zcsend.at[0 if up else 1,p,yy],zcrecv.at[p,yy],s.up if up else s.down)
    c_c=lambda p,yy: remote(both(p,yy),both(p,yy),ccsend.at[p,yy],ccrecv.at[p,yy],s.sibling)
    def c_arrive(p,below):
        for yy in (0,1):
            if below is not None: c_z(p,yy,below).wait_recv()
            onward(below,lambda up: c_z(p,yy,up).start())
            c_c(p,yy).start()
    def arrive(r):
        def act(p,below):
            src=None
            if below is None: src=slab
            else: zcopy(p,below).wait_recv()
            onward(below,lambda up: zcopy(p,up,src).start())
            k=copies(p,src)
            k["xown"]().start(); k["yown"]().start(); k["cown"]().start()
        s.ring(r,act)
    def second(r):
        def act(p,below):
            k=copies(p,None)
            k["xown"]().wait_recv(); k["yfwd"]().start(); k["cx"]().start()
            k["yown"]().wait_recv(); k["xfwd"]().start(); k["cy"]().start()
        s.ring(r,act)
    def third(r):
        def act(p,below):
            k=copies(p,None)
            k["yfwd"]().wait_recv(); k["ca"]().start()
            k["xfwd"]().wait_recv(); k["cb"]().start()
        s.ring(r,act)
    def finish(r):
        def act(p,below):
            src=slab if below is None else None
            k=copies(p,src)
            for n in ("cown","cx","cy","ca","cb"): k[n]().wait_recv()
            for n in k: k[n]().wait_send()
            onward(below,lambda up: zcopy(p,up,src).wait_send())
            for yy in (0,1):
                onward(below,lambda up: c_z(p,yy,up).wait_send())
                remote(both(p,yy),out.at[pl.ds(p*2,2),yy*2+1-c,C],ccsend.at[p,yy],ccrecv.at[p,yy],s.sibling).wait_recv()
                c_c(p,yy).wait_send()
        s.ring(r,act)
    c_x().start(); c_y().start()
    for r in range(planes+2):
        if r<planes: arrive(r)
        if r==0:
            c_x().wait_recv(); c_xy().start()
        if r==1:
            c_y().wait_recv(); c_xy().wait_recv(); own.wait()
            c_arrive(z,None)
        if 1<=r<=planes: second(r-1)
        if 2<=r<=planes: s.ring(r-1,c_arrive)
        if r>=2: third(r-2)
    for r in range(planes): finish(r)
    for k in (c_x,c_y,c_xy): k().wait_send()

def gather_all(master,vector,dp,collective):
    rows=master.shape[0]*BLK+16; planes=dp//2
    last=rows-rows//5//16*16; cuts=(last//2//16*16,last)
    dma=pltpu.SemaphoreType.DMA
    return pl.pallas_call(partial(gather_kernel,planes,cuts),
        out_shape=jax.ShapeDtypeStruct((dp,4,rows,BLK),jnp.bfloat16),
        in_specs=[VMEM_SPEC,VMEM_SPEC],out_specs=ANY_SPEC,
        scratch_shapes=[pltpu.VMEM((rows,BLK),jnp.bfloat16),dma((9,planes)),dma((9,planes)),dma((2,planes)),dma((planes,)),dma,
            dma((3,)),dma((3,)),dma((2,planes,2)),dma((planes,2)),dma((planes,2)),dma((planes,2))],
        compiler_params=pltpu.CompilerParams(collective_id=collective,has_side_effects=True),name="gather_all")(master,vector[None,:])

def reduce_kernel(planes,half,slots,source,inner,extra,out,theirs,mine,lsem,g,rc,acc,ya,xb,xa,yb,own,zin,send,recv,zsend,zrecv):
    s=Spot(planes); rows=g.shape[2]; z,x,y,c,mp=s.z,s.x,s.y,s.c,s.mp
    A,B=pl.ds(0,half),pl.ds(half,rows-half)
    mx,my=s.across_x,s.across_y
    xo,yo,co=1-x,1-y,1-c
    bring=lambda held,k,parity: pltpu.make_async_copy(source.at[:,k*2+parity],held.at[:,k],lsem.at[k*2+parity])
    for held,parity in ((theirs,co),(mine,c)):
        for k in (0,1): bring(held,k,parity).start()
    s.greet()
    f32=lambda v: v.astype(jnp.float32)
    def core(p,xx,yy):
        k=xx*2+yy
        return remote(g.at[p*2+xx,yy*2+co],rc.at[p*4+k],send.at[k,p],recv.at[k,p],s.sibling)
    def toya(p,xx): return remote(acc.at[p*4+xx*2+yo,A],ya.at[p*2+xx],send.at[4+xx,p],recv.at[4+xx,p],my)
    def toxb(p,yy): return remote(acc.at[p*4+xo*2+yy,B],xb.at[p*2+yy],send.at[6+yy,p],recv.at[6+yy,p],mx)
    def toxa(p): return remote(ya.at[p*2+xo],xa.at[p],send.at[8,p],recv.at[8,p],mx)
    def toyb(p): return remote(xb.at[p*2+yo],yb.at[p],send.at[9,p],recv.at[9,p],my)
    def toz(p,up): return remote(own.at[p],zin.at[0 if up else 1,p],zsend.at[p],zrecv.at[0 if up else 1,p],s.up if up else s.down)
    def pack(p,parity,held):
        for xx in (0,1):
            d=p*2+xx
            def one(k,_):
                block=inner[d*slots+k]
                for yy in (0,1):
                    g[d,yy*2+parity,pl.ds(pl.multiple_of(k*BLK,BLK),BLK),:]=held[block,yy]
                return 0
            lax.fori_loop(0,slots,one,0)
            for yy in (0,1): g[d,yy*2+parity,slots*BLK:,:]=extra[d,yy*2+parity]
    def start(p,_):
        pack(p,co,theirs)
        for xx in (0,1):
            for yy in (0,1): core(p,xx,yy).start()
    def first(p,_):
        pack(p,c,mine)
        for xx in (0,1):
            for yy in (0,1):
                core(p,xx,yy).wait_recv()
                acc[p*4+xx*2+yy]=(f32(g[p*2+xx,yy*2+c])+f32(rc[p*4+xx*2+yy])).astype(acc.dtype)
        for e in (0,1): toya(p,e).start(); toxb(p,e).start()
    def second(p,_):
        for e in (0,1):
            toya(p,e).wait_recv()
            ya[p*2+e]=(f32(acc[p*4+e*2+y,A])+f32(ya[p*2+e])).astype(ya.dtype)
        toxa(p).start()
        for e in (0,1):
            toxb(p,e).wait_recv()
            xb[p*2+e]=(f32(acc[p*4+x*2+e,B])+f32(xb[p*2+e])).astype(xb.dtype)
        toyb(p).start()
    def third(p,below):
        toxa(p).wait_recv()
        av=f32(ya[p*2+x])+f32(xa[p])
        toyb(p).wait_recv()
        bv=f32(xb[p*2+y])+f32(yb[p])
        if below is None:
            out[A]=av; out[B]=bv
            @pl.when(z>0)
            def _():
                toz(p,True).wait_recv()
                out[...]=out[...]+f32(zin[0,p])
            @pl.when(z<planes-1)
            def _():
                toz(p,False).wait_recv()
                out[...]=out[...]+f32(zin[1,p])
            return
        own[p,A]=av.astype(own.dtype); own[p,B]=bv.astype(own.dtype)
        up=not below
        has=(z>0) if up else (z<planes-1)
        @pl.when(has)
        def _():
            toz(p,up).wait_recv()
            own[p,A]=(av+f32(zin[0 if up else 1,p,A])).astype(own.dtype)
            own[p,B]=(bv+f32(zin[0 if up else 1,p,B])).astype(own.dtype)
        toz(p,up).start()
    def finish(p,below):
        for xx in (0,1):
            for yy in (0,1): core(p,xx,yy).wait_send()
        for e in (0,1): toya(p,e).wait_send(); toxb(p,e).wait_send()
        toxa(p).wait_send(); toyb(p).wait_send()
        if below is not None: toz(p,not below).wait_send()
    order=list(range(planes-1,-1,-1))
    for k in (0,1): bring(theirs,k,co).wait()
    for r in order: s.ring(r,start)
    for k in (0,1): bring(mine,k,c).wait()
    n=len(order)
    for i in range(n+2):
        if i<n: s.ring(order[i],first)
        if 0<=i-1<n: s.ring(order[i-1],second)
        if 0<=i-2<n: s.ring(order[i-2],third)
    for r in order: s.ring(r,finish)

def reduce_all(g,extra,inner,slots,collective):
    dp=extra.shape[0]; rows,cols=slots*BLK+extra.shape[2],g.shape[3]; planes=dp//2; half=rows//2//16*16
    dma=pltpu.SemaphoreType.DMA; bf=lambda *sh: pltpu.VMEM(sh+(cols,),g.dtype)
    return pl.pallas_call(partial(reduce_kernel,planes,half,slots),
        out_shape=jax.ShapeDtypeStruct((rows,cols),jnp.float32),in_specs=[ANY_SPEC,pl.BlockSpec(memory_space=pltpu.SMEM),VMEM_SPEC],out_specs=VMEM_SPEC,
        scratch_shapes=[pltpu.VMEM((g.shape[0],2)+g.shape[2:],g.dtype)]*2+[dma((4,)),bf(dp,4,rows),bf(planes*4,rows),bf(planes*4,rows),bf(planes*2,half),bf(planes*2,rows-half),bf(planes,half),bf(planes,rows-half),
            bf(planes,rows),bf(2,planes,rows),dma((10,planes)),dma((10,planes)),dma((planes,)),dma((2,planes))],
        compiler_params=pltpu.CompilerParams(collective_id=collective,has_side_effects=True,vmem_limit_bytes=56<<20),name="reduce_all")(g,inner,extra)
D=512; HD=128; FF=1024; LAYERS=2; BLK=128; HEADS=4
NORM_EPSILON=1e-5; MASK_VALUE=-1e30
f32=jnp.float32; bf16=jnp.bfloat16
SMEM_SPEC=pl.BlockSpec(memory_space=pltpu.SMEM)
SCALE=HD**-0.5; LOG2E=math.log2(math.e)
ROOT=math.sqrt(2/math.pi)

def nn(a,b): return lax.dot_general(a,b,(((1,),(0,)),((),())),preferred_element_type=f32)
def nt(a,b): return lax.dot_general(a,b,(((1,),(1,)),((),())),preferred_element_type=f32)
def tn(a,b): return lax.dot_general(a,b,(((0,),(0,)),((),())),preferred_element_type=f32)

def normed(r):
    center=r-jnp.mean(r,axis=-1,keepdims=True)
    rho=lax.rsqrt(jnp.mean(center*center,axis=-1,keepdims=True)+NORM_EPSILON)
    return center*rho,rho
def norm_back(dy,xhat,rho,gain):
    inner=dy*gain
    return rho*(inner-jnp.mean(inner,axis=-1,keepdims=True)-xhat*jnp.mean(inner*xhat,axis=-1,keepdims=True))
def gelu(v): return 0.5*v*(1+jnp.tanh(ROOT*(v+0.044715*v*v*v)))
def gelu_both(v):
    sq=v*v
    t=jnp.tanh(ROOT*v*(1+0.044715*sq))
    half=0.5*(1+t)
    return v*half,half+0.5*v*(1-t*t)*(ROOT*(1+3*0.044715*sq))
def colsum(v): return jnp.sum(v,axis=0,keepdims=True)

COLS_TILE=(3,4,2,4)
FIRST_BLOCK=(0,12,16,24)
LAYER_BLOCKS=32
CH=160
KB=320
FS=FF//HEADS

def rows_at(i,n): return pl.ds(pl.multiple_of(i*n,n),n)

class Weights:
    def __init__(self,refs): self.q,self.kv,self.out,self.up,self.down=refs
    def fill(self,layer,owners,wallv):
        base=layer*LAYER_BLOCKS
        def tiles(b):
            slot=owners[b]
            return [wallv[slot,j] for j in range(HEADS)]
        def by_row(r,_):
            rows=rows_at(r,BLK)
            for c in range(3):
                for j,v in enumerate(tiles(base+r*3+c)):
                    if c==0: self.q[rows,j*BLK:(j+1)*BLK]=v
                    else: self.kv[rows,j*2*BLK+(c-1)*BLK:j*2*BLK+c*BLK]=v
            for c in range(2):
                for j,v in enumerate(tiles(base+FIRST_BLOCK[2]+r*2+c)): self.up[rows,j*FS+c*BLK:j*FS+(c+1)*BLK]=v
            return 0
        lax.fori_loop(0,D//BLK,by_row,0)
        for c in range(4):
            for j,v in enumerate(tiles(base+FIRST_BLOCK[1]+c)): self.out[j*BLK:(j+1)*BLK,c*BLK:(c+1)*BLK]=v
            for r in range(2):
                for j,v in enumerate(tiles(base+FIRST_BLOCK[3]+r*4+c)): self.down[j*FS+r*BLK:j*FS+(r+1)*BLK,c*BLK:(c+1)*BLK]=v

def key_of(j): return slice(j*2*HD,j*2*HD+HD)
def value_of(j): return slice(j*2*HD+HD,(j+1)*2*HD)

def project(w,h_full,KV,rows): KV[rows,:]=nn(h_full[rows,:],w.kv[...]).astype(bf16)

def queries(w,h_full,start,q):
    def one(i,_):
        q[rows_at(i,CH),:]=nn(h_full[pl.ds(pl.multiple_of(start+i*CH,CH),CH),:],w.q[...]).astype(bf16)
        return 0
    lax.fori_loop(0,q.shape[0]//CH,one,0)

def forward(w,gains,own_rows,KV,q,heads,lse,bias,hidden,r1,r2,emit):
    keys=KV.shape[0]; chunks=q.shape[0]//CH
    lane=lax.broadcasted_iota(jnp.int32,(CH,BLK),1)
    def attend(i,_):
        rows=rows_at(i,CH)
        stats=jnp.zeros((CH,BLK),f32)
        scores=lambda j: nt(q[rows,j*HD:(j+1)*HD],KV[:,key_of(j)])
        s=scores(0)
        for j in range(HEADS):
            later=scores(j+1) if j+1<HEADS else None
            s=s+bias[rows,:].astype(f32)
            peak=jnp.max(s,axis=1,keepdims=True)
            p=jnp.exp2((s-peak)*(SCALE*LOG2E))
            total=jnp.sum(p,axis=1,keepdims=True)
            o=nn(p.astype(bf16),KV[:,value_of(j)])/total
            heads[rows,j*HD:(j+1)*HD]=o.astype(bf16)
            stats=jnp.where(lane==j,peak*(SCALE*LOG2E)+jnp.log2(total),stats)
            s=later
        lse[rows,:]=stats
        a=own_rows(i)+nn(heads[rows,:],w.out[...])
        r1[rows,:]=a
        first=normed(a)[0]*gains[0:1,:]+gains[1:2,:]
        hid=nn(first.astype(bf16),w.up[...])
        hidden[rows,:]=hid
        b=first+nn(gelu(hid).astype(bf16),w.down[...])
        r2[rows,:]=b
        emit(i,normed(b)[0]*gains[2:3,:]+gains[3:4,:])
        return 0
    lax.fori_loop(0,chunks,attend,0)

def backward(w,gains,start,h_full,upper,KV,q,heads,lse,biasT,hidden,r1,r2,
        dm,act,dhid,first,datt,dheads,delta,grad,dq,dqa,dhp,vec,put,exchange):
    share=q.shape[0]; keys=KV.shape[0]; chunks=share//CH
    lane=lax.broadcasted_iota(jnp.int32,(CH,BLK),1)
    def part(i,carry):
        rows=rows_at(i,CH)
        dy=upper(i)
        xhat,rho=normed(r2[rows,:])
        g2,s2=colsum(dy*xhat),colsum(dy)
        sg=norm_back(dy,xhat,rho,gains[2:3,:])
        dmb=sg.astype(bf16); dm[rows,:]=dmb
        a,slope=gelu_both(hidden[rows,:])
        act[rows,:]=a.astype(bf16)
        dh=(nt(dmb,w.down[...])*slope).astype(bf16)
        dhid[rows,:]=dh
        fu=sg+nt(dh,w.up[...])
        xhat,rho=normed(r1[rows,:])
        first[rows,:]=(xhat*gains[0:1,:]+gains[1:2,:]).astype(bf16)
        g1,s1=colsum(fu*xhat),colsum(fu)
        f=norm_back(fu,xhat,rho,gains[0:1,:])
        grad[rows,:]=f
        fb=f.astype(bf16); datt[rows,:]=fb
        dhe=nt(fb,w.out[...]).astype(bf16)
        dheads[rows,:]=dhe
        prod=dhe.astype(f32)*heads[rows,:].astype(f32)
        stats=jnp.zeros((CH,BLK),f32)
        for j in range(HEADS):
            stats=jnp.where(lane==j,jnp.sum(prod[:,j*HD:(j+1)*HD],axis=1,keepdims=True),stats)
        delta[rows,:]=stats
        return tuple(c+v for c,v in zip(carry,(g1,s1,g2,s2)))
    zero=jnp.zeros((1,D),f32)
    for k,v in enumerate(lax.fori_loop(0,chunks,part,(zero,)*4)): vec(k,v)
    lseT=jnp.transpose(lse[...]); deltaT=jnp.transpose(delta[...])
    dqa[...]=jnp.zeros(dqa.shape,f32)
    blocks=keys//KB
    def nth(t): return lax.rem(exchange.lead+t,blocks)
    def keyblock(t,_):
        kb=nth(t)
        rows=rows_at(kb,KB)
        head=lambda j: slice(j*HD,(j+1)*HD)
        both=lambda j: (nt(KV[rows,key_of(j)],q[:,head(j)]),nt(KV[rows,value_of(j)],dheads[:,head(j)]))
        now=both(0)
        for j in range(HEADS):
            later=both(j+1) if j+1<HEADS else None
            s,dp=now
            p=jnp.exp2((s+biasT[rows,:].astype(f32))*(SCALE*LOG2E)-lseT[j:j+1,:])
            ds=(p*(dp-deltaT[j:j+1,:])).astype(bf16)
            dqa[head(j),:]+=tn(KV[rows,key_of(j)],ds)
            dv=nn(p.astype(bf16),dheads[:,head(j)])
            dk=nn(ds,q[:,head(j)])*SCALE
            KV[rows,key_of(j)]=dk.astype(bf16)
            KV[rows,value_of(j)]=dv.astype(bf16)
            now=later
        dhp[rows,:]=nt(KV[rows,:],w.kv[...]).astype(bf16)
        for sub in range(KB//CH): exchange.send(kb*(KB//CH)+sub)
        @pl.when(t>0)
        def _():
            for sub in range(KB//CH): exchange.turn(nth(t-1)*(KB//CH)+sub)
        return 0
    lax.fori_loop(0,blocks,keyblock,0)
    dq[...]=(jnp.transpose(dqa[...])*SCALE).astype(bf16)
    def own(i,_):
        rows=rows_at(i,CH)
        grad[rows,:]=grad[rows,:]+nt(dq[rows,:],w.q[...])
        return 0
    lax.fori_loop(0,chunks,own,0)
    def tiles(value,place):
        value=value.astype(bf16)
        for r in range(value.shape[0]//BLK):
            for c in range(value.shape[1]//BLK):
                put(*place(r,c),value[r*BLK:(r+1)*BLK,c*BLK:(c+1)*BLK])
    tiles(tn(act[...],dm[...]),lambda r,c: (FIRST_BLOCK[3]+r%2*4+c,r//2))
    for sub in range(KB//CH): exchange.turn(nth(blocks-1)*(KB//CH)+sub)
    tiles(tn(first[...],dhid[...]),lambda r,c: (FIRST_BLOCK[2]+r*2+c%2,c//2))
    tiles(tn(heads[...],datt[...]),lambda r,c: (FIRST_BLOCK[1]+c,r))
    tiles(tn(h_full[pl.ds(pl.multiple_of(start,CH),share),:],dq[...]),lambda r,c: (r*3,c))
    tiles(tn(h_full[:keys,:],KV[...]),lambda r,c: (r*3+1+c%2,c//2))
    exchange.finish()

class Exchange:
    def __init__(self,s,terms,grad,rc,acc,ry,send,recv,count):
        self.s,self.terms,self.grad,self.rc,self.acc,self.ry,self.count=s,terms,grad,rc,acc,ry,count
        self.n=send.shape[1]
        self.lead=jnp.where(s.y==0,2*self.n//(KB//CH),0)
        at=lambda k,i: rows_at(k*self.n+i,CH)
        self.at=at
        co=1-s.c
        self.a=lambda i: remote(terms.at[at((1-s.y)*2+co,i)],rc.at[0,rows_at(i,CH)],send.at[0,i],recv.at[0,i],s.sibling)
        self.b=lambda i: remote(terms.at[at(s.y*2+co,i)],rc.at[1,rows_at(i,CH)],send.at[1,i],recv.at[1,i],s.sibling)
        self.o=lambda i: remote(acc.at[rows_at(i,CH)],ry.at[rows_at(i,CH)],send.at[2,i],recv.at[2,i],s.across_y)
    def owner(self,b):
        o=b//self.n
        return o//2==self.s.y,o%2==self.s.c,b%self.n
    def send(self,b):
        y,c,i=self.owner(b)
        @pl.when(jnp.logical_not(c)&jnp.logical_not(y))
        def _(): self.a(i).start()
        @pl.when(jnp.logical_not(c)&y)
        def _(): self.b(i).start()
    def turn(self,b):
        y,c,i=self.owner(b)
        @pl.when(c&jnp.logical_not(y))
        def _():
            self.a(i).wait_recv()
            rows=rows_at(i,CH)
            self.acc[rows,:]=(self.terms[rows_at(b,CH),:].astype(f32)+self.rc[0,rows,:].astype(f32)).astype(bf16)
            self.o(i).start()
    def finish(self):
        s=self.s
        for i in range(self.n):
            rows=pl.ds(i*CH,CH)
            @pl.when(s.mp*self.n+i<self.count)
            def _():
                self.b(i).wait_recv()
                t=self.grad[rows]+(self.terms[self.at(s.mp,i)].astype(f32)+self.rc[1,rows].astype(f32))
                self.o(i).wait_recv()
                self.grad[rows]=t+self.ry[rows].astype(f32)
        for i in range(self.n):
            @pl.when(((1-s.y)*2+1-s.c)*self.n+i<self.count)
            def _(): self.a(i).wait_send()
            @pl.when((s.y*2+1-s.c)*self.n+i<self.count)
            def _(): self.b(i).wait_send()
            @pl.when(((1-s.y)*2+s.c)*self.n+i<self.count)
            def _(): self.o(i).wait_send()

def layers_kernel(slots,owners,sizes,tokens,cot,wall,qline, layer_out,tokens_grad,g,extra,
        more,gains,vec,wallv,tok,h2,cotv,KV1,KV2,q1,q2,heads1,heads2,lse1,lse2,hid1,hid2,ra1,ra2,rb1,rb2,bias,biasT,
        dm,act,dhid,first,datt,dheads,delta,dq,dqa,dhp,rc,acc,ry,wa,wb,wc,wd,we,xa,xb,xc,xd,xe,lsem,ssend,srecv,tsend,trecv):
    s=Spot(1); mp=s.mp; share=q1.shape[0]; keys=KV1.shape[0]; chunks=share//CH
    start=mp*share
    def bring(k,_):
        pltpu.make_async_copy(wall.at[k//slots,:,rows_at(k%slots,BLK),:],wallv.at[k],lsem.at[1]).start()
        return 0
    lax.fori_loop(0,wallv.shape[0],bring,0)
    loads=[pltpu.make_async_copy(tokens,tok,lsem.at[0]),pltpu.make_async_copy(wallv,wallv,lsem.at[1]),
           pltpu.make_async_copy(cot.at[pl.ds(pl.multiple_of(start,CH),share)],cotv,lsem.at[2])]
    loads.append(pltpu.make_async_copy(wall.at[:,:,pl.ds(slots*BLK,wall.shape[2]-slots*BLK),:],more,lsem.at[5]))
    for c in (0,2,3): loads[c].start()
    bar=pltpu.get_barrier_semaphore()
    for who in (s.across_y,s.sibling): pl.semaphore_signal(bar,inc=1,device_id=who,device_id_type=MESH)
    ends=[]; total=jnp.int32(0)
    for k in range(sizes.shape[1]):
        total=total+sizes[0,k]; ends.append(total)
    def hood(index):
        h=jnp.zeros(index.shape,jnp.int32)
        for e in ends: h=h+(index>=e).astype(jnp.int32)
        return h
    def own_hood(index,queries):
        row=start+index
        return jnp.where(row<keys,hood(row),queries)
    key_line=hood(lax.broadcasted_iota(jnp.int32,(1,keys),1))
    row_line=own_hood(lax.broadcasted_iota(jnp.int32,(1,share),1),qline[...])
    column=jnp.transpose(jnp.broadcast_to(row_line.astype(f32),(8,share)))[:,0:1].astype(jnp.int32)
    def mask(i):
        rows=pl.ds(i*CH,CH)
        col=column[i*CH:(i+1)*CH,:]
        bias[rows,:]=jnp.where(col==key_line,0.0,MASK_VALUE).astype(bf16)
    for i in range(chunks): mask(i)
    def maskT(i,_):
        rows=rows_at(i,KB)
        col=hood(lax.broadcasted_iota(jnp.int32,(KB,1),0)+i*KB)
        biasT[rows,:]=jnp.where(col==row_line,0.0,MASK_VALUE).astype(bf16)
        return 0
    lax.fori_loop(0,keys//KB,maskT,0)
    w1,w2=Weights((wa,wb,wc,wd,we)),Weights((xa,xb,xc,xd,xe))
    loads[1].wait()
    w1.fill(0,owners,wallv)
    loads[0].wait()
    pl.semaphore_wait(bar,2)
    at=lambda k,i: pl.ds(pl.multiple_of(k*share+i*CH,CH),CH)
    far=s.across_y[1]
    over=lambda i: remote(h2.at[at(mp,i)],h2.at[at(mp,i)],ssend.at[0,i],srecv.at[0,i],s.across_y)
    near=lambda i: remote(h2.at[at(mp,i)],h2.at[at(mp,i)],ssend.at[1,i],srecv.at[1,i],s.sibling)
    on=lambda i: remote(h2.at[at(far,i)],h2.at[at(far,i)],ssend.at[2,i],srecv.at[2,i],s.sibling)
    loads[3].wait()
    n=LAYERS*4*D//(more.shape[0]*HEADS)
    for e in range(more.shape[0]*HEADS):
        pair=more[e//HEADS,e%HEADS].astype(f32)
        where=e*n
        gains[where//D:where//D+1,where%D:where%D+n]=(pair[0:1]+pair[1:2])[:,:n]
    g1,g2=gains[0:4],gains[4:8]
    def emit1(i,v):
        layer_out[rows_at(i,CH),:]=v
        h2[at(mp,i),:]=v.astype(bf16)
        over(i).start(); near(i).start()
    def every(kb,_):
        project(w1,tok,KV1,rows_at(kb,KB))
        return 0
    lax.fori_loop(0,keys//KB,every,0)
    queries(w1,tok,start,q1)
    forward(w1,g1,lambda i: tok[at(mp,i),:].astype(f32),KV1,q1,heads1,lse1,bias,hid1,ra1,rb1,emit1)
    w2.fill(1,owners,wallv)
    def arrived(k,i):
        @pl.when(k*chunks+i<keys//CH)
        def _(): project(w2,h2,KV2,at(k,i))
    for i in range(chunks): arrived(mp,i)
    queries(w2,h2,start,q2)
    for i in range(chunks):
        near(i).wait_recv(); arrived(s.sibling[1],i)
    for i in range(chunks):
        over(i).wait_recv(); on(i).start(); arrived(far,i)
    for i in range(chunks):
        on(i).wait_recv(); arrived(s.y_sibling,i)
    def emit2(i,v): layer_out[rows_at(i,CH),:]=v
    forward(w2,g2,lambda i: layer_out[rows_at(i,CH),:],KV2,q2,heads2,lse2,bias,hid2,ra2,rb2,emit2)
    for i in range(chunks):
        for k in (over,near,on): k(i).wait_send()
    def put(layer):
        def store(b,j,v):
            b=b+layer*LAYER_BLOCKS
            wallv[b,j]=v
        return store
    def keep(layer):
        def store(k,v): vec[layer*4+k:layer*4+k+1,:]=v
        return store
    loads[2].wait()
    half=wallv.shape[0]//2
    flush=[pltpu.make_async_copy(wallv.at[pl.ds(k*half,half)],g.at[pl.ds(k*half,half)],lsem.at[3+k]) for k in range(2)]
    backward(w2,g2,start,h2,lambda i: cotv[rows_at(i,CH),:].astype(f32),KV2,q2,heads2,lse2,biasT,hid2,ra2,rb2,
        dm,act,dhid,first,datt,dheads,delta,tokens_grad,dq,dqa,dhp,keep(1),put(1),Exchange(s,dhp,tokens_grad,rc.at[0],acc,ry.at[0],tsend.at[0],trecv.at[0],keys//CH))
    flush[1].start()
    backward(w1,g1,start,tok,lambda i: tokens_grad[rows_at(i,CH),:],KV1,q1,heads1,lse1,biasT,hid1,ra1,rb1,
        dm,act,dhid,first,datt,dheads,delta,tokens_grad,dq,dqa,dhp,keep(0),put(0),Exchange(s,dhp,tokens_grad,rc.at[1],acc,ry.at[1],tsend.at[1],trecv.at[1],keys//CH))
    flush[0].start()
    top=lax.broadcasted_iota(jnp.int32,(16,BLK),0)==0
    for e in range(more.shape[0]*HEADS):
        where=e*n
        row=vec[where//D:where//D+1,where%D:where%D+n]
        if n<BLK: row=jnp.concatenate([row,jnp.zeros((1,BLK-n),f32)],axis=1)
        extra[e//HEADS,e%HEADS]=jnp.where(top,row,0.0).astype(bf16)
    flush[1].wait(); flush[0].wait()

def run_layers(owners,sizes,tokens,cot,wall,qline,keys,slots,collective):
    rows=tokens.shape[0]; share=rows//HEADS; chunks=share//CH
    v=pltpu.VMEM; dma=pltpu.SemaphoreType.DMA; V_=VMEM_SPEC
    two=lambda shape,t: [v(shape,t)]*2
    weights=[v((D,D),bf16),v((D,HEADS*2*HD),bf16),v((D,D),bf16),v((D,FF),bf16),v((FF,D),bf16)]
    blocks=(LAYERS*LAYER_BLOCKS,HEADS,BLK,BLK)
    tail=(wall.shape[0],HEADS,wall.shape[2]-slots*BLK,BLK)
    scratch=[v(tail,bf16),v((LAYERS*4,D),f32),v((LAYERS*4,D),f32),v(blocks,bf16),v((rows,D),bf16),v((rows,D),bf16),v((share,D),bf16)]
    scratch+=two((keys,HEADS*2*HD),bf16)+two((share,D),bf16)+two((share,D),bf16)+two((share,BLK),f32)+two((share,FF),f32)+two((share,D),f32)+two((share,D),f32)
    scratch+=[v((share,keys),bf16),v((keys,share),bf16)]
    scratch+=[v((share,D),bf16),v((share,FF),bf16),v((share,FF),bf16),v((share,D),bf16),v((share,D),bf16),v((share,D),bf16),v((share,BLK),f32),v((share,D),bf16),v((D,share),f32)]
    scratch+=[v((rows,D),bf16),v((2,2,share,D),bf16),v((share,D),bf16),v((2,share,D),bf16)]+weights+weights
    scratch+=[dma((6,)),dma((3,chunks)),dma((3,chunks)),dma((2,3,chunks)),dma((2,3,chunks))]
    shape=jax.ShapeDtypeStruct
    return pl.pallas_call(partial(layers_kernel,slots),
        out_shape=[shape((share,D),f32),shape((share,D),f32),shape(blocks,bf16),shape(tail,bf16)],
        in_specs=[SMEM_SPEC,SMEM_SPEC,ANY_SPEC,ANY_SPEC,ANY_SPEC,V_],out_specs=[V_,V_,ANY_SPEC,V_],scratch_shapes=scratch,
        compiler_params=pltpu.CompilerParams(collective_id=collective,has_side_effects=True,vmem_limit_bytes=60<<20),name="layers")(
        owners,sizes,tokens,cot,wall,qline)
BLK=128; STEP=10
BETA_ONE=0.9; BETA_TWO=0.95; BETA_STATS=0.95; RATE_MATRIX=0.12; DECAY_WEIGHT=0.01; ADAM_EPSILON=1e-8

def split(x):
    hi=x.astype(jnp.bfloat16)
    return hi,(x-hi.astype(jnp.float32)).astype(jnp.bfloat16)
def dot3(a,b,ca,cb):
    dims=(((ca,),(cb,)),((),()))
    ah,al=a; bh,bl=b
    d=lambda x,y: lax.dot_general(x,y,dims,preferred_element_type=jnp.float32)
    return d(ah,bh)+(d(ah,bl)+d(al,bh))
def dotf(a,b,ca,cb):
    return lax.dot_general(a,b,(((ca,),(cb,)),((),())),preferred_element_type=jnp.float32,precision=lax.Precision.HIGHEST)

def in_groups(count,step,body):
    step=math.gcd(count,step)
    def run(i,_):
        for k in range(step): body(i*step+k)
        return 0
    lax.fori_loop(0,count//step,run,0)

PANEL=32
def soap_kernel(slots,g_ref,m_ref,v_ref,l_ref,r_ref,ql_ref,qr_ref,w_ref,vm_ref,vs_ref,vw_ref,pa,pb, oa,ob,mo,vo,lo,ro,qlo,qro,wo,vmo,vso,vwo, x_ref, a_ref, b_ref, f_ref, psem):
    passed=[pltpu.make_async_copy(pa,oa,psem.at[0]),pltpu.make_async_copy(pb,ob,psem.at[1])]
    for copy in passed: copy.start()
    width=vm_ref.shape[1]
    vmo[...],vso[...],vwo[...]=adam_vector(g_ref[slots*BLK:slots*BLK+1,:width],vm_ref[...],vs_ref[...],vw_ref[...])
    def first(i):
        g=g_ref[pl.ds(pl.multiple_of(i*BLK,BLK),BLK),:]; ql=split(ql_ref[i]); qr=split(qr_ref[i])
        gs=split(g)
        m=BETA_ONE*m_ref[i]+(1-BETA_ONE)*g
        mo[i]=m
        def turn(v):
            return dot3(split(dot3(ql,v,0,0)),qr,1,0)
        tg=turn(gs)
        v=BETA_TWO*v_ref[i]+(1-BETA_TWO)*tg*tg
        vo[i]=v
        d=turn(split(m))/(1-BETA_ONE**STEP)/(jnp.sqrt(v/(1-BETA_TWO**STEP))+ADAM_EPSILON)
        u=dot3(split(dot3(ql,split(d),1,0)),qr,1,1)
        w=w_ref[i]
        wo[i]=w-RATE_MATRIX*(u+DECAY_WEIGHT*w)
        ln=BETA_STATS*l_ref[i]+(1-BETA_STATS)*dot3(gs,gs,1,1)
        rn=BETA_STATS*r_ref[i]+(1-BETA_STATS)*dot3(gs,gs,0,0)
        lo[i]=ln; ro[i]=rn
        al=dot3(split(ln),ql,1,0); ar=dot3(split(rn),qr,1,0)
        a_ref[2*i]=al; a_ref[2*i+1]=ar
        x_ref[2*i]=dotf(al,al,0,0); x_ref[2*i+1]=dotf(ar,ar,0,0)
    in_groups(slots,4,first)
    n=2*slots
    lane=lax.broadcasted_iota(jnp.int32,(8,BLK),1)
    sub=lax.broadcasted_iota(jnp.int32,(8,BLK),0)
    for p in range(BLK//8):
        end=(p*8//PANEL+1)*PANEL//8
        def step(kk,_):
            k=p*8+kk
            idx=jnp.full((8,BLK),k,jnp.int32)
            atk=lane==k
            below=sub>kk
            done=(lane<=k)|(lane>=end*8)
            rows=[jnp.broadcast_to(x_ref[m,pl.ds(k,1),:],(8,BLK)) for m in range(n)]
            fs=[jnp.take_along_axis(x_ref[m,p*8:(p+1)*8,:],idx,axis=1) for m in range(n)]
            for m in range(n): f_ref[m]=fs[m]
            rinv=[1.0/jnp.broadcast_to(f_ref[m,pl.ds(kk,1),:],(8,BLK)) for m in range(n)]
            scaled=[jnp.where(atk,1.0,row)*ri for row,ri in zip(rows,rinv)]
            for m in range(n):
                b_ref[m,pl.ds(k%PANEL,1),:]=jnp.where(done,scaled[m],0.0)[0:1,:]
                for t in range(p,end):
                    v=x_ref[m,t*8:(t+1)*8,:]
                    f=fs[m] if t==p else jnp.take_along_axis(v,idx,axis=1)
                    new=jnp.where(atk,0.0,v)-f*scaled[m]
                    if t==p: new=jnp.where(below,new,v)
                    x_ref[m,t*8:(t+1)*8,:]=new
            return 0
        lax.fori_loop(0,8,step,0)
        if (p+1)*8%PANEL==0 and p<BLK//8-1:
            lo_,hi_=(p+1)*8-PANEL,(p+1)*8
            keep=lax.broadcasted_iota(jnp.int32,(BLK-hi_,BLK),1)
            keep=(keep<lo_)|(keep>=hi_)
            def trail(m):
                u=dotf(x_ref[m,lo_:hi_,:],b_ref[m],0,0)
                x_ref[m,hi_:,:]=jnp.where(keep,x_ref[m,hi_:,:],0.0)-u[hi_:,:]
            in_groups(n,8,trail)
    r=lax.broadcasted_iota(jnp.int32,(BLK,BLK),0); c=lax.broadcasted_iota(jnp.int32,(BLK,BLK),1)
    def last(i):
        for s,out in ((0,qlo),(1,qro)):
            x=x_ref[2*i+s]
            piv=jnp.sum(jnp.where(r==c,x,0.0),axis=1,keepdims=True)
            inv=jnp.where(r==c,1.0,jnp.where(r>c,x,0.0))*lax.rsqrt(piv)
            out[i]=dot3(split(a_ref[2*i+s]),split(inv),1,1)
    in_groups(slots,4,last)
    for copy in passed: copy.wait()

def soap(g,m,v,l,r,ql,qr,w,vm,vs,vw,pa,pb):
    slots=m.shape[0]
    sh=jax.ShapeDtypeStruct((slots,BLK,BLK),jnp.float32); line=jax.ShapeDtypeStruct((1,vm.shape[0]),jnp.float32)
    space=pl.BlockSpec(memory_space=pltpu.VMEM)
    out=pl.pallas_call(partial(soap_kernel,slots),out_shape=[jax.ShapeDtypeStruct(e.shape,e.dtype) for e in (pa,pb)]+[sh]*7+[line]*3,in_specs=[space]*11+[ANY_SPEC]*2,out_specs=[ANY_SPEC]*2+[space]*10,
        scratch_shapes=[pltpu.VMEM((2*slots,BLK,BLK),jnp.float32)]*2+[pltpu.VMEM((2*slots,PANEL,BLK),jnp.float32),pltpu.VMEM((2*slots,8,BLK),jnp.float32),pltpu.SemaphoreType.DMA((2,))],
        compiler_params=pltpu.CompilerParams(vmem_limit_bytes=48<<20),name="soap")(g,m,v,l,r,ql,qr,w,vm[None],vs[None],vw[None],pa,pb)
    return tuple(out[:9])+tuple(o[0] for o in out[9:])

def inverse(owners):
    index=jnp.arange(owners.shape[0],dtype=jnp.int32)
    return jnp.sum(jnp.where(owners[:,None]==index[None,:],index[:,None],0),axis=0)

def local(tokens,cotangent,context_sizes,query_hoods,owners,master_blocks,first_blocks,second_blocks,left_blocks,right_blocks,
        left_bases,right_bases,vector_master,vector_moment,vector_square):
    dp=lax.axis_size("dp")
    rows=tokens.shape[0]; keys=rows-query_hoods.shape[0]; share=rows//HEADS; slots=master_blocks.shape[0]
    wall=gather_all(master_blocks,vector_master,dp,0)
    hoods=jnp.pad(query_hoods,(share-query_hoods.shape[0],0))
    layer_out,tokens_grad,g,extra=run_layers(owners,context_sizes,tokens,cotangent,wall,hoods[None,:],keys,slots,1)
    total=reduce_all(g,extra,inverse(owners),slots,2)
    return soap(total,first_blocks,second_blocks,left_blocks,right_blocks,left_bases,right_bases,master_blocks,
        vector_moment,vector_square,vector_master,layer_out,tokens_grad)


def solution(mesh):
    return jax.shard_map(
        local,
        mesh=mesh,
        in_specs=(
            P("dp", None),
            P("dp", None),
            P("dp", None),
            P("dp"),
            P(),
            P("dp", "mp", None),
            P("dp", "mp", None),
            P("dp", "mp", None),
            P("dp", "mp", None),
            P("dp", "mp", None),
            P("dp", "mp", None),
            P("dp", "mp", None),
            P(("dp", "mp")),
            P(("dp", "mp")),
            P(("dp", "mp")),
        ),
        out_specs=(
            P(("dp", "mp"), None),
            P(("dp", "mp"), None),
            P("dp", "mp", None),
            P("dp", "mp", None),
            P("dp", "mp", None),
            P("dp", "mp", None),
            P("dp", "mp", None),
            P("dp", "mp", None),
            P("dp", "mp", None),
            P(("dp", "mp")),
            P(("dp", "mp")),
            P(("dp", "mp")),
        ),
        check_vma=False,
    )
```

```python
import math
from functools import partial

import jax
import jax.numpy as jnp
from jax import lax
from jax.experimental import pallas as pl
from jax.experimental.pallas import tpu as pltpu
from jax.sharding import PartitionSpec as P

RATE_VECTOR = 0.6
def adam_vector(grad, first, second, weight):
    first_new = BETA_ONE * first + (1.0 - BETA_ONE) * grad
    second_new = BETA_TWO * second + (1.0 - BETA_TWO) * grad * grad
    weight_new = weight - RATE_VECTOR * (first_new / (1.0 - BETA_ONE**STEP)) / (
        jnp.sqrt(second_new / (1.0 - BETA_TWO**STEP)) + ADAM_EPSILON
    )
    return (first_new, second_new, weight_new)


MESH=pl.DeviceIdType.MESH
BLK=128
VMEM_SPEC=pl.BlockSpec(memory_space=pltpu.VMEM)
ANY_SPEC=pl.BlockSpec(memory_space=pl.ANY)

def remote(src,dst,send,recv,device):
    return pltpu.make_async_remote_copy(src_ref=src,dst_ref=dst,send_sem=send,recv_sem=recv,device_id=device,device_id_type=MESH)

class Spot:
    def __init__(self,planes):
        dp,mp=lax.axis_index("dp"),lax.axis_index("mp")
        self.dp,self.mp,self.planes=dp,mp,planes
        self.z,self.x=dp//2,dp%2
        self.y,self.c=mp//2,mp%2
        self.across_x=(dp+1-2*self.x,mp)
        self.across_y=(dp,(mp+2)%4)
        self.sibling=(dp,mp+1-2*self.c)
        self.y_sibling=3-mp
        self.up=(jnp.minimum(dp+2,2*planes-1),mp)
        self.down=(jnp.maximum(dp-2,0),mp)
    def greet(self):
        bar=pltpu.get_barrier_semaphore()
        for who in (self.across_x,self.across_y,self.sibling):
            pl.semaphore_signal(bar,inc=1,device_id=who,device_id_type=MESH)
        @pl.when(self.z<self.planes-1)
        def _(): pl.semaphore_signal(bar,inc=1,device_id=self.up,device_id_type=MESH)
        @pl.when(self.z>0)
        def _(): pl.semaphore_signal(bar,inc=1,device_id=self.down,device_id_type=MESH)
        pl.semaphore_wait(bar,3+jnp.minimum(self.z,1)+jnp.minimum(self.planes-1-self.z,1))
    def ring(self,r,action):
        if r==0:
            action(self.z,None); return
        @pl.when(self.z>=r)
        def _(): action(self.z-r,True)
        @pl.when(self.z+r<self.planes)
        def _(): action(self.z+r,False)

def gather_kernel(planes,cuts,master,vector,out,slab,send,recv,zsend,zrecv,lsem,csend,crecv,zcsend,zcrecv,ccsend,ccrecv):
    for k in range(master.shape[0]): slab[k*BLK:(k+1)*BLK,:]=master[k].astype(slab.dtype)
    n=vector.shape[1]
    high=vector[...].astype(slab.dtype).astype(jnp.float32)
    pair=jnp.where(lax.broadcasted_iota(jnp.int32,(16,n),0)==0,high,vector[...]-high)
    if n<BLK: pair=jnp.concatenate([pair,jnp.zeros((16,BLK-n),jnp.float32)],axis=1)
    slab[master.shape[0]*BLK:,:]=pair.astype(slab.dtype)
    s=Spot(planes); rows=slab.shape[0]; z,x,y,c,mp=s.z,s.x,s.y,s.c,s.mp
    A,B,AB,C=pl.ds(0,cuts[0]),pl.ds(cuts[0],cuts[1]-cuts[0]),pl.ds(0,cuts[1]),pl.ds(cuts[1],rows-cuts[1])
    mx,my=s.across_x,s.across_y
    own=pltpu.make_async_copy(slab,out.at[s.dp,mp],lsem); own.start()
    s.greet()
    def at(p,xx,yy,cc): return out.at[p*2+xx,yy*2+cc]
    xo,yo=1-x,1-y
    def copies(p,src):
        here=at(p,x,y,c) if src is None else src
        f=lambda k,a,b,w: remote(a,b,send.at[k,p],recv.at[k,p],w)
        return dict(
            xown=lambda: f(0,here.at[AB],at(p,x,y,c).at[AB],mx), yown=lambda: f(1,here.at[AB],at(p,x,y,c).at[AB],my),
            cown=lambda: f(2,here.at[AB],at(p,x,y,c).at[AB],s.sibling),
            yfwd=lambda: f(3,at(p,xo,y,c).at[A],at(p,xo,y,c).at[A],my),
            xfwd=lambda: f(4,at(p,x,yo,c).at[B],at(p,x,yo,c).at[B],mx),
            cx=lambda: f(5,at(p,xo,y,c).at[AB],at(p,xo,y,c).at[AB],s.sibling), cy=lambda: f(6,at(p,x,yo,c).at[AB],at(p,x,yo,c).at[AB],s.sibling),
            ca=lambda: f(7,at(p,xo,yo,c).at[A],at(p,xo,yo,c).at[A],s.sibling),
            cb=lambda: f(8,at(p,xo,yo,c).at[B],at(p,xo,yo,c).at[B],s.sibling))
    def zcopy(p,up,src=None):
        here=at(p,x,y,c) if src is None else src
        return remote(here.at[AB],at(p,x,y,c).at[AB],zsend.at[0 if up else 1,p],zrecv.at[p],s.up if up else s.down)
    def onward(below,action):
        if below is None or below:
            @pl.when(z<planes-1)
            def _(): action(True)
        if below is None or not below:
            @pl.when(z>0)
            def _(): action(False)
    c_x=lambda: remote(slab.at[C],at(z,x,y,c).at[C],csend.at[0],crecv.at[0],mx)
    c_y=lambda: remote(slab.at[C],at(z,x,y,c).at[C],csend.at[1],crecv.at[1],my)
    c_xy=lambda: remote(at(z,xo,y,c).at[C],at(z,xo,y,c).at[C],csend.at[2],crecv.at[2],my)
    both=lambda p,yy: out.at[pl.ds(p*2,2),yy*2+c,C]
    c_z=lambda p,yy,up: remote(both(p,yy),both(p,yy),zcsend.at[0 if up else 1,p,yy],zcrecv.at[p,yy],s.up if up else s.down)
    c_c=lambda p,yy: remote(both(p,yy),both(p,yy),ccsend.at[p,yy],ccrecv.at[p,yy],s.sibling)
    def c_arrive(p,below):
        for yy in (0,1):
            if below is not None: c_z(p,yy,below).wait_recv()
            onward(below,lambda up: c_z(p,yy,up).start())
            c_c(p,yy).start()
    def arrive(r):
        def act(p,below):
            src=None
            if below is None: src=slab
            else: zcopy(p,below).wait_recv()
            onward(below,lambda up: zcopy(p,up,src).start())
            k=copies(p,src)
            k["xown"]().start(); k["yown"]().start(); k["cown"]().start()
        s.ring(r,act)
    def second(r):
        def act(p,below):
            k=copies(p,None)
            k["xown"]().wait_recv(); k["yfwd"]().start(); k["cx"]().start()
            k["yown"]().wait_recv(); k["xfwd"]().start(); k["cy"]().start()
        s.ring(r,act)
    def third(r):
        def act(p,below):
            k=copies(p,None)
            k["yfwd"]().wait_recv(); k["ca"]().start()
            k["xfwd"]().wait_recv(); k["cb"]().start()
        s.ring(r,act)
    def finish(r):
        def act(p,below):
            src=slab if below is None else None
            k=copies(p,src)
            for n in ("cown","cx","cy","ca","cb"): k[n]().wait_recv()
            for n in k: k[n]().wait_send()
            onward(below,lambda up: zcopy(p,up,src).wait_send())
            for yy in (0,1):
                onward(below,lambda up: c_z(p,yy,up).wait_send())
                remote(both(p,yy),out.at[pl.ds(p*2,2),yy*2+1-c,C],ccsend.at[p,yy],ccrecv.at[p,yy],s.sibling).wait_recv()
                c_c(p,yy).wait_send()
        s.ring(r,act)
    c_x().start(); c_y().start()
    for r in range(planes+2):
        if r<planes: arrive(r)
        if r==0:
            c_x().wait_recv(); c_xy().start()
        if r==1:
            c_y().wait_recv(); c_xy().wait_recv(); own.wait()
            c_arrive(z,None)
        if 1<=r<=planes: second(r-1)
        if 2<=r<=planes: s.ring(r-1,c_arrive)
        if r>=2: third(r-2)
    for r in range(planes): finish(r)
    for k in (c_x,c_y,c_xy): k().wait_send()

def gather_all(master,vector,dp,collective):
    rows=master.shape[0]*BLK+16; planes=dp//2
    last=rows-rows//5//16*16; cuts=(last//2//16*16,last)
    dma=pltpu.SemaphoreType.DMA
    return pl.pallas_call(partial(gather_kernel,planes,cuts),
        out_shape=jax.ShapeDtypeStruct((dp,4,rows,BLK),jnp.bfloat16),
        in_specs=[VMEM_SPEC,VMEM_SPEC],out_specs=ANY_SPEC,
        scratch_shapes=[pltpu.VMEM((rows,BLK),jnp.bfloat16),dma((9,planes)),dma((9,planes)),dma((2,planes)),dma((planes,)),dma,
            dma((3,)),dma((3,)),dma((2,planes,2)),dma((planes,2)),dma((planes,2)),dma((planes,2))],
        compiler_params=pltpu.CompilerParams(collective_id=collective,has_side_effects=True),name="gather_all")(master,vector[None,:])

def reduce_kernel(planes,cuts,slots,source,inner,extra,out,theirs,mine,lsem,g,rc,acc,ya,xb,xa,yb,own,zin,send,recv,zsend,zrecv,zc,cy,cx,csum,zcs,zcr,cs,cr):
    s=Spot(planes); rows=g.shape[2]; half,last=cuts; z,x,y,c,mp=s.z,s.x,s.y,s.c,s.mp
    A,B,AB,C=pl.ds(0,half),pl.ds(half,last-half),pl.ds(0,last),pl.ds(last,rows-last)
    mx,my=s.across_x,s.across_y
    xo,yo,co=1-x,1-y,1-c
    bring=lambda held,k,parity: pltpu.make_async_copy(source.at[:,k*2+parity],held.at[:,k],lsem.at[k*2+parity])
    for held,parity in ((theirs,co),(mine,c)):
        for k in (0,1): bring(held,k,parity).start()
    s.greet()
    f32=lambda v: v.astype(jnp.float32)
    def core(p,xx,yy):
        k=xx*2+yy
        return remote(g.at[p*2+xx,yy*2+co],rc.at[p*4+k],send.at[k,p],recv.at[k,p],s.sibling)
    def toya(p,xx): return remote(acc.at[p*4+xx*2+yo,A],ya.at[p*2+xx],send.at[4+xx,p],recv.at[4+xx,p],my)
    def toxb(p,yy): return remote(acc.at[p*4+xo*2+yy,B],xb.at[p*2+yy],send.at[6+yy,p],recv.at[6+yy,p],mx)
    def toxa(p): return remote(ya.at[p*2+xo],xa.at[p],send.at[8,p],recv.at[8,p],mx)
    def toyb(p): return remote(xb.at[p*2+yo],yb.at[p],send.at[9,p],recv.at[9,p],my)
    def toz(p,up): return remote(own.at[p],zin.at[0 if up else 1,p],zsend.at[p],zrecv.at[0 if up else 1,p],s.up if up else s.down)
    def pack(p,parity,held):
        for xx in (0,1):
            d=p*2+xx
            def one(k,_):
                block=inner[d*slots+k]
                for yy in (0,1):
                    g[d,yy*2+parity,pl.ds(pl.multiple_of(k*BLK,BLK),BLK),:]=held[block,yy]
                return 0
            lax.fori_loop(0,slots,one,0)
            for yy in (0,1): g[d,yy*2+parity,slots*BLK:,:]=extra[d,yy*2+parity]
    def start(p,_):
        pack(p,co,theirs)
        for xx in (0,1):
            for yy in (0,1): core(p,xx,yy).start()
    def first(p,_):
        pack(p,c,mine)
        for xx in (0,1):
            for yy in (0,1):
                core(p,xx,yy).wait_recv()
                acc[p*4+xx*2+yy]=(f32(g[p*2+xx,yy*2+c])+f32(rc[p*4+xx*2+yy])).astype(acc.dtype)
        for e in (0,1): toya(p,e).start(); toxb(p,e).start()
    def second(p,_):
        for e in (0,1):
            toya(p,e).wait_recv()
            ya[p*2+e]=(f32(acc[p*4+e*2+y,A])+f32(ya[p*2+e])).astype(ya.dtype)
        toxa(p).start()
        for e in (0,1):
            toxb(p,e).wait_recv()
            xb[p*2+e]=(f32(acc[p*4+x*2+e,B])+f32(xb[p*2+e])).astype(xb.dtype)
        toyb(p).start()
    def third(p,below):
        toxa(p).wait_recv()
        av=f32(ya[p*2+x])+f32(xa[p])
        toyb(p).wait_recv()
        bv=f32(xb[p*2+y])+f32(yb[p])
        if below is None:
            out[A]=av; out[B]=bv
            @pl.when(z>0)
            def _():
                toz(p,True).wait_recv()
                out[AB]=out[AB]+f32(zin[0,p])
            @pl.when(z<planes-1)
            def _():
                toz(p,False).wait_recv()
                out[AB]=out[AB]+f32(zin[1,p])
            return
        own[p,A]=av.astype(own.dtype); own[p,B]=bv.astype(own.dtype)
        up=not below
        has=(z>0) if up else (z<planes-1)
        @pl.when(has)
        def _():
            toz(p,up).wait_recv()
            own[p,A]=(av+f32(zin[0 if up else 1,p,A])).astype(own.dtype)
            own[p,B]=(bv+f32(zin[0 if up else 1,p,B])).astype(own.dtype)
        toz(p,up).start()
    toc=lambda p,up: remote(acc.at[pl.ds(p*4,4),C],zc.at[0 if up else 1,p],zcs.at[p],zcr.at[0 if up else 1,p],s.up if up else s.down)
    cyc=lambda xx: remote(acc.at[z*4+xx*2+yo,C],cy.at[xx],cs.at[xx],cr.at[xx],my)
    cxc=lambda: remote(csum.at[xo],cx,cs.at[2],cr.at[2],mx)
    def c_take(p,up):
        @pl.when((z>0) if up else (z<planes-1))
        def _():
            toc(p,up).wait_recv()
            for k in range(4):
                acc[p*4+k,C]=(f32(acc[p*4+k,C])+f32(zc[0 if up else 1,p,k])).astype(acc.dtype)
    def c_stage(p,below):
        if below is None:
            c_take(p,True); c_take(p,False)
            for xx in (0,1): cyc(xx).start()
            return
        c_take(p,not below)
        toc(p,not below).start()
    def c_across():
        for xx in (0,1):
            cyc(xx).wait_recv()
            csum[xx]=(f32(acc[z*4+xx*2+y,C])+f32(cy[xx])).astype(csum.dtype)
        cxc().start()
    def c_end():
        cxc().wait_recv()
        out[C]=f32(csum[x])+f32(cx[...])
    def finish(p,below):
        for xx in (0,1):
            for yy in (0,1): core(p,xx,yy).wait_send()
        for e in (0,1): toya(p,e).wait_send(); toxb(p,e).wait_send()
        toxa(p).wait_send(); toyb(p).wait_send()
        if below is not None:
            toz(p,not below).wait_send(); toc(p,not below).wait_send()
    order=list(range(planes-1,-1,-1))
    for k in (0,1): bring(theirs,k,co).wait()
    for r in order: s.ring(r,start)
    for k in (0,1): bring(mine,k,c).wait()
    n=len(order)
    for i in range(n+2):
        if i<n: s.ring(order[i],first)
        if 0<=i-1<n:
            s.ring(order[i-1],second)
            s.ring(order[i-1],c_stage)
        if i==n+1: c_across()
        if 0<=i-2<n: s.ring(order[i-2],third)
    c_end()
    for r in order: s.ring(r,finish)
    cyc(0).wait_send(); cyc(1).wait_send(); cxc().wait_send()

def reduce_all(g,extra,inner,slots,collective):
    dp=extra.shape[0]; rows,cols=slots*BLK+extra.shape[2],g.shape[3]; planes=dp//2; last=rows-rows//5//16*16; half=last//2//16*16; part=rows-last
    dma=pltpu.SemaphoreType.DMA; bf=lambda *sh: pltpu.VMEM(sh+(cols,),g.dtype)
    return pl.pallas_call(partial(reduce_kernel,planes,(half,last),slots),
        out_shape=jax.ShapeDtypeStruct((rows,cols),jnp.float32),in_specs=[ANY_SPEC,pl.BlockSpec(memory_space=pltpu.SMEM),VMEM_SPEC],out_specs=VMEM_SPEC,
        scratch_shapes=[pltpu.VMEM((g.shape[0],2)+g.shape[2:],g.dtype)]*2+[dma((4,)),bf(dp,4,rows),bf(planes*4,rows),bf(planes*4,rows),bf(planes*2,half),bf(planes*2,last-half),bf(planes,half),bf(planes,last-half),
            bf(planes,last),bf(2,planes,last),dma((10,planes)),dma((10,planes)),dma((planes,)),dma((2,planes)),
            bf(2,planes,4,part),bf(2,part),bf(part),bf(2,part),dma((planes,)),dma((2,planes)),dma((3,)),dma((3,))],
        compiler_params=pltpu.CompilerParams(collective_id=collective,has_side_effects=True,vmem_limit_bytes=56<<20),name="reduce_all")(g,inner,extra)
D=512; HD=128; FF=1024; LAYERS=2; BLK=128; HEADS=4
NORM_EPSILON=1e-5; MASK_VALUE=-1e30
f32=jnp.float32; bf16=jnp.bfloat16
SMEM_SPEC=pl.BlockSpec(memory_space=pltpu.SMEM)
SCALE=HD**-0.5; LOG2E=math.log2(math.e)
ROOT=math.sqrt(2/math.pi)

def nn(a,b): return lax.dot_general(a,b,(((1,),(0,)),((),())),preferred_element_type=f32)
def nt(a,b): return lax.dot_general(a,b,(((1,),(1,)),((),())),preferred_element_type=f32)
def tn(a,b): return lax.dot_general(a,b,(((0,),(0,)),((),())),preferred_element_type=f32)

def normed(r):
    center=r-jnp.mean(r,axis=-1,keepdims=True)
    rho=lax.rsqrt(jnp.mean(center*center,axis=-1,keepdims=True)+NORM_EPSILON)
    return center*rho,rho
def norm_back(dy,xhat,rho,gain):
    inner=dy*gain
    return rho*(inner-jnp.mean(inner,axis=-1,keepdims=True)-xhat*jnp.mean(inner*xhat,axis=-1,keepdims=True))
def gelu(v): return 0.5*v*(1+jnp.tanh(ROOT*(v+0.044715*v*v*v)))
def gelu_both(v):
    sq=v*v
    t=jnp.tanh(ROOT*v*(1+0.044715*sq))
    half=0.5*(1+t)
    return v*half,half+0.5*v*(1-t*t)*(ROOT*(1+3*0.044715*sq))
def colsum(v): return jnp.sum(v,axis=0,keepdims=True)

COLS_TILE=(3,4,2,4)
FIRST_BLOCK=(0,12,16,24)
LAYER_BLOCKS=32
CH=160
KB=320
FS=FF//HEADS

def rows_at(i,n): return pl.ds(pl.multiple_of(i*n,n),n)

class Weights:
    def __init__(self,refs): self.q,self.kv,self.out,self.up,self.down=refs
    def fill(self,layer,owners,wallv):
        base=layer*LAYER_BLOCKS
        def tiles(b):
            slot=owners[b]
            return [wallv[slot,j] for j in range(HEADS)]
        def by_row(r,_):
            rows=rows_at(r,BLK)
            for c in range(3):
                for j,v in enumerate(tiles(base+r*3+c)):
                    if c==0: self.q[rows,j*BLK:(j+1)*BLK]=v
                    else: self.kv[rows,j*2*BLK+(c-1)*BLK:j*2*BLK+c*BLK]=v
            for c in range(2):
                for j,v in enumerate(tiles(base+FIRST_BLOCK[2]+r*2+c)): self.up[rows,j*FS+c*BLK:j*FS+(c+1)*BLK]=v
            return 0
        lax.fori_loop(0,D//BLK,by_row,0)
        for c in range(4):
            for j,v in enumerate(tiles(base+FIRST_BLOCK[1]+c)): self.out[j*BLK:(j+1)*BLK,c*BLK:(c+1)*BLK]=v
            for r in range(2):
                for j,v in enumerate(tiles(base+FIRST_BLOCK[3]+r*4+c)): self.down[j*FS+r*BLK:j*FS+(r+1)*BLK,c*BLK:(c+1)*BLK]=v

def key_of(j): return slice(j*2*HD,j*2*HD+HD)
def value_of(j): return slice(j*2*HD+HD,(j+1)*2*HD)

def project(w,h_full,KV,rows): KV[rows,:]=nn(h_full[rows,:],w.kv[...]).astype(bf16)

def queries(w,h_full,start,q):
    def one(i,_):
        q[rows_at(i,CH),:]=nn(h_full[pl.ds(pl.multiple_of(start+i*CH,CH),CH),:],w.q[...]).astype(bf16)
        return 0
    lax.fori_loop(0,q.shape[0]//CH,one,0)

def forward(w,gains,own_rows,KV,q,heads,lse,bias,hidden,r1,r2,emit):
    keys=KV.shape[0]; chunks=q.shape[0]//CH
    lane=lax.broadcasted_iota(jnp.int32,(CH,BLK),1)
    def attend(i,_):
        rows=rows_at(i,CH)
        stats=jnp.zeros((CH,BLK),f32)
        scores=lambda j: nt(q[rows,j*HD:(j+1)*HD],KV[:,key_of(j)])
        s=scores(0)
        for j in range(HEADS):
            later=scores(j+1) if j+1<HEADS else None
            s=s+bias[rows,:].astype(f32)
            peak=jnp.max(s,axis=1,keepdims=True)
            p=jnp.exp2((s-peak)*(SCALE*LOG2E))
            total=jnp.sum(p,axis=1,keepdims=True)
            o=nn(p.astype(bf16),KV[:,value_of(j)])/total
            heads[rows,j*HD:(j+1)*HD]=o.astype(bf16)
            stats=jnp.where(lane==j,peak*(SCALE*LOG2E)+jnp.log2(total),stats)
            s=later
        lse[rows,:]=stats
        a=own_rows(i)+nn(heads[rows,:],w.out[...])
        r1[rows,:]=a
        first=normed(a)[0]*gains[0:1,:]+gains[1:2,:]
        hid=nn(first.astype(bf16),w.up[...])
        hidden[rows,:]=hid
        b=first+nn(gelu(hid).astype(bf16),w.down[...])
        r2[rows,:]=b
        emit(i,normed(b)[0]*gains[2:3,:]+gains[3:4,:])
        return 0
    lax.fori_loop(0,chunks,attend,0)

def backward(w,gains,start,h_full,upper,KV,q,heads,lse,biasT,hidden,r1,r2,
        dm,act,dhid,first,datt,dheads,delta,grad,dq,dqa,dhp,vec,put,exchange):
    share=q.shape[0]; keys=KV.shape[0]; chunks=share//CH
    lane=lax.broadcasted_iota(jnp.int32,(CH,BLK),1)
    def part(i,carry):
        rows=rows_at(i,CH)
        dy=upper(i)
        xhat,rho=normed(r2[rows,:])
        g2,s2=colsum(dy*xhat),colsum(dy)
        sg=norm_back(dy,xhat,rho,gains[2:3,:])
        dmb=sg.astype(bf16); dm[rows,:]=dmb
        a,slope=gelu_both(hidden[rows,:])
        act[rows,:]=a.astype(bf16)
        dh=(nt(dmb,w.down[...])*slope).astype(bf16)
        dhid[rows,:]=dh
        fu=sg+nt(dh,w.up[...])
        xhat,rho=normed(r1[rows,:])
        first[rows,:]=(xhat*gains[0:1,:]+gains[1:2,:]).astype(bf16)
        g1,s1=colsum(fu*xhat),colsum(fu)
        f=norm_back(fu,xhat,rho,gains[0:1,:])
        grad[rows,:]=f
        fb=f.astype(bf16); datt[rows,:]=fb
        dhe=nt(fb,w.out[...]).astype(bf16)
        dheads[rows,:]=dhe
        prod=dhe.astype(f32)*heads[rows,:].astype(f32)
        stats=jnp.zeros((CH,BLK),f32)
        for j in range(HEADS):
            stats=jnp.where(lane==j,jnp.sum(prod[:,j*HD:(j+1)*HD],axis=1,keepdims=True),stats)
        delta[rows,:]=stats
        return tuple(c+v for c,v in zip(carry,(g1,s1,g2,s2)))
    zero=jnp.zeros((1,D),f32)
    for k,v in enumerate(lax.fori_loop(0,chunks,part,(zero,)*4)): vec(k,v)
    lseT=jnp.transpose(lse[...]); deltaT=jnp.transpose(delta[...])
    dqa[...]=jnp.zeros(dqa.shape,f32)
    blocks=keys//KB
    def nth(t): return lax.rem(exchange.lead+t,blocks)
    def keyblock(t,_):
        kb=nth(t)
        rows=rows_at(kb,KB)
        head=lambda j: slice(j*HD,(j+1)*HD)
        both=lambda j: (nt(KV[rows,key_of(j)],q[:,head(j)]),nt(KV[rows,value_of(j)],dheads[:,head(j)]))
        now=both(0)
        for j in range(HEADS):
            later=both(j+1) if j+1<HEADS else None
            s,dp=now
            p=jnp.exp2((s+biasT[rows,:].astype(f32))*(SCALE*LOG2E)-lseT[j:j+1,:])
            ds=(p*(dp-deltaT[j:j+1,:])).astype(bf16)
            dqa[head(j),:]+=tn(KV[rows,key_of(j)],ds)
            dv=nn(p.astype(bf16),dheads[:,head(j)])
            dk=nn(ds,q[:,head(j)])*SCALE
            KV[rows,key_of(j)]=dk.astype(bf16)
            KV[rows,value_of(j)]=dv.astype(bf16)
            now=later
        dhp[rows,:]=nt(KV[rows,:],w.kv[...]).astype(bf16)
        for sub in range(KB//CH): exchange.send(kb*(KB//CH)+sub)
        @pl.when(t>0)
        def _():
            for sub in range(KB//CH): exchange.turn(nth(t-1)*(KB//CH)+sub)
        return 0
    lax.fori_loop(0,blocks,keyblock,0)
    dq[...]=(jnp.transpose(dqa[...])*SCALE).astype(bf16)
    def own(i,_):
        rows=rows_at(i,CH)
        grad[rows,:]=grad[rows,:]+nt(dq[rows,:],w.q[...])
        return 0
    lax.fori_loop(0,chunks,own,0)
    def tiles(value,place):
        value=value.astype(bf16)
        for r in range(value.shape[0]//BLK):
            for c in range(value.shape[1]//BLK):
                put(*place(r,c),value[r*BLK:(r+1)*BLK,c*BLK:(c+1)*BLK])
    tiles(tn(act[...],dm[...]),lambda r,c: (FIRST_BLOCK[3]+r%2*4+c,r//2))
    for sub in range(KB//CH): exchange.turn(nth(blocks-1)*(KB//CH)+sub)
    tiles(tn(first[...],dhid[...]),lambda r,c: (FIRST_BLOCK[2]+r*2+c%2,c//2))
    tiles(tn(heads[...],datt[...]),lambda r,c: (FIRST_BLOCK[1]+c,r))
    tiles(tn(h_full[pl.ds(pl.multiple_of(start,CH),share),:],dq[...]),lambda r,c: (r*3,c))
    tiles(tn(h_full[:keys,:],KV[...]),lambda r,c: (r*3+1+c%2,c//2))
    exchange.finish()

class Exchange:
    def __init__(self,s,terms,grad,rc,acc,ry,send,recv,count):
        self.s,self.terms,self.grad,self.rc,self.acc,self.ry,self.count=s,terms,grad,rc,acc,ry,count
        self.n=send.shape[1]
        self.lead=jnp.where(s.y==0,2*self.n//(KB//CH),0)
        at=lambda k,i: rows_at(k*self.n+i,CH)
        self.at=at
        co=1-s.c
        self.a=lambda i: remote(terms.at[at((1-s.y)*2+co,i)],rc.at[0,rows_at(i,CH)],send.at[0,i],recv.at[0,i],s.sibling)
        self.b=lambda i: remote(terms.at[at(s.y*2+co,i)],rc.at[1,rows_at(i,CH)],send.at[1,i],recv.at[1,i],s.sibling)
        self.o=lambda i: remote(acc.at[rows_at(i,CH)],ry.at[rows_at(i,CH)],send.at[2,i],recv.at[2,i],s.across_y)
    def owner(self,b):
        o=b//self.n
        return o//2==self.s.y,o%2==self.s.c,b%self.n
    def send(self,b):
        y,c,i=self.owner(b)
        @pl.when(jnp.logical_not(c)&jnp.logical_not(y))
        def _(): self.a(i).start()
        @pl.when(jnp.logical_not(c)&y)
        def _(): self.b(i).start()
    def turn(self,b):
        y,c,i=self.owner(b)
        @pl.when(c&jnp.logical_not(y))
        def _():
            self.a(i).wait_recv()
            rows=rows_at(i,CH)
            self.acc[rows,:]=(self.terms[rows_at(b,CH),:].astype(f32)+self.rc[0,rows,:].astype(f32)).astype(bf16)
            self.o(i).start()
    def finish(self):
        s=self.s
        for i in range(self.n):
            rows=pl.ds(i*CH,CH)
            @pl.when(s.mp*self.n+i<self.count)
            def _():
                self.b(i).wait_recv()
                t=self.grad[rows]+(self.terms[self.at(s.mp,i)].astype(f32)+self.rc[1,rows].astype(f32))
                self.o(i).wait_recv()
                self.grad[rows]=t+self.ry[rows].astype(f32)
        for i in range(self.n):
            @pl.when(((1-s.y)*2+1-s.c)*self.n+i<self.count)
            def _(): self.a(i).wait_send()
            @pl.when((s.y*2+1-s.c)*self.n+i<self.count)
            def _(): self.b(i).wait_send()
            @pl.when(((1-s.y)*2+s.c)*self.n+i<self.count)
            def _(): self.o(i).wait_send()

def layers_kernel(slots,owners,sizes,tokens,cot,wall,qline, layer_out,tokens_grad,g,extra,
        more,gains,vec,wallv,tok,h2,cotv,KV1,KV2,q1,q2,heads1,heads2,lse1,lse2,hid1,hid2,ra1,ra2,rb1,rb2,bias,biasT,
        dm,act,dhid,first,datt,dheads,delta,dq,dqa,dhp,rc,acc,ry,wa,wb,wc,wd,we,xa,xb,xc,xd,xe,lsem,ssend,srecv,tsend,trecv):
    s=Spot(1); mp=s.mp; share=q1.shape[0]; keys=KV1.shape[0]; chunks=share//CH
    start=mp*share
    def bring(k,_):
        pltpu.make_async_copy(wall.at[k//slots,:,rows_at(k%slots,BLK),:],wallv.at[k],lsem.at[1]).start()
        return 0
    lax.fori_loop(0,wallv.shape[0],bring,0)
    loads=[pltpu.make_async_copy(tokens,tok,lsem.at[0]),pltpu.make_async_copy(wallv,wallv,lsem.at[1]),
           pltpu.make_async_copy(cot.at[pl.ds(pl.multiple_of(start,CH),share)],cotv,lsem.at[2])]
    loads.append(pltpu.make_async_copy(wall.at[:,:,pl.ds(slots*BLK,wall.shape[2]-slots*BLK),:],more,lsem.at[5]))
    for c in (0,2,3): loads[c].start()
    bar=pltpu.get_barrier_semaphore()
    for who in (s.across_y,s.sibling): pl.semaphore_signal(bar,inc=1,device_id=who,device_id_type=MESH)
    ends=[]; total=jnp.int32(0)
    for k in range(sizes.shape[1]):
        total=total+sizes[0,k]; ends.append(total)
    def hood(index):
        h=jnp.zeros(index.shape,jnp.int32)
        for e in ends: h=h+(index>=e).astype(jnp.int32)
        return h
    def own_hood(index,queries):
        row=start+index
        return jnp.where(row<keys,hood(row),queries)
    key_line=hood(lax.broadcasted_iota(jnp.int32,(1,keys),1))
    row_line=own_hood(lax.broadcasted_iota(jnp.int32,(1,share),1),qline[...])
    column=jnp.transpose(jnp.broadcast_to(row_line.astype(f32),(8,share)))[:,0:1].astype(jnp.int32)
    def mask(i):
        rows=pl.ds(i*CH,CH)
        col=column[i*CH:(i+1)*CH,:]
        bias[rows,:]=jnp.where(col==key_line,0.0,MASK_VALUE).astype(bf16)
    for i in range(chunks): mask(i)
    def maskT(i,_):
        rows=rows_at(i,KB)
        col=hood(lax.broadcasted_iota(jnp.int32,(KB,1),0)+i*KB)
        biasT[rows,:]=jnp.where(col==row_line,0.0,MASK_VALUE).astype(bf16)
        return 0
    lax.fori_loop(0,keys//KB,maskT,0)
    w1,w2=Weights((wa,wb,wc,wd,we)),Weights((xa,xb,xc,xd,xe))
    loads[1].wait()
    w1.fill(0,owners,wallv)
    loads[0].wait()
    pl.semaphore_wait(bar,2)
    at=lambda k,i: pl.ds(pl.multiple_of(k*share+i*CH,CH),CH)
    far=s.across_y[1]
    over=lambda i: remote(h2.at[at(mp,i)],h2.at[at(mp,i)],ssend.at[0,i],srecv.at[0,i],s.across_y)
    near=lambda i: remote(h2.at[at(mp,i)],h2.at[at(mp,i)],ssend.at[1,i],srecv.at[1,i],s.sibling)
    on=lambda i: remote(h2.at[at(far,i)],h2.at[at(far,i)],ssend.at[2,i],srecv.at[2,i],s.sibling)
    loads[3].wait()
    n=LAYERS*4*D//(more.shape[0]*HEADS)
    for e in range(more.shape[0]*HEADS):
        pair=more[e//HEADS,e%HEADS].astype(f32)
        where=e*n
        gains[where//D:where//D+1,where%D:where%D+n]=(pair[0:1]+pair[1:2])[:,:n]
    g1,g2=gains[0:4],gains[4:8]
    def emit1(i,v):
        layer_out[rows_at(i,CH),:]=v
        h2[at(mp,i),:]=v.astype(bf16)
        over(i).start(); near(i).start()
    def every(kb,_):
        project(w1,tok,KV1,rows_at(kb,KB))
        return 0
    lax.fori_loop(0,keys//KB,every,0)
    queries(w1,tok,start,q1)
    forward(w1,g1,lambda i: tok[at(mp,i),:].astype(f32),KV1,q1,heads1,lse1,bias,hid1,ra1,rb1,emit1)
    w2.fill(1,owners,wallv)
    def arrived(k,i):
        @pl.when(k*chunks+i<keys//CH)
        def _(): project(w2,h2,KV2,at(k,i))
    for i in range(chunks): arrived(mp,i)
    queries(w2,h2,start,q2)
    for i in range(chunks):
        near(i).wait_recv(); arrived(s.sibling[1],i)
    for i in range(chunks):
        over(i).wait_recv(); on(i).start(); arrived(far,i)
    for i in range(chunks):
        on(i).wait_recv(); arrived(s.y_sibling,i)
    def emit2(i,v): layer_out[rows_at(i,CH),:]=v
    forward(w2,g2,lambda i: layer_out[rows_at(i,CH),:],KV2,q2,heads2,lse2,bias,hid2,ra2,rb2,emit2)
    for i in range(chunks):
        for k in (over,near,on): k(i).wait_send()
    def put(layer):
        def store(b,j,v):
            b=b+layer*LAYER_BLOCKS
            wallv[b,j]=v
        return store
    def keep(layer):
        def store(k,v): vec[layer*4+k:layer*4+k+1,:]=v
        return store
    loads[2].wait()
    half=wallv.shape[0]//2
    flush=[pltpu.make_async_copy(wallv.at[pl.ds(k*half,half)],g.at[pl.ds(k*half,half)],lsem.at[3+k]) for k in range(2)]
    backward(w2,g2,start,h2,lambda i: cotv[rows_at(i,CH),:].astype(f32),KV2,q2,heads2,lse2,biasT,hid2,ra2,rb2,
        dm,act,dhid,first,datt,dheads,delta,tokens_grad,dq,dqa,dhp,keep(1),put(1),Exchange(s,dhp,tokens_grad,rc.at[0],acc,ry.at[0],tsend.at[0],trecv.at[0],keys//CH))
    flush[1].start()
    backward(w1,g1,start,tok,lambda i: tokens_grad[rows_at(i,CH),:],KV1,q1,heads1,lse1,biasT,hid1,ra1,rb1,
        dm,act,dhid,first,datt,dheads,delta,tokens_grad,dq,dqa,dhp,keep(0),put(0),Exchange(s,dhp,tokens_grad,rc.at[1],acc,ry.at[1],tsend.at[1],trecv.at[1],keys//CH))
    flush[0].start()
    top=lax.broadcasted_iota(jnp.int32,(16,BLK),0)==0
    for e in range(more.shape[0]*HEADS):
        where=e*n
        row=vec[where//D:where//D+1,where%D:where%D+n]
        if n<BLK: row=jnp.concatenate([row,jnp.zeros((1,BLK-n),f32)],axis=1)
        extra[e//HEADS,e%HEADS]=jnp.where(top,row,0.0).astype(bf16)
    flush[1].wait(); flush[0].wait()

def run_layers(owners,sizes,tokens,cot,wall,qline,keys,slots,collective):
    rows=tokens.shape[0]; share=rows//HEADS; chunks=share//CH
    v=pltpu.VMEM; dma=pltpu.SemaphoreType.DMA; V_=VMEM_SPEC
    two=lambda shape,t: [v(shape,t)]*2
    weights=[v((D,D),bf16),v((D,HEADS*2*HD),bf16),v((D,D),bf16),v((D,FF),bf16),v((FF,D),bf16)]
    blocks=(LAYERS*LAYER_BLOCKS,HEADS,BLK,BLK)
    tail=(wall.shape[0],HEADS,wall.shape[2]-slots*BLK,BLK)
    scratch=[v(tail,bf16),v((LAYERS*4,D),f32),v((LAYERS*4,D),f32),v(blocks,bf16),v((rows,D),bf16),v((rows,D),bf16),v((share,D),bf16)]
    scratch+=two((keys,HEADS*2*HD),bf16)+two((share,D),bf16)+two((share,D),bf16)+two((share,BLK),f32)+two((share,FF),f32)+two((share,D),f32)+two((share,D),f32)
    scratch+=[v((share,keys),bf16),v((keys,share),bf16)]
    scratch+=[v((share,D),bf16),v((share,FF),bf16),v((share,FF),bf16),v((share,D),bf16),v((share,D),bf16),v((share,D),bf16),v((share,BLK),f32),v((share,D),bf16),v((D,share),f32)]
    scratch+=[v((rows,D),bf16),v((2,2,share,D),bf16),v((share,D),bf16),v((2,share,D),bf16)]+weights+weights
    scratch+=[dma((6,)),dma((3,chunks)),dma((3,chunks)),dma((2,3,chunks)),dma((2,3,chunks))]
    shape=jax.ShapeDtypeStruct
    return pl.pallas_call(partial(layers_kernel,slots),
        out_shape=[shape((share,D),f32),shape((share,D),f32),shape(blocks,bf16),shape(tail,bf16)],
        in_specs=[SMEM_SPEC,SMEM_SPEC,ANY_SPEC,ANY_SPEC,ANY_SPEC,V_],out_specs=[V_,V_,ANY_SPEC,V_],scratch_shapes=scratch,
        compiler_params=pltpu.CompilerParams(collective_id=collective,has_side_effects=True,vmem_limit_bytes=60<<20),name="layers")(
        owners,sizes,tokens,cot,wall,qline)
BLK=128; STEP=10
BETA_ONE=0.9; BETA_TWO=0.95; BETA_STATS=0.95; RATE_MATRIX=0.12; DECAY_WEIGHT=0.01; ADAM_EPSILON=1e-8

def split(x):
    hi=x.astype(jnp.bfloat16)
    return hi,(x-hi.astype(jnp.float32)).astype(jnp.bfloat16)
def dot3(a,b,ca,cb):
    dims=(((ca,),(cb,)),((),()))
    ah,al=a; bh,bl=b
    d=lambda x,y: lax.dot_general(x,y,dims,preferred_element_type=jnp.float32)
    return d(ah,bh)+(d(ah,bl)+d(al,bh))
def dotf(a,b,ca,cb):
    return lax.dot_general(a,b,(((ca,),(cb,)),((),())),preferred_element_type=jnp.float32,precision=lax.Precision.HIGHEST)

def in_groups(count,step,body):
    step=math.gcd(count,step)
    def run(i,_):
        for k in range(step): body(i*step+k)
        return 0
    lax.fori_loop(0,count//step,run,0)

PANEL=32
def soap_kernel(slots,g_ref,m_ref,v_ref,l_ref,r_ref,ql_ref,qr_ref,w_ref,vm_ref,vs_ref,vw_ref,pa,pb, oa,ob,mo,vo,lo,ro,qlo,qro,wo,vmo,vso,vwo, x_ref, a_ref, b_ref, f_ref, psem):
    passed=[pltpu.make_async_copy(pa,oa,psem.at[0]),pltpu.make_async_copy(pb,ob,psem.at[1])]
    for copy in passed: copy.start()
    width=vm_ref.shape[1]
    vmo[...],vso[...],vwo[...]=adam_vector(g_ref[slots*BLK:slots*BLK+1,:width],vm_ref[...],vs_ref[...],vw_ref[...])
    def first(i):
        g=g_ref[pl.ds(pl.multiple_of(i*BLK,BLK),BLK),:]; ql=split(ql_ref[i]); qr=split(qr_ref[i])
        gs=split(g)
        m=BETA_ONE*m_ref[i]+(1-BETA_ONE)*g
        mo[i]=m
        def turn(v):
            return dot3(split(dot3(ql,v,0,0)),qr,1,0)
        tg=turn(gs)
        v=BETA_TWO*v_ref[i]+(1-BETA_TWO)*tg*tg
        vo[i]=v
        d=turn(split(m))/(1-BETA_ONE**STEP)/(jnp.sqrt(v/(1-BETA_TWO**STEP))+ADAM_EPSILON)
        u=dot3(split(dot3(ql,split(d),1,0)),qr,1,1)
        w=w_ref[i]
        wo[i]=w-RATE_MATRIX*(u+DECAY_WEIGHT*w)
        ln=BETA_STATS*l_ref[i]+(1-BETA_STATS)*dot3(gs,gs,1,1)
        rn=BETA_STATS*r_ref[i]+(1-BETA_STATS)*dot3(gs,gs,0,0)
        lo[i]=ln; ro[i]=rn
        al=dot3(split(ln),ql,1,0); ar=dot3(split(rn),qr,1,0)
        a_ref[2*i]=al; a_ref[2*i+1]=ar
        x_ref[2*i]=dotf(al,al,0,0); x_ref[2*i+1]=dotf(ar,ar,0,0)
    in_groups(slots,4,first)
    n=2*slots
    lane=lax.broadcasted_iota(jnp.int32,(8,BLK),1)
    sub=lax.broadcasted_iota(jnp.int32,(8,BLK),0)
    for p in range(BLK//8):
        end=(p*8//PANEL+1)*PANEL//8
        def step(kk,_):
            k=p*8+kk
            idx=jnp.full((8,BLK),k,jnp.int32)
            atk=lane==k
            below=sub>kk
            done=(lane<=k)|(lane>=end*8)
            rows=[jnp.broadcast_to(x_ref[m,pl.ds(k,1),:],(8,BLK)) for m in range(n)]
            fs=[jnp.take_along_axis(x_ref[m,p*8:(p+1)*8,:],idx,axis=1) for m in range(n)]
            for m in range(n): f_ref[m]=fs[m]
            rinv=[1.0/jnp.broadcast_to(f_ref[m,pl.ds(kk,1),:],(8,BLK)) for m in range(n)]
            scaled=[jnp.where(atk,1.0,row)*ri for row,ri in zip(rows,rinv)]
            for m in range(n):
                b_ref[m,pl.ds(k%PANEL,1),:]=jnp.where(done,scaled[m],0.0)[0:1,:]
                for t in range(p,end):
                    v=x_ref[m,t*8:(t+1)*8,:]
                    f=fs[m] if t==p else jnp.take_along_axis(v,idx,axis=1)
                    new=jnp.where(atk,0.0,v)-f*scaled[m]
                    if t==p: new=jnp.where(below,new,v)
                    x_ref[m,t*8:(t+1)*8,:]=new
            return 0
        lax.fori_loop(0,8,step,0)
        if (p+1)*8%PANEL==0 and p<BLK//8-1:
            lo_,hi_=(p+1)*8-PANEL,(p+1)*8
            keep=lax.broadcasted_iota(jnp.int32,(BLK-hi_,BLK),1)
            keep=(keep<lo_)|(keep>=hi_)
            def trail(m):
                u=dotf(x_ref[m,lo_:hi_,:],b_ref[m],0,0)
                x_ref[m,hi_:,:]=jnp.where(keep,x_ref[m,hi_:,:],0.0)-u[hi_:,:]
            in_groups(n,8,trail)
    r=lax.broadcasted_iota(jnp.int32,(BLK,BLK),0); c=lax.broadcasted_iota(jnp.int32,(BLK,BLK),1)
    def last(i):
        for s,out in ((0,qlo),(1,qro)):
            x=x_ref[2*i+s]
            piv=jnp.sum(jnp.where(r==c,x,0.0),axis=1,keepdims=True)
            inv=jnp.where(r==c,1.0,jnp.where(r>c,x,0.0))*lax.rsqrt(piv)
            out[i]=dot3(split(a_ref[2*i+s]),split(inv),1,1)
    in_groups(slots,4,last)
    for copy in passed: copy.wait()

def soap(g,m,v,l,r,ql,qr,w,vm,vs,vw,pa,pb):
    slots=m.shape[0]
    sh=jax.ShapeDtypeStruct((slots,BLK,BLK),jnp.float32); line=jax.ShapeDtypeStruct((1,vm.shape[0]),jnp.float32)
    space=pl.BlockSpec(memory_space=pltpu.VMEM)
    out=pl.pallas_call(partial(soap_kernel,slots),out_shape=[jax.ShapeDtypeStruct(e.shape,e.dtype) for e in (pa,pb)]+[sh]*7+[line]*3,in_specs=[space]*11+[ANY_SPEC]*2,out_specs=[ANY_SPEC]*2+[space]*10,
        scratch_shapes=[pltpu.VMEM((2*slots,BLK,BLK),jnp.float32)]*2+[pltpu.VMEM((2*slots,PANEL,BLK),jnp.float32),pltpu.VMEM((2*slots,8,BLK),jnp.float32),pltpu.SemaphoreType.DMA((2,))],
        compiler_params=pltpu.CompilerParams(vmem_limit_bytes=48<<20),name="soap")(g,m,v,l,r,ql,qr,w,vm[None],vs[None],vw[None],pa,pb)
    return tuple(out[:9])+tuple(o[0] for o in out[9:])

def inverse(owners):
    index=jnp.arange(owners.shape[0],dtype=jnp.int32)
    return jnp.sum(jnp.where(owners[:,None]==index[None,:],index[:,None],0),axis=0)

def local(tokens,cotangent,context_sizes,query_hoods,owners,master_blocks,first_blocks,second_blocks,left_blocks,right_blocks,
        left_bases,right_bases,vector_master,vector_moment,vector_square):
    dp=lax.axis_size("dp")
    rows=tokens.shape[0]; keys=rows-query_hoods.shape[0]; share=rows//HEADS; slots=master_blocks.shape[0]
    wall=gather_all(master_blocks,vector_master,dp,0)
    hoods=jnp.pad(query_hoods,(share-query_hoods.shape[0],0))
    layer_out,tokens_grad,g,extra=run_layers(owners,context_sizes,tokens,cotangent,wall,hoods[None,:],keys,slots,1)
    total=reduce_all(g,extra,inverse(owners),slots,2)
    return soap(total,first_blocks,second_blocks,left_blocks,right_blocks,left_bases,right_bases,master_blocks,
        vector_moment,vector_square,vector_master,layer_out,tokens_grad)


def solution(mesh):
    return jax.shard_map(
        local,
        mesh=mesh,
        in_specs=(
            P("dp", None),
            P("dp", None),
            P("dp", None),
            P("dp"),
            P(),
            P("dp", "mp", None),
            P("dp", "mp", None),
            P("dp", "mp", None),
            P("dp", "mp", None),
            P("dp", "mp", None),
            P("dp", "mp", None),
            P("dp", "mp", None),
            P(("dp", "mp")),
            P(("dp", "mp")),
            P(("dp", "mp")),
        ),
        out_specs=(
            P(("dp", "mp"), None),
            P(("dp", "mp"), None),
            P("dp", "mp", None),
            P("dp", "mp", None),
            P("dp", "mp", None),
            P("dp", "mp", None),
            P("dp", "mp", None),
            P("dp", "mp", None),
            P("dp", "mp", None),
            P(("dp", "mp")),
            P(("dp", "mp")),
            P(("dp", "mp")),
        ),
        check_vma=False,
    )
```

```python
import math
from functools import partial

import jax
import jax.numpy as jnp
from jax import lax
from jax.experimental import pallas as pl
from jax.experimental.pallas import tpu as pltpu
from jax.sharding import PartitionSpec as P

RATE_VECTOR = 0.6
def adam_vector(grad, first, second, weight):
    first_new = BETA_ONE * first + (1.0 - BETA_ONE) * grad
    second_new = BETA_TWO * second + (1.0 - BETA_TWO) * grad * grad
    weight_new = weight - RATE_VECTOR * (first_new / (1.0 - BETA_ONE**STEP)) / (
        jnp.sqrt(second_new / (1.0 - BETA_TWO**STEP)) + ADAM_EPSILON
    )
    return (first_new, second_new, weight_new)


MESH=pl.DeviceIdType.MESH
BLK=128
VMEM_SPEC=pl.BlockSpec(memory_space=pltpu.VMEM)
ANY_SPEC=pl.BlockSpec(memory_space=pl.ANY)

def remote(src,dst,send,recv,device):
    return pltpu.make_async_remote_copy(src_ref=src,dst_ref=dst,send_sem=send,recv_sem=recv,device_id=device,device_id_type=MESH)

class Spot:
    def __init__(self,planes):
        dp,mp=lax.axis_index("dp"),lax.axis_index("mp")
        self.dp,self.mp,self.planes=dp,mp,planes
        self.z,self.x=dp//2,dp%2
        self.y,self.c=mp//2,mp%2
        self.across_x=(dp+1-2*self.x,mp)
        self.across_y=(dp,(mp+2)%4)
        self.sibling=(dp,mp+1-2*self.c)
        self.y_sibling=3-mp
        self.up=(jnp.minimum(dp+2,2*planes-1),mp)
        self.down=(jnp.maximum(dp-2,0),mp)
    def greet(self):
        bar=pltpu.get_barrier_semaphore()
        for who in (self.across_x,self.across_y,self.sibling):
            pl.semaphore_signal(bar,inc=1,device_id=who,device_id_type=MESH)
        @pl.when(self.z<self.planes-1)
        def _(): pl.semaphore_signal(bar,inc=1,device_id=self.up,device_id_type=MESH)
        @pl.when(self.z>0)
        def _(): pl.semaphore_signal(bar,inc=1,device_id=self.down,device_id_type=MESH)
        return lambda: pl.semaphore_wait(bar,3+jnp.minimum(self.z,1)+jnp.minimum(self.planes-1-self.z,1))
    def ring(self,r,action):
        if r==0:
            action(self.z,None); return
        @pl.when(self.z>=r)
        def _(): action(self.z-r,True)
        @pl.when(self.z+r<self.planes)
        def _(): action(self.z+r,False)

def gather_kernel(planes,cuts,master,vector,out,slab,send,recv,zsend,zrecv,lsem,csend,crecv,zcsend,zcrecv,ccsend,ccrecv):
    s=Spot(planes); met=s.greet()
    for k in range(master.shape[0]): slab[k*BLK:(k+1)*BLK,:]=master[k].astype(slab.dtype)
    n=vector.shape[1]
    high=vector[...].astype(slab.dtype).astype(jnp.float32)
    pair=jnp.where(lax.broadcasted_iota(jnp.int32,(16,n),0)==0,high,vector[...]-high)
    if n<BLK: pair=jnp.concatenate([pair,jnp.zeros((16,BLK-n),jnp.float32)],axis=1)
    slab[master.shape[0]*BLK:,:]=pair.astype(slab.dtype)
    rows=slab.shape[0]; z,x,y,c,mp=s.z,s.x,s.y,s.c,s.mp
    A,B,AB,C=pl.ds(0,cuts[0]),pl.ds(cuts[0],cuts[1]-cuts[0]),pl.ds(0,cuts[1]),pl.ds(cuts[1],rows-cuts[1])
    mx,my=s.across_x,s.across_y
    own=pltpu.make_async_copy(slab,out.at[s.dp,mp],lsem); own.start()
    met()
    def at(p,xx,yy,cc): return out.at[p*2+xx,yy*2+cc]
    xo,yo=1-x,1-y
    def copies(p,src):
        here=at(p,x,y,c) if src is None else src
        f=lambda k,a,b,w: remote(a,b,send.at[k,p],recv.at[k,p],w)
        return dict(
            xown=lambda: f(0,here.at[AB],at(p,x,y,c).at[AB],mx), yown=lambda: f(1,here.at[AB],at(p,x,y,c).at[AB],my),
            cown=lambda: f(2,here.at[AB],at(p,x,y,c).at[AB],s.sibling),
            yfwd=lambda: f(3,at(p,xo,y,c).at[A],at(p,xo,y,c).at[A],my),
            xfwd=lambda: f(4,at(p,x,yo,c).at[B],at(p,x,yo,c).at[B],mx),
            cx=lambda: f(5,at(p,xo,y,c).at[AB],at(p,xo,y,c).at[AB],s.sibling), cy=lambda: f(6,at(p,x,yo,c).at[AB],at(p,x,yo,c).at[AB],s.sibling),
            ca=lambda: f(7,at(p,xo,yo,c).at[A],at(p,xo,yo,c).at[A],s.sibling),
            cb=lambda: f(8,at(p,xo,yo,c).at[B],at(p,xo,yo,c).at[B],s.sibling))
    def zcopy(p,up,src=None):
        here=at(p,x,y,c) if src is None else src
        return remote(here.at[AB],at(p,x,y,c).at[AB],zsend.at[0 if up else 1,p],zrecv.at[p],s.up if up else s.down)
    def onward(below,action):
        if below is None or below:
            @pl.when(z<planes-1)
            def _(): action(True)
        if below is None or not below:
            @pl.when(z>0)
            def _(): action(False)
    c_x=lambda: remote(slab.at[C],at(z,x,y,c).at[C],csend.at[0],crecv.at[0],mx)
    c_y=lambda: remote(slab.at[C],at(z,x,y,c).at[C],csend.at[1],crecv.at[1],my)
    c_xy=lambda: remote(at(z,xo,y,c).at[C],at(z,xo,y,c).at[C],csend.at[2],crecv.at[2],my)
    both=lambda p,yy: out.at[pl.ds(p*2,2),yy*2+c,C]
    c_z=lambda p,yy,up: remote(both(p,yy),both(p,yy),zcsend.at[0 if up else 1,p,yy],zcrecv.at[p,yy],s.up if up else s.down)
    c_c=lambda p,yy: remote(both(p,yy),both(p,yy),ccsend.at[p,yy],ccrecv.at[p,yy],s.sibling)
    def c_arrive(p,below):
        for yy in (0,1):
            if below is not None: c_z(p,yy,below).wait_recv()
            onward(below,lambda up: c_z(p,yy,up).start())
            c_c(p,yy).start()
    def arrive(r):
        def act(p,below):
            src=None
            if below is None: src=slab
            else: zcopy(p,below).wait_recv()
            onward(below,lambda up: zcopy(p,up,src).start())
            k=copies(p,src)
            k["xown"]().start(); k["yown"]().start(); k["cown"]().start()
        s.ring(r,act)
    def second(r):
        def act(p,below):
            k=copies(p,None)
            k["xown"]().wait_recv(); k["yfwd"]().start(); k["cx"]().start()
            k["yown"]().wait_recv(); k["xfwd"]().start(); k["cy"]().start()
        s.ring(r,act)
    def third(r):
        def act(p,below):
            k=copies(p,None)
            k["yfwd"]().wait_recv(); k["ca"]().start()
            k["xfwd"]().wait_recv(); k["cb"]().start()
        s.ring(r,act)
    def finish(r):
        def act(p,below):
            src=slab if below is None else None
            k=copies(p,src)
            for n in ("cown","cx","cy","ca","cb"): k[n]().wait_recv()
            for n in k: k[n]().wait_send()
            onward(below,lambda up: zcopy(p,up,src).wait_send())
            for yy in (0,1):
                onward(below,lambda up: c_z(p,yy,up).wait_send())
                remote(both(p,yy),out.at[pl.ds(p*2,2),yy*2+1-c,C],ccsend.at[p,yy],ccrecv.at[p,yy],s.sibling).wait_recv()
                c_c(p,yy).wait_send()
        s.ring(r,act)
    c_x().start(); c_y().start()
    for r in range(planes+2):
        if r<planes: arrive(r)
        if r==0:
            c_x().wait_recv(); c_xy().start()
        if r==1:
            c_y().wait_recv(); c_xy().wait_recv(); own.wait()
            c_arrive(z,None)
        if 1<=r<=planes: second(r-1)
        if 2<=r<=planes: s.ring(r-1,c_arrive)
        if r>=2: third(r-2)
    for r in range(planes): finish(r)
    for k in (c_x,c_y,c_xy): k().wait_send()

def gather_all(master,vector,dp,collective):
    rows=master.shape[0]*BLK+16; planes=dp//2
    last=rows-rows//5//16*16; cuts=(last//2//16*16,last)
    dma=pltpu.SemaphoreType.DMA
    return pl.pallas_call(partial(gather_kernel,planes,cuts),
        out_shape=jax.ShapeDtypeStruct((dp,4,rows,BLK),jnp.bfloat16),
        in_specs=[VMEM_SPEC,VMEM_SPEC],out_specs=ANY_SPEC,
        scratch_shapes=[pltpu.VMEM((rows,BLK),jnp.bfloat16),dma((9,planes)),dma((9,planes)),dma((2,planes)),dma((planes,)),dma,
            dma((3,)),dma((3,)),dma((2,planes,2)),dma((planes,2)),dma((planes,2)),dma((planes,2))],
        compiler_params=pltpu.CompilerParams(collective_id=collective,has_side_effects=True),name="gather_all")(master,vector[None,:])

def reduce_kernel(planes,cuts,slots,source,inner,extra,out,theirs,mine,lsem,g,rc,acc,ya,xb,xa,yb,own,zin,send,recv,zsend,zrecv,zc,cy,cx,csum,zcs,zcr,cs,cr):
    s=Spot(planes); rows=g.shape[2]; half,last=cuts; z,x,y,c,mp=s.z,s.x,s.y,s.c,s.mp
    A,B,AB,C=pl.ds(0,half),pl.ds(half,last-half),pl.ds(0,last),pl.ds(last,rows-last)
    mx,my=s.across_x,s.across_y
    xo,yo,co=1-x,1-y,1-c
    bring=lambda held,k,parity: pltpu.make_async_copy(source.at[:,k*2+parity],held.at[:,k],lsem.at[k*2+parity])
    for held,parity in ((theirs,co),(mine,c)):
        for k in (0,1): bring(held,k,parity).start()
    s.greet()()
    f32=lambda v: v.astype(jnp.float32)
    def core(p,xx,yy):
        k=xx*2+yy
        return remote(g.at[p*2+xx,yy*2+co],rc.at[p*4+k],send.at[k,p],recv.at[k,p],s.sibling)
    def toya(p,xx): return remote(acc.at[p*4+xx*2+yo,A],ya.at[p*2+xx],send.at[4+xx,p],recv.at[4+xx,p],my)
    def toxb(p,yy): return remote(acc.at[p*4+xo*2+yy,B],xb.at[p*2+yy],send.at[6+yy,p],recv.at[6+yy,p],mx)
    def toxa(p): return remote(ya.at[p*2+xo],xa.at[p],send.at[8,p],recv.at[8,p],mx)
    def toyb(p): return remote(xb.at[p*2+yo],yb.at[p],send.at[9,p],recv.at[9,p],my)
    def toz(p,up): return remote(own.at[p],zin.at[0 if up else 1,p],zsend.at[p],zrecv.at[0 if up else 1,p],s.up if up else s.down)
    def pack(p,parity,held):
        for xx in (0,1):
            d=p*2+xx
            def one(k,_):
                block=inner[0,d*slots+k]
                for yy in (0,1):
                    g[d,yy*2+parity,pl.ds(pl.multiple_of(k*BLK,BLK),BLK),:]=held[block,yy]
                return 0
            lax.fori_loop(0,slots,one,0)
            for yy in (0,1): g[d,yy*2+parity,slots*BLK:,:]=extra[d,yy*2+parity]
    def start(p,_):
        pack(p,co,theirs)
        for xx in (0,1):
            for yy in (0,1): core(p,xx,yy).start()
    def first(p,_):
        pack(p,c,mine)
        for xx in (0,1):
            for yy in (0,1):
                core(p,xx,yy).wait_recv()
                acc[p*4+xx*2+yy]=(f32(g[p*2+xx,yy*2+c])+f32(rc[p*4+xx*2+yy])).astype(acc.dtype)
        for e in (0,1): toya(p,e).start(); toxb(p,e).start()
    def second(p,_):
        for e in (0,1):
            toya(p,e).wait_recv()
            ya[p*2+e]=(f32(acc[p*4+e*2+y,A])+f32(ya[p*2+e])).astype(ya.dtype)
        toxa(p).start()
        for e in (0,1):
            toxb(p,e).wait_recv()
            xb[p*2+e]=(f32(acc[p*4+x*2+e,B])+f32(xb[p*2+e])).astype(xb.dtype)
        toyb(p).start()
    def third(p,below):
        toxa(p).wait_recv()
        av=f32(ya[p*2+x])+f32(xa[p])
        toyb(p).wait_recv()
        bv=f32(xb[p*2+y])+f32(yb[p])
        if below is None:
            out[A]=av; out[B]=bv
            @pl.when(z>0)
            def _():
                toz(p,True).wait_recv()
                out[AB]=out[AB]+f32(zin[0,p])
            @pl.when(z<planes-1)
            def _():
                toz(p,False).wait_recv()
                out[AB]=out[AB]+f32(zin[1,p])
            return
        own[p,A]=av.astype(own.dtype); own[p,B]=bv.astype(own.dtype)
        up=not below
        has=(z>0) if up else (z<planes-1)
        @pl.when(has)
        def _():
            toz(p,up).wait_recv()
            own[p,A]=(av+f32(zin[0 if up else 1,p,A])).astype(own.dtype)
            own[p,B]=(bv+f32(zin[0 if up else 1,p,B])).astype(own.dtype)
        toz(p,up).start()
    toc=lambda p,up: remote(acc.at[pl.ds(p*4,4),C],zc.at[0 if up else 1,p],zcs.at[p],zcr.at[0 if up else 1,p],s.up if up else s.down)
    cyc=lambda xx: remote(acc.at[z*4+xx*2+yo,C],cy.at[xx],cs.at[xx],cr.at[xx],my)
    cxc=lambda: remote(csum.at[xo],cx,cs.at[2],cr.at[2],mx)
    def c_take(p,up):
        @pl.when((z>0) if up else (z<planes-1))
        def _():
            toc(p,up).wait_recv()
            for k in range(4):
                acc[p*4+k,C]=(f32(acc[p*4+k,C])+f32(zc[0 if up else 1,p,k])).astype(acc.dtype)
    def c_stage(p,below):
        if below is None:
            c_take(p,True); c_take(p,False)
            for xx in (0,1): cyc(xx).start()
            return
        c_take(p,not below)
        toc(p,not below).start()
    def c_across():
        for xx in (0,1):
            cyc(xx).wait_recv()
            csum[xx]=(f32(acc[z*4+xx*2+y,C])+f32(cy[xx])).astype(csum.dtype)
        cxc().start()
    def c_end():
        cxc().wait_recv()
        out[C]=f32(csum[x])+f32(cx[...])
    def finish(p,below):
        for xx in (0,1):
            for yy in (0,1): core(p,xx,yy).wait_send()
        for e in (0,1): toya(p,e).wait_send(); toxb(p,e).wait_send()
        toxa(p).wait_send(); toyb(p).wait_send()
        if below is not None:
            toz(p,not below).wait_send(); toc(p,not below).wait_send()
    order=list(range(planes-1,-1,-1))
    for k in (0,1): bring(theirs,k,co).wait()
    for r in order: s.ring(r,start)
    for k in (0,1): bring(mine,k,c).wait()
    n=len(order)
    for i in range(n+2):
        if i<n: s.ring(order[i],first)
        if 0<=i-1<n:
            s.ring(order[i-1],second)
            s.ring(order[i-1],c_stage)
        if i==n+1: c_across()
        if 0<=i-2<n: s.ring(order[i-2],third)
    c_end()
    for r in order: s.ring(r,finish)
    cyc(0).wait_send(); cyc(1).wait_send(); cxc().wait_send()

def reduce_all(g,extra,inner,slots,collective):
    dp=extra.shape[0]; rows,cols=slots*BLK+extra.shape[2],g.shape[3]; planes=dp//2; last=rows-rows//5//16*16; half=last//2//16*16; part=rows-last
    dma=pltpu.SemaphoreType.DMA; bf=lambda *sh: pltpu.VMEM(sh+(cols,),g.dtype)
    return pl.pallas_call(partial(reduce_kernel,planes,(half,last),slots),
        out_shape=jax.ShapeDtypeStruct((rows,cols),jnp.float32),in_specs=[ANY_SPEC,pl.BlockSpec(memory_space=pltpu.SMEM),VMEM_SPEC],out_specs=VMEM_SPEC,
        scratch_shapes=[pltpu.VMEM((g.shape[0],2)+g.shape[2:],g.dtype)]*2+[dma((4,)),bf(dp,4,rows),bf(planes*4,rows),bf(planes*4,rows),bf(planes*2,half),bf(planes*2,last-half),bf(planes,half),bf(planes,last-half),
            bf(planes,last),bf(2,planes,last),dma((10,planes)),dma((10,planes)),dma((planes,)),dma((2,planes)),
            bf(2,planes,4,part),bf(2,part),bf(part),bf(2,part),dma((planes,)),dma((2,planes)),dma((3,)),dma((3,))],
        compiler_params=pltpu.CompilerParams(collective_id=collective,has_side_effects=True,vmem_limit_bytes=56<<20),name="reduce_all")(g,inner,extra)
D=512; HD=128; FF=1024; LAYERS=2; BLK=128; HEADS=4
NORM_EPSILON=1e-5; MASK_VALUE=-1e30
f32=jnp.float32; bf16=jnp.bfloat16
SMEM_SPEC=pl.BlockSpec(memory_space=pltpu.SMEM)
SCALE=HD**-0.5; LOG2E=math.log2(math.e)
ROOT=math.sqrt(2/math.pi)

def nn(a,b): return lax.dot_general(a,b,(((1,),(0,)),((),())),preferred_element_type=f32)
def nt(a,b): return lax.dot_general(a,b,(((1,),(1,)),((),())),preferred_element_type=f32)
def tn(a,b): return lax.dot_general(a,b,(((0,),(0,)),((),())),preferred_element_type=f32)

def normed(r):
    center=r-jnp.mean(r,axis=-1,keepdims=True)
    rho=lax.rsqrt(jnp.mean(center*center,axis=-1,keepdims=True)+NORM_EPSILON)
    return center*rho,rho
def norm_back(dy,xhat,rho,gain):
    inner=dy*gain
    return rho*(inner-jnp.mean(inner,axis=-1,keepdims=True)-xhat*jnp.mean(inner*xhat,axis=-1,keepdims=True))
def gelu(v): return 0.5*v*(1+jnp.tanh(ROOT*(v+0.044715*v*v*v)))
def gelu_both(v):
    sq=v*v
    t=jnp.tanh(ROOT*v*(1+0.044715*sq))
    half=0.5*(1+t)
    return v*half,half+0.5*v*(1-t*t)*(ROOT*(1+3*0.044715*sq))
def colsum(v): return jnp.sum(v,axis=0,keepdims=True)

COLS_TILE=(3,4,2,4)
FIRST_BLOCK=(0,12,16,24)
LAYER_BLOCKS=32
CH=160
KB=320
FS=FF//HEADS

def rows_at(i,n): return pl.ds(pl.multiple_of(i*n,n),n)

class Weights:
    def __init__(self,refs): self.q,self.kv,self.out,self.up,self.down=refs
    def fill(self,layer,owners,wallv):
        base=layer*LAYER_BLOCKS
        def tiles(b):
            slot=owners[b]
            return [wallv[slot,j] for j in range(HEADS)]
        def by_row(r,_):
            rows=rows_at(r,BLK)
            for c in range(3):
                for j,v in enumerate(tiles(base+r*3+c)):
                    if c==0: self.q[rows,j*BLK:(j+1)*BLK]=v
                    else: self.kv[rows,j*2*BLK+(c-1)*BLK:j*2*BLK+c*BLK]=v
            for c in range(2):
                for j,v in enumerate(tiles(base+FIRST_BLOCK[2]+r*2+c)): self.up[rows,j*FS+c*BLK:j*FS+(c+1)*BLK]=v
            return 0
        lax.fori_loop(0,D//BLK,by_row,0)
        for c in range(4):
            for j,v in enumerate(tiles(base+FIRST_BLOCK[1]+c)): self.out[j*BLK:(j+1)*BLK,c*BLK:(c+1)*BLK]=v
            for r in range(2):
                for j,v in enumerate(tiles(base+FIRST_BLOCK[3]+r*4+c)): self.down[j*FS+r*BLK:j*FS+(r+1)*BLK,c*BLK:(c+1)*BLK]=v

def key_of(j): return slice(j*2*HD,j*2*HD+HD)
def value_of(j): return slice(j*2*HD+HD,(j+1)*2*HD)

def project(w,h_full,KV,rows): KV[rows,:]=nn(h_full[rows,:],w.kv[...]).astype(bf16)

def queries(w,h_full,start,q):
    def one(i,_):
        q[rows_at(i,CH),:]=nn(h_full[pl.ds(pl.multiple_of(start+i*CH,CH),CH),:],w.q[...]).astype(bf16)
        return 0
    lax.fori_loop(0,q.shape[0]//CH,one,0)

def forward(w,gains,own_rows,KV,q,heads,lse,bias,hidden,r1,r2,emit):
    keys=KV.shape[0]; chunks=q.shape[0]//CH
    lane=lax.broadcasted_iota(jnp.int32,(CH,BLK),1)
    def attend(i,_):
        rows=rows_at(i,CH)
        stats=jnp.zeros((CH,BLK),f32)
        scores=lambda j: nt(q[rows,j*HD:(j+1)*HD],KV[:,key_of(j)])
        s=scores(0)
        for j in range(HEADS):
            later=scores(j+1) if j+1<HEADS else None
            s=s+bias[rows,:].astype(f32)
            peak=jnp.max(s,axis=1,keepdims=True)
            p=jnp.exp2((s-peak)*(SCALE*LOG2E))
            total=jnp.sum(p,axis=1,keepdims=True)
            o=nn(p.astype(bf16),KV[:,value_of(j)])/total
            heads[rows,j*HD:(j+1)*HD]=o.astype(bf16)
            stats=jnp.where(lane==j,peak*(SCALE*LOG2E)+jnp.log2(total),stats)
            s=later
        lse[rows,:]=stats
        a=own_rows(i)+nn(heads[rows,:],w.out[...])
        r1[rows,:]=a
        first=normed(a)[0]*gains[0:1,:]+gains[1:2,:]
        hid=nn(first.astype(bf16),w.up[...])
        hidden[rows,:]=hid
        b=first+nn(gelu(hid).astype(bf16),w.down[...])
        r2[rows,:]=b
        emit(i,normed(b)[0]*gains[2:3,:]+gains[3:4,:])
        return 0
    lax.fori_loop(0,chunks,attend,0)

def backward(w,gains,start,h_full,upper,KV,q,heads,lse,biasT,hidden,r1,r2,
        dm,act,dhid,first,datt,dheads,delta,grad,dq,dqa,dhp,vec,put,exchange):
    share=q.shape[0]; keys=KV.shape[0]; chunks=share//CH
    lane=lax.broadcasted_iota(jnp.int32,(CH,BLK),1)
    def part(i,carry):
        rows=rows_at(i,CH)
        dy=upper(i)
        xhat,rho=normed(r2[rows,:])
        g2,s2=colsum(dy*xhat),colsum(dy)
        sg=norm_back(dy,xhat,rho,gains[2:3,:])
        dmb=sg.astype(bf16); dm[rows,:]=dmb
        a,slope=gelu_both(hidden[rows,:])
        act[rows,:]=a.astype(bf16)
        dh=(nt(dmb,w.down[...])*slope).astype(bf16)
        dhid[rows,:]=dh
        fu=sg+nt(dh,w.up[...])
        xhat,rho=normed(r1[rows,:])
        first[rows,:]=(xhat*gains[0:1,:]+gains[1:2,:]).astype(bf16)
        g1,s1=colsum(fu*xhat),colsum(fu)
        f=norm_back(fu,xhat,rho,gains[0:1,:])
        grad[rows,:]=f
        fb=f.astype(bf16); datt[rows,:]=fb
        dhe=nt(fb,w.out[...]).astype(bf16)
        dheads[rows,:]=dhe
        prod=dhe.astype(f32)*heads[rows,:].astype(f32)
        stats=jnp.zeros((CH,BLK),f32)
        for j in range(HEADS):
            stats=jnp.where(lane==j,jnp.sum(prod[:,j*HD:(j+1)*HD],axis=1,keepdims=True),stats)
        delta[rows,:]=stats
        return tuple(c+v for c,v in zip(carry,(g1,s1,g2,s2)))
    zero=jnp.zeros((1,D),f32)
    for k,v in enumerate(lax.fori_loop(0,chunks,part,(zero,)*4)): vec(k,v)
    lseT=jnp.transpose(lse[...]); deltaT=jnp.transpose(delta[...])
    dqa[...]=jnp.zeros(dqa.shape,f32)
    blocks=keys//KB
    def nth(t): return lax.rem(exchange.lead+t,blocks)
    def keyblock(t,_):
        kb=nth(t)
        rows=rows_at(kb,KB)
        head=lambda j: slice(j*HD,(j+1)*HD)
        both=lambda j: (nt(KV[rows,key_of(j)],q[:,head(j)]),nt(KV[rows,value_of(j)],dheads[:,head(j)]))
        now=both(0)
        for j in range(HEADS):
            later=both(j+1) if j+1<HEADS else None
            s,dp=now
            p=jnp.exp2((s+biasT[rows,:].astype(f32))*(SCALE*LOG2E)-lseT[j:j+1,:])
            ds=(p*(dp-deltaT[j:j+1,:])).astype(bf16)
            dqa[head(j),:]+=tn(KV[rows,key_of(j)],ds)
            dv=nn(p.astype(bf16),dheads[:,head(j)])
            dk=nn(ds,q[:,head(j)])*SCALE
            KV[rows,key_of(j)]=dk.astype(bf16)
            KV[rows,value_of(j)]=dv.astype(bf16)
            now=later
        dhp[rows,:]=nt(KV[rows,:],w.kv[...]).astype(bf16)
        for sub in range(KB//CH): exchange.send(kb*(KB//CH)+sub)
        @pl.when(t>0)
        def _():
            for sub in range(KB//CH): exchange.turn(nth(t-1)*(KB//CH)+sub)
        return 0
    lax.fori_loop(0,blocks,keyblock,0)
    dq[...]=(jnp.transpose(dqa[...])*SCALE).astype(bf16)
    def own(i,_):
        rows=rows_at(i,CH)
        grad[rows,:]=grad[rows,:]+nt(dq[rows,:],w.q[...])
        return 0
    lax.fori_loop(0,chunks,own,0)
    def tiles(value,place):
        value=value.astype(bf16)
        for r in range(value.shape[0]//BLK):
            for c in range(value.shape[1]//BLK):
                put(*place(r,c),value[r*BLK:(r+1)*BLK,c*BLK:(c+1)*BLK])
    tiles(tn(act[...],dm[...]),lambda r,c: (FIRST_BLOCK[3]+r%2*4+c,r//2))
    for sub in range(KB//CH): exchange.turn(nth(blocks-1)*(KB//CH)+sub)
    tiles(tn(first[...],dhid[...]),lambda r,c: (FIRST_BLOCK[2]+r*2+c%2,c//2))
    tiles(tn(heads[...],datt[...]),lambda r,c: (FIRST_BLOCK[1]+c,r))
    tiles(tn(h_full[pl.ds(pl.multiple_of(start,CH),share),:],dq[...]),lambda r,c: (r*3,c))
    tiles(tn(h_full[:keys,:],KV[...]),lambda r,c: (r*3+1+c%2,c//2))
    exchange.finish()

class Exchange:
    def __init__(self,s,terms,grad,rc,acc,ry,send,recv,count):
        self.s,self.terms,self.grad,self.rc,self.acc,self.ry,self.count=s,terms,grad,rc,acc,ry,count
        self.n=send.shape[1]
        self.lead=jnp.where(s.y==0,2*self.n//(KB//CH),0)
        at=lambda k,i: rows_at(k*self.n+i,CH)
        self.at=at
        co=1-s.c
        self.a=lambda i: remote(terms.at[at((1-s.y)*2+co,i)],rc.at[0,rows_at(i,CH)],send.at[0,i],recv.at[0,i],s.sibling)
        self.b=lambda i: remote(terms.at[at(s.y*2+co,i)],rc.at[1,rows_at(i,CH)],send.at[1,i],recv.at[1,i],s.sibling)
        self.o=lambda i: remote(acc.at[rows_at(i,CH)],ry.at[rows_at(i,CH)],send.at[2,i],recv.at[2,i],s.across_y)
    def owner(self,b):
        o=b//self.n
        return o//2==self.s.y,o%2==self.s.c,b%self.n
    def send(self,b):
        y,c,i=self.owner(b)
        @pl.when(jnp.logical_not(c)&jnp.logical_not(y))
        def _(): self.a(i).start()
        @pl.when(jnp.logical_not(c)&y)
        def _(): self.b(i).start()
    def turn(self,b):
        y,c,i=self.owner(b)
        @pl.when(c&jnp.logical_not(y))
        def _():
            self.a(i).wait_recv()
            rows=rows_at(i,CH)
            self.acc[rows,:]=(self.terms[rows_at(b,CH),:].astype(f32)+self.rc[0,rows,:].astype(f32)).astype(bf16)
            self.o(i).start()
    def finish(self):
        s=self.s
        for i in range(self.n):
            rows=pl.ds(i*CH,CH)
            @pl.when(s.mp*self.n+i<self.count)
            def _():
                self.b(i).wait_recv()
                t=self.grad[rows]+(self.terms[self.at(s.mp,i)].astype(f32)+self.rc[1,rows].astype(f32))
                self.o(i).wait_recv()
                self.grad[rows]=t+self.ry[rows].astype(f32)
        for i in range(self.n):
            @pl.when(((1-s.y)*2+1-s.c)*self.n+i<self.count)
            def _(): self.a(i).wait_send()
            @pl.when((s.y*2+1-s.c)*self.n+i<self.count)
            def _(): self.b(i).wait_send()
            @pl.when(((1-s.y)*2+s.c)*self.n+i<self.count)
            def _(): self.o(i).wait_send()

def layers_kernel(slots,owners,sizes,tokens,cot,wall,qline, layer_out,tokens_grad,g,extra,inner,
        more,gains,vec,wallv,tok,h2,cotv,KV1,KV2,q1,q2,heads1,heads2,lse1,lse2,hid1,hid2,ra1,ra2,rb1,rb2,bias,biasT,
        dm,act,dhid,first,datt,dheads,delta,dq,dqa,dhp,rc,acc,ry,wa,wb,wc,wd,we,xa,xb,xc,xd,xe,lsem,ssend,srecv,tsend,trecv):
    s=Spot(1); mp=s.mp; share=q1.shape[0]; keys=KV1.shape[0]; chunks=share//CH
    start=mp*share
    def bring(k,_):
        pltpu.make_async_copy(wall.at[k//slots,:,rows_at(k%slots,BLK),:],wallv.at[k],lsem.at[1]).start()
        return 0
    lax.fori_loop(0,wallv.shape[0],bring,0)
    loads=[pltpu.make_async_copy(tokens,tok,lsem.at[0]),pltpu.make_async_copy(wallv,wallv,lsem.at[1]),
           pltpu.make_async_copy(cot.at[pl.ds(pl.multiple_of(start,CH),share)],cotv,lsem.at[2])]
    loads.append(pltpu.make_async_copy(wall.at[:,:,pl.ds(slots*BLK,wall.shape[2]-slots*BLK),:],more,lsem.at[5]))
    for c in (0,2,3): loads[c].start()
    bar=pltpu.get_barrier_semaphore()
    for who in (s.across_y,s.sibling): pl.semaphore_signal(bar,inc=1,device_id=who,device_id_type=MESH)
    ends=[]; total=jnp.int32(0)
    for k in range(sizes.shape[1]):
        total=total+sizes[0,k]; ends.append(total)
    def hood(index):
        h=jnp.zeros(index.shape,jnp.int32)
        for e in ends: h=h+(index>=e).astype(jnp.int32)
        return h
    def own_hood(index,queries):
        row=start+index
        return jnp.where(row<keys,hood(row),queries)
    key_line=hood(lax.broadcasted_iota(jnp.int32,(1,keys),1))
    row_line=own_hood(lax.broadcasted_iota(jnp.int32,(1,share),1),qline[...])
    slot=lax.broadcasted_iota(jnp.int32,inner.shape,1); held=jnp.zeros(inner.shape,jnp.int32)
    for b in range(inner.shape[1]): held=jnp.where(slot==owners[b],b,held)
    inner[...]=held
    column=jnp.transpose(jnp.broadcast_to(row_line.astype(f32),(8,share)))[:,0:1].astype(jnp.int32)
    def mask(i):
        rows=pl.ds(i*CH,CH)
        col=column[i*CH:(i+1)*CH,:]
        bias[rows,:]=jnp.where(col==key_line,0.0,MASK_VALUE).astype(bf16)
    for i in range(chunks): mask(i)
    def maskT(i,_):
        rows=rows_at(i,KB)
        col=hood(lax.broadcasted_iota(jnp.int32,(KB,1),0)+i*KB)
        biasT[rows,:]=jnp.where(col==row_line,0.0,MASK_VALUE).astype(bf16)
        return 0
    lax.fori_loop(0,keys//KB,maskT,0)
    w1,w2=Weights((wa,wb,wc,wd,we)),Weights((xa,xb,xc,xd,xe))
    loads[1].wait()
    w1.fill(0,owners,wallv)
    loads[0].wait()
    pl.semaphore_wait(bar,2)
    at=lambda k,i: pl.ds(pl.multiple_of(k*share+i*CH,CH),CH)
    far=s.across_y[1]
    over=lambda i: remote(h2.at[at(mp,i)],h2.at[at(mp,i)],ssend.at[0,i],srecv.at[0,i],s.across_y)
    near=lambda i: remote(h2.at[at(mp,i)],h2.at[at(mp,i)],ssend.at[1,i],srecv.at[1,i],s.sibling)
    on=lambda i: remote(h2.at[at(far,i)],h2.at[at(far,i)],ssend.at[2,i],srecv.at[2,i],s.sibling)
    loads[3].wait()
    n=LAYERS*4*D//(more.shape[0]*HEADS)
    for e in range(more.shape[0]*HEADS):
        pair=more[e//HEADS,e%HEADS].astype(f32)
        where=e*n
        gains[where//D:where//D+1,where%D:where%D+n]=(pair[0:1]+pair[1:2])[:,:n]
    g1,g2=gains[0:4],gains[4:8]
    def emit1(i,v):
        layer_out[rows_at(i,CH),:]=v
        h2[at(mp,i),:]=v.astype(bf16)
        over(i).start(); near(i).start()
    def every(kb,_):
        project(w1,tok,KV1,rows_at(kb,KB))
        return 0
    lax.fori_loop(0,keys//KB,every,0)
    queries(w1,tok,start,q1)
    forward(w1,g1,lambda i: tok[at(mp,i),:].astype(f32),KV1,q1,heads1,lse1,bias,hid1,ra1,rb1,emit1)
    w2.fill(1,owners,wallv)
    def arrived(k,i):
        @pl.when(k*chunks+i<keys//CH)
        def _(): project(w2,h2,KV2,at(k,i))
    for i in range(chunks): arrived(mp,i)
    queries(w2,h2,start,q2)
    for i in range(chunks):
        near(i).wait_recv(); arrived(s.sibling[1],i)
    for i in range(chunks):
        over(i).wait_recv(); on(i).start(); arrived(far,i)
    for i in range(chunks):
        on(i).wait_recv(); arrived(s.y_sibling,i)
    def emit2(i,v): layer_out[rows_at(i,CH),:]=v
    forward(w2,g2,lambda i: layer_out[rows_at(i,CH),:],KV2,q2,heads2,lse2,bias,hid2,ra2,rb2,emit2)
    for i in range(chunks):
        for k in (over,near,on): k(i).wait_send()
    def put(layer):
        def store(b,j,v):
            b=b+layer*LAYER_BLOCKS
            wallv[b,j]=v
        return store
    def keep(layer):
        def store(k,v): vec[layer*4+k:layer*4+k+1,:]=v
        return store
    loads[2].wait()
    half=wallv.shape[0]//2
    flush=[pltpu.make_async_copy(wallv.at[pl.ds(k*half,half)],g.at[pl.ds(k*half,half)],lsem.at[3+k]) for k in range(2)]
    backward(w2,g2,start,h2,lambda i: cotv[rows_at(i,CH),:].astype(f32),KV2,q2,heads2,lse2,biasT,hid2,ra2,rb2,
        dm,act,dhid,first,datt,dheads,delta,tokens_grad,dq,dqa,dhp,keep(1),put(1),Exchange(s,dhp,tokens_grad,rc.at[0],acc,ry.at[0],tsend.at[0],trecv.at[0],keys//CH))
    flush[1].start()
    backward(w1,g1,start,tok,lambda i: tokens_grad[rows_at(i,CH),:],KV1,q1,heads1,lse1,biasT,hid1,ra1,rb1,
        dm,act,dhid,first,datt,dheads,delta,tokens_grad,dq,dqa,dhp,keep(0),put(0),Exchange(s,dhp,tokens_grad,rc.at[1],acc,ry.at[1],tsend.at[1],trecv.at[1],keys//CH))
    flush[0].start()
    top=lax.broadcasted_iota(jnp.int32,(16,BLK),0)==0
    for e in range(more.shape[0]*HEADS):
        where=e*n
        row=vec[where//D:where//D+1,where%D:where%D+n]
        if n<BLK: row=jnp.concatenate([row,jnp.zeros((1,BLK-n),f32)],axis=1)
        extra[e//HEADS,e%HEADS]=jnp.where(top,row,0.0).astype(bf16)
    flush[1].wait(); flush[0].wait()

def run_layers(owners,sizes,tokens,cot,wall,qline,keys,slots,collective):
    rows=tokens.shape[0]; share=rows//HEADS; chunks=share//CH
    v=pltpu.VMEM; dma=pltpu.SemaphoreType.DMA; V_=VMEM_SPEC
    two=lambda shape,t: [v(shape,t)]*2
    weights=[v((D,D),bf16),v((D,HEADS*2*HD),bf16),v((D,D),bf16),v((D,FF),bf16),v((FF,D),bf16)]
    blocks=(LAYERS*LAYER_BLOCKS,HEADS,BLK,BLK)
    tail=(wall.shape[0],HEADS,wall.shape[2]-slots*BLK,BLK)
    scratch=[v(tail,bf16),v((LAYERS*4,D),f32),v((LAYERS*4,D),f32),v(blocks,bf16),v((rows,D),bf16),v((rows,D),bf16),v((share,D),bf16)]
    scratch+=two((keys,HEADS*2*HD),bf16)+two((share,D),bf16)+two((share,D),bf16)+two((share,BLK),f32)+two((share,FF),f32)+two((share,D),f32)+two((share,D),f32)
    scratch+=[v((share,keys),bf16),v((keys,share),bf16)]
    scratch+=[v((share,D),bf16),v((share,FF),bf16),v((share,FF),bf16),v((share,D),bf16),v((share,D),bf16),v((share,D),bf16),v((share,BLK),f32),v((share,D),bf16),v((D,share),f32)]
    scratch+=[v((rows,D),bf16),v((2,2,share,D),bf16),v((share,D),bf16),v((2,share,D),bf16)]+weights+weights
    scratch+=[dma((6,)),dma((3,chunks)),dma((3,chunks)),dma((2,3,chunks)),dma((2,3,chunks))]
    shape=jax.ShapeDtypeStruct
    return pl.pallas_call(partial(layers_kernel,slots),
        out_shape=[shape((share,D),f32),shape((share,D),f32),shape(blocks,bf16),shape(tail,bf16),shape((1,blocks[0]),jnp.int32)],
        in_specs=[SMEM_SPEC,SMEM_SPEC,ANY_SPEC,ANY_SPEC,ANY_SPEC,V_],out_specs=[V_,V_,ANY_SPEC,V_,V_],scratch_shapes=scratch,
        compiler_params=pltpu.CompilerParams(collective_id=collective,has_side_effects=True,vmem_limit_bytes=60<<20),name="layers")(
        owners,sizes,tokens,cot,wall,qline)
BLK=128; STEP=10
BETA_ONE=0.9; BETA_TWO=0.95; BETA_STATS=0.95; RATE_MATRIX=0.12; DECAY_WEIGHT=0.01; ADAM_EPSILON=1e-8

def split(x):
    hi=x.astype(jnp.bfloat16)
    return hi,(x-hi.astype(jnp.float32)).astype(jnp.bfloat16)
def dot3(a,b,ca,cb):
    dims=(((ca,),(cb,)),((),()))
    ah,al=a; bh,bl=b
    d=lambda x,y: lax.dot_general(x,y,dims,preferred_element_type=jnp.float32)
    return d(ah,bh)+(d(ah,bl)+d(al,bh))
def dotf(a,b,ca,cb):
    return lax.dot_general(a,b,(((ca,),(cb,)),((),())),preferred_element_type=jnp.float32,precision=lax.Precision.HIGHEST)

def in_groups(count,step,body):
    step=math.gcd(count,step)
    def run(i,_):
        for k in range(step): body(i*step+k)
        return 0
    lax.fori_loop(0,count//step,run,0)

PANEL=32
def soap_kernel(slots,g_hbm,m_ref,v_ref,l_ref,r_ref,ql_ref,qr_ref,w_ref,vm_ref,vs_ref,vw_ref,pa,pb, oa,ob,mo,vo,lo,ro,qlo,qro,wo,vmo,vso,vwo, x_ref, a_ref, b_ref, f_ref, psem, g_ref):
    arrive=pltpu.make_async_copy(g_hbm,g_ref,psem.at[2]); arrive.start()
    passed=[pltpu.make_async_copy(pa,oa,psem.at[0]),pltpu.make_async_copy(pb,ob,psem.at[1])]
    for copy in passed: copy.start()
    arrive.wait()
    width=vm_ref.shape[1]
    vmo[...],vso[...],vwo[...]=adam_vector(g_ref[slots*BLK:slots*BLK+1,:width],vm_ref[...],vs_ref[...],vw_ref[...])
    def first(i):
        g=g_ref[pl.ds(pl.multiple_of(i*BLK,BLK),BLK),:]; ql=split(ql_ref[i]); qr=split(qr_ref[i])
        gs=split(g)
        m=BETA_ONE*m_ref[i]+(1-BETA_ONE)*g
        mo[i]=m
        def turn(v):
            return dot3(split(dot3(ql,v,0,0)),qr,1,0)
        tg=turn(gs)
        v=BETA_TWO*v_ref[i]+(1-BETA_TWO)*tg*tg
        vo[i]=v
        d=turn(split(m))/(1-BETA_ONE**STEP)/(jnp.sqrt(v/(1-BETA_TWO**STEP))+ADAM_EPSILON)
        u=dot3(split(dot3(ql,split(d),1,0)),qr,1,1)
        w=w_ref[i]
        wo[i]=w-RATE_MATRIX*(u+DECAY_WEIGHT*w)
        ln=BETA_STATS*l_ref[i]+(1-BETA_STATS)*dot3(gs,gs,1,1)
        rn=BETA_STATS*r_ref[i]+(1-BETA_STATS)*dot3(gs,gs,0,0)
        lo[i]=ln; ro[i]=rn
        al=dot3(split(ln),ql,1,0); ar=dot3(split(rn),qr,1,0)
        a_ref[2*i]=al; a_ref[2*i+1]=ar
        x_ref[2*i]=dotf(al,al,0,0); x_ref[2*i+1]=dotf(ar,ar,0,0)
    in_groups(slots,4,first)
    n=2*slots
    lane=lax.broadcasted_iota(jnp.int32,(8,BLK),1)
    sub=lax.broadcasted_iota(jnp.int32,(8,BLK),0)
    for p in range(BLK//8):
        end=(p*8//PANEL+1)*PANEL//8
        def step(kk,_):
            k=p*8+kk
            idx=jnp.full((8,BLK),k,jnp.int32)
            atk=lane==k
            below=sub>kk
            done=(lane<=k)|(lane>=end*8)
            rows=[jnp.broadcast_to(x_ref[m,pl.ds(k,1),:],(8,BLK)) for m in range(n)]
            fs=[jnp.take_along_axis(x_ref[m,p*8:(p+1)*8,:],idx,axis=1) for m in range(n)]
            for m in range(n): f_ref[m]=fs[m]
            rinv=[1.0/jnp.broadcast_to(f_ref[m,pl.ds(kk,1),:],(8,BLK)) for m in range(n)]
            scaled=[jnp.where(atk,1.0,row)*ri for row,ri in zip(rows,rinv)]
            for m in range(n):
                b_ref[m,pl.ds(k%PANEL,1),:]=jnp.where(done,scaled[m],0.0)[0:1,:]
                for t in range(p,end):
                    v=x_ref[m,t*8:(t+1)*8,:]
                    f=fs[m] if t==p else jnp.take_along_axis(v,idx,axis=1)
                    new=jnp.where(atk,0.0,v)-f*scaled[m]
                    if t==p: new=jnp.where(below,new,v)
                    x_ref[m,t*8:(t+1)*8,:]=new
            return 0
        lax.fori_loop(0,8,step,0)
        if (p+1)*8%PANEL==0 and p<BLK//8-1:
            lo_,hi_=(p+1)*8-PANEL,(p+1)*8
            keep=lax.broadcasted_iota(jnp.int32,(BLK-hi_,BLK),1)
            keep=(keep<lo_)|(keep>=hi_)
            def trail(m):
                u=dotf(x_ref[m,lo_:hi_,:],b_ref[m],0,0)
                x_ref[m,hi_:,:]=jnp.where(keep,x_ref[m,hi_:,:],0.0)-u[hi_:,:]
            in_groups(n,8,trail)
    r=lax.broadcasted_iota(jnp.int32,(BLK,BLK),0); c=lax.broadcasted_iota(jnp.int32,(BLK,BLK),1)
    def last(i):
        for s,out in ((0,qlo),(1,qro)):
            x=x_ref[2*i+s]
            piv=jnp.sum(jnp.where(r==c,x,0.0),axis=1,keepdims=True)
            inv=jnp.where(r==c,1.0,jnp.where(r>c,x,0.0))*lax.rsqrt(piv)
            out[i]=dot3(split(a_ref[2*i+s]),split(inv),1,1)
    in_groups(slots,4,last)
    for copy in passed: copy.wait()

def soap(g,m,v,l,r,ql,qr,w,vm,vs,vw,pa,pb):
    slots=m.shape[0]
    sh=jax.ShapeDtypeStruct((slots,BLK,BLK),jnp.float32); line=jax.ShapeDtypeStruct((1,vm.shape[0]),jnp.float32)
    space=pl.BlockSpec(memory_space=pltpu.VMEM)
    out=pl.pallas_call(partial(soap_kernel,slots),out_shape=[jax.ShapeDtypeStruct(e.shape,e.dtype) for e in (pa,pb)]+[sh]*7+[line]*3,in_specs=[ANY_SPEC]+[space]*10+[ANY_SPEC]*2,out_specs=[ANY_SPEC]*2+[space]*10,
        scratch_shapes=[pltpu.VMEM((2*slots,BLK,BLK),jnp.float32)]*2+[pltpu.VMEM((2*slots,PANEL,BLK),jnp.float32),pltpu.VMEM((2*slots,8,BLK),jnp.float32),pltpu.SemaphoreType.DMA((3,)),pltpu.VMEM(g.shape,g.dtype)],
        compiler_params=pltpu.CompilerParams(vmem_limit_bytes=48<<20),name="soap")(g,m,v,l,r,ql,qr,w,vm[None],vs[None],vw[None],pa,pb)
    return tuple(out[:9])+tuple(o[0] for o in out[9:])

def local(tokens,cotangent,context_sizes,query_hoods,owners,master_blocks,first_blocks,second_blocks,left_blocks,right_blocks,
        left_bases,right_bases,vector_master,vector_moment,vector_square):
    dp=lax.axis_size("dp")
    rows=tokens.shape[0]; keys=rows-query_hoods.shape[0]; share=rows//HEADS; slots=master_blocks.shape[0]
    wall=gather_all(master_blocks,vector_master,dp,0)
    hoods=jnp.pad(query_hoods,(share-query_hoods.shape[0],0))
    layer_out,tokens_grad,g,extra,inner=run_layers(owners,context_sizes,tokens,cotangent,wall,hoods[None,:],keys,slots,1)
    total=reduce_all(g,extra,inner,slots,2)
    return soap(total,first_blocks,second_blocks,left_blocks,right_blocks,left_bases,right_bases,master_blocks,
        vector_moment,vector_square,vector_master,layer_out,tokens_grad)


def solution(mesh):
    return jax.shard_map(
        local,
        mesh=mesh,
        in_specs=(
            P("dp", None),
            P("dp", None),
            P("dp", None),
            P("dp"),
            P(),
            P("dp", "mp", None),
            P("dp", "mp", None),
            P("dp", "mp", None),
            P("dp", "mp", None),
            P("dp", "mp", None),
            P("dp", "mp", None),
            P("dp", "mp", None),
            P(("dp", "mp")),
            P(("dp", "mp")),
            P(("dp", "mp")),
        ),
        out_specs=(
            P(("dp", "mp"), None),
            P(("dp", "mp"), None),
            P("dp", "mp", None),
            P("dp", "mp", None),
            P("dp", "mp", None),
            P("dp", "mp", None),
            P("dp", "mp", None),
            P("dp", "mp", None),
            P("dp", "mp", None),
            P(("dp", "mp")),
            P(("dp", "mp")),
            P(("dp", "mp")),
        ),
        check_vma=False,
    )
```
